32 devices in a mesh: seq: 8 (over z, x), fsdp: 4 (over y, core).
Axes of the slice: x: 2, y: 2, z: 4, core: 2. Of those that a mesh axis runs over, the one named last changes fastest.
Arguments:
- tokens: bfloat16 [4, 8192, 1024], P('fsdp', 'seq'), may hold values from -6 to 6
- cotangent: bfloat16 [4, 8192, 1024], P('fsdp', 'seq'), may hold values from -6 to 6
- lengths: int32 [4], P('fsdp'), may hold values from 2048 to 8192, as said below
- triple_weight: float32 [1024, 3072], P('seq', 'fsdp'), may hold values from -0.1875 to 0.1875
- output_weight: float32 [1024, 1024], P('seq', 'fsdp'), may hold values from -6 to 6
- expand_weight: float32 [1024, 5248], P('seq', 'fsdp'), may hold values from -0.1875 to 0.1875
- shrink_weight: float32 [2624, 1024], P('fsdp', 'seq'), may hold values from -0.125 to 0.125
- norm_gains: float32 [2, 1024], replicated, may hold values from 0.5 to 1.5
- side_bases: float32 [4, 1024, 1024], P(None, 'seq'), may hold values from -1 to 1, as said below
- output_right: float32 [1024, 1024], P('fsdp'), may hold values from -1 to 1, as said below
- triple_first: float32 [1024, 3072], P('seq', 'fsdp'), may hold values from -28 to 28
- triple_second: float32 [1024, 3072], P('seq', 'fsdp'), may hold values from 409.6 to 1638.4
- output_first: float32 [1024, 1024], P('seq', 'fsdp'), may hold values from -2.5 to 2.5
- output_second: float32 [1024, 1024], P('seq', 'fsdp'), may hold values from 0.52 to 2
- expand_first: float32 [1024, 5248], P('seq', 'fsdp'), may hold values from -16 to 16
- expand_second: float32 [1024, 5248], P('seq', 'fsdp'), may hold values from 147.456 to 589.824
- shrink_first: float32 [2624, 1024], P('fsdp', 'seq'), may hold values from -28 to 28
- shrink_second: float32 [2624, 1024], P('fsdp', 'seq'), may hold values from 409.6 to 1638.4
- gains_first: float32 [2, 1024], replicated, may hold values from -32 to 32
- gains_second: float32 [2, 1024], replicated, may hold values from 589.824 to 2359.296
Outputs:
- mixed: bfloat16 [4, 8192, 1024], P('fsdp', 'seq')
- token_gradient: bfloat16 [4, 8192, 1024], P('fsdp', 'seq')
- triple_gradient: float32 [1024, 3072], P('seq', 'fsdp')
- output_gradient: float32 [1024, 1024], P('seq', 'fsdp')
- expand_gradient: float32 [1024, 5248], P('seq', 'fsdp')
- shrink_gradient: float32 [2624, 1024], P('fsdp', 'seq')
- gains_gradient: float32 [2, 1024], replicated
- triple_average: float32 [1024, 3072], P('seq', 'fsdp')
- triple_variance: float32 [1024, 3072], P('seq', 'fsdp')
- triple_updated: float32 [1024, 3072], P('seq', 'fsdp')
- triple_copy: bfloat16 [1024, 3072], P('seq', 'fsdp')
- output_average: float32 [1024, 1024], P('seq', 'fsdp')
- output_variance: float32 [1024, 1024], P('seq', 'fsdp')
- output_updated: float32 [1024, 1024], P('seq', 'fsdp')
- output_copy: bfloat16 [1024, 1024], P('seq', 'fsdp')
- expand_average: float32 [1024, 5248], P('seq', 'fsdp')
- expand_variance: float32 [1024, 5248], P('seq', 'fsdp')
- expand_updated: float32 [1024, 5248], P('seq', 'fsdp')
- expand_copy: bfloat16 [1024, 5248], P('seq', 'fsdp')
- shrink_average: float32 [2624, 1024], P('fsdp', 'seq')
- shrink_variance: float32 [2624, 1024], P('fsdp', 'seq')
- shrink_updated: float32 [2624, 1024], P('fsdp', 'seq')
- shrink_copy: bfloat16 [2624, 1024], P('fsdp', 'seq')
- gains_average: float32 [2, 1024], replicated
- gains_variance: float32 [2, 1024], replicated
- gains_updated: float32 [2, 1024], replicated
The draws below stay inside these ranges and needn't reach their ends.
Inputs may be any that keep to these rules, and one draw needn't show every extreme that they name: Row r holds one sequence in its first lengths[r] slots, the rest is padding; some row is full. `side_bases`: each of the four matrices is orthogonal. `output_right`: orthogonal.
All inputs are finite; a program needn't handle non-finite values.
Results may differ from the reference program's by a relative error of at most 0.028.
Values may be sent and summed in bfloat16 or wider, within the bound.
No kernel may reach another device: no remote copies, remote signals or barrier semaphores. Data moves between devices by JAX's collectives and lax.ppermute only.
A program may use at most 448 MiB of HBM per device.

```python
import math
import jax
import jax.numpy as jnp
from jax import lax

D = 1024
HEADS = 16
HEAD_DIM = 64
FF = 2624
ROW = 8192
LMIN = 2048
STEP = 10
ROWS = 4


def dense_basis(key, count, size):
    sign_key, order_key = jax.random.split(key)
    index = jnp.arange(size, dtype=jnp.float32)
    angle = jnp.pi * ((2.0 * index[None, :] + 1.0) * index[:, None]) / (2.0 * size)
    table = jnp.cos(angle) * jnp.sqrt(2.0 / size)
    table = jnp.where(index[:, None] == 0.0, table * jnp.sqrt(0.5), table)
    signs = jax.random.rademacher(sign_key, (count, 2, size), dtype=jnp.float32)
    orders = jax.vmap(lambda member: jax.random.permutation(member, size))(jax.random.split(order_key, count))
    shuffled = table[orders]
    return (signs[:, 0, :, None] * shuffled * signs[:, 1, None, :]).astype(jnp.float32)


def draw_lengths(key, part):
    key = jax.random.fold_in(key, 11)
    first_key, second_key = jax.random.split(key)
    drawn = jax.random.randint(first_key, (ROWS,), LMIN, ROW + 1)
    chosen = jax.random.randint(second_key, (), 0, ROWS)
    return jnp.where(jnp.arange(ROWS) == chosen, ROW, drawn).astype(jnp.int32)


def draw_side_bases(key, part):
    key = jax.random.fold_in(key, 5)
    return dense_basis(key, 4, D)


def draw_output_right(key, part):
    key = jax.random.fold_in(key, 7)
    return dense_basis(key, 1, D)[0]


def shard_levels(stream_key, extent, cuts, smallest, high):
    def one(axis_at, shards_of):
        steps = jax.random.uniform(jax.random.fold_in(jax.random.fold_in(stream_key, 6), axis_at), (shards_of,), jnp.float32, smallest / len(cuts), high / len(cuts))
        return jnp.repeat(jnp.exp(steps), extent[axis_at] // shards_of).reshape((-1,) + (1,) * (len(extent) - axis_at - 1))

    level = one(*cuts[0])
    for cut in cuts[1:]:
        level = level * one(*cut)
    return level


def scatter_about(stream_key, shape, scale, limit, cuts=(), kind=jnp.bfloat16):
    loudness = shard_levels(stream_key, shape, cuts, -0.22, 0.18) if cuts else 1.0
    array = jax.random.normal(stream_key, shape, jnp.float32) * scale * loudness
    return jnp.minimum(jnp.maximum(array, -limit), limit).astype(kind)


def setup_inputs(seed: int = 0) -> dict:
    key_of = jax.random.split(jax.random.key(seed), 21)
    tokens = scatter_about(key_of[0], (ROWS, ROW, D), 1.0, 6.0, ((0, 4), (1, 8)))
    cotangent = scatter_about(key_of[1], (ROWS, ROW, D), 1.0, 6.0, ((0, 4), (1, 8)))
    lengths = draw_lengths(jax.random.fold_in(key_of[20], 71), 0)
    triple_weight = scatter_about(key_of[3], (D, 3 * D), D ** -0.5, 0.1875, ((0, 8), (1, 4)), jnp.float32)
    output_weight = scatter_about(key_of[4], (D, D), (D * 8 // ROW) ** -0.5, 6.0, ((0, 8), (1, 4)), jnp.float32)
    expand_weight = scatter_about(key_of[5], (D, 2 * FF), D ** -0.5, 0.1875, ((0, 8), (1, 4)), jnp.float32)
    shrink_weight = scatter_about(key_of[6], (FF, D), FF ** -0.5, 0.125, ((0, 4), (1, 8)), jnp.float32)
    norm_gains = jnp.clip(1.0 + 0.1 * jax.random.normal(key_of[7], (2, D), jnp.float32), 0.5, 1.5)
    side_bases = draw_side_bases(jax.random.fold_in(key_of[20], 71), 0)
    output_right = draw_output_right(jax.random.fold_in(key_of[20], 71), 0)
    triple_first = scatter_about(key_of[10], (D, 3 * D), (0.025 * (ROWS * ROW) ** 0.5), 28.0, ((0, 8), (1, 4)), jnp.float32)
    triple_second = jnp.clip(jnp.exp(math.log(1638.4) - 1.3862944 * jax.random.uniform(key_of[11], (D, 3 * D), jnp.float32) ** shard_levels(key_of[11], (D, 3 * D), ((0, 8), (1, 4)), -0.2, 0.2)), 409.6, 1638.4)
    output_first = scatter_about(key_of[12], (D, D), (0.08 * ROWS ** 0.5), 2.5, ((0, 8), (1, 4)), jnp.float32)
    output_second = jnp.clip(jnp.exp(math.log(2.0) - 1.3470737 * jax.random.uniform(key_of[13], (D, D), jnp.float32) ** shard_levels(key_of[13], (D, D), ((0, 8), (1, 4)), -0.2, 0.2)), 0.52, 2.0)
    expand_first = scatter_about(key_of[14], (D, 2 * FF), (0.015 * (ROWS * ROW) ** 0.5), 16.0, ((0, 8), (1, 4)), jnp.float32)
    expand_second = jnp.clip(jnp.exp(math.log(589.824) - 1.3862944 * jax.random.uniform(key_of[15], (D, 2 * FF), jnp.float32) ** shard_levels(key_of[15], (D, 2 * FF), ((0, 8), (1, 4)), -0.2, 0.2)), 147.456, 589.824)
    shrink_first = scatter_about(key_of[16], (FF, D), (0.025 * (ROWS * ROW) ** 0.5), 28.0, ((0, 4), (1, 8)), jnp.float32)
    shrink_second = jnp.clip(jnp.exp(math.log(1638.4) - 1.3862944 * jax.random.uniform(key_of[17], (FF, D), jnp.float32) ** shard_levels(key_of[17], (FF, D), ((0, 4), (1, 8)), -0.2, 0.2)), 409.6, 1638.4)
    gains_first = scatter_about(key_of[18], (2, D), (0.03 * (ROWS * ROW) ** 0.5), 32.0, (), jnp.float32)
    gains_second = jnp.clip(jnp.exp(jax.random.uniform(key_of[19], (2, D), jnp.float32, math.log(589.824), math.log(2359.296))), 589.824, 2359.296)
    return {"tokens": tokens, "cotangent": cotangent, "lengths": lengths, "triple_weight": triple_weight, "output_weight": output_weight, "expand_weight": expand_weight, "shrink_weight": shrink_weight, "norm_gains": norm_gains, "side_bases": side_bases, "output_right": output_right, "triple_first": triple_first, "triple_second": triple_second, "output_first": output_first, "output_second": output_second, "expand_first": expand_first, "expand_second": expand_second, "shrink_first": shrink_first, "shrink_second": shrink_second, "gains_first": gains_first, "gains_second": gains_second}


ROPE_BASE = 160000.0
NORM_EPS = 1e-05
NEG_LARGE = -1e+30
BETA_ONE = 0.95
BETA_TWO = 0.95
ADAM_EPS = 1e-08
DECAY_RATE = 0.01
WEIGHT_RATES = (0.03, 1.0, 0.03, 0.03)
GAINS_RATE = 0.8
HIGHEST = lax.Precision.HIGHEST

@jax.custom_vjp
def low(v):
    return lax.optimization_barrier(v.astype(jnp.bfloat16)).astype(jnp.float32)

@jax.custom_vjp
def low_back(v):
    return v

def low_keep(v):
    return (low(v), None)

def low_pass(kept, grad):
    return (grad,)

def back_keep(v):
    return (v, None)

def back_low(kept, grad):
    return (low(grad),)
low.defvjp(low_keep, low_pass)
low_back.defvjp(back_keep, back_low)

def layer_norm(values, gain):
    centre = values - lax.optimization_barrier(jnp.mean(values, axis=-1, keepdims=True))
    spread = lax.optimization_barrier(jnp.mean(centre * centre, axis=-1, keepdims=True))
    return centre * lax.rsqrt(spread + NORM_EPS) * gain

def rotary_tables(position, head_size):
    halves = head_size // 2
    frequency = ROPE_BASE ** (-2.0 * jnp.arange(halves, dtype=jnp.float32) / head_size)
    angle = position.astype(jnp.float32)[:, None] * frequency[None, :]
    return (jnp.concatenate([jnp.cos(angle), jnp.cos(angle)], -1), jnp.concatenate([jnp.sin(angle), jnp.sin(angle)], -1))

def turn(values, cosine, sine):
    halves = values.shape[-1] // 2
    rolled = jnp.concatenate([-values[..., halves:], values[..., :halves]], -1)
    return values * cosine[:, None, :] + rolled * sine[:, None, :]

def row_forward(row_input, row_valid, params, cosine, sine):
    triple, output, expand, shrink, gains = params
    count = row_input.shape[0]
    first = low(layer_norm(row_input, gains[0]))
    joint = low_back(jnp.dot(first, low(triple), precision=HIGHEST))
    queries = low(turn(joint[:, :D].reshape(count, HEADS, HEAD_DIM), cosine, sine))
    keys = low(turn(joint[:, D:2 * D].reshape(count, HEADS, HEAD_DIM), cosine, sine))
    values = low(joint[:, 2 * D:].reshape(count, HEADS, HEAD_DIM))
    block = min(512, count)

    def attend_block(query_block):
        raw = jnp.einsum('qhd,khd->hqk', query_block, keys, precision=HIGHEST) * HEAD_DIM ** (-0.5)
        scores = low_back(raw)
        scores = jnp.where(row_valid[None, None, :] > 0, scores, NEG_LARGE)
        peak = lax.optimization_barrier(jnp.max(scores, axis=-1, keepdims=True))
        weights = jnp.exp(scores - peak)
        prob = weights / lax.optimization_barrier(jnp.sum(weights, axis=-1, keepdims=True))
        return jnp.einsum('hqk,khd->qhd', low(prob), values, precision=HIGHEST)
    blocks = queries.reshape(count // block, block, HEADS, HEAD_DIM)
    attend = lax.map(jax.checkpoint(attend_block), blocks).reshape(count, D)
    branch = low_back(jnp.dot(low(low_back(attend)), low(output), precision=HIGHEST))
    middle = row_input + branch
    second = low(layer_norm(middle, gains[1]))
    inner = low_back(jnp.dot(second, low(expand), precision=HIGHEST))
    hidden = low(jax.nn.gelu(inner[:, :FF], approximate=False) * inner[:, FF:])
    shrunk = low_back(jnp.dot(hidden, low(shrink), precision=HIGHEST))
    return (middle + shrunk) * row_valid[:, None]

def adam_step(rotated, first, second):
    average = BETA_ONE * first + (1.0 - BETA_ONE) * rotated
    variance = BETA_TWO * second + (1.0 - BETA_TWO) * rotated * rotated
    direction = average / (1.0 - BETA_ONE ** STEP) / (jnp.sqrt(variance / (1.0 - BETA_TWO ** STEP)) + ADAM_EPS)
    return (average, variance, direction)

def brief(values):
    return values.astype(jnp.bfloat16)

def mult(left, right):
    return jnp.dot(left, right, preferred_element_type=jnp.float32)

def reference(tokens, cotangent, lengths, triple_weight, output_weight, expand_weight, shrink_weight, norm_gains, side_bases, output_right, triple_first, triple_second, output_first, output_second, expand_first, expand_second, shrink_first, shrink_second, gains_first, gains_second):
    position = jnp.arange(ROW, dtype=jnp.int32)
    cosine, sine = rotary_tables(position, HEAD_DIM)
    valid = (position[None, :] < lengths[:, None]).astype(jnp.float32)
    inputs = tokens.astype(jnp.float32)
    weights = (triple_weight, output_weight, expand_weight, shrink_weight, norm_gains)

    def whole_layer(values, params):

        def one_row(pair):
            return row_forward(pair[0], pair[1], params, cosine, sine)
        return lax.map(jax.checkpoint(one_row), (values, valid))
    output, pullback = jax.vjp(whole_layer, inputs, weights)
    token_back, gradients = pullback(cotangent.astype(jnp.float32))
    triple_grad, output_grad, expand_grad, shrink_grad, gains_grad = gradients
    bases_low = brief(side_bases)
    right_low = brief(output_right)
    triple_turned = mult(bases_low[0].T, brief(triple_grad))
    output_left = mult(bases_low[1].T, brief(output_grad))
    output_turned = mult(brief(output_left), right_low)
    expand_turned = mult(bases_low[2].T, brief(expand_grad))
    shrink_turned = mult(brief(shrink_grad), bases_low[3])
    triple_average, triple_variance, triple_direction = adam_step(triple_turned, triple_first, triple_second)
    output_average, output_variance, output_direction = adam_step(output_turned, output_first, output_second)
    expand_average, expand_variance, expand_direction = adam_step(expand_turned, expand_first, expand_second)
    shrink_average, shrink_variance, shrink_direction = adam_step(shrink_turned, shrink_first, shrink_second)
    gains_average, gains_variance, gains_direction = adam_step(gains_grad, gains_first, gains_second)
    triple_back = mult(bases_low[0], brief(triple_direction))
    output_middle = brief(mult(brief(output_direction), right_low.T))
    output_back = mult(bases_low[1], output_middle)
    expand_back = mult(bases_low[2], brief(expand_direction))
    shrink_back = mult(brief(shrink_direction), bases_low[3].T)
    triple_updated = (triple_weight - WEIGHT_RATES[0] * triple_back) * (1.0 - WEIGHT_RATES[0] * DECAY_RATE)
    output_updated = (output_weight - WEIGHT_RATES[1] * output_back) * (1.0 - WEIGHT_RATES[1] * DECAY_RATE)
    expand_updated = (expand_weight - WEIGHT_RATES[2] * expand_back) * (1.0 - WEIGHT_RATES[2] * DECAY_RATE)
    shrink_updated = (shrink_weight - WEIGHT_RATES[3] * shrink_back) * (1.0 - WEIGHT_RATES[3] * DECAY_RATE)
    gains_updated = norm_gains - GAINS_RATE * gains_direction
    return (output.astype(jnp.bfloat16), token_back.astype(jnp.bfloat16), triple_grad, output_grad, expand_grad, shrink_grad, gains_grad, triple_average, triple_variance, triple_updated, triple_updated.astype(jnp.bfloat16), output_average, output_variance, output_updated, output_updated.astype(jnp.bfloat16), expand_average, expand_variance, expand_updated, expand_updated.astype(jnp.bfloat16), shrink_average, shrink_variance, shrink_updated, shrink_updated.astype(jnp.bfloat16), gains_average, gains_variance, gains_updated)
```

```python
import functools
import math

import jax
import jax.numpy as jnp
from jax import lax
from jax.experimental import pallas as pl
from jax.experimental.pallas import tpu as pltpu
from jax.sharding import Mesh
from jax.sharding import PartitionSpec as P

HEADS = 16
HEAD_DIM = 64
FF = 2624
STEP = 10


ROPE_BASE = 160000.0
NORM_EPS = 1e-05
NEG_LARGE = -1e30
BETA_ONE = 0.95
BETA_TWO = 0.95
ADAM_EPS = 1e-08
DECAY_RATE = 0.01
WEIGHT_RATES = (0.03, 1.0, 0.03, 0.03)
GAINS_RATE = 0.8


def layer_norm(values, gain):
    centre = values - jnp.mean(values, axis=-1, keepdims=True)
    spread = jnp.mean(centre * centre, axis=-1, keepdims=True)
    return centre * lax.rsqrt(spread + NORM_EPS) * gain


def rotary_tables(position):
    halves = HEAD_DIM // 2
    frequency = ROPE_BASE ** (-2.0 * jnp.arange(halves, dtype=jnp.float32) / HEAD_DIM)
    angle = frequency[:, None] * position.astype(jnp.float32)[None, :]
    return jnp.cos(angle), jnp.sin(angle)


def outer_sum(left, right):
    return lax.dot_general(
        left, right, (((0,), (0,)), ((), ())), preferred_element_type=jnp.float32
    )


def back_product(left, right):
    return lax.dot_general(
        left, right, (((1,), (1,)), ((), ())), preferred_element_type=jnp.float32
    )


def plain_product(left, right):
    return jnp.dot(left, right, preferred_element_type=jnp.float32)


NT = (((1,), (1,)), ((), ()))
SAFE_BOUND = 60.0
MASK = -1e30
VMEM_LIMIT = 60 * 1024 * 1024


def extra_rows(rows, length, size=HEAD_DIM):
    place = lax.broadcasted_iota(jnp.int32, (size, length), 0)
    block = jnp.zeros((size, length), jnp.float32)
    for index, row in enumerate(rows):
        block = jnp.where(place == index, row, block)
    return block.astype(jnp.bfloat16)


def three_parts(row):
    high = row.astype(jnp.bfloat16).astype(jnp.float32)
    middle = (row - high).astype(jnp.bfloat16).astype(jnp.float32)
    return [high, middle, row - high - middle]


def mask_row(start, length, limit):
    place = start + lax.broadcasted_iota(jnp.int32, (1, length), 1)
    return jnp.where(place < limit, 0.0, MASK)


def project_kernel(pieces_ref, first_ref, cosine_ref, sine_ref, out_ref, rows_ref):
    shards, _, heads = pieces_ref.shape[:3]
    lanes = pieces_ref.shape[-1]
    weight = jnp.concatenate(
        [pieces_ref[shard].reshape(3 * heads * HEAD_DIM, lanes) for shard in range(shards)], axis=1
    )
    product = lax.dot_general(weight, first_ref[...], NT, preferred_element_type=jnp.float32)
    cosine, sine = cosine_ref[...], sine_ref[...]
    half = HEAD_DIM // 2
    for head in range(heads):
        for part in range(3):
            base = (part * heads + head) * HEAD_DIM
            rows_ref[head, part] = weight[base : base + HEAD_DIM]
        for part, scale in ((0, HEAD_DIM**-0.5), (1, 1.0)):
            base = (part * heads + head) * HEAD_DIM
            upper, lower = product[base : base + half], product[base + half : base + HEAD_DIM]
            turned_upper = (upper * cosine - lower * sine).astype(jnp.bfloat16)
            turned_lower = (lower * cosine + upper * sine).astype(jnp.bfloat16)
            place = part * HEAD_DIM
            out_ref[head, place : place + half, :] = turned_upper * jnp.bfloat16(scale)
            out_ref[head, place + half : place + HEAD_DIM, :] = turned_lower * jnp.bfloat16(
                scale
            )
        base = (2 * heads + head) * HEAD_DIM
        out_ref[head, 2 * HEAD_DIM :, :] = product[base : base + HEAD_DIM].astype(jnp.bfloat16)


def project_heads(pieces, first, cosine, sine, phases, phase):
    shards, lanes = pieces.shape[0], pieces.shape[-1]
    count, width = first.shape
    pieces = pieces.reshape(shards, 3, shards, phases, HEAD_DIM, lanes)
    group = min(4, shards)
    half = HEAD_DIM // 2
    return pl.pallas_call(
        project_kernel,
        grid=(shards // group,),
        in_specs=[
            pl.BlockSpec(
                (shards, 3, group, None, HEAD_DIM, lanes), lambda g: (0, 0, g, phase, 0, 0)
            ),
            pl.BlockSpec((count, width), lambda g: (0, 0)),
            pl.BlockSpec((half, count), lambda g: (0, 0)),
            pl.BlockSpec((half, count), lambda g: (0, 0)),
        ],
        out_specs=[
            pl.BlockSpec((group, 3 * HEAD_DIM, count), lambda g: (g, 0, 0)),
            pl.BlockSpec((group, 3, HEAD_DIM, width), lambda g: (g, 0, 0, 0)),
        ],
        out_shape=[
            jax.ShapeDtypeStruct((shards, 3 * HEAD_DIM, count), jnp.bfloat16),
            jax.ShapeDtypeStruct((shards, 3, HEAD_DIM, width), jnp.bfloat16),
        ],
        compiler_params=pltpu.CompilerParams(vmem_limit_bytes=VMEM_LIMIT),
        cost_estimate=pl.CostEstimate(
            flops=6 * width * width * count // phases,
            bytes_accessed=20 * width * width // phases,
            transcendentals=0,
        ),
    )(pieces, first, cosine, sine)


def forward_kernel(
    length_ref,
    own_ref,
    other_ref,
    out_ref,
    log_ref,
    query_ref,
    key_ref,
    value_ref,
    peak_ref,
    bound_ref,
):
    row, index = pl.program_id(0), pl.program_id(1)
    shards, _, local = own_ref.shape
    limit = length_ref[row]
    ratio = max(1, 2048 // local)
    blocks = (limit + local - 1) // local

    def prepare(joint_ref, first):
        query_most = jnp.zeros((1, 1), jnp.float32)
        key_most = jnp.zeros((1, 1), jnp.float32)
        for shard in range(shards):
            place = slice(shard * local, (shard + 1) * local)
            key = joint_ref[shard, HEAD_DIM : 2 * HEAD_DIM, :]
            wide_key = key.astype(jnp.float32)
            key_size = jnp.sum(wide_key * wide_key, axis=0, keepdims=True)
            key_most = jnp.maximum(key_most, jnp.max(key_size, axis=1, keepdims=True))
            extra = extra_rows([mask_row(shard * local, local, limit), 1.0], local)
            key_ref[place, :] = jnp.concatenate([key, extra], axis=0).T
            value_ref[:HEAD_DIM, place] = joint_ref[shard, 2 * HEAD_DIM :, :]
            value_ref[HEAD_DIM:, place] = extra_rows([1.0], local, 16)
        for block in range(shards // 2):
            query = joint_ref[2 * block + first, :HEAD_DIM, :]
            wide_query = query.astype(jnp.float32)
            query_size = jnp.sum(wide_query * wide_query, axis=0, keepdims=True)
            query_most = jnp.maximum(query_most, jnp.max(query_size, axis=1, keepdims=True))
            query_ref[block] = query
        bound_ref[0] = (jnp.sqrt(query_most) * jnp.sqrt(key_most))[0, 0]

    for which, joint_ref in enumerate((own_ref, other_ref)):
        pl.when((index == 0) & (row == which))(
            functools.partial(prepare, joint_ref, which)
        )

    mine = 2 * index + row < blocks

    @pl.when(jnp.logical_not(mine))
    def padding():
        out_ref[...] = jnp.zeros_like(out_ref)
        log_ref[...] = jnp.zeros_like(log_ref)

    @pl.when(mine)
    def compute():
        query = query_ref[index]
        peak_ref[...] = jnp.zeros_like(peak_ref)

        @pl.when(bound_ref[0] > SAFE_BOUND)
        def find_peak():
            plain = jnp.concatenate([query, extra_rows([1.0], local)], axis=0)

            def step(block, peak):
                place = pl.ds(pl.multiple_of(block * local, local), local)
                scores = jnp.dot(key_ref[place, :], plain, preferred_element_type=jnp.float32)
                return jnp.maximum(peak, jnp.max(scores, axis=0, keepdims=True))

            peak = lax.fori_loop(0, blocks, step, jnp.full((1, local), MASK, jnp.float32))
            peak_ref[...] = peak.astype(jnp.bfloat16).astype(jnp.float32)

        peak = peak_ref[...]
        augmented = jnp.concatenate([query, extra_rows([1.0, -peak], local)], axis=0)

        def attend(start, size, total):
            place = pl.ds(pl.multiple_of(start, local), size)
            scores = jnp.dot(key_ref[place, :], augmented, preferred_element_type=jnp.float32)
            weights = jnp.exp(scores).astype(jnp.bfloat16)
            return total + jnp.dot(
                value_ref[:, place], weights, preferred_element_type=jnp.float32
            )

        large = blocks // ratio
        total = lax.fori_loop(
            0,
            large,
            lambda block, total: attend(block * (ratio * local), ratio * local, total),
            jnp.zeros((HEAD_DIM + 16, local), jnp.float32),
        )
        total = lax.fori_loop(
            large * ratio, blocks, lambda block, total: attend(block * local, local, total), total
        )
        mass = total[HEAD_DIM : HEAD_DIM + 1, :]
        out_ref[0, 0] = (total[:HEAD_DIM, :] / mass).astype(jnp.bfloat16)
        log_ref[0, 0] = peak + jnp.log(mass)


def attend_forward(lengths, own, other):
    shards, _, local = own.shape
    total = shards * local
    half = shards // 2
    joint = pl.BlockSpec((shards, 3 * HEAD_DIM, local), lambda r, i: (0, 0, 0))
    return pl.pallas_call(
        forward_kernel,
        grid=(2, half),
        in_specs=[pl.BlockSpec(memory_space=pltpu.SMEM), joint, joint],
        out_specs=[
            pl.BlockSpec((1, 1, HEAD_DIM, local), lambda r, i: (r, i, 0, 0)),
            pl.BlockSpec((1, 1, 1, local), lambda r, i: (r, i, 0, 0)),
        ],
        out_shape=[
            jax.ShapeDtypeStruct((2, half, HEAD_DIM, local), jnp.bfloat16),
            jax.ShapeDtypeStruct((2, half, 1, local), jnp.float32),
        ],
        scratch_shapes=[
            pltpu.VMEM((half, HEAD_DIM, local), jnp.bfloat16),
            pltpu.VMEM((total, 2 * HEAD_DIM), jnp.bfloat16),
            pltpu.VMEM((HEAD_DIM + 16, total), jnp.bfloat16),
            pltpu.VMEM((1, local), jnp.float32),
            pltpu.SMEM((1,), jnp.float32),
        ],
        compiler_params=pltpu.CompilerParams(vmem_limit_bytes=VMEM_LIMIT),
        cost_estimate=pl.CostEstimate(
            flops=10 * HEAD_DIM * total * total,
            bytes_accessed=16 * HEAD_DIM * total,
            transcendentals=total * total,
        ),
    )(lengths, own, other)


def backward_kernel(
    length_ref,
    own_ref,
    other_ref,
    own_back_ref,
    other_back_ref,
    out_ref,
    log_ref,
    cosine_ref,
    sine_ref,
    own_grad_ref,
    other_grad_ref,
    query_ref,
    wide_ref,
    query_flat,
    back_flat,
    query_sum,
):
    row, index = pl.program_id(0), pl.program_id(1)
    shards, _, local = own_ref.shape
    limit = length_ref[row]
    ratio = max(1, 2048 // local)
    blocks = (limit + local - 1) // local
    mine = (blocks + 1 - row) // 2
    half = HEAD_DIM // 2

    def turned_back(wide, shard):
        cosine, sine = cosine_ref[shard], sine_ref[shard]
        upper, lower = wide[:half], wide[half:]
        return jnp.concatenate(
            [upper * cosine + lower * sine, lower * cosine - upper * sine], axis=0
        ).astype(jnp.bfloat16)

    def prepare(joint_ref, back_ref, first):
        for block in range(shards // 2):
            place = slice(block * local, (block + 1) * local)
            query = joint_ref[2 * block + first, :HEAD_DIM, :]
            back = back_ref[2 * block + first]
            extra = extra_rows([1.0] + three_parts(-log_ref[first, block]), local)
            query_ref[place, :] = jnp.concatenate([query, extra], axis=0).T
            balance = jnp.sum(
                back.astype(jnp.float32) * out_ref[first, block].astype(jnp.float32),
                axis=0,
                keepdims=True,
            )
            extra = extra_rows(three_parts(-balance), local)
            wide_ref[place, :] = jnp.concatenate([back, extra], axis=0).T
            query_flat[:, place] = query
            back_flat[:, place] = back
        query_sum[...] = jnp.zeros_like(query_sum)

    def work(joint_ref, grad_ref):
        key = joint_ref[index, HEAD_DIM : 2 * HEAD_DIM, :]
        value = joint_ref[index, 2 * HEAD_DIM :, :]
        mask = mask_row(index * local, local, limit)
        wide_key = jnp.concatenate([key, extra_rows([mask, 1.0, 1.0, 1.0], local)], axis=0)
        wide_value = jnp.concatenate([value, extra_rows([1.0, 1.0, 1.0], local)], axis=0)

        def gather(start, size, carry):
            key_sum, value_sum = carry
            place = pl.ds(pl.multiple_of(start, local), size)
            scores = jnp.dot(query_ref[place, :], wide_key, preferred_element_type=jnp.float32)
            chance = jnp.exp(scores)
            change = jnp.dot(wide_ref[place, :], wide_value, preferred_element_type=jnp.float32)
            chance_low = chance.astype(jnp.bfloat16)
            score_back = (chance * change).astype(jnp.bfloat16)
            value_sum = value_sum + jnp.dot(
                back_flat[:, place], chance_low, preferred_element_type=jnp.float32
            )
            key_sum = key_sum + jnp.dot(
                query_flat[:, place], score_back, preferred_element_type=jnp.float32
            )
            query_sum[:, place] += lax.dot_general(
                key, score_back, NT, preferred_element_type=jnp.float32
            )
            return (key_sum, value_sum)

        large = mine // ratio
        zero = jnp.zeros((HEAD_DIM, local), jnp.float32)
        carry = lax.fori_loop(
            0,
            large,
            lambda block, carry: gather(block * (ratio * local), ratio * local, carry),
            (zero, zero),
        )
        key_sum, value_sum = lax.fori_loop(
            large * ratio, mine, lambda block, carry: gather(block * local, local, carry), carry
        )
        grad_ref[index, HEAD_DIM : 2 * HEAD_DIM, :] = turned_back(key_sum, index)
        grad_ref[index, 2 * HEAD_DIM :, :] = value_sum.astype(jnp.bfloat16)

    def padding(grad_ref):
        grad_ref[index, HEAD_DIM:, :] = jnp.zeros((2 * HEAD_DIM, local), jnp.bfloat16)

    def finish(grad_ref, first):
        for block in range(shards // 2):
            place = slice(block * local, (block + 1) * local)
            shard = 2 * block + first
            grad_ref[shard, :HEAD_DIM, :] = turned_back(
                query_sum[:, place] * HEAD_DIM**-0.5, shard
            )
            grad_ref[shard + 1 - 2 * first, :HEAD_DIM, :] = jnp.zeros(
                (HEAD_DIM, local), jnp.bfloat16
            )

    sides = ((own_ref, own_back_ref, own_grad_ref), (other_ref, other_back_ref, other_grad_ref))
    for which, (joint_ref, back_ref, grad_ref) in enumerate(sides):
        here = row == which
        pl.when(here & (index == 0))(functools.partial(prepare, joint_ref, back_ref, which))
        pl.when(here & (index < blocks))(functools.partial(work, joint_ref, grad_ref))
        pl.when(here & (index >= blocks))(functools.partial(padding, grad_ref))
        pl.when(here & (index == shards - 1))(functools.partial(finish, grad_ref, which))


def attend_backward(lengths, own, other, own_back, other_back, out, log_mass, cosine, sine):
    shards, _, local = own.shape
    total = shards * local
    half = shards // 2
    whole = lambda *shape: pl.BlockSpec(shape, lambda r, i: (0,) * len(shape))
    grad = jax.ShapeDtypeStruct((shards, 3 * HEAD_DIM, local), jnp.bfloat16)
    return pl.pallas_call(
        backward_kernel,
        grid=(2, shards),
        in_specs=[pl.BlockSpec(memory_space=pltpu.SMEM)]
        + [whole(shards, 3 * HEAD_DIM, local)] * 2
        + [whole(shards, HEAD_DIM, local)] * 2
        + [whole(2, half, HEAD_DIM, local), whole(2, half, 1, local)]
        + [whole(shards, HEAD_DIM // 2, local)] * 2,
        out_specs=[whole(shards, 3 * HEAD_DIM, local)] * 2,
        out_shape=[grad, grad],
        scratch_shapes=[
            pltpu.VMEM((total // 2, 2 * HEAD_DIM), jnp.bfloat16),
            pltpu.VMEM((total // 2, 2 * HEAD_DIM), jnp.bfloat16),
            pltpu.VMEM((HEAD_DIM, total // 2), jnp.bfloat16),
            pltpu.VMEM((HEAD_DIM, total // 2), jnp.bfloat16),
            pltpu.VMEM((HEAD_DIM, total // 2), jnp.float32),
        ],
        compiler_params=pltpu.CompilerParams(vmem_limit_bytes=VMEM_LIMIT),
        cost_estimate=pl.CostEstimate(
            flops=26 * HEAD_DIM * total * total,
            bytes_accessed=40 * HEAD_DIM * total,
            transcendentals=total * total,
        ),
    )(lengths, own, other, own_back, other_back, out, log_mass, cosine, sine)


TN = (((0,), (0,)), ((), ()))
PLAIN = (((1,), (0,)), ((), ()))
LANES = 128
GROUPS = 4
RUNS = 8
UNITS = FF // GROUPS
EXPAND_RUN = -(-2 * UNITS // (16 * RUNS)) * 16
SHRINK_RUN = -(-UNITS // (16 * RUNS)) * 16


def run_segments(start, stop, run):
    segments = []
    while start < stop:
        index = start // run
        end = min(stop, (index + 1) * run)
        segments.append((index, start - index * run, start, end - start))
        start = end
    return segments


def feed_kernel(
    second_ref,
    upstream_ref,
    active_ref,
    gate_ref,
    shrink_ref,
    shrunk_ref,
    second_back_ref,
    parts_ref,
    grads_ref,
    zero_ref,
    send_ref,
    zero_send_ref,
):
    index = pl.program_id(0)

    def joined(ref):
        return jnp.concatenate([ref[piece, 0] for piece in range(ref.shape[0])], axis=1)

    def product(left, right, dims):
        return lax.dot_general(left, right, dims, preferred_element_type=jnp.float32)

    def grad_copies(half, pair):
        moves = []
        for kind, member in ((0, pair), (1, pair + 2)):
            for run, place, offset, size in run_segments(
                half * UNITS, (half + 1) * UNITS, EXPAND_RUN
            ):
                moves.append((kind, offset - half * UNITS, run, member, place, size))
        for run, place, offset, size in run_segments(0, UNITS, SHRINK_RUN):
            moves.append((2, offset, run, 2 * pair + half, EXPAND_RUN + place, size))
        return [
            pltpu.make_async_copy(
                grads_ref.at[half, kind, pl.ds(offset, size), :],
                parts_ref.at[run, member, pl.ds(place, size), :],
                send_ref.at[half, number],
            )
            for number, (kind, offset, run, member, place, size) in enumerate(moves)
        ]

    def zero_copies():
        moves = []
        for member in range(GROUPS):
            for base, run_size, total in ((0, EXPAND_RUN, 2 * UNITS), (EXPAND_RUN, SHRINK_RUN, UNITS)):
                for run, place, _, size in run_segments(total, RUNS * run_size, run_size):
                    moves.append((run, member, base + place, size))
        return [
            pltpu.make_async_copy(
                zero_ref.at[pl.ds(0, size), :],
                parts_ref.at[run, member, pl.ds(place, size), :],
                zero_send_ref.at[number],
            )
            for number, (run, member, place, size) in enumerate(moves)
        ]

    @pl.when(index == 0)
    def fill():
        zero_ref[...] = jnp.zeros_like(zero_ref)
        for copy in zero_copies():
            copy.start()

    active, gate, shrink = joined(active_ref), joined(gate_ref), joined(shrink_ref)
    second, upstream = second_ref[...], upstream_ref[...]
    input_active = product(second, active, NT)
    input_gate = product(second, gate, NT)
    hidden_back = product(upstream, shrink, NT)
    below = 0.5 + 0.5 * lax.erf(input_active * 0.5**0.5)
    bell = jnp.exp(-0.5 * input_active * input_active) * (0.5 / math.pi) ** 0.5
    curve = input_active * below
    hidden = (curve * input_gate).astype(jnp.bfloat16)
    active_back = (hidden_back * input_gate * (below + input_active * bell)).astype(jnp.bfloat16)
    gate_back = (hidden_back * curve).astype(jnp.bfloat16)
    shrunk = product(hidden, shrink, PLAIN)
    second_back = product(active_back, active, PLAIN) + product(gate_back, gate, PLAIN)

    @pl.when(index == 0)
    def begin():
        shrunk_ref[...] = shrunk
        second_back_ref[...] = second_back

    @pl.when(index > 0)
    def add():
        shrunk_ref[...] += shrunk
        second_back_ref[...] += second_back

    for half in range(2):

        @pl.when(index % 2 == half)
        def send(half=half):
            pair = index // 2

            @pl.when(index >= 2)
            def free():
                for copy in grad_copies(half, pair - 1):
                    copy.wait()

            grads_ref[half, 0] = product(active_back, second, TN).astype(jnp.bfloat16)
            grads_ref[half, 1] = product(gate_back, second, TN).astype(jnp.bfloat16)
            grads_ref[half, 2] = product(hidden, upstream, TN).astype(jnp.bfloat16)
            for copy in grad_copies(half, pair):
                copy.start()

    @pl.when(index == GROUPS - 1)
    def drain():
        for half in range(2):
            for copy in grad_copies(half, 1):
                copy.wait()
        for copy in zero_copies():
            copy.wait()


def feed_forward(second, upstream, pieces):
    count, width = second.shape
    block = (RUNS, 1, UNITS, LANES)
    held = pl.BlockSpec((count, width), lambda i: (0, 0), pipeline_mode=pl.Buffered(1))
    wide = jax.ShapeDtypeStruct((count, width), jnp.float32)
    run = EXPAND_RUN + SHRINK_RUN
    copies = max(
        2 * len(run_segments(half * UNITS, (half + 1) * UNITS, EXPAND_RUN)) for half in range(2)
    ) + len(run_segments(0, UNITS, SHRINK_RUN))
    return pl.pallas_call(
        feed_kernel,
        grid=(GROUPS,),
        in_specs=[
            held,
            held,
            pl.BlockSpec(block, lambda i: (0, i // 2, i % 2, 0)),
            pl.BlockSpec(block, lambda i: (0, i // 2 + 2, i % 2, 0)),
            pl.BlockSpec(block, lambda i: (0, i, 2, 0)),
        ],
        out_specs=[held, held, pl.BlockSpec(memory_space=pl.ANY)],
        out_shape=[wide, wide, jax.ShapeDtypeStruct((RUNS, GROUPS, run, width), jnp.bfloat16)],
        scratch_shapes=[
            pltpu.VMEM((2, 3, UNITS, width), jnp.bfloat16),
            pltpu.VMEM((max(EXPAND_RUN, SHRINK_RUN), width), jnp.bfloat16),
            pltpu.SemaphoreType.DMA((2, copies)),
            pltpu.SemaphoreType.DMA((GROUPS * 8,)),
        ],
        compiler_params=pltpu.CompilerParams(vmem_limit_bytes=VMEM_LIMIT),
        cost_estimate=pl.CostEstimate(
            flops=18 * count * width * FF,
            bytes_accessed=12 * FF * width + 16 * count * width,
            transcendentals=2 * count * FF,
        ),
    )(second, upstream, pieces, pieces, pieces)


def adam_step(rotated, first, second):
    average = BETA_ONE * first + (1.0 - BETA_ONE) * rotated
    variance = BETA_TWO * second + (1.0 - BETA_TWO) * rotated * rotated
    direction = (
        average / (1.0 - BETA_ONE**STEP) / (jnp.sqrt(variance / (1.0 - BETA_TWO**STEP)) + ADAM_EPS)
    )
    return (average, variance, direction)


def body(
    tokens,
    cotangent,
    lengths,
    triple_weight,
    output_weight,
    expand_weight,
    shrink_weight,
    norm_gains,
    side_bases,
    output_right,
    triple_first,
    triple_second,
    output_first,
    output_second,
    expand_first,
    expand_second,
    shrink_first,
    shrink_second,
    gains_first,
    gains_second,
):
    rows_here, local_len, width = tokens.shape
    count = rows_here * local_len
    shards = lax.axis_size("seq")
    groups = lax.axis_size("outer") * lax.axis_size("core")
    phases = HEADS // shards
    piece = width // shards
    fsdp = ("outer", "core")
    everyone = ("seq",) + fsdp
    offset = lax.axis_index("seq") * local_len
    position = offset + jnp.arange(local_len, dtype=jnp.int32)
    cosine, sine = rotary_tables(position)
    every = jnp.arange(shards * local_len, dtype=jnp.int32)
    all_cosine, all_sine = (
        table.reshape(HEAD_DIM // 2, shards, local_len).transpose(1, 0, 2)
        for table in rotary_tables(every)
    )
    valid = (position[None, :] < lengths[:, None]).astype(jnp.float32).reshape(count, 1)
    exchange = functools.partial(lax.all_to_all, axis_name="seq", split_axis=0, concat_axis=0)

    def gathered(shard):
        flat = lax.all_gather(shard, everyone, axis=0, tiled=False)
        return flat.reshape((shards, groups) + shard.shape)

    triple_pieces = gathered(triple_weight.T.astype(jnp.bfloat16))
    output_columns = width // groups
    lanes = min(piece, output_columns)

    def fold(block):
        rows = block.shape[0]
        return block.reshape(rows, -1, lanes).transpose(1, 0, 2).reshape(-1, lanes)

    bases_low = side_bases.astype(jnp.bfloat16)
    right_low = output_right.astype(jnp.bfloat16)
    member = lax.axis_index("outer") * lax.axis_size("core") + lax.axis_index("core")
    base_rows = piece // groups
    flat = tokens.reshape(count, width).astype(jnp.float32)
    first_normed, first_back = jax.vjp(layer_norm, flat, norm_gains[0])
    first_low = first_normed.astype(jnp.bfloat16)
    projected = [
        project_heads(triple_pieces, first_low, cosine, sine, phases, phase)
        for phase in range(phases)
    ]
    triple_rows = [rows for _, rows in projected]
    joints = [exchange(joint) for joint, _ in projected]
    other_shards = jnp.concatenate(
        [
            expand_weight.T.astype(jnp.bfloat16),
            shrink_weight.astype(jnp.bfloat16),
            fold(output_weight.astype(jnp.bfloat16)),
        ],
        axis=0,
    )
    other_shards, joints[0] = lax.optimization_barrier((other_shards, joints[0]))
    other_pieces = gathered(other_shards)
    expand_rows = 2 * FF // groups
    shrink_rows = FF // groups
    output_rows = (
        other_pieces[:, :, expand_rows + shrink_rows :]
        .reshape(shards, groups, output_columns // lanes, phases, HEAD_DIM, lanes)
        .transpose(3, 0, 4, 1, 2, 5)
        .reshape(phases, shards * HEAD_DIM, width)
    )
    canonical = (shards, groups, piece) == (RUNS, GROUPS, LANES)
    if canonical:
        feed_pieces = other_pieces
    else:
        feed_pieces = [
            other_pieces[:, :, start:end]
            .transpose(1, 2, 0, 3)
            .reshape(GROUPS, -1, RUNS, LANES)
            .transpose(2, 0, 1, 3)
            for start, end in ((0, expand_rows), (expand_rows, expand_rows + shrink_rows))
        ]
        feed_pieces = jnp.concatenate(feed_pieces, axis=2)
    chosen = jnp.stack([bases_low[0], bases_low[2], bases_low[3]])
    chosen = lax.dynamic_slice_in_dim(chosen, member * base_rows, base_rows, 1)
    bases_full = gathered(chosen).transpose(2, 0, 1, 3, 4).reshape(3, width, width)

    swap = functools.partial(lax.ppermute, axis_name="core", perm=[(0, 1), (1, 0)])
    both_lengths = jnp.concatenate([lengths, swap(lengths)])
    others = [swap(joint) for joint in joints]
    forwards = [attend_forward(both_lengths, *pair) for pair in zip(joints, others)]
    attends = [
        exchange(
            jnp.stack([outcome[0], swap(outcome[1])], axis=1).reshape(shards, HEAD_DIM, count)
        )
        for outcome, _ in forwards
    ]
    attends = [attend.reshape(shards * HEAD_DIM, count) for attend in attends]
    expand_height = -(-expand_rows // (16 * shards)) * 16
    shrink_height = -(-shrink_rows // (16 * shards)) * 16

    def to_rows(block):
        block = exchange(block)
        return block.transpose(1, 0, 2).reshape(block.shape[1], -1)

    def to_pieces(rows):
        return exchange(rows.reshape(rows.shape[0], shards, -1).transpose(1, 0, 2))

    def padded(block, height):
        block = jnp.pad(block, ((0, height * shards - block.shape[0]), (0, 0)))
        return block.reshape(shards, height, piece)

    def by_phase(block):
        return (
            block.reshape(-1, phases, HEAD_DIM, piece)
            .transpose(1, 0, 2, 3)
            .reshape(phases, shards, -1, piece)
        )

    def from_phases(blocks):
        block = jnp.stack(blocks).astype(jnp.float32).reshape(phases, -1, HEAD_DIM, piece)
        return block.transpose(1, 0, 2, 3).reshape(-1, piece)

    moments = []
    for expand, shrink, triple in (
        (expand_first, shrink_first, triple_first),
        (expand_second, shrink_second, triple_second),
    ):
        moments += [padded(expand.T, expand_height), padded(shrink, shrink_height)]
        moments += list(by_phase(triple.T))
    moments, _ = lax.optimization_barrier((moments, attends[0]))
    heights = [moment.shape[1] for moment in moments]
    moments = to_rows(jnp.concatenate(moments, axis=1))
    edges = [sum(heights[:index]) for index in range(len(heights) + 1)]
    moments = [moments[start:end] for start, end in zip(edges, edges[1:])]
    moments = list(zip(moments[: phases + 2], moments[phases + 2 :]))

    branch = sum(outer_sum(attends[phase], output_rows[phase]) for phase in range(phases))
    middle = flat + branch
    second_normed, second_back = jax.vjp(layer_norm, middle, norm_gains[1])
    second_low = second_normed.astype(jnp.bfloat16)
    upstream = cotangent.reshape(count, width).astype(jnp.float32) * valid
    upstream_low = upstream.astype(jnp.bfloat16)
    shrunk, second_change, parts = feed_forward(second_low, upstream_low, feed_pieces)
    mixed = ((middle + shrunk) * valid).astype(jnp.bfloat16).reshape(tokens.shape)
    second_input, second_gain = second_back(second_change)
    middle_back = upstream + second_input
    branch_low = middle_back.astype(jnp.bfloat16)
    moments, branch_low = lax.optimization_barrier((moments, branch_low))
    attend_backs = [
        exchange(
            back_product(output_rows[phase], branch_low)
            .astype(jnp.bfloat16)
            .reshape(shards, HEAD_DIM, count)
        )
        for phase in range(phases)
    ]

    def cut(product, height):
        block = product.reshape(groups, -1, width)
        block = jnp.pad(block, ((0, 0), (0, height * shards - block.shape[1]), (0, 0)))
        return block.reshape(groups, shards, height, width)

    if not canonical:
        parts = parts.transpose(1, 0, 2, 3)
        parts = [
            cut(block.reshape(GROUPS, -1, width)[:, : size // GROUPS], height)
            for block, size, height in (
                (parts[:, :, :EXPAND_RUN], 2 * FF, expand_height),
                (parts[:, :, EXPAND_RUN:], FF, shrink_height),
            )
        ]
        parts = jnp.concatenate(parts, axis=2).transpose(1, 0, 2, 3)
    parts = parts.reshape(shards * groups, -1, width)
    owned = lax.psum_scatter(parts, everyone, scatter_dimension=0, tiled=False)
    feed_height = expand_height + shrink_height

    def shared_sum(blocks):
        core = lax.axis_index("core")
        mine = lax.dynamic_index_in_dim(blocks, core, 1, keepdims=False)
        other = lax.dynamic_index_in_dim(blocks, 1 - core, 1, keepdims=False)
        both = (mine.astype(jnp.float32) + swap(other).astype(jnp.float32)).astype(jnp.bfloat16)
        both = both.swapaxes(0, 1).reshape((-1,) + both.shape[2:])
        terms = lax.all_to_all(both, ("seq", "outer"), 0, 0)
        return jnp.sum(terms.astype(jnp.float32), axis=0).astype(jnp.bfloat16)

    outer = lax.axis_size("outer")
    output_part = jnp.stack(
        [
            jnp.dot(attend, branch_low, preferred_element_type=jnp.float32)
            .astype(jnp.bfloat16)
            .reshape(shards, HEAD_DIM, width)
            for attend in attends
        ],
        axis=1,
    )
    output_low = shared_sum(
        output_part.reshape(shards, piece, outer, -1, output_columns).transpose(2, 3, 0, 1, 4)
    )

    def soap_rows(rows, base, moment):
        rotated = plain_product(rows, base)
        direction = adam_step(rotated, *moment)[2]
        step = back_product(direction.astype(jnp.bfloat16), base)
        return rotated.astype(jnp.bfloat16), step.astype(jnp.bfloat16)

    expand_turns, expand_steps = soap_rows(owned[:expand_height], bases_full[1], moments[0])
    shrink_turns, shrink_steps = soap_rows(
        owned[expand_height:feed_height], bases_full[2], moments[1]
    )
    settled = to_pieces(
        jnp.concatenate(
            [owned[:feed_height], expand_turns, shrink_turns, expand_steps, shrink_steps]
        )
    )

    output_left = exchange(
        outer_sum(bases_low[1], output_low).astype(jnp.bfloat16).reshape(shards, piece, -1)
    )
    output_left = jnp.sum(output_left.astype(jnp.float32), axis=0).astype(jnp.bfloat16)
    output_turned = plain_product(output_left, right_low).astype(jnp.bfloat16)
    output_turned = lax.all_to_all(
        output_turned.reshape(piece, groups, output_columns).transpose(1, 0, 2), fsdp, 0, 0
    )
    output_turned = jnp.sum(output_turned.astype(jnp.float32), axis=0)
    other_backs = [swap(attend_back) for attend_back in attend_backs]
    grads = []
    for phase in range(phases):
        own_grad, other_grad = attend_backward(
            both_lengths,
            joints[phase],
            others[phase],
            attend_backs[phase],
            other_backs[phase],
            *forwards[phase],
            all_cosine,
            all_sine,
        )
        grad = own_grad.astype(jnp.float32) + swap(other_grad).astype(jnp.float32)
        grads.append(exchange(grad.astype(jnp.bfloat16)))
    joint_backs = []
    triple_lows, triple_turns, triple_steps = [], [], []
    for phase in range(phases):
        if phase == phases - 1:
            earlier = (triple_lows, triple_turns, triple_steps, settled, output_turned)
            earlier, grads[phase] = lax.optimization_barrier((earlier, grads[phase]))
            triple_lows, triple_turns, triple_steps, settled, output_turned = earlier
        joint_backs.append(grads[phase].reshape(shards * 3 * HEAD_DIM, count))
        part = jnp.dot(joint_backs[phase], first_low, preferred_element_type=jnp.float32)
        part = part.astype(jnp.bfloat16).reshape(shards, 3, HEAD_DIM, width).transpose(1, 0, 2, 3)
        rows = shared_sum(part.reshape(outer, -1, shards, part.size // (width * shards * groups), width))
        turns, steps = soap_rows(rows, bases_full[0], moments[2 + phase])
        low, turned, step = jnp.split(to_pieces(jnp.concatenate([rows, turns, steps])), 3, axis=1)
        triple_lows.append(low)
        triple_turns.append(turned)
        triple_steps.append(step)

    def settled_piece(start, height, size):
        return settled[:, start : start + height].reshape(-1, piece)[:size].astype(jnp.float32)

    expand_gradient, expand_turned_grad, expand_back = (
        settled_piece(index * feed_height, expand_height, expand_rows).T for index in range(3)
    )
    shrink_gradient, shrink_turned_grad, shrink_back = (
        settled_piece(index * feed_height + expand_height, shrink_height, shrink_rows)
        for index in range(3)
    )
    expand_average, expand_variance, _ = adam_step(expand_turned_grad, expand_first, expand_second)
    shrink_average, shrink_variance, _ = adam_step(shrink_turned_grad, shrink_first, shrink_second)
    output_average, output_variance, output_direction = adam_step(
        output_turned, output_first, output_second
    )
    output_wide = lax.all_gather(output_direction.astype(jnp.bfloat16), fsdp, axis=1, tiled=True)
    output_middle = back_product(output_wide, right_low).astype(jnp.bfloat16)
    output_back = plain_product(
        bases_low[1], lax.all_gather(output_middle, "seq", axis=0, tiled=True)
    )
    triple_turned = from_phases(triple_turns).T
    triple_back = from_phases(triple_steps).T
    triple_gradient = from_phases(triple_lows).T
    triple_average, triple_variance, _ = adam_step(triple_turned, triple_first, triple_second)
    first_input, first_gain = first_back(
        sum(
            outer_sum(joint_backs[phase], triple_rows[phase].reshape(-1, width))
            for phase in range(phases)
        )
    )
    token_gradient = (middle_back + first_input).astype(jnp.bfloat16).reshape(tokens.shape)
    gains_gradient = jnp.stack([first_gain, second_gain])
    for axis in ("core", "outer", "seq"):
        members = range(lax.axis_size(axis))
        for step in range(len(members).bit_length() - 1):
            pairs = [(member, member ^ (1 << step)) for member in members]
            gains_gradient = gains_gradient + lax.ppermute(gains_gradient, axis, pairs)
    gains_average, gains_variance, gains_direction = adam_step(
        gains_gradient, gains_first, gains_second
    )
    output_gradient = output_low.astype(jnp.float32)
    triple_updated = (triple_weight - WEIGHT_RATES[0] * triple_back) * (
        1.0 - WEIGHT_RATES[0] * DECAY_RATE
    )
    output_updated = (output_weight - WEIGHT_RATES[1] * output_back) * (
        1.0 - WEIGHT_RATES[1] * DECAY_RATE
    )
    expand_updated = (expand_weight - WEIGHT_RATES[2] * expand_back) * (
        1.0 - WEIGHT_RATES[2] * DECAY_RATE
    )
    shrink_updated = (shrink_weight - WEIGHT_RATES[3] * shrink_back) * (
        1.0 - WEIGHT_RATES[3] * DECAY_RATE
    )
    gains_updated = norm_gains - GAINS_RATE * gains_direction
    return (
        mixed,
        token_gradient,
        triple_gradient,
        output_gradient,
        expand_gradient,
        shrink_gradient,
        gains_gradient,
        triple_average,
        triple_variance,
        triple_updated,
        triple_updated.astype(jnp.bfloat16),
        output_average,
        output_variance,
        output_updated,
        output_updated.astype(jnp.bfloat16),
        expand_average,
        expand_variance,
        expand_updated,
        expand_updated.astype(jnp.bfloat16),
        shrink_average,
        shrink_variance,
        shrink_updated,
        shrink_updated.astype(jnp.bfloat16),
        gains_average,
        gains_variance,
        gains_updated,
    )


def solution(mesh):
    in_specs = (
        P(("outer", "core"), "seq", None),
        P(("outer", "core"), "seq", None),
        P(("outer", "core")),
        P("seq", ("outer", "core")),
        P("seq", ("outer", "core")),
        P("seq", ("outer", "core")),
        P(("outer", "core"), "seq"),
        P(),
        P(None, "seq", None),
        P(("outer", "core"), None),
        P("seq", ("outer", "core")),
        P("seq", ("outer", "core")),
        P("seq", ("outer", "core")),
        P("seq", ("outer", "core")),
        P("seq", ("outer", "core")),
        P("seq", ("outer", "core")),
        P(("outer", "core"), "seq"),
        P(("outer", "core"), "seq"),
        P(),
        P(),
    )
    out_specs = (
        P(("outer", "core"), "seq", None),
        P(("outer", "core"), "seq", None),
        P("seq", ("outer", "core")),
        P("seq", ("outer", "core")),
        P("seq", ("outer", "core")),
        P(("outer", "core"), "seq"),
        P(),
        P("seq", ("outer", "core")),
        P("seq", ("outer", "core")),
        P("seq", ("outer", "core")),
        P("seq", ("outer", "core")),
        P("seq", ("outer", "core")),
        P("seq", ("outer", "core")),
        P("seq", ("outer", "core")),
        P("seq", ("outer", "core")),
        P("seq", ("outer", "core")),
        P("seq", ("outer", "core")),
        P("seq", ("outer", "core")),
        P("seq", ("outer", "core")),
        P(("outer", "core"), "seq"),
        P(("outer", "core"), "seq"),
        P(("outer", "core"), "seq"),
        P(("outer", "core"), "seq"),
        P(),
        P(),
        P(),
    )
    groups = mesh.shape["fsdp"]
    devices = mesh.devices.reshape(mesh.shape["seq"], groups // 2, 2)
    split = Mesh(devices, ("seq", "outer", "core"))
    return jax.shard_map(body, mesh=split, in_specs=in_specs, out_specs=out_specs, check_vma=False)
```

```python
import functools
import math

import jax
import jax.numpy as jnp
from jax import lax
from jax.experimental import pallas as pl
from jax.experimental.pallas import tpu as pltpu
from jax.sharding import Mesh
from jax.sharding import PartitionSpec as P

HEADS = 16
HEAD_DIM = 64
FF = 2624
STEP = 10


ROPE_BASE = 160000.0
NORM_EPS = 1e-05
NEG_LARGE = -1e30
BETA_ONE = 0.95
BETA_TWO = 0.95
ADAM_EPS = 1e-08
DECAY_RATE = 0.01
WEIGHT_RATES = (0.03, 1.0, 0.03, 0.03)
GAINS_RATE = 0.8


def layer_norm(values, gain):
    centre = values - jnp.mean(values, axis=-1, keepdims=True)
    spread = jnp.mean(centre * centre, axis=-1, keepdims=True)
    return centre * lax.rsqrt(spread + NORM_EPS) * gain


def rotary_tables(position):
    halves = HEAD_DIM // 2
    frequency = ROPE_BASE ** (-2.0 * jnp.arange(halves, dtype=jnp.float32) / HEAD_DIM)
    angle = frequency[:, None] * position.astype(jnp.float32)[None, :]
    return jnp.cos(angle), jnp.sin(angle)


def outer_sum(left, right):
    return lax.dot_general(
        left, right, (((0,), (0,)), ((), ())), preferred_element_type=jnp.float32
    )


def back_product(left, right):
    return lax.dot_general(
        left, right, (((1,), (1,)), ((), ())), preferred_element_type=jnp.float32
    )


def plain_product(left, right):
    return jnp.dot(left, right, preferred_element_type=jnp.float32)


NT = (((1,), (1,)), ((), ()))
SAFE_BOUND = 60.0
MASK = -1e30
VMEM_LIMIT = 60 * 1024 * 1024


def extra_rows(rows, length, size=HEAD_DIM):
    place = lax.broadcasted_iota(jnp.int32, (size, length), 0)
    block = jnp.zeros((size, length), jnp.float32)
    for index, row in enumerate(rows):
        block = jnp.where(place == index, row, block)
    return block.astype(jnp.bfloat16)


def three_parts(row):
    high = row.astype(jnp.bfloat16).astype(jnp.float32)
    middle = (row - high).astype(jnp.bfloat16).astype(jnp.float32)
    return [high, middle, row - high - middle]


def mask_row(start, length, limit):
    place = start + lax.broadcasted_iota(jnp.int32, (1, length), 1)
    return jnp.where(place < limit, 0.0, MASK)


def project_kernel(pieces_ref, first_ref, cosine_ref, sine_ref, out_ref, rows_ref):
    shards, _, heads = pieces_ref.shape[:3]
    lanes = pieces_ref.shape[-1]
    weight = jnp.concatenate(
        [pieces_ref[shard].reshape(3 * heads * HEAD_DIM, lanes) for shard in range(shards)], axis=1
    )
    product = lax.dot_general(weight, first_ref[...], NT, preferred_element_type=jnp.float32)
    cosine, sine = cosine_ref[...], sine_ref[...]
    half = HEAD_DIM // 2
    for head in range(heads):
        for part in range(3):
            base = (part * heads + head) * HEAD_DIM
            rows_ref[head, part] = weight[base : base + HEAD_DIM]
        for part, scale in ((0, HEAD_DIM**-0.5), (1, 1.0)):
            base = (part * heads + head) * HEAD_DIM
            upper, lower = product[base : base + half], product[base + half : base + HEAD_DIM]
            turned_upper = (upper * cosine - lower * sine).astype(jnp.bfloat16)
            turned_lower = (lower * cosine + upper * sine).astype(jnp.bfloat16)
            place = part * HEAD_DIM
            out_ref[head, place : place + half, :] = turned_upper * jnp.bfloat16(scale)
            out_ref[head, place + half : place + HEAD_DIM, :] = turned_lower * jnp.bfloat16(
                scale
            )
        base = (2 * heads + head) * HEAD_DIM
        out_ref[head, 2 * HEAD_DIM :, :] = product[base : base + HEAD_DIM].astype(jnp.bfloat16)


def project_heads(pieces, first, cosine, sine):
    shards, lanes = pieces.shape[0], pieces.shape[-1]
    count, width = first.shape
    pieces = pieces.reshape(shards, 3, shards, HEAD_DIM, lanes)
    group = min(4, shards)
    half = HEAD_DIM // 2
    return pl.pallas_call(
        project_kernel,
        grid=(shards // group,),
        in_specs=[
            pl.BlockSpec(
                (shards, 3, group, HEAD_DIM, lanes), lambda g: (0, 0, g, 0, 0)
            ),
            pl.BlockSpec((count, width), lambda g: (0, 0)),
            pl.BlockSpec((half, count), lambda g: (0, 0)),
            pl.BlockSpec((half, count), lambda g: (0, 0)),
        ],
        out_specs=[
            pl.BlockSpec((group, 3 * HEAD_DIM, count), lambda g: (g, 0, 0)),
            pl.BlockSpec((group, 3, HEAD_DIM, width), lambda g: (g, 0, 0, 0)),
        ],
        out_shape=[
            jax.ShapeDtypeStruct((shards, 3 * HEAD_DIM, count), jnp.bfloat16),
            jax.ShapeDtypeStruct((shards, 3, HEAD_DIM, width), jnp.bfloat16),
        ],
        compiler_params=pltpu.CompilerParams(vmem_limit_bytes=VMEM_LIMIT),
        cost_estimate=pl.CostEstimate(
            flops=6 * width * shards * HEAD_DIM * count,
            bytes_accessed=20 * width * shards * HEAD_DIM,
            transcendentals=0,
        ),
    )(pieces, first, cosine, sine)


def forward_kernel(
    length_ref,
    own_ref,
    other_ref,
    out_ref,
    log_ref,
    query_ref,
    key_ref,
    value_ref,
    peak_ref,
    bound_ref,
):
    row, index = pl.program_id(0), pl.program_id(1)
    shards, _, local = own_ref.shape
    limit = length_ref[row]
    ratio = max(1, 2048 // local)
    blocks = (limit + local - 1) // local

    def prepare(joint_ref, first):
        query_most = jnp.zeros((1, 1), jnp.float32)
        key_most = jnp.zeros((1, 1), jnp.float32)
        for shard in range(shards):
            place = slice(shard * local, (shard + 1) * local)
            key = joint_ref[shard, HEAD_DIM : 2 * HEAD_DIM, :]
            wide_key = key.astype(jnp.float32)
            key_size = jnp.sum(wide_key * wide_key, axis=0, keepdims=True)
            key_most = jnp.maximum(key_most, jnp.max(key_size, axis=1, keepdims=True))
            extra = extra_rows([mask_row(shard * local, local, limit), 1.0], local)
            key_ref[place, :] = jnp.concatenate([key, extra], axis=0).T
            value_ref[:HEAD_DIM, place] = joint_ref[shard, 2 * HEAD_DIM :, :]
            value_ref[HEAD_DIM:, place] = extra_rows([1.0], local, 16)
        for block in range(shards // 2):
            query = joint_ref[2 * block + first, :HEAD_DIM, :]
            wide_query = query.astype(jnp.float32)
            query_size = jnp.sum(wide_query * wide_query, axis=0, keepdims=True)
            query_most = jnp.maximum(query_most, jnp.max(query_size, axis=1, keepdims=True))
            query_ref[block] = query
        bound_ref[0] = (jnp.sqrt(query_most) * jnp.sqrt(key_most))[0, 0]

    for which, joint_ref in enumerate((own_ref, other_ref)):
        pl.when((index == 0) & (row == which))(
            functools.partial(prepare, joint_ref, which)
        )

    mine = 2 * index + row < blocks

    @pl.when(jnp.logical_not(mine))
    def padding():
        out_ref[...] = jnp.zeros_like(out_ref)
        log_ref[...] = jnp.zeros_like(log_ref)

    @pl.when(mine)
    def compute():
        query = query_ref[index]
        peak_ref[...] = jnp.zeros_like(peak_ref)

        @pl.when(bound_ref[0] > SAFE_BOUND)
        def find_peak():
            plain = jnp.concatenate([query, extra_rows([1.0], local)], axis=0)

            def step(block, peak):
                place = pl.ds(pl.multiple_of(block * local, local), local)
                scores = jnp.dot(key_ref[place, :], plain, preferred_element_type=jnp.float32)
                return jnp.maximum(peak, jnp.max(scores, axis=0, keepdims=True))

            peak = lax.fori_loop(0, blocks, step, jnp.full((1, local), MASK, jnp.float32))
            peak_ref[...] = peak.astype(jnp.bfloat16).astype(jnp.float32)

        peak = peak_ref[...]
        augmented = jnp.concatenate([query, extra_rows([1.0, -peak], local)], axis=0)

        def attend(start, size, total):
            place = pl.ds(pl.multiple_of(start, local), size)
            scores = jnp.dot(key_ref[place, :], augmented, preferred_element_type=jnp.float32)
            weights = jnp.exp(scores).astype(jnp.bfloat16)
            return total + jnp.dot(
                value_ref[:, place], weights, preferred_element_type=jnp.float32
            )

        large = blocks // ratio
        total = lax.fori_loop(
            0,
            large,
            lambda block, total: attend(block * (ratio * local), ratio * local, total),
            jnp.zeros((HEAD_DIM + 16, local), jnp.float32),
        )
        total = lax.fori_loop(
            large * ratio, blocks, lambda block, total: attend(block * local, local, total), total
        )
        mass = total[HEAD_DIM : HEAD_DIM + 1, :]
        out_ref[0, 0] = (total[:HEAD_DIM, :] / mass).astype(jnp.bfloat16)
        log_ref[0, 0] = peak + jnp.log(mass)


def attend_forward(lengths, own, other):
    shards, _, local = own.shape
    total = shards * local
    half = shards // 2
    joint = pl.BlockSpec((shards, 3 * HEAD_DIM, local), lambda r, i: (0, 0, 0))
    return pl.pallas_call(
        forward_kernel,
        grid=(2, half),
        in_specs=[pl.BlockSpec(memory_space=pltpu.SMEM), joint, joint],
        out_specs=[
            pl.BlockSpec((1, 1, HEAD_DIM, local), lambda r, i: (r, i, 0, 0)),
            pl.BlockSpec((1, 1, 1, local), lambda r, i: (r, i, 0, 0)),
        ],
        out_shape=[
            jax.ShapeDtypeStruct((2, half, HEAD_DIM, local), jnp.bfloat16),
            jax.ShapeDtypeStruct((2, half, 1, local), jnp.float32),
        ],
        scratch_shapes=[
            pltpu.VMEM((half, HEAD_DIM, local), jnp.bfloat16),
            pltpu.VMEM((total, 2 * HEAD_DIM), jnp.bfloat16),
            pltpu.VMEM((HEAD_DIM + 16, total), jnp.bfloat16),
            pltpu.VMEM((1, local), jnp.float32),
            pltpu.SMEM((1,), jnp.float32),
        ],
        compiler_params=pltpu.CompilerParams(vmem_limit_bytes=VMEM_LIMIT),
        cost_estimate=pl.CostEstimate(
            flops=total * total,
            bytes_accessed=HEAD_DIM * total,
            transcendentals=0,
        ),
    )(lengths, own, other)


def backward_kernel(
    length_ref,
    own_ref,
    other_ref,
    own_back_ref,
    other_back_ref,
    out_ref,
    log_ref,
    cosine_ref,
    sine_ref,
    own_grad_ref,
    other_grad_ref,
    query_ref,
    wide_ref,
    query_flat,
    back_flat,
    query_sum,
):
    row, index = pl.program_id(0), pl.program_id(1)
    shards, _, local = own_ref.shape
    limit = length_ref[row]
    ratio = max(1, 2048 // local)
    blocks = (limit + local - 1) // local
    mine = (blocks + 1 - row) // 2
    half = HEAD_DIM // 2

    def turned_back(wide, shard):
        cosine, sine = cosine_ref[shard], sine_ref[shard]
        upper, lower = wide[:half], wide[half:]
        return jnp.concatenate(
            [upper * cosine + lower * sine, lower * cosine - upper * sine], axis=0
        ).astype(jnp.bfloat16)

    def prepare(joint_ref, back_ref, first):
        for block in range(shards // 2):
            place = slice(block * local, (block + 1) * local)
            query = joint_ref[2 * block + first, :HEAD_DIM, :]
            back = back_ref[2 * block + first]
            extra = extra_rows([1.0] + three_parts(-log_ref[first, block]), local)
            query_ref[place, :] = jnp.concatenate([query, extra], axis=0).T
            balance = jnp.sum(
                back.astype(jnp.float32) * out_ref[first, block].astype(jnp.float32),
                axis=0,
                keepdims=True,
            )
            extra = extra_rows(three_parts(-balance), local)
            wide_ref[place, :] = jnp.concatenate([back, extra], axis=0).T
            query_flat[:, place] = query
            back_flat[:, place] = back
        query_sum[...] = jnp.zeros_like(query_sum)

    def work(joint_ref, grad_ref):
        key = joint_ref[index, HEAD_DIM : 2 * HEAD_DIM, :]
        value = joint_ref[index, 2 * HEAD_DIM :, :]
        mask = mask_row(index * local, local, limit)
        wide_key = jnp.concatenate([key, extra_rows([mask, 1.0, 1.0, 1.0], local)], axis=0)
        wide_value = jnp.concatenate([value, extra_rows([1.0, 1.0, 1.0], local)], axis=0)

        def gather(start, size, carry):
            key_sum, value_sum = carry
            place = pl.ds(pl.multiple_of(start, local), size)
            scores = jnp.dot(query_ref[place, :], wide_key, preferred_element_type=jnp.float32)
            chance = jnp.exp(scores)
            change = jnp.dot(wide_ref[place, :], wide_value, preferred_element_type=jnp.float32)
            chance_low = chance.astype(jnp.bfloat16)
            score_back = (chance * change).astype(jnp.bfloat16)
            value_sum = value_sum + jnp.dot(
                back_flat[:, place], chance_low, preferred_element_type=jnp.float32
            )
            key_sum = key_sum + jnp.dot(
                query_flat[:, place], score_back, preferred_element_type=jnp.float32
            )
            query_sum[:, place] += lax.dot_general(
                key, score_back, NT, preferred_element_type=jnp.float32
            )
            return (key_sum, value_sum)

        large = mine // ratio
        zero = jnp.zeros((HEAD_DIM, local), jnp.float32)
        carry = lax.fori_loop(
            0,
            large,
            lambda block, carry: gather(block * (ratio * local), ratio * local, carry),
            (zero, zero),
        )
        key_sum, value_sum = lax.fori_loop(
            large * ratio, mine, lambda block, carry: gather(block * local, local, carry), carry
        )
        grad_ref[index, HEAD_DIM : 2 * HEAD_DIM, :] = turned_back(key_sum, index)
        grad_ref[index, 2 * HEAD_DIM :, :] = value_sum.astype(jnp.bfloat16)

    def padding(grad_ref):
        grad_ref[index, HEAD_DIM:, :] = jnp.zeros((2 * HEAD_DIM, local), jnp.bfloat16)

    def finish(grad_ref, first):
        for block in range(shards // 2):
            place = slice(block * local, (block + 1) * local)
            shard = 2 * block + first
            grad_ref[shard, :HEAD_DIM, :] = turned_back(
                query_sum[:, place] * HEAD_DIM**-0.5, shard
            )
            grad_ref[shard + 1 - 2 * first, :HEAD_DIM, :] = jnp.zeros(
                (HEAD_DIM, local), jnp.bfloat16
            )

    sides = ((own_ref, own_back_ref, own_grad_ref), (other_ref, other_back_ref, other_grad_ref))
    for which, (joint_ref, back_ref, grad_ref) in enumerate(sides):
        here = row == which
        pl.when(here & (index == 0))(functools.partial(prepare, joint_ref, back_ref, which))
        pl.when(here & (index < blocks))(functools.partial(work, joint_ref, grad_ref))
        pl.when(here & (index >= blocks))(functools.partial(padding, grad_ref))
        pl.when(here & (index == shards - 1))(functools.partial(finish, grad_ref, which))


def attend_backward(lengths, own, other, own_back, other_back, out, log_mass, cosine, sine):
    shards, _, local = own.shape
    total = shards * local
    half = shards // 2
    whole = lambda *shape: pl.BlockSpec(shape, lambda r, i: (0,) * len(shape))
    grad = jax.ShapeDtypeStruct((shards, 3 * HEAD_DIM, local), jnp.bfloat16)
    return pl.pallas_call(
        backward_kernel,
        grid=(2, shards),
        in_specs=[pl.BlockSpec(memory_space=pltpu.SMEM)]
        + [whole(shards, 3 * HEAD_DIM, local)] * 2
        + [whole(shards, HEAD_DIM, local)] * 2
        + [whole(2, half, HEAD_DIM, local), whole(2, half, 1, local)]
        + [whole(shards, HEAD_DIM // 2, local)] * 2,
        out_specs=[whole(shards, 3 * HEAD_DIM, local)] * 2,
        out_shape=[grad, grad],
        scratch_shapes=[
            pltpu.VMEM((total // 2, 2 * HEAD_DIM), jnp.bfloat16),
            pltpu.VMEM((total // 2, 2 * HEAD_DIM), jnp.bfloat16),
            pltpu.VMEM((HEAD_DIM, total // 2), jnp.bfloat16),
            pltpu.VMEM((HEAD_DIM, total // 2), jnp.bfloat16),
            pltpu.VMEM((HEAD_DIM, total // 2), jnp.float32),
        ],
        compiler_params=pltpu.CompilerParams(vmem_limit_bytes=VMEM_LIMIT),
        cost_estimate=pl.CostEstimate(
            flops=total * total,
            bytes_accessed=HEAD_DIM * total,
            transcendentals=0,
        ),
    )(lengths, own, other, own_back, other_back, out, log_mass, cosine, sine)


TN = (((0,), (0,)), ((), ()))
PLAIN = (((1,), (0,)), ((), ()))
LANES = 128
GROUPS = 4
RUNS = 8
UNITS = FF // GROUPS
EXPAND_RUN = -(-2 * UNITS // (16 * RUNS)) * 16
SHRINK_RUN = -(-UNITS // (16 * RUNS)) * 16


def run_segments(start, stop, run):
    segments = []
    while start < stop:
        index = start // run
        end = min(stop, (index + 1) * run)
        segments.append((index, start - index * run, start, end - start))
        start = end
    return segments


def feed_kernel(
    second_ref,
    upstream_ref,
    active_ref,
    gate_ref,
    shrink_ref,
    shrunk_ref,
    second_back_ref,
    parts_ref,
    grads_ref,
    zero_ref,
    send_ref,
    zero_send_ref,
):
    index = pl.program_id(0)

    def joined(ref):
        return jnp.concatenate([ref[piece, 0] for piece in range(ref.shape[0])], axis=1)

    def product(left, right, dims):
        return lax.dot_general(left, right, dims, preferred_element_type=jnp.float32)

    def grad_copies(half, pair):
        moves = []
        for kind, member in ((0, pair), (1, pair + 2)):
            for run, place, offset, size in run_segments(
                half * UNITS, (half + 1) * UNITS, EXPAND_RUN
            ):
                moves.append((kind, offset - half * UNITS, run, member, place, size))
        for run, place, offset, size in run_segments(0, UNITS, SHRINK_RUN):
            moves.append((2, offset, run, 2 * pair + half, EXPAND_RUN + place, size))
        return [
            pltpu.make_async_copy(
                grads_ref.at[half, kind, pl.ds(offset, size), :],
                parts_ref.at[run, member, pl.ds(place, size), :],
                send_ref.at[half, number],
            )
            for number, (kind, offset, run, member, place, size) in enumerate(moves)
        ]

    def zero_copies():
        moves = []
        for member in range(GROUPS):
            for base, run_size, total in ((0, EXPAND_RUN, 2 * UNITS), (EXPAND_RUN, SHRINK_RUN, UNITS)):
                for run, place, _, size in run_segments(total, RUNS * run_size, run_size):
                    moves.append((run, member, base + place, size))
        return [
            pltpu.make_async_copy(
                zero_ref.at[pl.ds(0, size), :],
                parts_ref.at[run, member, pl.ds(place, size), :],
                zero_send_ref.at[number],
            )
            for number, (run, member, place, size) in enumerate(moves)
        ]

    @pl.when(index == 0)
    def fill():
        zero_ref[...] = jnp.zeros_like(zero_ref)
        for copy in zero_copies():
            copy.start()

    active, gate, shrink = joined(active_ref), joined(gate_ref), joined(shrink_ref)
    second, upstream = second_ref[...], upstream_ref[...]
    input_active = product(second, active, NT)
    input_gate = product(second, gate, NT)
    hidden_back = product(upstream, shrink, NT)
    below = 0.5 + 0.5 * lax.erf(input_active * 0.5**0.5)
    bell = jnp.exp(-0.5 * input_active * input_active) * (0.5 / math.pi) ** 0.5
    curve = input_active * below
    hidden = (curve * input_gate).astype(jnp.bfloat16)
    active_back = (hidden_back * input_gate * (below + input_active * bell)).astype(jnp.bfloat16)
    gate_back = (hidden_back * curve).astype(jnp.bfloat16)
    shrunk = product(hidden, shrink, PLAIN)
    second_back = product(active_back, active, PLAIN) + product(gate_back, gate, PLAIN)

    @pl.when(index == 0)
    def begin():
        shrunk_ref[...] = shrunk
        second_back_ref[...] = second_back

    @pl.when(index > 0)
    def add():
        shrunk_ref[...] += shrunk
        second_back_ref[...] += second_back

    for half in range(2):

        @pl.when(index % 2 == half)
        def send(half=half):
            pair = index // 2

            @pl.when(index >= 2)
            def free():
                for copy in grad_copies(half, pair - 1):
                    copy.wait()

            grads_ref[half, 0] = product(active_back, second, TN).astype(jnp.bfloat16)
            grads_ref[half, 1] = product(gate_back, second, TN).astype(jnp.bfloat16)
            grads_ref[half, 2] = product(hidden, upstream, TN).astype(jnp.bfloat16)
            for copy in grad_copies(half, pair):
                copy.start()

    @pl.when(index == GROUPS - 1)
    def drain():
        for half in range(2):
            for copy in grad_copies(half, 1):
                copy.wait()
        for copy in zero_copies():
            copy.wait()


def feed_forward(second, upstream, pieces):
    count, width = second.shape
    block = (RUNS, 1, UNITS, LANES)
    held = pl.BlockSpec((count, width), lambda i: (0, 0), pipeline_mode=pl.Buffered(1))
    wide = jax.ShapeDtypeStruct((count, width), jnp.float32)
    run = EXPAND_RUN + SHRINK_RUN
    copies = max(
        2 * len(run_segments(half * UNITS, (half + 1) * UNITS, EXPAND_RUN)) for half in range(2)
    ) + len(run_segments(0, UNITS, SHRINK_RUN))
    return pl.pallas_call(
        feed_kernel,
        grid=(GROUPS,),
        in_specs=[
            held,
            held,
            pl.BlockSpec(block, lambda i: (0, i // 2, i % 2, 0)),
            pl.BlockSpec(block, lambda i: (0, i // 2 + 2, i % 2, 0)),
            pl.BlockSpec(block, lambda i: (0, i, 2, 0)),
        ],
        out_specs=[held, held, pl.BlockSpec(memory_space=pl.ANY)],
        out_shape=[wide, wide, jax.ShapeDtypeStruct((RUNS, GROUPS, run, width), jnp.bfloat16)],
        scratch_shapes=[
            pltpu.VMEM((2, 3, UNITS, width), jnp.bfloat16),
            pltpu.VMEM((max(EXPAND_RUN, SHRINK_RUN), width), jnp.bfloat16),
            pltpu.SemaphoreType.DMA((2, copies)),
            pltpu.SemaphoreType.DMA((GROUPS * 8,)),
        ],
        compiler_params=pltpu.CompilerParams(vmem_limit_bytes=VMEM_LIMIT),
        cost_estimate=pl.CostEstimate(
            flops=count * width,
            bytes_accessed=count * width,
            transcendentals=0,
        ),
    )(second, upstream, pieces, pieces, pieces)


def adam_step(rotated, first, second):
    average = BETA_ONE * first + (1.0 - BETA_ONE) * rotated
    variance = BETA_TWO * second + (1.0 - BETA_TWO) * rotated * rotated
    direction = (
        average / (1.0 - BETA_ONE**STEP) / (jnp.sqrt(variance / (1.0 - BETA_TWO**STEP)) + ADAM_EPS)
    )
    return (average, variance, direction)


def body(
    tokens,
    cotangent,
    lengths,
    triple_weight,
    output_weight,
    expand_weight,
    shrink_weight,
    norm_gains,
    side_bases,
    output_right,
    triple_first,
    triple_second,
    output_first,
    output_second,
    expand_first,
    expand_second,
    shrink_first,
    shrink_second,
    gains_first,
    gains_second,
):
    rows_here, local_len, width = tokens.shape
    count = rows_here * local_len
    shards = lax.axis_size("seq")
    groups = lax.axis_size("outer") * lax.axis_size("core")
    phases = HEADS // shards
    piece = width // shards
    fsdp = ("outer", "core")
    everyone = ("seq",) + fsdp
    offset = lax.axis_index("seq") * local_len
    position = offset + jnp.arange(local_len, dtype=jnp.int32)
    cosine, sine = rotary_tables(position)
    every = jnp.arange(shards * local_len, dtype=jnp.int32)
    all_cosine, all_sine = (
        table.reshape(HEAD_DIM // 2, shards, local_len).transpose(1, 0, 2)
        for table in rotary_tables(every)
    )
    valid = (position[None, :] < lengths[:, None]).astype(jnp.float32).reshape(count, 1)
    exchange = functools.partial(lax.all_to_all, axis_name="seq", split_axis=0, concat_axis=0)

    def tied(*values):
        return lax.optimization_barrier(values)

    def gathered(shard):
        flat = lax.all_gather(shard, everyone, axis=0, tiled=False)
        return flat.reshape((shards, groups) + shard.shape)

    triple_shards = (
        triple_weight.T.astype(jnp.bfloat16)
        .reshape(-1, phases, HEAD_DIM, piece)
        .transpose(1, 0, 2, 3)
        .reshape(phases, -1, piece)
    )
    triple_pieces = [gathered(triple_shards[0])]
    for phase in range(1, phases):
        shard, triple_pieces[-1] = tied(triple_shards[phase], triple_pieces[-1])
        triple_pieces.append(gathered(shard))
    output_columns = width // groups
    lanes = min(piece, output_columns)

    def fold(block):
        rows = block.shape[0]
        return block.reshape(rows, -1, lanes).transpose(1, 0, 2).reshape(-1, lanes)

    bases_low = side_bases.astype(jnp.bfloat16)
    right_low = output_right.astype(jnp.bfloat16)
    member = lax.axis_index("outer") * lax.axis_size("core") + lax.axis_index("core")
    base_rows = piece // groups
    flat = tokens.reshape(count, width).astype(jnp.float32)
    first_normed, first_back = jax.vjp(layer_norm, flat, norm_gains[0])
    first_low = first_normed.astype(jnp.bfloat16)
    projected = [
        project_heads(pieces, first_low, cosine, sine) for pieces in triple_pieces
    ]
    triple_rows = [rows for _, rows in projected]
    joints = [exchange(joint) for joint, _ in projected]
    other_shards = jnp.concatenate(
        [
            expand_weight.T.astype(jnp.bfloat16),
            shrink_weight.astype(jnp.bfloat16),
            fold(output_weight.astype(jnp.bfloat16)),
        ],
        axis=0,
    )
    other_shards, joints[0] = tied(other_shards, joints[0])
    other_pieces = gathered(other_shards)
    chosen = jnp.stack([bases_low[0], bases_low[2], bases_low[3]])
    chosen = lax.dynamic_slice_in_dim(chosen, member * base_rows, base_rows, 1)
    chosen, other_pieces = tied(chosen, other_pieces)
    bases_full = gathered(chosen)
    expand_rows = 2 * FF // groups
    shrink_rows = FF // groups
    output_rows = (
        other_pieces[:, :, expand_rows + shrink_rows :]
        .reshape(shards, groups, output_columns // lanes, phases, HEAD_DIM, lanes)
        .transpose(3, 0, 4, 1, 2, 5)
        .reshape(phases, shards * HEAD_DIM, width)
    )
    canonical = (shards, groups, piece) == (RUNS, GROUPS, LANES)
    if canonical:
        feed_pieces = other_pieces
    else:
        feed_pieces = [
            other_pieces[:, :, start:end]
            .transpose(1, 2, 0, 3)
            .reshape(GROUPS, -1, RUNS, LANES)
            .transpose(2, 0, 1, 3)
            for start, end in ((0, expand_rows), (expand_rows, expand_rows + shrink_rows))
        ]
        feed_pieces = jnp.concatenate(feed_pieces, axis=2)
    swap = functools.partial(lax.ppermute, axis_name="core", perm=[(0, 1), (1, 0)])
    both_lengths = jnp.concatenate([lengths, swap(lengths)])
    others, forwards, attends = [], [], []
    for phase in range(phases):
        others.append(swap(joints[phase]))
        outcome = attend_forward(both_lengths, joints[phase], others[phase])
        if phase:
            attends[-1], outcome = tied(attends[-1], outcome)
        if phase < phases - 1:
            joints[phase + 1], outcome = tied(joints[phase + 1], outcome)
        forwards.append(outcome)
        attend = jnp.stack([outcome[0][0], swap(outcome[0][1])], axis=1)
        attends.append(exchange(attend.reshape(shards, HEAD_DIM, count)))
    attends = [attend.reshape(shards * HEAD_DIM, count) for attend in attends]
    expand_height = -(-expand_rows // (16 * shards)) * 16
    shrink_height = -(-shrink_rows // (16 * shards)) * 16

    def to_rows(block):
        block = exchange(block)
        return block.transpose(1, 0, 2).reshape(block.shape[1], -1)

    def padded(block, height):
        block = jnp.pad(block, ((0, height * shards - block.shape[0]), (0, 0)))
        return block.reshape(shards, height, piece)

    def by_phase(block):
        return (
            block.reshape(-1, phases, HEAD_DIM, piece)
            .transpose(1, 0, 2, 3)
            .reshape(phases, shards, -1, piece)
        )

    def from_phases(blocks):
        block = jnp.stack(blocks).astype(jnp.float32).reshape(phases, -1, HEAD_DIM, piece)
        return block.transpose(1, 0, 2, 3).reshape(-1, piece)

    moments = []
    for expand, shrink, triple in (
        (expand_first, shrink_first, triple_first),
        (expand_second, shrink_second, triple_second),
    ):
        moments += [padded(expand.T, expand_height), padded(shrink, shrink_height)]
        moments += list(by_phase(triple.T))
    moments, attends[-1], feed_pieces = tied(moments, attends[-1], feed_pieces)
    heights = [moment.shape[1] for moment in moments]
    moments = to_rows(jnp.concatenate(moments, axis=1))
    edges = [sum(heights[:index]) for index in range(len(heights) + 1)]
    moments = [moments[start:end] for start, end in zip(edges, edges[1:])]
    moments = list(zip(moments[: phases + 2], moments[phases + 2 :]))
    branch = sum(outer_sum(attends[phase], output_rows[phase]) for phase in range(phases))
    middle = flat + branch
    second_normed, second_back = jax.vjp(layer_norm, middle, norm_gains[1])
    second_low = second_normed.astype(jnp.bfloat16)
    upstream = cotangent.reshape(count, width).astype(jnp.float32) * valid
    upstream_low = upstream.astype(jnp.bfloat16)
    shrunk, second_change, parts = feed_forward(second_low, upstream_low, feed_pieces)
    moments, bases_full, shrunk, second_change, parts = tied(
        moments, bases_full, shrunk, second_change, parts
    )
    bases_full = bases_full.transpose(2, 0, 1, 3, 4).reshape(3, width, width)
    mixed = ((middle + shrunk) * valid).astype(jnp.bfloat16).reshape(tokens.shape)
    second_input, second_gain = second_back(second_change)
    middle_back = upstream + second_input
    branch_low = middle_back.astype(jnp.bfloat16)
    def halved(blocks, axis, dim):
        size = lax.axis_size(axis)
        place = lax.axis_index(axis)
        while size > 1:
            size //= 2
            shape = blocks.shape
            blocks = blocks.reshape(shape[:dim] + (2, size) + shape[dim + 1 :])
            side = (place // size) % 2
            mine = lax.dynamic_index_in_dim(blocks, side, dim, keepdims=False)
            other = lax.dynamic_index_in_dim(blocks, 1 - side, dim, keepdims=False)
            pairs = [(member, member ^ size) for member in range(lax.axis_size(axis))]
            other = lax.ppermute(other, axis, pairs)
            blocks = (mine.astype(jnp.float32) + other.astype(jnp.float32)).astype(jnp.bfloat16)
        return jnp.squeeze(blocks, dim)

    def doubled(block, axis):
        block = block[None]
        place = lax.axis_index(axis)
        step = 1
        while step < lax.axis_size(axis):
            pairs = [(member, member ^ step) for member in range(lax.axis_size(axis))]
            other = lax.ppermute(block, axis, pairs)
            upper = (place // step) % 2 == 1
            block = jnp.concatenate(
                [jnp.where(upper, other, block), jnp.where(upper, block, other)], axis=0
            )
            step *= 2
        return block

    def near_sum(blocks):
        return halved(halved(blocks, "core", 1), "outer", 0)

    def merged(*blocks):
        sizes = [math.prod(block.shape[1:]) for block in blocks]
        flat = [block.reshape(shards, -1, piece) for block in blocks]
        flat = exchange(jnp.concatenate(flat, axis=1))
        results, start = [], 0
        for block, size in zip(blocks, sizes):
            rows = size // piece
            results.append(flat[:, start : start + rows].reshape(block.shape))
            start += rows
        return results

    def widened(block):
        rows = piece * output_columns // count
        block = block.reshape(shards, piece // rows, rows, output_columns)
        return block.swapaxes(1, 2).reshape(shards, rows, count)

    def narrowed(block):
        rows = block.shape[1]
        block = block.reshape(shards, rows, piece // rows, output_columns)
        return block.swapaxes(1, 2).reshape(shards, piece, output_columns)

    def far_sum(terms):
        return jnp.sum(terms.astype(jnp.float32), axis=0).astype(jnp.bfloat16)

    def cut_rows(rows):
        return rows.reshape(rows.shape[0], shards, piece).transpose(1, 0, 2)

    outer = lax.axis_size("outer")
    output_part = jnp.stack(
        [
            jnp.dot(attend, branch_low, preferred_element_type=jnp.float32)
            .astype(jnp.bfloat16)
            .reshape(shards, HEAD_DIM, width)
            for attend in attends
        ],
        axis=1,
    )
    output_terms = near_sum(
        output_part.reshape(shards, piece, outer, -1, output_columns).transpose(2, 3, 0, 1, 4)
    )
    backs = [
        back_product(rows, branch_low).astype(jnp.bfloat16).reshape(shards, HEAD_DIM, count)
        for rows in output_rows
    ]
    attend_backs = [exchange(back) for back in backs[:-1]]
    late_back = exchange(jnp.concatenate([backs[-1], widened(output_terms)], axis=1))

    def cut(product, height):
        block = product.reshape(groups, -1, width)
        block = jnp.pad(block, ((0, 0), (0, height * shards - block.shape[1]), (0, 0)))
        return block.reshape(groups, shards, height, width)

    if not canonical:
        parts = parts.transpose(1, 0, 2, 3)
        parts = [
            cut(block.reshape(GROUPS, -1, width)[:, : size // GROUPS], height)
            for block, size, height in (
                (parts[:, :, :EXPAND_RUN], 2 * FF, expand_height),
                (parts[:, :, EXPAND_RUN:], FF, shrink_height),
            )
        ]
        parts = jnp.concatenate(parts, axis=2).transpose(1, 0, 2, 3)
    parts = parts.reshape(shards * groups, -1, width)
    owned = lax.psum_scatter(parts, everyone, scatter_dimension=0, tiled=False)
    feed_height = expand_height + shrink_height

    def soap_rows(rows, base, moment):
        rotated = plain_product(rows, base)
        direction = adam_step(rotated, *moment)[2]
        step = back_product(direction.astype(jnp.bfloat16), base)
        return rotated.astype(jnp.bfloat16), step.astype(jnp.bfloat16)

    def rotate_left(late):
        low = far_sum(narrowed(late[:, HEAD_DIM:]))
        left = outer_sum(bases_low[1], low).astype(jnp.bfloat16)
        return low, widened(left.reshape(shards, piece, output_columns))

    other_backs, grads = [], []
    for phase in range(phases):
        if phase == phases - 1:
            attend_backs.append(late_back[:, :HEAD_DIM])
        other_backs.append(swap(attend_backs[phase]))
        own_grad, other_grad = attend_backward(
            both_lengths,
            joints[phase],
            others[phase],
            attend_backs[phase],
            other_backs[phase],
            *forwards[phase],
            all_cosine,
            all_sine,
        )
        if phase == phases - 2:
            late_back, own_grad, other_grad = tied(late_back, own_grad, other_grad)
        if phase < phases - 1:
            grad = own_grad.astype(jnp.float32) + swap(other_grad).astype(jnp.float32)
            grad = grad.astype(jnp.bfloat16)
            if phase == phases - 2:
                output_low, output_left = rotate_left(late_back)
                grad = jnp.concatenate([grad, output_left], axis=1)
            grads.append(exchange(grad))
    grads, owned, own_grad, other_grad = tied(grads, owned, own_grad, other_grad)
    grad = own_grad.astype(jnp.float32) + swap(other_grad).astype(jnp.float32)
    grads.append(exchange(grad.astype(jnp.bfloat16)))
    if phases > 1:
        output_left = grads[-2][:, 3 * HEAD_DIM :]
        grads[-2] = grads[-2][:, : 3 * HEAD_DIM]
    else:
        output_low, output_left = rotate_left(late_back)
        output_left = exchange(output_left)
    output_left = far_sum(narrowed(output_left))

    def triple_sum(grad):
        joint_back = grad.reshape(shards * 3 * HEAD_DIM, count)
        part = jnp.dot(joint_back, first_low, preferred_element_type=jnp.float32)
        part = part.astype(jnp.bfloat16).reshape(shards, 3, HEAD_DIM, width).swapaxes(0, 1)
        return near_sum(part.reshape(outer, groups // outer, shards, -1, width)), joint_back

    def triple_rest(terms, phase):
        rows = far_sum(terms)
        return jnp.concatenate([rows, *soap_rows(rows, bases_full[0], moments[2 + phase])])

    last = phases - 1
    summed = [triple_sum(grads[phase]) for phase in range(last)]
    feed_rows = jnp.concatenate(
        [
            owned,
            *soap_rows(owned[:expand_height], bases_full[1], moments[0]),
            *soap_rows(owned[expand_height:], bases_full[2], moments[1]),
        ]
    )
    grads[last], summed, feed_rows = tied(grads[last], summed, feed_rows)
    settled = exchange(cut_rows(feed_rows))
    summed.append(triple_sum(grads[last]))
    joint_backs = [joint_back for _, joint_back in summed]
    terms = exchange(jnp.concatenate([term for term, _ in summed], axis=1))
    terms = jnp.split(terms, phases, axis=1)
    triple_done = [triple_rest(term, phase) for phase, term in enumerate(terms)]
    output_turned = plain_product(output_left, right_low).astype(jnp.bfloat16)
    output_turned = near_sum(
        output_turned.reshape(piece, outer, -1, output_columns).transpose(1, 2, 0, 3)
    ).astype(jnp.float32)
    output_average, output_variance, output_direction = adam_step(
        output_turned, output_first, output_second
    )
    output_wide = doubled(doubled(output_direction.astype(jnp.bfloat16), "core"), "outer")
    output_wide = output_wide.reshape(groups, piece, output_columns).swapaxes(0, 1)
    output_middle = back_product(output_wide.reshape(piece, width), right_low)
    *triple_done, output_middle = merged(
        *[cut_rows(rows) for rows in triple_done],
        jnp.broadcast_to(output_middle.astype(jnp.bfloat16), (shards, piece, output_columns)),
    )
    output_back = plain_product(bases_low[1], output_middle.reshape(width, output_columns))
    triple_lows, triple_turns, triple_steps = zip(
        *[jnp.split(done, 3, axis=1) for done in triple_done]
    )

    def settled_piece(start, height, size):
        return settled[:, start : start + height].reshape(-1, piece)[:size].astype(jnp.float32)

    expand_gradient, expand_turned_grad, expand_back = (
        settled_piece(start, expand_height, expand_rows).T
        for start in (0, feed_height, feed_height + expand_height)
    )
    shrink_gradient, shrink_turned_grad, shrink_back = (
        settled_piece(start, shrink_height, shrink_rows)
        for start in (
            expand_height,
            feed_height + 2 * expand_height,
            feed_height + 2 * expand_height + shrink_height,
        )
    )
    expand_average, expand_variance, _ = adam_step(expand_turned_grad, expand_first, expand_second)
    shrink_average, shrink_variance, _ = adam_step(shrink_turned_grad, shrink_first, shrink_second)
    triple_turned = from_phases(triple_turns).T
    triple_back = from_phases(triple_steps).T
    triple_gradient = from_phases(triple_lows).T
    triple_average, triple_variance, _ = adam_step(triple_turned, triple_first, triple_second)
    first_input, first_gain = first_back(
        sum(
            outer_sum(joint_back, rows.reshape(-1, width))
            for joint_back, rows in zip(joint_backs, triple_rows)
        )
    )
    token_gradient = (middle_back + first_input).astype(jnp.bfloat16).reshape(tokens.shape)
    gains_gradient = jnp.stack([first_gain, second_gain])
    for axis in ("core", "outer", "seq"):
        members = range(lax.axis_size(axis))
        for step in range(len(members).bit_length() - 1):
            pairs = [(member, member ^ (1 << step)) for member in members]
            gains_gradient = gains_gradient + lax.ppermute(gains_gradient, axis, pairs)
    gains_average, gains_variance, gains_direction = adam_step(
        gains_gradient, gains_first, gains_second
    )
    output_gradient = output_low.astype(jnp.float32)
    triple_updated = (triple_weight - WEIGHT_RATES[0] * triple_back) * (
        1.0 - WEIGHT_RATES[0] * DECAY_RATE
    )
    output_updated = (output_weight - WEIGHT_RATES[1] * output_back) * (
        1.0 - WEIGHT_RATES[1] * DECAY_RATE
    )
    expand_updated = (expand_weight - WEIGHT_RATES[2] * expand_back) * (
        1.0 - WEIGHT_RATES[2] * DECAY_RATE
    )
    shrink_updated = (shrink_weight - WEIGHT_RATES[3] * shrink_back) * (
        1.0 - WEIGHT_RATES[3] * DECAY_RATE
    )
    gains_updated = norm_gains - GAINS_RATE * gains_direction
    return (
        mixed,
        token_gradient,
        triple_gradient,
        output_gradient,
        expand_gradient,
        shrink_gradient,
        gains_gradient,
        triple_average,
        triple_variance,
        triple_updated,
        triple_updated.astype(jnp.bfloat16),
        output_average,
        output_variance,
        output_updated,
        output_updated.astype(jnp.bfloat16),
        expand_average,
        expand_variance,
        expand_updated,
        expand_updated.astype(jnp.bfloat16),
        shrink_average,
        shrink_variance,
        shrink_updated,
        shrink_updated.astype(jnp.bfloat16),
        gains_average,
        gains_variance,
        gains_updated,
    )


def solution(mesh):
    in_specs = (
        P(("outer", "core"), "seq", None),
        P(("outer", "core"), "seq", None),
        P(("outer", "core")),
        P("seq", ("outer", "core")),
        P("seq", ("outer", "core")),
        P("seq", ("outer", "core")),
        P(("outer", "core"), "seq"),
        P(),
        P(None, "seq", None),
        P(("outer", "core"), None),
        P("seq", ("outer", "core")),
        P("seq", ("outer", "core")),
        P("seq", ("outer", "core")),
        P("seq", ("outer", "core")),
        P("seq", ("outer", "core")),
        P("seq", ("outer", "core")),
        P(("outer", "core"), "seq"),
        P(("outer", "core"), "seq"),
        P(),
        P(),
    )
    out_specs = (
        P(("outer", "core"), "seq", None),
        P(("outer", "core"), "seq", None),
        P("seq", ("outer", "core")),
        P("seq", ("outer", "core")),
        P("seq", ("outer", "core")),
        P(("outer", "core"), "seq"),
        P(),
        P("seq", ("outer", "core")),
        P("seq", ("outer", "core")),
        P("seq", ("outer", "core")),
        P("seq", ("outer", "core")),
        P("seq", ("outer", "core")),
        P("seq", ("outer", "core")),
        P("seq", ("outer", "core")),
        P("seq", ("outer", "core")),
        P("seq", ("outer", "core")),
        P("seq", ("outer", "core")),
        P("seq", ("outer", "core")),
        P("seq", ("outer", "core")),
        P(("outer", "core"), "seq"),
        P(("outer", "core"), "seq"),
        P(("outer", "core"), "seq"),
        P(("outer", "core"), "seq"),
        P(),
        P(),
        P(),
    )
    groups = mesh.shape["fsdp"]
    devices = mesh.devices.reshape(mesh.shape["seq"], groups // 2, 2)
    split = Mesh(devices, ("seq", "outer", "core"))
    return jax.shard_map(body, mesh=split, in_specs=in_specs, out_specs=out_specs, check_vma=False)
```

```python
import functools
import math

import jax
import jax.numpy as jnp
from jax import lax
from jax.experimental import pallas as pl
from jax.experimental.pallas import tpu as pltpu
from jax.sharding import Mesh
from jax.sharding import PartitionSpec as P

HEADS = 16
HEAD_DIM = 64
FF = 2624
STEP = 10


ROPE_BASE = 160000.0
NORM_EPS = 1e-05
NEG_LARGE = -1e30
BETA_ONE = 0.95
BETA_TWO = 0.95
ADAM_EPS = 1e-08
DECAY_RATE = 0.01
WEIGHT_RATES = (0.03, 1.0, 0.03, 0.03)
GAINS_RATE = 0.8


def layer_norm(values, gain):
    centre = values - jnp.mean(values, axis=-1, keepdims=True)
    spread = jnp.mean(centre * centre, axis=-1, keepdims=True)
    return centre * lax.rsqrt(spread + NORM_EPS) * gain


def rotary_tables(position):
    halves = HEAD_DIM // 2
    frequency = ROPE_BASE ** (-2.0 * jnp.arange(halves, dtype=jnp.float32) / HEAD_DIM)
    angle = frequency[:, None] * position.astype(jnp.float32)[None, :]
    return jnp.cos(angle), jnp.sin(angle)


def outer_sum(left, right):
    return lax.dot_general(
        left, right, (((0,), (0,)), ((), ())), preferred_element_type=jnp.float32
    )


def back_product(left, right):
    return lax.dot_general(
        left, right, (((1,), (1,)), ((), ())), preferred_element_type=jnp.float32
    )


def plain_product(left, right):
    return jnp.dot(left, right, preferred_element_type=jnp.float32)


NT = (((1,), (1,)), ((), ()))
SAFE_BOUND = 60.0
MASK = -1e30
VMEM_LIMIT = 60 * 1024 * 1024


def extra_rows(rows, length, size=HEAD_DIM):
    place = lax.broadcasted_iota(jnp.int32, (size, length), 0)
    block = jnp.zeros((size, length), jnp.float32)
    for index, row in enumerate(rows):
        block = jnp.where(place == index, row, block)
    return block.astype(jnp.bfloat16)


def three_parts(row):
    high = row.astype(jnp.bfloat16).astype(jnp.float32)
    middle = (row - high).astype(jnp.bfloat16).astype(jnp.float32)
    return [high, middle, row - high - middle]


def mask_row(start, length, limit):
    place = start + lax.broadcasted_iota(jnp.int32, (1, length), 1)
    return jnp.where(place < limit, 0.0, MASK)


def project_kernel(pieces_ref, first_ref, cosine_ref, sine_ref, out_ref, rows_ref):
    shards, _, heads = pieces_ref.shape[:3]
    lanes = pieces_ref.shape[-1]
    weight = jnp.concatenate(
        [pieces_ref[shard].reshape(3 * heads * HEAD_DIM, lanes) for shard in range(shards)], axis=1
    )
    product = lax.dot_general(weight, first_ref[...], NT, preferred_element_type=jnp.float32)
    cosine, sine = cosine_ref[...], sine_ref[...]
    half = HEAD_DIM // 2
    for head in range(heads):
        for part in range(3):
            base = (part * heads + head) * HEAD_DIM
            rows_ref[head, part] = weight[base : base + HEAD_DIM]
        for part, scale in ((0, HEAD_DIM**-0.5), (1, 1.0)):
            base = (part * heads + head) * HEAD_DIM
            upper, lower = product[base : base + half], product[base + half : base + HEAD_DIM]
            turned_upper = (upper * cosine - lower * sine).astype(jnp.bfloat16)
            turned_lower = (lower * cosine + upper * sine).astype(jnp.bfloat16)
            place = part * HEAD_DIM
            out_ref[head, place : place + half, :] = turned_upper * jnp.bfloat16(scale)
            out_ref[head, place + half : place + HEAD_DIM, :] = turned_lower * jnp.bfloat16(
                scale
            )
        base = (2 * heads + head) * HEAD_DIM
        out_ref[head, 2 * HEAD_DIM :, :] = product[base : base + HEAD_DIM].astype(jnp.bfloat16)


def project_heads(pieces, first, cosine, sine):
    shards, lanes = pieces.shape[0], pieces.shape[-1]
    count, width = first.shape
    pieces = pieces.reshape(shards, 3, shards, HEAD_DIM, lanes)
    group = min(4, shards)
    half = HEAD_DIM // 2
    return pl.pallas_call(
        project_kernel,
        grid=(shards // group,),
        in_specs=[
            pl.BlockSpec(
                (shards, 3, group, HEAD_DIM, lanes), lambda g: (0, 0, g, 0, 0)
            ),
            pl.BlockSpec((count, width), lambda g: (0, 0)),
            pl.BlockSpec((half, count), lambda g: (0, 0)),
            pl.BlockSpec((half, count), lambda g: (0, 0)),
        ],
        out_specs=[
            pl.BlockSpec((group, 3 * HEAD_DIM, count), lambda g: (g, 0, 0)),
            pl.BlockSpec((group, 3, HEAD_DIM, width), lambda g: (g, 0, 0, 0)),
        ],
        out_shape=[
            jax.ShapeDtypeStruct((shards, 3 * HEAD_DIM, count), jnp.bfloat16),
            jax.ShapeDtypeStruct((shards, 3, HEAD_DIM, width), jnp.bfloat16),
        ],
        compiler_params=pltpu.CompilerParams(vmem_limit_bytes=VMEM_LIMIT),
        cost_estimate=pl.CostEstimate(
            flops=6 * width * shards * HEAD_DIM * count,
            bytes_accessed=20 * width * shards * HEAD_DIM,
            transcendentals=0,
        ),
    )(pieces, first, cosine, sine)


def forward_kernel(
    length_ref,
    own_ref,
    other_ref,
    out_ref,
    log_ref,
    query_ref,
    key_ref,
    value_ref,
    peak_ref,
    bound_ref,
):
    row, index = pl.program_id(0), pl.program_id(1)
    shards, _, local = own_ref.shape
    limit = length_ref[row]
    ratio = max(1, 2048 // local)
    blocks = (limit + local - 1) // local

    def prepare(joint_ref, first):
        query_most = jnp.zeros((1, 1), jnp.float32)
        key_most = jnp.zeros((1, 1), jnp.float32)
        for shard in range(shards):
            place = slice(shard * local, (shard + 1) * local)
            key = joint_ref[shard, HEAD_DIM : 2 * HEAD_DIM, :]
            wide_key = key.astype(jnp.float32)
            key_size = jnp.sum(wide_key * wide_key, axis=0, keepdims=True)
            key_most = jnp.maximum(key_most, jnp.max(key_size, axis=1, keepdims=True))
            extra = extra_rows([mask_row(shard * local, local, limit), 1.0], local)
            key_ref[place, :] = jnp.concatenate([key, extra], axis=0).T
            value_ref[:HEAD_DIM, place] = joint_ref[shard, 2 * HEAD_DIM :, :]
            value_ref[HEAD_DIM:, place] = extra_rows([1.0], local, 16)
        for block in range(shards // 2):
            query = joint_ref[2 * block + first, :HEAD_DIM, :]
            wide_query = query.astype(jnp.float32)
            query_size = jnp.sum(wide_query * wide_query, axis=0, keepdims=True)
            query_most = jnp.maximum(query_most, jnp.max(query_size, axis=1, keepdims=True))
            query_ref[block] = query
        bound_ref[0] = (jnp.sqrt(query_most) * jnp.sqrt(key_most))[0, 0]

    for which, joint_ref in enumerate((own_ref, other_ref)):
        pl.when((index == 0) & (row == which))(
            functools.partial(prepare, joint_ref, which)
        )

    mine = 2 * index + row < blocks

    @pl.when(jnp.logical_not(mine))
    def padding():
        out_ref[...] = jnp.zeros_like(out_ref)
        log_ref[...] = jnp.zeros_like(log_ref)

    @pl.when(mine)
    def compute():
        query = query_ref[index]
        peak_ref[...] = jnp.zeros_like(peak_ref)

        @pl.when(bound_ref[0] > SAFE_BOUND)
        def find_peak():
            plain = jnp.concatenate([query, extra_rows([1.0], local)], axis=0)

            def step(block, peak):
                place = pl.ds(pl.multiple_of(block * local, local), local)
                scores = jnp.dot(key_ref[place, :], plain, preferred_element_type=jnp.float32)
                return jnp.maximum(peak, jnp.max(scores, axis=0, keepdims=True))

            peak = lax.fori_loop(0, blocks, step, jnp.full((1, local), MASK, jnp.float32))
            peak_ref[...] = peak.astype(jnp.bfloat16).astype(jnp.float32)

        peak = peak_ref[...]
        augmented = jnp.concatenate([query, extra_rows([1.0, -peak], local)], axis=0)

        def attend(start, size, total):
            place = pl.ds(pl.multiple_of(start, local), size)
            scores = jnp.dot(key_ref[place, :], augmented, preferred_element_type=jnp.float32)
            weights = jnp.exp(scores).astype(jnp.bfloat16)
            return total + jnp.dot(
                value_ref[:, place], weights, preferred_element_type=jnp.float32
            )

        large = blocks // ratio
        total = lax.fori_loop(
            0,
            large,
            lambda block, total: attend(block * (ratio * local), ratio * local, total),
            jnp.zeros((HEAD_DIM + 16, local), jnp.float32),
        )
        total = lax.fori_loop(
            large * ratio, blocks, lambda block, total: attend(block * local, local, total), total
        )
        mass = total[HEAD_DIM : HEAD_DIM + 1, :]
        out_ref[0, 0] = (total[:HEAD_DIM, :] / mass).astype(jnp.bfloat16)
        log_ref[0, 0] = peak + jnp.log(mass)


def attend_forward(lengths, own, other):
    shards, _, local = own.shape
    total = shards * local
    half = shards // 2
    joint = pl.BlockSpec((shards, 3 * HEAD_DIM, local), lambda r, i: (0, 0, 0))
    return pl.pallas_call(
        forward_kernel,
        grid=(2, half),
        in_specs=[pl.BlockSpec(memory_space=pltpu.SMEM), joint, joint],
        out_specs=[
            pl.BlockSpec((1, 1, HEAD_DIM, local), lambda r, i: (r, i, 0, 0)),
            pl.BlockSpec((1, 1, 1, local), lambda r, i: (r, i, 0, 0)),
        ],
        out_shape=[
            jax.ShapeDtypeStruct((2, half, HEAD_DIM, local), jnp.bfloat16),
            jax.ShapeDtypeStruct((2, half, 1, local), jnp.float32),
        ],
        scratch_shapes=[
            pltpu.VMEM((half, HEAD_DIM, local), jnp.bfloat16),
            pltpu.VMEM((total, 2 * HEAD_DIM), jnp.bfloat16),
            pltpu.VMEM((HEAD_DIM + 16, total), jnp.bfloat16),
            pltpu.VMEM((1, local), jnp.float32),
            pltpu.SMEM((1,), jnp.float32),
        ],
        compiler_params=pltpu.CompilerParams(vmem_limit_bytes=VMEM_LIMIT),
        cost_estimate=pl.CostEstimate(
            flops=total * total,
            bytes_accessed=HEAD_DIM * total,
            transcendentals=0,
        ),
    )(lengths, own, other)


def backward_kernel(
    length_ref,
    own_ref,
    other_ref,
    own_back_ref,
    other_back_ref,
    out_ref,
    log_ref,
    cosine_ref,
    sine_ref,
    own_grad_ref,
    other_grad_ref,
    query_ref,
    wide_ref,
    query_flat,
    back_flat,
    query_sum,
):
    row, index = pl.program_id(0), pl.program_id(1)
    shards, _, local = own_ref.shape
    limit = length_ref[row]
    ratio = max(1, 2048 // local)
    blocks = (limit + local - 1) // local
    mine = (blocks + 1 - row) // 2
    half = HEAD_DIM // 2

    def turned_back(wide, shard):
        cosine, sine = cosine_ref[shard], sine_ref[shard]
        upper, lower = wide[:half], wide[half:]
        return jnp.concatenate(
            [upper * cosine + lower * sine, lower * cosine - upper * sine], axis=0
        ).astype(jnp.bfloat16)

    def prepare(joint_ref, back_ref, first):
        for block in range(shards // 2):
            place = slice(block * local, (block + 1) * local)
            query = joint_ref[2 * block + first, :HEAD_DIM, :]
            back = back_ref[2 * block + first]
            extra = extra_rows([1.0] + three_parts(-log_ref[first, block]), local)
            query_ref[place, :] = jnp.concatenate([query, extra], axis=0).T
            balance = jnp.sum(
                back.astype(jnp.float32) * out_ref[first, block].astype(jnp.float32),
                axis=0,
                keepdims=True,
            )
            extra = extra_rows(three_parts(-balance), local)
            wide_ref[place, :] = jnp.concatenate([back, extra], axis=0).T
            query_flat[:, place] = query
            back_flat[:, place] = back
        query_sum[...] = jnp.zeros_like(query_sum)

    def work(joint_ref, grad_ref):
        key = joint_ref[index, HEAD_DIM : 2 * HEAD_DIM, :]
        value = joint_ref[index, 2 * HEAD_DIM :, :]
        mask = mask_row(index * local, local, limit)
        wide_key = jnp.concatenate([key, extra_rows([mask, 1.0, 1.0, 1.0], local)], axis=0)
        wide_value = jnp.concatenate([value, extra_rows([1.0, 1.0, 1.0], local)], axis=0)

        def gather(start, size, carry):
            key_sum, value_sum = carry
            place = pl.ds(pl.multiple_of(start, local), size)
            scores = jnp.dot(query_ref[place, :], wide_key, preferred_element_type=jnp.float32)
            chance = jnp.exp(scores)
            change = jnp.dot(wide_ref[place, :], wide_value, preferred_element_type=jnp.float32)
            chance_low = chance.astype(jnp.bfloat16)
            score_back = (chance * change).astype(jnp.bfloat16)
            value_sum = value_sum + jnp.dot(
                back_flat[:, place], chance_low, preferred_element_type=jnp.float32
            )
            key_sum = key_sum + jnp.dot(
                query_flat[:, place], score_back, preferred_element_type=jnp.float32
            )
            query_sum[:, place] += lax.dot_general(
                key, score_back, NT, preferred_element_type=jnp.float32
            )
            return (key_sum, value_sum)

        large = mine // ratio
        zero = jnp.zeros((HEAD_DIM, local), jnp.float32)
        carry = lax.fori_loop(
            0,
            large,
            lambda block, carry: gather(block * (ratio * local), ratio * local, carry),
            (zero, zero),
        )
        key_sum, value_sum = lax.fori_loop(
            large * ratio, mine, lambda block, carry: gather(block * local, local, carry), carry
        )
        grad_ref[index, HEAD_DIM : 2 * HEAD_DIM, :] = turned_back(key_sum, index)
        grad_ref[index, 2 * HEAD_DIM :, :] = value_sum.astype(jnp.bfloat16)

    def padding(grad_ref):
        grad_ref[index, HEAD_DIM:, :] = jnp.zeros((2 * HEAD_DIM, local), jnp.bfloat16)

    def finish(grad_ref, first):
        for block in range(shards // 2):
            place = slice(block * local, (block + 1) * local)
            shard = 2 * block + first
            grad_ref[shard, :HEAD_DIM, :] = turned_back(
                query_sum[:, place] * HEAD_DIM**-0.5, shard
            )
            grad_ref[shard + 1 - 2 * first, :HEAD_DIM, :] = jnp.zeros(
                (HEAD_DIM, local), jnp.bfloat16
            )

    sides = ((own_ref, own_back_ref, own_grad_ref), (other_ref, other_back_ref, other_grad_ref))
    for which, (joint_ref, back_ref, grad_ref) in enumerate(sides):
        here = row == which
        pl.when(here & (index == 0))(functools.partial(prepare, joint_ref, back_ref, which))
        pl.when(here & (index < blocks))(functools.partial(work, joint_ref, grad_ref))
        pl.when(here & (index >= blocks))(functools.partial(padding, grad_ref))
        pl.when(here & (index == shards - 1))(functools.partial(finish, grad_ref, which))


def attend_backward(lengths, own, other, own_back, other_back, out, log_mass, cosine, sine):
    shards, _, local = own.shape
    total = shards * local
    half = shards // 2
    whole = lambda *shape: pl.BlockSpec(shape, lambda r, i: (0,) * len(shape))
    grad = jax.ShapeDtypeStruct((shards, 3 * HEAD_DIM, local), jnp.bfloat16)
    return pl.pallas_call(
        backward_kernel,
        grid=(2, shards),
        in_specs=[pl.BlockSpec(memory_space=pltpu.SMEM)]
        + [whole(shards, 3 * HEAD_DIM, local)] * 2
        + [whole(shards, HEAD_DIM, local)] * 2
        + [whole(2, half, HEAD_DIM, local), whole(2, half, 1, local)]
        + [whole(shards, HEAD_DIM // 2, local)] * 2,
        out_specs=[whole(shards, 3 * HEAD_DIM, local)] * 2,
        out_shape=[grad, grad],
        scratch_shapes=[
            pltpu.VMEM((total // 2, 2 * HEAD_DIM), jnp.bfloat16),
            pltpu.VMEM((total // 2, 2 * HEAD_DIM), jnp.bfloat16),
            pltpu.VMEM((HEAD_DIM, total // 2), jnp.bfloat16),
            pltpu.VMEM((HEAD_DIM, total // 2), jnp.bfloat16),
            pltpu.VMEM((HEAD_DIM, total // 2), jnp.float32),
        ],
        compiler_params=pltpu.CompilerParams(vmem_limit_bytes=VMEM_LIMIT),
        cost_estimate=pl.CostEstimate(
            flops=total * total,
            bytes_accessed=HEAD_DIM * total,
            transcendentals=0,
        ),
    )(lengths, own, other, own_back, other_back, out, log_mass, cosine, sine)


TN = (((0,), (0,)), ((), ()))
PLAIN = (((1,), (0,)), ((), ()))
LANES = 128
GROUPS = 4
RUNS = 8
UNITS = FF // GROUPS
EXPAND_RUN = -(-2 * UNITS // (16 * RUNS)) * 16
SHRINK_RUN = -(-UNITS // (16 * RUNS)) * 16


def run_segments(start, stop, run):
    segments = []
    while start < stop:
        index = start // run
        end = min(stop, (index + 1) * run)
        segments.append((index, start - index * run, start, end - start))
        start = end
    return segments


def feed_kernel(
    second_ref,
    upstream_ref,
    active_ref,
    gate_ref,
    shrink_ref,
    shrunk_ref,
    second_back_ref,
    parts_ref,
    grads_ref,
    zero_ref,
    send_ref,
    zero_send_ref,
):
    index = pl.program_id(0)

    def joined(ref):
        return jnp.concatenate([ref[piece, 0] for piece in range(ref.shape[0])], axis=1)

    def product(left, right, dims):
        return lax.dot_general(left, right, dims, preferred_element_type=jnp.float32)

    def grad_copies(half, pair):
        moves = []
        for kind, member in ((0, pair), (1, pair + 2)):
            for run, place, offset, size in run_segments(
                half * UNITS, (half + 1) * UNITS, EXPAND_RUN
            ):
                moves.append((kind, offset - half * UNITS, run, member, place, size))
        for run, place, offset, size in run_segments(0, UNITS, SHRINK_RUN):
            moves.append((2, offset, run, 2 * pair + half, EXPAND_RUN + place, size))
        return [
            pltpu.make_async_copy(
                grads_ref.at[half, kind, pl.ds(offset, size), :],
                parts_ref.at[run, member, pl.ds(place, size), :],
                send_ref.at[half, number],
            )
            for number, (kind, offset, run, member, place, size) in enumerate(moves)
        ]

    def zero_copies():
        moves = []
        for member in range(GROUPS):
            for base, run_size, total in ((0, EXPAND_RUN, 2 * UNITS), (EXPAND_RUN, SHRINK_RUN, UNITS)):
                for run, place, _, size in run_segments(total, RUNS * run_size, run_size):
                    moves.append((run, member, base + place, size))
        return [
            pltpu.make_async_copy(
                zero_ref.at[pl.ds(0, size), :],
                parts_ref.at[run, member, pl.ds(place, size), :],
                zero_send_ref.at[number],
            )
            for number, (run, member, place, size) in enumerate(moves)
        ]

    @pl.when(index == 0)
    def fill():
        zero_ref[...] = jnp.zeros_like(zero_ref)
        for copy in zero_copies():
            copy.start()

    active, gate, shrink = joined(active_ref), joined(gate_ref), joined(shrink_ref)
    second, upstream = second_ref[...], upstream_ref[...]
    input_active = product(second, active, NT)
    input_gate = product(second, gate, NT)
    hidden_back = product(upstream, shrink, NT)
    below = 0.5 + 0.5 * lax.erf(input_active * 0.5**0.5)
    bell = jnp.exp(-0.5 * input_active * input_active) * (0.5 / math.pi) ** 0.5
    curve = input_active * below
    hidden = (curve * input_gate).astype(jnp.bfloat16)
    active_back = (hidden_back * input_gate * (below + input_active * bell)).astype(jnp.bfloat16)
    gate_back = (hidden_back * curve).astype(jnp.bfloat16)
    shrunk = product(hidden, shrink, PLAIN)
    second_back = product(active_back, active, PLAIN) + product(gate_back, gate, PLAIN)

    @pl.when(index == 0)
    def begin():
        shrunk_ref[...] = shrunk
        second_back_ref[...] = second_back

    @pl.when(index > 0)
    def add():
        shrunk_ref[...] += shrunk
        second_back_ref[...] += second_back

    for half in range(2):

        @pl.when(index % 2 == half)
        def send(half=half):
            pair = index // 2

            @pl.when(index >= 2)
            def free():
                for copy in grad_copies(half, pair - 1):
                    copy.wait()

            grads_ref[half, 0] = product(active_back, second, TN).astype(jnp.bfloat16)
            grads_ref[half, 1] = product(gate_back, second, TN).astype(jnp.bfloat16)
            grads_ref[half, 2] = product(hidden, upstream, TN).astype(jnp.bfloat16)
            for copy in grad_copies(half, pair):
                copy.start()

    @pl.when(index == GROUPS - 1)
    def drain():
        for half in range(2):
            for copy in grad_copies(half, 1):
                copy.wait()
        for copy in zero_copies():
            copy.wait()


def feed_forward(second, upstream, pieces):
    count, width = second.shape
    block = (RUNS, 1, UNITS, LANES)
    held = pl.BlockSpec((count, width), lambda i: (0, 0), pipeline_mode=pl.Buffered(1))
    wide = jax.ShapeDtypeStruct((count, width), jnp.float32)
    run = EXPAND_RUN + SHRINK_RUN
    copies = max(
        2 * len(run_segments(half * UNITS, (half + 1) * UNITS, EXPAND_RUN)) for half in range(2)
    ) + len(run_segments(0, UNITS, SHRINK_RUN))
    return pl.pallas_call(
        feed_kernel,
        grid=(GROUPS,),
        in_specs=[
            held,
            held,
            pl.BlockSpec(block, lambda i: (0, i // 2, i % 2, 0)),
            pl.BlockSpec(block, lambda i: (0, i // 2 + 2, i % 2, 0)),
            pl.BlockSpec(block, lambda i: (0, i, 2, 0)),
        ],
        out_specs=[held, held, pl.BlockSpec(memory_space=pl.ANY)],
        out_shape=[wide, wide, jax.ShapeDtypeStruct((RUNS, GROUPS, run, width), jnp.bfloat16)],
        scratch_shapes=[
            pltpu.VMEM((2, 3, UNITS, width), jnp.bfloat16),
            pltpu.VMEM((max(EXPAND_RUN, SHRINK_RUN), width), jnp.bfloat16),
            pltpu.SemaphoreType.DMA((2, copies)),
            pltpu.SemaphoreType.DMA((GROUPS * 8,)),
        ],
        compiler_params=pltpu.CompilerParams(vmem_limit_bytes=VMEM_LIMIT),
        cost_estimate=pl.CostEstimate(
            flops=count * width,
            bytes_accessed=count * width,
            transcendentals=0,
        ),
    )(second, upstream, pieces, pieces, pieces)


def enter_kernel(*refs):
    phases = (len(refs) - 9) // 2
    attend_refs, weight_refs = refs[:phases], refs[phases : 2 * phases]
    limit_ref, token_ref, cotangent_ref, gain_ref = refs[2 * phases : 2 * phases + 4]
    middle_ref, normal_ref, second_ref, upstream_ref, spread_ref = refs[2 * phases + 4 :]
    middle = token_ref[...].astype(jnp.float32)
    for attend_ref, weight_ref in zip(attend_refs, weight_refs):
        middle += lax.dot_general(
            attend_ref[...], weight_ref[...], TN, preferred_element_type=jnp.float32
        )
    block = middle.shape[0]
    centre = middle - jnp.mean(middle, axis=1, keepdims=True)
    scale = lax.rsqrt(jnp.mean(centre * centre, axis=1, keepdims=True) + NORM_EPS)
    normal = centre * scale
    place = pl.program_id(0) * block + lax.broadcasted_iota(jnp.int32, (block, 1), 0)
    middle_ref[...] = middle
    normal_ref[...] = normal
    spread_ref[...] = scale
    second_ref[...] = (normal * gain_ref[1:2, :]).astype(jnp.bfloat16)
    upstream_ref[...] = jnp.where(place < limit_ref[0], cotangent_ref[...], jnp.bfloat16(0.0))


def enter_feed(attends, weights, limit, tokens, cotangent, gains):
    count, width = tokens.shape
    block = min(256, count)
    rows = pl.BlockSpec((block, width), lambda i: (i, 0))
    wide = jax.ShapeDtypeStruct((count, width), jnp.float32)
    low = jax.ShapeDtypeStruct((count, width), jnp.bfloat16)
    return pl.pallas_call(
        enter_kernel,
        grid=(count // block,),
        in_specs=[pl.BlockSpec((attend.shape[0], block), lambda i: (0, i)) for attend in attends]
        + [pl.BlockSpec(weight.shape, lambda i: (0, 0)) for weight in weights]
        + [pl.BlockSpec(memory_space=pltpu.SMEM), rows, rows]
        + [pl.BlockSpec(gains.shape, lambda i: (0, 0))],
        out_specs=[rows, rows, rows, rows, pl.BlockSpec((block, 1), lambda i: (i, 0))],
        out_shape=[wide, wide, low, low, jax.ShapeDtypeStruct((count, 1), jnp.float32)],
        compiler_params=pltpu.CompilerParams(vmem_limit_bytes=VMEM_LIMIT),
        cost_estimate=pl.CostEstimate(
            flops=2 * count * width * width, bytes_accessed=20 * count * width, transcendentals=0
        ),
    )(*attends, *weights, limit, tokens, cotangent, gains)


def leave_kernel(*refs):
    phases = (len(refs) - 12) // 2
    weight_refs, back_refs = refs[:phases], refs[-phases:]
    limit_ref, shrunk_ref, change_ref, middle_ref, normal_ref, spread_ref = refs[phases : phases + 6]
    upstream_ref, gain_ref = refs[phases + 6 : phases + 8]
    mixed_ref, middle_back_ref, branch_ref, gain_grad_ref = refs[phases + 8 : phases + 12]
    index = pl.program_id(0)
    block = mixed_ref.shape[0]
    place = index * block + lax.broadcasted_iota(jnp.int32, (block, 1), 0)
    mixed = middle_ref[...] + shrunk_ref[...]
    mixed_ref[...] = jnp.where(place < limit_ref[0], mixed, 0.0).astype(jnp.bfloat16)
    change, normal = change_ref[...], normal_ref[...]
    gain_grad = jnp.sum(change * normal, axis=0, keepdims=True)

    @pl.when(index == 0)
    def begin():
        gain_grad_ref[...] = gain_grad

    @pl.when(index > 0)
    def add():
        gain_grad_ref[...] += gain_grad

    inner = change * gain_ref[1:2, :]
    inner = (
        inner
        - jnp.mean(inner, axis=1, keepdims=True)
        - normal * jnp.mean(inner * normal, axis=1, keepdims=True)
    )
    middle_back = upstream_ref[...].astype(jnp.float32) + spread_ref[...] * inner
    branch = middle_back.astype(jnp.bfloat16)
    middle_back_ref[...] = middle_back
    branch_ref[...] = branch
    for weight_ref, back_ref in zip(weight_refs, back_refs):
        back_ref[...] = lax.dot_general(
            weight_ref[...], branch, NT, preferred_element_type=jnp.float32
        ).astype(jnp.bfloat16)


def leave_feed(weights, limit, shrunk, change, middle, normal, spread, upstream, gains):
    count, width = shrunk.shape
    block = min(256, count)
    rows = pl.BlockSpec((block, width), lambda i: (i, 0))
    wide = jax.ShapeDtypeStruct((count, width), jnp.float32)
    low = jax.ShapeDtypeStruct((count, width), jnp.bfloat16)
    return pl.pallas_call(
        leave_kernel,
        grid=(count // block,),
        in_specs=[pl.BlockSpec(weight.shape, lambda i: (0, 0)) for weight in weights]
        + [pl.BlockSpec(memory_space=pltpu.SMEM), rows, rows, rows, rows]
        + [pl.BlockSpec((block, 1), lambda i: (i, 0)), rows]
        + [pl.BlockSpec(gains.shape, lambda i: (0, 0))],
        out_specs=[rows, rows, rows, pl.BlockSpec((1, width), lambda i: (0, 0))]
        + [pl.BlockSpec((weight.shape[0], block), lambda i: (0, i)) for weight in weights],
        out_shape=[low, wide, low, jax.ShapeDtypeStruct((1, width), jnp.float32)]
        + [jax.ShapeDtypeStruct((weight.shape[0], count), jnp.bfloat16) for weight in weights],
        compiler_params=pltpu.CompilerParams(vmem_limit_bytes=VMEM_LIMIT),
        cost_estimate=pl.CostEstimate(
            flops=2 * count * width * width, bytes_accessed=28 * count * width, transcendentals=0
        ),
    )(*weights, limit, shrunk, change, middle, normal, spread, upstream, gains)


def adam_step(rotated, first, second):
    average = BETA_ONE * first + (1.0 - BETA_ONE) * rotated
    variance = BETA_TWO * second + (1.0 - BETA_TWO) * rotated * rotated
    direction = (
        average / (1.0 - BETA_ONE**STEP) / (jnp.sqrt(variance / (1.0 - BETA_TWO**STEP)) + ADAM_EPS)
    )
    return (average, variance, direction)


def body(
    tokens,
    cotangent,
    lengths,
    triple_weight,
    output_weight,
    expand_weight,
    shrink_weight,
    norm_gains,
    side_bases,
    output_right,
    triple_first,
    triple_second,
    output_first,
    output_second,
    expand_first,
    expand_second,
    shrink_first,
    shrink_second,
    gains_first,
    gains_second,
):
    rows_here, local_len, width = tokens.shape
    count = rows_here * local_len
    shards = lax.axis_size("seq")
    groups = lax.axis_size("outer") * lax.axis_size("core")
    phases = HEADS // shards
    piece = width // shards
    fsdp = ("outer", "core")
    everyone = ("seq",) + fsdp
    offset = lax.axis_index("seq") * local_len
    position = offset + jnp.arange(local_len, dtype=jnp.int32)
    cosine, sine = rotary_tables(position)
    every = jnp.arange(shards * local_len, dtype=jnp.int32)
    all_cosine, all_sine = (
        table.reshape(HEAD_DIM // 2, shards, local_len).transpose(1, 0, 2)
        for table in rotary_tables(every)
    )
    valid = (position[None, :] < lengths[:, None]).astype(jnp.float32).reshape(count, 1)
    exchange = functools.partial(lax.all_to_all, axis_name="seq", split_axis=0, concat_axis=0)

    def tied(*values):
        return lax.optimization_barrier(values)

    def gathered(shard):
        flat = lax.all_gather(shard, everyone, axis=0, tiled=False)
        return flat.reshape((shards, groups) + shard.shape)

    triple_shards = (
        triple_weight.T.astype(jnp.bfloat16)
        .reshape(-1, phases, HEAD_DIM, piece)
        .transpose(1, 0, 2, 3)
        .reshape(phases, -1, piece)
    )
    triple_pieces = [gathered(triple_shards[0])]
    for phase in range(1, phases):
        shard, triple_pieces[-1] = tied(triple_shards[phase], triple_pieces[-1])
        triple_pieces.append(gathered(shard))
    output_columns = width // groups
    lanes = min(piece, output_columns)

    def fold(block):
        rows = block.shape[0]
        return block.reshape(rows, -1, lanes).transpose(1, 0, 2).reshape(-1, lanes)

    bases_low = side_bases.astype(jnp.bfloat16)
    right_low = output_right.astype(jnp.bfloat16)
    member = lax.axis_index("outer") * lax.axis_size("core") + lax.axis_index("core")
    base_rows = piece // groups
    flat = tokens.reshape(count, width).astype(jnp.float32)
    first_normed, first_back = jax.vjp(layer_norm, flat, norm_gains[0])
    first_low = first_normed.astype(jnp.bfloat16)
    projected = [
        project_heads(pieces, first_low, cosine, sine) for pieces in triple_pieces
    ]
    triple_rows = [rows for _, rows in projected]
    joints = [exchange(joint) for joint, _ in projected]
    other_shards = jnp.concatenate(
        [
            expand_weight.T.astype(jnp.bfloat16),
            shrink_weight.astype(jnp.bfloat16),
            fold(output_weight.astype(jnp.bfloat16)),
        ],
        axis=0,
    )
    other_shards, joints[0] = tied(other_shards, joints[0])
    other_pieces = gathered(other_shards)
    chosen = jnp.stack([bases_low[0], bases_low[2], bases_low[3]])
    chosen = lax.dynamic_slice_in_dim(chosen, member * base_rows, base_rows, 1)
    expand_rows = 2 * FF // groups
    shrink_rows = FF // groups
    output_rows = list(
        other_pieces[:, :, expand_rows + shrink_rows :]
        .reshape(shards, groups, output_columns // lanes, phases, HEAD_DIM, lanes)
        .transpose(3, 0, 4, 1, 2, 5)
        .reshape(phases, shards * HEAD_DIM, width)
    )
    canonical = (shards, groups, piece) == (RUNS, GROUPS, LANES)
    if canonical:
        feed_pieces = other_pieces
    else:
        feed_pieces = [
            other_pieces[:, :, start:end]
            .transpose(1, 2, 0, 3)
            .reshape(GROUPS, -1, RUNS, LANES)
            .transpose(2, 0, 1, 3)
            for start, end in ((0, expand_rows), (expand_rows, expand_rows + shrink_rows))
        ]
        feed_pieces = jnp.concatenate(feed_pieces, axis=2)
    swap = functools.partial(lax.ppermute, axis_name="core", perm=[(0, 1), (1, 0)])
    both_lengths = jnp.concatenate([lengths, swap(lengths)])
    others, forwards, attends = [], [], []
    for phase in range(phases):
        others.append(swap(joints[phase]))
        outcome = attend_forward(both_lengths, joints[phase], others[phase])
        if phase:
            attends[-1], outcome = tied(attends[-1], outcome)
        if phase < phases - 1:
            joints[phase + 1], outcome = tied(joints[phase + 1], outcome)
        forwards.append(outcome)
        attend = jnp.stack([outcome[0][0], swap(outcome[0][1])], axis=1)
        attends.append(exchange(attend.reshape(shards, HEAD_DIM, count)))
    chosen, forwards[-1] = tied(chosen, forwards[-1])
    bases_full = gathered(chosen)
    attends = [attend.reshape(shards * HEAD_DIM, count) for attend in attends]
    expand_height = -(-expand_rows // (16 * shards)) * 16
    shrink_height = -(-shrink_rows // (16 * shards)) * 16

    def to_rows(block):
        block = exchange(block)
        return block.transpose(1, 0, 2).reshape(block.shape[1], -1)

    def padded(block, height):
        block = jnp.pad(block, ((0, height * shards - block.shape[0]), (0, 0)))
        return block.reshape(shards, height, piece)

    def by_phase(block):
        return (
            block.reshape(-1, phases, HEAD_DIM, piece)
            .transpose(1, 0, 2, 3)
            .reshape(phases, shards, -1, piece)
        )

    def from_phases(blocks):
        block = jnp.stack(blocks).astype(jnp.float32).reshape(phases, -1, HEAD_DIM, piece)
        return block.transpose(1, 0, 2, 3).reshape(-1, piece)

    moments = []
    for expand, shrink, triple in (
        (expand_first, shrink_first, triple_first),
        (expand_second, shrink_second, triple_second),
    ):
        moments += [padded(expand.T, expand_height), padded(shrink, shrink_height)]
        moments += list(by_phase(triple.T))
    moments, attends[-1], feed_pieces = tied(moments, attends[-1], feed_pieces)
    heights = [moment.shape[1] for moment in moments]
    moments = to_rows(jnp.concatenate(moments, axis=1))
    edges = [sum(heights[:index]) for index in range(len(heights) + 1)]
    moments = [moments[start:end] for start, end in zip(edges, edges[1:])]
    moments = list(zip(moments[: phases + 2], moments[phases + 2 :]))
    inside = jnp.clip(lengths - offset, 0, local_len)
    middle, second_normal, second_low, upstream_low, second_spread = enter_feed(
        attends,
        output_rows,
        inside,
        tokens.reshape(count, width),
        cotangent.reshape(count, width),
        norm_gains,
    )
    shrunk, second_change, parts = feed_forward(second_low, upstream_low, feed_pieces)
    moments, bases_full, shrunk, second_change, parts = tied(
        moments, bases_full, shrunk, second_change, parts
    )
    bases_full = bases_full.transpose(2, 0, 1, 3, 4).reshape(3, width, width)
    mixed, middle_back, branch_low, second_gain, *backs = leave_feed(
        output_rows,
        inside,
        shrunk,
        second_change,
        middle,
        second_normal,
        second_spread,
        upstream_low,
        norm_gains,
    )
    mixed = mixed.reshape(tokens.shape)
    second_gain = second_gain[0]
    backs = [back.reshape(shards, HEAD_DIM, count) for back in backs]
    attend_backs = [exchange(back) for back in backs]

    def halved(blocks, axis, dim):
        size = lax.axis_size(axis)
        place = lax.axis_index(axis)
        while size > 1:
            size //= 2
            shape = blocks.shape
            blocks = blocks.reshape(shape[:dim] + (2, size) + shape[dim + 1 :])
            side = (place // size) % 2
            mine = lax.dynamic_index_in_dim(blocks, side, dim, keepdims=False)
            other = lax.dynamic_index_in_dim(blocks, 1 - side, dim, keepdims=False)
            pairs = [(member, member ^ size) for member in range(lax.axis_size(axis))]
            other = lax.ppermute(other, axis, pairs)
            blocks = (mine.astype(jnp.float32) + other.astype(jnp.float32)).astype(jnp.bfloat16)
        return jnp.squeeze(blocks, dim)

    def doubled(block, axis):
        block = block[None]
        place = lax.axis_index(axis)
        step = 1
        while step < lax.axis_size(axis):
            pairs = [(member, member ^ step) for member in range(lax.axis_size(axis))]
            other = lax.ppermute(block, axis, pairs)
            upper = (place // step) % 2 == 1
            block = jnp.concatenate(
                [jnp.where(upper, other, block), jnp.where(upper, block, other)], axis=0
            )
            step *= 2
        return block

    def near_sum(blocks):
        return halved(halved(blocks, "core", 1), "outer", 0)

    def merged(*blocks):
        sizes = [math.prod(block.shape[1:]) for block in blocks]
        flat = [block.reshape(shards, -1, piece) for block in blocks]
        flat = exchange(jnp.concatenate(flat, axis=1))
        results, start = [], 0
        for block, size in zip(blocks, sizes):
            rows = size // piece
            results.append(flat[:, start : start + rows].reshape(block.shape))
            start += rows
        return results

    def widened(block):
        rows = piece * output_columns // count
        block = block.reshape(-1, piece // rows, rows, output_columns)
        return block.swapaxes(1, 2).reshape(shards, -1, count)

    def narrowed(block):
        rows = piece * output_columns // count
        block = block.reshape(-1, rows, piece // rows, output_columns)
        return block.swapaxes(1, 2).reshape(shards, -1, piece, output_columns)

    def far_sum(terms):
        return jnp.sum(terms.astype(jnp.float32), axis=0).astype(jnp.bfloat16)

    def cut_rows(rows):
        return rows.reshape(rows.shape[0], shards, piece).transpose(1, 0, 2)

    outer = lax.axis_size("outer")
    output_part = jnp.stack(
        [
            jnp.dot(attend, branch_low, preferred_element_type=jnp.float32)
            .astype(jnp.bfloat16)
            .reshape(shards, HEAD_DIM, width)
            for attend in attends
        ],
        axis=1,
    )
    output_terms = halved(
        output_part.reshape(shards, piece, outer, -1, output_columns).transpose(0, 2, 3, 1, 4),
        "core",
        2,
    )
    def cut(product, height):
        block = product.reshape(groups, -1, width)
        block = jnp.pad(block, ((0, 0), (0, height * shards - block.shape[1]), (0, 0)))
        return block.reshape(groups, shards, height, width)

    if not canonical:
        parts = parts.transpose(1, 0, 2, 3)
        parts = [
            cut(block.reshape(GROUPS, -1, width)[:, : size // GROUPS], height)
            for block, size, height in (
                (parts[:, :, :EXPAND_RUN], 2 * FF, expand_height),
                (parts[:, :, EXPAND_RUN:], FF, shrink_height),
            )
        ]
        parts = jnp.concatenate(parts, axis=2).transpose(1, 0, 2, 3)
    parts = parts.reshape(shards * groups, -1, width)
    owned = lax.psum_scatter(parts, everyone, scatter_dimension=0, tiled=False)
    feed_height = expand_height + shrink_height

    def soap_rows(rows, base, moment):
        rotated = plain_product(rows, base)
        direction = adam_step(rotated, *moment)[2]
        step = back_product(direction.astype(jnp.bfloat16), base)
        return rotated.astype(jnp.bfloat16), step.astype(jnp.bfloat16)

    other_backs, grads = [], []
    for phase in range(phases):
        other_backs.append(swap(attend_backs[phase]))
        own_grad, other_grad = attend_backward(
            both_lengths,
            joints[phase],
            others[phase],
            attend_backs[phase],
            other_backs[phase],
            *forwards[phase],
            all_cosine,
            all_sine,
        )
        if phase < phases - 1:
            attend_backs[phase + 1], output_terms, own_grad, other_grad = tied(
                attend_backs[phase + 1], output_terms, own_grad, other_grad
            )
        else:
            grads, owned, own_grad, other_grad = tied(grads, owned, own_grad, other_grad)
        grad = own_grad.astype(jnp.float32) + swap(other_grad).astype(jnp.float32)
        grad = grad.astype(jnp.bfloat16)
        if phase == 0:
            grad = jnp.concatenate([grad, widened(output_terms)], axis=1)
        grads.append(exchange(grad))
    output_low = halved(far_sum(narrowed(grads[0][:, 3 * HEAD_DIM :])), "outer", 0)
    grads[0] = grads[0][:, : 3 * HEAD_DIM]
    output_left = outer_sum(bases_low[1], output_low).astype(jnp.bfloat16)
    output_left = output_left.reshape(shards, piece, output_columns)

    def triple_sum(grad):
        joint_back = grad.reshape(shards * 3 * HEAD_DIM, count)
        part = jnp.dot(joint_back, first_low, preferred_element_type=jnp.float32)
        part = part.astype(jnp.bfloat16).reshape(shards, 3, HEAD_DIM, width).swapaxes(0, 1)
        return near_sum(part.reshape(outer, groups // outer, shards, -1, width)), joint_back

    def triple_rest(terms, phase):
        rows = far_sum(terms)
        return jnp.concatenate([rows, *soap_rows(rows, bases_full[0], moments[2 + phase])])

    last = phases - 1
    summed = [triple_sum(grads[phase]) for phase in range(last)]
    feed_rows = jnp.concatenate(
        [
            owned,
            *soap_rows(owned[:expand_height], bases_full[1], moments[0]),
            *soap_rows(owned[expand_height:], bases_full[2], moments[1]),
        ]
    )
    grads[last], summed, feed_rows, output_left = tied(
        grads[last], summed, feed_rows, output_left
    )
    settled, output_left = merged(cut_rows(feed_rows), output_left)
    output_left = far_sum(output_left)
    summed.append(triple_sum(grads[last]))
    joint_backs = [joint_back for _, joint_back in summed]
    terms = exchange(jnp.concatenate([term for term, _ in summed], axis=1))
    terms = jnp.split(terms, phases, axis=1)
    triple_done = [triple_rest(term, phase) for phase, term in enumerate(terms)]
    output_turned = plain_product(output_left, right_low).astype(jnp.bfloat16)
    output_turned = near_sum(
        output_turned.reshape(piece, outer, -1, output_columns).transpose(1, 2, 0, 3)
    ).astype(jnp.float32)
    output_average, output_variance, output_direction = adam_step(
        output_turned, output_first, output_second
    )
    output_wide = doubled(doubled(output_direction.astype(jnp.bfloat16), "core"), "outer")
    output_wide = output_wide.reshape(groups, piece, output_columns).swapaxes(0, 1)
    output_middle = back_product(output_wide.reshape(piece, width), right_low)
    *triple_done, output_middle = merged(
        *[cut_rows(rows) for rows in triple_done],
        jnp.broadcast_to(output_middle.astype(jnp.bfloat16), (shards, piece, output_columns)),
    )
    output_back = plain_product(bases_low[1], output_middle.reshape(width, output_columns))
    triple_lows, triple_turns, triple_steps = zip(
        *[jnp.split(done, 3, axis=1) for done in triple_done]
    )

    def settled_piece(start, height, size):
        return settled[:, start : start + height].reshape(-1, piece)[:size].astype(jnp.float32)

    expand_gradient, expand_turned_grad, expand_back = (
        settled_piece(start, expand_height, expand_rows).T
        for start in (0, feed_height, feed_height + expand_height)
    )
    shrink_gradient, shrink_turned_grad, shrink_back = (
        settled_piece(start, shrink_height, shrink_rows)
        for start in (
            expand_height,
            feed_height + 2 * expand_height,
            feed_height + 2 * expand_height + shrink_height,
        )
    )
    expand_average, expand_variance, _ = adam_step(expand_turned_grad, expand_first, expand_second)
    shrink_average, shrink_variance, _ = adam_step(shrink_turned_grad, shrink_first, shrink_second)
    triple_turned = from_phases(triple_turns).T
    triple_back = from_phases(triple_steps).T
    triple_gradient = from_phases(triple_lows).T
    triple_average, triple_variance, _ = adam_step(triple_turned, triple_first, triple_second)
    first_input, first_gain = first_back(
        sum(
            outer_sum(joint_back, rows.reshape(-1, width))
            for joint_back, rows in zip(joint_backs, triple_rows)
        )
    )
    token_gradient = (middle_back + first_input).astype(jnp.bfloat16).reshape(tokens.shape)
    gains_gradient = jnp.stack([first_gain, second_gain])
    for axis in ("core", "outer", "seq"):
        members = range(lax.axis_size(axis))
        for step in range(len(members).bit_length() - 1):
            pairs = [(member, member ^ (1 << step)) for member in members]
            gains_gradient = gains_gradient + lax.ppermute(gains_gradient, axis, pairs)
    gains_average, gains_variance, gains_direction = adam_step(
        gains_gradient, gains_first, gains_second
    )
    output_gradient = output_low.astype(jnp.float32)
    triple_updated = (triple_weight - WEIGHT_RATES[0] * triple_back) * (
        1.0 - WEIGHT_RATES[0] * DECAY_RATE
    )
    output_updated = (output_weight - WEIGHT_RATES[1] * output_back) * (
        1.0 - WEIGHT_RATES[1] * DECAY_RATE
    )
    expand_updated = (expand_weight - WEIGHT_RATES[2] * expand_back) * (
        1.0 - WEIGHT_RATES[2] * DECAY_RATE
    )
    shrink_updated = (shrink_weight - WEIGHT_RATES[3] * shrink_back) * (
        1.0 - WEIGHT_RATES[3] * DECAY_RATE
    )
    gains_updated = norm_gains - GAINS_RATE * gains_direction
    return (
        mixed,
        token_gradient,
        triple_gradient,
        output_gradient,
        expand_gradient,
        shrink_gradient,
        gains_gradient,
        triple_average,
        triple_variance,
        triple_updated,
        triple_updated.astype(jnp.bfloat16),
        output_average,
        output_variance,
        output_updated,
        output_updated.astype(jnp.bfloat16),
        expand_average,
        expand_variance,
        expand_updated,
        expand_updated.astype(jnp.bfloat16),
        shrink_average,
        shrink_variance,
        shrink_updated,
        shrink_updated.astype(jnp.bfloat16),
        gains_average,
        gains_variance,
        gains_updated,
    )


def solution(mesh):
    in_specs = (
        P(("outer", "core"), "seq", None),
        P(("outer", "core"), "seq", None),
        P(("outer", "core")),
        P("seq", ("outer", "core")),
        P("seq", ("outer", "core")),
        P("seq", ("outer", "core")),
        P(("outer", "core"), "seq"),
        P(),
        P(None, "seq", None),
        P(("outer", "core"), None),
        P("seq", ("outer", "core")),
        P("seq", ("outer", "core")),
        P("seq", ("outer", "core")),
        P("seq", ("outer", "core")),
        P("seq", ("outer", "core")),
        P("seq", ("outer", "core")),
        P(("outer", "core"), "seq"),
        P(("outer", "core"), "seq"),
        P(),
        P(),
    )
    out_specs = (
        P(("outer", "core"), "seq", None),
        P(("outer", "core"), "seq", None),
        P("seq", ("outer", "core")),
        P("seq", ("outer", "core")),
        P("seq", ("outer", "core")),
        P(("outer", "core"), "seq"),
        P(),
        P("seq", ("outer", "core")),
        P("seq", ("outer", "core")),
        P("seq", ("outer", "core")),
        P("seq", ("outer", "core")),
        P("seq", ("outer", "core")),
        P("seq", ("outer", "core")),
        P("seq", ("outer", "core")),
        P("seq", ("outer", "core")),
        P("seq", ("outer", "core")),
        P("seq", ("outer", "core")),
        P("seq", ("outer", "core")),
        P("seq", ("outer", "core")),
        P(("outer", "core"), "seq"),
        P(("outer", "core"), "seq"),
        P(("outer", "core"), "seq"),
        P(("outer", "core"), "seq"),
        P(),
        P(),
        P(),
    )
    groups = mesh.shape["fsdp"]
    devices = mesh.devices.reshape(mesh.shape["seq"], groups // 2, 2)
    split = Mesh(devices, ("seq", "outer", "core"))
    return jax.shard_map(body, mesh=split, in_specs=in_specs, out_specs=out_specs, check_vma=False)
```

```python
import functools
import math

import jax
import jax.numpy as jnp
from jax import lax
from jax.experimental import pallas as pl
from jax.experimental.pallas import tpu as pltpu
from jax.sharding import Mesh
from jax.sharding import PartitionSpec as P

HEADS = 16
HEAD_DIM = 64
FF = 2624
STEP = 10


ROPE_BASE = 160000.0
NORM_EPS = 1e-05
NEG_LARGE = -1e30
BETA_ONE = 0.95
BETA_TWO = 0.95
ADAM_EPS = 1e-08
DECAY_RATE = 0.01
WEIGHT_RATES = (0.03, 1.0, 0.03, 0.03)
GAINS_RATE = 0.8


def layer_norm(values, gain):
    centre = values - jnp.mean(values, axis=-1, keepdims=True)
    spread = jnp.mean(centre * centre, axis=-1, keepdims=True)
    return centre * lax.rsqrt(spread + NORM_EPS) * gain


def rotary_tables(position):
    halves = HEAD_DIM // 2
    frequency = ROPE_BASE ** (-2.0 * jnp.arange(halves, dtype=jnp.float32) / HEAD_DIM)
    angle = frequency[:, None] * position.astype(jnp.float32)[None, :]
    return jnp.cos(angle), jnp.sin(angle)


def outer_sum(left, right):
    return lax.dot_general(
        left, right, (((0,), (0,)), ((), ())), preferred_element_type=jnp.float32
    )


def back_product(left, right):
    return lax.dot_general(
        left, right, (((1,), (1,)), ((), ())), preferred_element_type=jnp.float32
    )


def plain_product(left, right):
    return jnp.dot(left, right, preferred_element_type=jnp.float32)


NT = (((1,), (1,)), ((), ()))
SAFE_BOUND = 60.0
MASK = -1e30
VMEM_LIMIT = 60 * 1024 * 1024


def extra_rows(rows, length, size=HEAD_DIM):
    place = lax.broadcasted_iota(jnp.int32, (size, length), 0)
    block = jnp.zeros((size, length), jnp.float32)
    for index, row in enumerate(rows):
        block = jnp.where(place == index, row, block)
    return block.astype(jnp.bfloat16)


def three_parts(row):
    high = row.astype(jnp.bfloat16).astype(jnp.float32)
    middle = (row - high).astype(jnp.bfloat16).astype(jnp.float32)
    return [high, middle, row - high - middle]


def mask_row(start, length, limit):
    place = start + lax.broadcasted_iota(jnp.int32, (1, length), 1)
    return jnp.where(place < limit, 0.0, MASK)


def project_kernel(pieces_ref, first_ref, cosine_ref, sine_ref, out_ref, rows_ref, *, group):
    shards, groups, size, _ = pieces_ref.shape
    cosine, sine = cosine_ref[...], sine_ref[...]
    half = HEAD_DIM // 2

    def chunk(part, head):
        start = (part * shards + head) * HEAD_DIM
        place = slice(start % size, start % size + HEAD_DIM)
        return jnp.concatenate(
            [pieces_ref[shard, start // size, place, :] for shard in range(shards)], axis=1
        )

    for begin in range(0, shards, group):
        heads = range(begin, begin + group)
        weight = jnp.concatenate([chunk(part, head) for head in heads for part in range(3)], axis=0)
        product = lax.dot_general(weight, first_ref[...], NT, preferred_element_type=jnp.float32)
        for index, head in enumerate(heads):
            for part in range(3):
                base = (3 * index + part) * HEAD_DIM
                rows_ref[head, part] = weight[base : base + HEAD_DIM]
            for part, scale in ((0, HEAD_DIM**-0.5), (1, 1.0)):
                base = (3 * index + part) * HEAD_DIM
                upper, lower = product[base : base + half], product[base + half : base + HEAD_DIM]
                turned_upper = (upper * cosine - lower * sine).astype(jnp.bfloat16)
                turned_lower = (lower * cosine + upper * sine).astype(jnp.bfloat16)
                place = part * HEAD_DIM
                scale = jnp.bfloat16(scale)
                out_ref[head, place : place + half, :] = turned_upper * scale
                out_ref[head, place + half : place + HEAD_DIM, :] = turned_lower * scale
            base = (3 * index + 2) * HEAD_DIM
            out_ref[head, 2 * HEAD_DIM :, :] = product[base : base + HEAD_DIM].astype(jnp.bfloat16)


def project_heads(pieces, first, cosine, sine, phase):
    shards, groups, _, size, lanes = pieces.shape
    count, width = first.shape
    half = HEAD_DIM // 2
    whole = lambda *shape: pl.BlockSpec(shape, lambda i: (0,) * len(shape))
    return pl.pallas_call(
        functools.partial(project_kernel, group=min(4, shards)),
        grid=(1,),
        in_specs=[
            pl.BlockSpec((shards, groups, None, size, lanes), lambda i: (0, 0, phase, 0, 0)),
            whole(count, width),
            whole(half, count),
            whole(half, count),
        ],
        out_specs=[whole(shards, 3 * HEAD_DIM, count), whole(shards, 3, HEAD_DIM, width)],
        out_shape=[
            jax.ShapeDtypeStruct((shards, 3 * HEAD_DIM, count), jnp.bfloat16),
            jax.ShapeDtypeStruct((shards, 3, HEAD_DIM, width), jnp.bfloat16),
        ],
        compiler_params=pltpu.CompilerParams(vmem_limit_bytes=VMEM_LIMIT),
        cost_estimate=pl.CostEstimate(
            flops=6 * width * shards * HEAD_DIM * count,
            bytes_accessed=20 * width * shards * HEAD_DIM,
            transcendentals=0,
        ),
    )(pieces, first, cosine, sine)


def forward_kernel(
    length_ref,
    own_ref,
    other_ref,
    out_ref,
    log_ref,
    query_ref,
    key_ref,
    value_ref,
    peak_ref,
    bound_ref,
):
    row, index = pl.program_id(0), pl.program_id(1)
    shards, _, local = own_ref.shape
    limit = length_ref[row]
    ratio = max(1, 2048 // local)
    blocks = (limit + local - 1) // local

    def prepare(joint_ref, first):
        query_most = jnp.zeros((1, 1), jnp.float32)
        key_most = jnp.zeros((1, 1), jnp.float32)
        for shard in range(shards):
            place = slice(shard * local, (shard + 1) * local)
            key = joint_ref[shard, HEAD_DIM : 2 * HEAD_DIM, :]
            wide_key = key.astype(jnp.float32)
            key_size = jnp.sum(wide_key * wide_key, axis=0, keepdims=True)
            key_most = jnp.maximum(key_most, jnp.max(key_size, axis=1, keepdims=True))
            extra = extra_rows([mask_row(shard * local, local, limit), 1.0], local)
            key_ref[place, :] = jnp.concatenate([key, extra], axis=0).T
            value_ref[:HEAD_DIM, place] = joint_ref[shard, 2 * HEAD_DIM :, :]
            value_ref[HEAD_DIM:, place] = extra_rows([1.0], local, 16)
        for block in range(shards // 2):
            query = joint_ref[2 * block + first, :HEAD_DIM, :]
            wide_query = query.astype(jnp.float32)
            query_size = jnp.sum(wide_query * wide_query, axis=0, keepdims=True)
            query_most = jnp.maximum(query_most, jnp.max(query_size, axis=1, keepdims=True))
            query_ref[block] = query
        bound_ref[0] = (jnp.sqrt(query_most) * jnp.sqrt(key_most))[0, 0]

    for which, joint_ref in enumerate((own_ref, other_ref)):
        pl.when((index == 0) & (row == which))(
            functools.partial(prepare, joint_ref, which)
        )

    mine = 2 * index + row < blocks

    @pl.when(jnp.logical_not(mine))
    def padding():
        out_ref[...] = jnp.zeros_like(out_ref)
        log_ref[...] = jnp.zeros_like(log_ref)

    @pl.when(mine)
    def compute():
        query = query_ref[index]
        peak_ref[...] = jnp.zeros_like(peak_ref)

        @pl.when(bound_ref[0] > SAFE_BOUND)
        def find_peak():
            plain = jnp.concatenate([query, extra_rows([1.0], local)], axis=0)

            def step(block, peak):
                place = pl.ds(pl.multiple_of(block * local, local), local)
                scores = jnp.dot(key_ref[place, :], plain, preferred_element_type=jnp.float32)
                return jnp.maximum(peak, jnp.max(scores, axis=0, keepdims=True))

            peak = lax.fori_loop(0, blocks, step, jnp.full((1, local), MASK, jnp.float32))
            peak_ref[...] = peak.astype(jnp.bfloat16).astype(jnp.float32)

        peak = peak_ref[...]
        augmented = jnp.concatenate([query, extra_rows([1.0, -peak], local)], axis=0)

        def attend(start, size, total):
            place = pl.ds(pl.multiple_of(start, local), size)
            scores = jnp.dot(key_ref[place, :], augmented, preferred_element_type=jnp.float32)
            weights = jnp.exp(scores).astype(jnp.bfloat16)
            return total + jnp.dot(
                value_ref[:, place], weights, preferred_element_type=jnp.float32
            )

        large = blocks // ratio
        total = lax.fori_loop(
            0,
            large,
            lambda block, total: attend(block * (ratio * local), ratio * local, total),
            jnp.zeros((HEAD_DIM + 16, local), jnp.float32),
        )
        total = lax.fori_loop(
            large * ratio, blocks, lambda block, total: attend(block * local, local, total), total
        )
        mass = total[HEAD_DIM : HEAD_DIM + 1, :]
        out_ref[0, 0] = (total[:HEAD_DIM, :] / mass).astype(jnp.bfloat16)
        log_ref[0, 0] = peak + jnp.log(mass)


def attend_forward(lengths, own, other):
    shards, _, local = own.shape
    total = shards * local
    half = shards // 2
    joint = pl.BlockSpec((shards, 3 * HEAD_DIM, local), lambda r, i: (0, 0, 0))
    return pl.pallas_call(
        forward_kernel,
        grid=(2, half),
        in_specs=[pl.BlockSpec(memory_space=pltpu.SMEM), joint, joint],
        out_specs=[
            pl.BlockSpec((1, 1, HEAD_DIM, local), lambda r, i: (r, i, 0, 0)),
            pl.BlockSpec((1, 1, 1, local), lambda r, i: (r, i, 0, 0)),
        ],
        out_shape=[
            jax.ShapeDtypeStruct((2, half, HEAD_DIM, local), jnp.bfloat16),
            jax.ShapeDtypeStruct((2, half, 1, local), jnp.float32),
        ],
        scratch_shapes=[
            pltpu.VMEM((half, HEAD_DIM, local), jnp.bfloat16),
            pltpu.VMEM((total, 2 * HEAD_DIM), jnp.bfloat16),
            pltpu.VMEM((HEAD_DIM + 16, total), jnp.bfloat16),
            pltpu.VMEM((1, local), jnp.float32),
            pltpu.SMEM((1,), jnp.float32),
        ],
        compiler_params=pltpu.CompilerParams(vmem_limit_bytes=VMEM_LIMIT),
        cost_estimate=pl.CostEstimate(
            flops=total * total,
            bytes_accessed=HEAD_DIM * total,
            transcendentals=0,
        ),
    )(lengths, own, other)


def backward_kernel(
    length_ref,
    own_ref,
    other_ref,
    own_back_ref,
    other_back_ref,
    out_ref,
    log_ref,
    cosine_ref,
    sine_ref,
    own_grad_ref,
    other_grad_ref,
    query_ref,
    wide_ref,
    query_flat,
    back_flat,
    query_sum,
):
    row, index = pl.program_id(0), pl.program_id(1)
    shards, _, local = own_ref.shape
    limit = length_ref[row]
    ratio = max(1, 2048 // local)
    blocks = (limit + local - 1) // local
    mine = (blocks + 1 - row) // 2
    half = HEAD_DIM // 2

    def turned_back(wide, shard):
        cosine, sine = cosine_ref[shard], sine_ref[shard]
        upper, lower = wide[:half], wide[half:]
        return jnp.concatenate(
            [upper * cosine + lower * sine, lower * cosine - upper * sine], axis=0
        ).astype(jnp.bfloat16)

    def prepare(joint_ref, back_ref, first):
        for block in range(shards // 2):
            place = slice(block * local, (block + 1) * local)
            query = joint_ref[2 * block + first, :HEAD_DIM, :]
            back = back_ref[2 * block + first]
            extra = extra_rows([1.0] + three_parts(-log_ref[first, block]), local)
            query_ref[place, :] = jnp.concatenate([query, extra], axis=0).T
            balance = jnp.sum(
                back.astype(jnp.float32) * out_ref[first, block].astype(jnp.float32),
                axis=0,
                keepdims=True,
            )
            extra = extra_rows(three_parts(-balance), local)
            wide_ref[place, :] = jnp.concatenate([back, extra], axis=0).T
            query_flat[:, place] = query
            back_flat[:, place] = back
        query_sum[...] = jnp.zeros_like(query_sum)

    def work(joint_ref, grad_ref):
        key = joint_ref[index, HEAD_DIM : 2 * HEAD_DIM, :]
        value = joint_ref[index, 2 * HEAD_DIM :, :]
        mask = mask_row(index * local, local, limit)
        wide_key = jnp.concatenate([key, extra_rows([mask, 1.0, 1.0, 1.0], local)], axis=0)
        wide_value = jnp.concatenate([value, extra_rows([1.0, 1.0, 1.0], local)], axis=0)

        def gather(start, size, carry):
            key_sum, value_sum = carry
            place = pl.ds(pl.multiple_of(start, local), size)
            scores = jnp.dot(query_ref[place, :], wide_key, preferred_element_type=jnp.float32)
            chance = jnp.exp(scores)
            change = jnp.dot(wide_ref[place, :], wide_value, preferred_element_type=jnp.float32)
            chance_low = chance.astype(jnp.bfloat16)
            score_back = (chance * change).astype(jnp.bfloat16)
            value_sum = value_sum + jnp.dot(
                back_flat[:, place], chance_low, preferred_element_type=jnp.float32
            )
            key_sum = key_sum + jnp.dot(
                query_flat[:, place], score_back, preferred_element_type=jnp.float32
            )
            query_sum[:, place] += lax.dot_general(
                key, score_back, NT, preferred_element_type=jnp.float32
            )
            return (key_sum, value_sum)

        large = mine // ratio
        zero = jnp.zeros((HEAD_DIM, local), jnp.float32)
        carry = lax.fori_loop(
            0,
            large,
            lambda block, carry: gather(block * (ratio * local), ratio * local, carry),
            (zero, zero),
        )
        key_sum, value_sum = lax.fori_loop(
            large * ratio, mine, lambda block, carry: gather(block * local, local, carry), carry
        )
        grad_ref[index, HEAD_DIM : 2 * HEAD_DIM, :] = turned_back(key_sum, index)
        grad_ref[index, 2 * HEAD_DIM :, :] = value_sum.astype(jnp.bfloat16)

    def padding(grad_ref):
        grad_ref[index, HEAD_DIM:, :] = jnp.zeros((2 * HEAD_DIM, local), jnp.bfloat16)

    def finish(grad_ref, first):
        for block in range(shards // 2):
            place = slice(block * local, (block + 1) * local)
            shard = 2 * block + first
            grad_ref[shard, :HEAD_DIM, :] = turned_back(
                query_sum[:, place] * HEAD_DIM**-0.5, shard
            )
            grad_ref[shard + 1 - 2 * first, :HEAD_DIM, :] = jnp.zeros(
                (HEAD_DIM, local), jnp.bfloat16
            )

    sides = ((own_ref, own_back_ref, own_grad_ref), (other_ref, other_back_ref, other_grad_ref))
    for which, (joint_ref, back_ref, grad_ref) in enumerate(sides):
        here = row == which
        pl.when(here & (index == 0))(functools.partial(prepare, joint_ref, back_ref, which))
        pl.when(here & (index < blocks))(functools.partial(work, joint_ref, grad_ref))
        pl.when(here & (index >= blocks))(functools.partial(padding, grad_ref))
        pl.when(here & (index == shards - 1))(functools.partial(finish, grad_ref, which))


def attend_backward(lengths, own, other, own_back, other_back, out, log_mass, cosine, sine):
    shards, _, local = own.shape
    total = shards * local
    half = shards // 2
    whole = lambda *shape: pl.BlockSpec(shape, lambda r, i: (0,) * len(shape))
    grad = jax.ShapeDtypeStruct((shards, 3 * HEAD_DIM, local), jnp.bfloat16)
    return pl.pallas_call(
        backward_kernel,
        grid=(2, shards),
        in_specs=[pl.BlockSpec(memory_space=pltpu.SMEM)]
        + [whole(shards, 3 * HEAD_DIM, local)] * 2
        + [whole(shards, HEAD_DIM, local)] * 2
        + [whole(2, half, HEAD_DIM, local), whole(2, half, 1, local)]
        + [whole(shards, HEAD_DIM // 2, local)] * 2,
        out_specs=[whole(shards, 3 * HEAD_DIM, local)] * 2,
        out_shape=[grad, grad],
        scratch_shapes=[
            pltpu.VMEM((total // 2, 2 * HEAD_DIM), jnp.bfloat16),
            pltpu.VMEM((total // 2, 2 * HEAD_DIM), jnp.bfloat16),
            pltpu.VMEM((HEAD_DIM, total // 2), jnp.bfloat16),
            pltpu.VMEM((HEAD_DIM, total // 2), jnp.bfloat16),
            pltpu.VMEM((HEAD_DIM, total // 2), jnp.float32),
        ],
        compiler_params=pltpu.CompilerParams(vmem_limit_bytes=VMEM_LIMIT),
        cost_estimate=pl.CostEstimate(
            flops=total * total,
            bytes_accessed=HEAD_DIM * total,
            transcendentals=0,
        ),
    )(lengths, own, other, own_back, other_back, out, log_mass, cosine, sine)


TN = (((0,), (0,)), ((), ()))
PLAIN = (((1,), (0,)), ((), ()))
LANES = 128
GROUPS = 4
RUNS = 8
UNITS = FF // GROUPS
EXPAND_RUN = -(-2 * UNITS // (16 * RUNS)) * 16
SHRINK_RUN = -(-UNITS // (16 * RUNS)) * 16


def run_segments(start, stop, run):
    segments = []
    while start < stop:
        index = start // run
        end = min(stop, (index + 1) * run)
        segments.append((index, start - index * run, start, end - start))
        start = end
    return segments


def feed_kernel(
    second_ref,
    upstream_ref,
    active_ref,
    gate_ref,
    shrink_ref,
    shrunk_ref,
    second_back_ref,
    parts_ref,
    grads_ref,
    zero_ref,
    send_ref,
    zero_send_ref,
):
    index = pl.program_id(0)

    def joined(ref):
        return jnp.concatenate([ref[piece, 0] for piece in range(ref.shape[0])], axis=1)

    def product(left, right, dims):
        return lax.dot_general(left, right, dims, preferred_element_type=jnp.float32)

    def grad_copies(half, pair):
        moves = []
        for kind, member in ((0, pair), (1, pair + 2)):
            for run, place, offset, size in run_segments(
                half * UNITS, (half + 1) * UNITS, EXPAND_RUN
            ):
                moves.append((kind, offset - half * UNITS, run, member, place, size))
        for run, place, offset, size in run_segments(0, UNITS, SHRINK_RUN):
            moves.append((2, offset, run, 2 * pair + half, EXPAND_RUN + place, size))
        return [
            pltpu.make_async_copy(
                grads_ref.at[half, kind, pl.ds(offset, size), :],
                parts_ref.at[run, member, pl.ds(place, size), :],
                send_ref.at[half, number],
            )
            for number, (kind, offset, run, member, place, size) in enumerate(moves)
        ]

    def zero_copies():
        moves = []
        for member in range(GROUPS):
            for base, run_size, total in ((0, EXPAND_RUN, 2 * UNITS), (EXPAND_RUN, SHRINK_RUN, UNITS)):
                for run, place, _, size in run_segments(total, RUNS * run_size, run_size):
                    moves.append((run, member, base + place, size))
        return [
            pltpu.make_async_copy(
                zero_ref.at[pl.ds(0, size), :],
                parts_ref.at[run, member, pl.ds(place, size), :],
                zero_send_ref.at[number],
            )
            for number, (run, member, place, size) in enumerate(moves)
        ]

    @pl.when(index == 0)
    def fill():
        zero_ref[...] = jnp.zeros_like(zero_ref)
        for copy in zero_copies():
            copy.start()

    active, gate, shrink = joined(active_ref), joined(gate_ref), joined(shrink_ref)
    second, upstream = second_ref[...], upstream_ref[...]
    input_active = product(second, active, NT)
    input_gate = product(second, gate, NT)
    hidden_back = product(upstream, shrink, NT)
    below = 0.5 + 0.5 * lax.erf(input_active * 0.5**0.5)
    bell = jnp.exp(-0.5 * input_active * input_active) * (0.5 / math.pi) ** 0.5
    curve = input_active * below
    hidden = (curve * input_gate).astype(jnp.bfloat16)
    active_back = (hidden_back * input_gate * (below + input_active * bell)).astype(jnp.bfloat16)
    gate_back = (hidden_back * curve).astype(jnp.bfloat16)
    shrunk = product(hidden, shrink, PLAIN)
    second_back = product(active_back, active, PLAIN) + product(gate_back, gate, PLAIN)

    @pl.when(index == 0)
    def begin():
        shrunk_ref[...] = shrunk
        second_back_ref[...] = second_back

    @pl.when(index > 0)
    def add():
        shrunk_ref[...] += shrunk
        second_back_ref[...] += second_back

    for half in range(2):

        @pl.when(index % 2 == half)
        def send(half=half):
            pair = index // 2

            @pl.when(index >= 2)
            def free():
                for copy in grad_copies(half, pair - 1):
                    copy.wait()

            grads_ref[half, 0] = product(active_back, second, TN).astype(jnp.bfloat16)
            grads_ref[half, 1] = product(gate_back, second, TN).astype(jnp.bfloat16)
            grads_ref[half, 2] = product(hidden, upstream, TN).astype(jnp.bfloat16)
            for copy in grad_copies(half, pair):
                copy.start()

    @pl.when(index == GROUPS - 1)
    def drain():
        for half in range(2):
            for copy in grad_copies(half, 1):
                copy.wait()
        for copy in zero_copies():
            copy.wait()


def feed_forward(second, upstream, pieces):
    count, width = second.shape
    block = (RUNS, 1, UNITS, LANES)
    held = pl.BlockSpec((count, width), lambda i: (0, 0), pipeline_mode=pl.Buffered(1))
    wide = jax.ShapeDtypeStruct((count, width), jnp.float32)
    run = EXPAND_RUN + SHRINK_RUN
    copies = max(
        2 * len(run_segments(half * UNITS, (half + 1) * UNITS, EXPAND_RUN)) for half in range(2)
    ) + len(run_segments(0, UNITS, SHRINK_RUN))
    return pl.pallas_call(
        feed_kernel,
        grid=(GROUPS,),
        in_specs=[
            held,
            held,
            pl.BlockSpec(block, lambda i: (0, i // 2, i % 2, 0)),
            pl.BlockSpec(block, lambda i: (0, i // 2 + 2, i % 2, 0)),
            pl.BlockSpec(block, lambda i: (0, i, 2, 0)),
        ],
        out_specs=[held, held, pl.BlockSpec(memory_space=pl.ANY)],
        out_shape=[wide, wide, jax.ShapeDtypeStruct((RUNS, GROUPS, run, width), jnp.bfloat16)],
        scratch_shapes=[
            pltpu.VMEM((2, 3, UNITS, width), jnp.bfloat16),
            pltpu.VMEM((max(EXPAND_RUN, SHRINK_RUN), width), jnp.bfloat16),
            pltpu.SemaphoreType.DMA((2, copies)),
            pltpu.SemaphoreType.DMA((GROUPS * 8,)),
        ],
        compiler_params=pltpu.CompilerParams(vmem_limit_bytes=VMEM_LIMIT),
        cost_estimate=pl.CostEstimate(
            flops=count * width,
            bytes_accessed=count * width,
            transcendentals=0,
        ),
    )(second, upstream, pieces, pieces, pieces)


def enter_kernel(*refs):
    phases = (len(refs) - 9) // 2
    attend_refs, weight_refs = refs[:phases], refs[phases : 2 * phases]
    limit_ref, token_ref, cotangent_ref, gain_ref = refs[2 * phases : 2 * phases + 4]
    middle_ref, normal_ref, second_ref, upstream_ref, spread_ref = refs[2 * phases + 4 :]
    middle = token_ref[...].astype(jnp.float32)
    for attend_ref, weight_ref in zip(attend_refs, weight_refs):
        middle += lax.dot_general(
            attend_ref[...], weight_ref[...], TN, preferred_element_type=jnp.float32
        )
    block = middle.shape[0]
    centre = middle - jnp.mean(middle, axis=1, keepdims=True)
    scale = lax.rsqrt(jnp.mean(centre * centre, axis=1, keepdims=True) + NORM_EPS)
    normal = centre * scale
    place = pl.program_id(0) * block + lax.broadcasted_iota(jnp.int32, (block, 1), 0)
    middle_ref[...] = middle
    normal_ref[...] = normal
    spread_ref[...] = scale
    second_ref[...] = (normal * gain_ref[1:2, :]).astype(jnp.bfloat16)
    upstream_ref[...] = jnp.where(place < limit_ref[0], cotangent_ref[...], jnp.bfloat16(0.0))


def enter_feed(attends, weights, limit, tokens, cotangent, gains):
    count, width = tokens.shape
    block = min(256, count)
    rows = pl.BlockSpec((block, width), lambda i: (i, 0))
    wide = jax.ShapeDtypeStruct((count, width), jnp.float32)
    low = jax.ShapeDtypeStruct((count, width), jnp.bfloat16)
    return pl.pallas_call(
        enter_kernel,
        grid=(count // block,),
        in_specs=[pl.BlockSpec((attend.shape[0], block), lambda i: (0, i)) for attend in attends]
        + [pl.BlockSpec(weight.shape, lambda i: (0, 0)) for weight in weights]
        + [pl.BlockSpec(memory_space=pltpu.SMEM), rows, rows]
        + [pl.BlockSpec(gains.shape, lambda i: (0, 0))],
        out_specs=[rows, rows, rows, rows, pl.BlockSpec((block, 1), lambda i: (i, 0))],
        out_shape=[wide, wide, low, low, jax.ShapeDtypeStruct((count, 1), jnp.float32)],
        compiler_params=pltpu.CompilerParams(vmem_limit_bytes=VMEM_LIMIT),
        cost_estimate=pl.CostEstimate(
            flops=2 * count * width * width, bytes_accessed=20 * count * width, transcendentals=0
        ),
    )(*attends, *weights, limit, tokens, cotangent, gains)


def leave_kernel(*refs):
    phases = (len(refs) - 12) // 2
    weight_refs, back_refs = refs[:phases], refs[-phases:]
    limit_ref, shrunk_ref, change_ref, middle_ref, normal_ref, spread_ref = refs[phases : phases + 6]
    upstream_ref, gain_ref = refs[phases + 6 : phases + 8]
    mixed_ref, middle_back_ref, branch_ref, gain_grad_ref = refs[phases + 8 : phases + 12]
    index = pl.program_id(0)
    block = mixed_ref.shape[0]
    place = index * block + lax.broadcasted_iota(jnp.int32, (block, 1), 0)
    mixed = middle_ref[...] + shrunk_ref[...]
    mixed_ref[...] = jnp.where(place < limit_ref[0], mixed, 0.0).astype(jnp.bfloat16)
    change, normal = change_ref[...], normal_ref[...]
    gain_grad = jnp.sum(change * normal, axis=0, keepdims=True)

    @pl.when(index == 0)
    def begin():
        gain_grad_ref[...] = gain_grad

    @pl.when(index > 0)
    def add():
        gain_grad_ref[...] += gain_grad

    inner = change * gain_ref[1:2, :]
    inner = (
        inner
        - jnp.mean(inner, axis=1, keepdims=True)
        - normal * jnp.mean(inner * normal, axis=1, keepdims=True)
    )
    middle_back = upstream_ref[...].astype(jnp.float32) + spread_ref[...] * inner
    branch = middle_back.astype(jnp.bfloat16)
    middle_back_ref[...] = middle_back
    branch_ref[...] = branch
    for weight_ref, back_ref in zip(weight_refs, back_refs):
        back_ref[...] = lax.dot_general(
            weight_ref[...], branch, NT, preferred_element_type=jnp.float32
        ).astype(jnp.bfloat16)


def leave_feed(weights, limit, shrunk, change, middle, normal, spread, upstream, gains):
    count, width = shrunk.shape
    block = min(256, count)
    rows = pl.BlockSpec((block, width), lambda i: (i, 0))
    wide = jax.ShapeDtypeStruct((count, width), jnp.float32)
    low = jax.ShapeDtypeStruct((count, width), jnp.bfloat16)
    return pl.pallas_call(
        leave_kernel,
        grid=(count // block,),
        in_specs=[pl.BlockSpec(weight.shape, lambda i: (0, 0)) for weight in weights]
        + [pl.BlockSpec(memory_space=pltpu.SMEM), rows, rows, rows, rows]
        + [pl.BlockSpec((block, 1), lambda i: (i, 0)), rows]
        + [pl.BlockSpec(gains.shape, lambda i: (0, 0))],
        out_specs=[rows, rows, rows, pl.BlockSpec((1, width), lambda i: (0, 0))]
        + [pl.BlockSpec((weight.shape[0], block), lambda i: (0, i)) for weight in weights],
        out_shape=[low, wide, low, jax.ShapeDtypeStruct((1, width), jnp.float32)]
        + [jax.ShapeDtypeStruct((weight.shape[0], count), jnp.bfloat16) for weight in weights],
        compiler_params=pltpu.CompilerParams(vmem_limit_bytes=VMEM_LIMIT),
        cost_estimate=pl.CostEstimate(
            flops=2 * count * width * width, bytes_accessed=28 * count * width, transcendentals=0
        ),
    )(*weights, limit, shrunk, change, middle, normal, spread, upstream, gains)


def adam_step(rotated, first, second):
    average = BETA_ONE * first + (1.0 - BETA_ONE) * rotated
    variance = BETA_TWO * second + (1.0 - BETA_TWO) * rotated * rotated
    direction = (
        average / (1.0 - BETA_ONE**STEP) / (jnp.sqrt(variance / (1.0 - BETA_TWO**STEP)) + ADAM_EPS)
    )
    return (average, variance, direction)


def body(
    tokens,
    cotangent,
    lengths,
    triple_weight,
    output_weight,
    expand_weight,
    shrink_weight,
    norm_gains,
    side_bases,
    output_right,
    triple_first,
    triple_second,
    output_first,
    output_second,
    expand_first,
    expand_second,
    shrink_first,
    shrink_second,
    gains_first,
    gains_second,
):
    rows_here, local_len, width = tokens.shape
    count = rows_here * local_len
    shards = lax.axis_size("seq")
    groups = lax.axis_size("outer") * lax.axis_size("core")
    phases = HEADS // shards
    piece = width // shards
    fsdp = ("outer", "core")
    everyone = ("seq",) + fsdp
    offset = lax.axis_index("seq") * local_len
    position = offset + jnp.arange(local_len, dtype=jnp.int32)
    cosine, sine = rotary_tables(position)
    every = jnp.arange(shards * local_len, dtype=jnp.int32)
    all_cosine, all_sine = (
        table.reshape(HEAD_DIM // 2, shards, local_len).transpose(1, 0, 2)
        for table in rotary_tables(every)
    )
    valid = (position[None, :] < lengths[:, None]).astype(jnp.float32).reshape(count, 1)
    exchange = functools.partial(lax.all_to_all, axis_name="seq", split_axis=0, concat_axis=0)

    def tied(*values):
        return lax.optimization_barrier(values)

    def gathered(shard):
        flat = lax.all_gather(shard, everyone, axis=0, tiled=False)
        return flat.reshape((shards, groups) + shard.shape)

    triple_shards = (
        triple_weight.T.astype(jnp.bfloat16)
        .reshape(-1, phases, HEAD_DIM, piece)
        .transpose(1, 0, 2, 3)
        .reshape(phases, -1, piece)
    )
    triple_pieces = gathered(triple_shards)
    output_columns = width // groups
    lanes = min(piece, output_columns)

    def fold(block):
        rows = block.shape[0]
        return block.reshape(rows, -1, lanes).transpose(1, 0, 2).reshape(-1, lanes)

    bases_low = side_bases.astype(jnp.bfloat16)
    right_low = output_right.astype(jnp.bfloat16)
    member = lax.axis_index("outer") * lax.axis_size("core") + lax.axis_index("core")
    base_rows = piece // groups
    flat = tokens.reshape(count, width).astype(jnp.float32)
    first_normed, first_back = jax.vjp(layer_norm, flat, norm_gains[0])
    first_low = first_normed.astype(jnp.bfloat16)
    other_shards = jnp.concatenate(
        [
            expand_weight.T.astype(jnp.bfloat16),
            shrink_weight.astype(jnp.bfloat16),
            fold(output_weight.astype(jnp.bfloat16)),
        ],
        axis=0,
    )
    other_shards, triple_pieces = tied(other_shards, triple_pieces)
    projected = [
        project_heads(triple_pieces, first_low, cosine, sine, phase) for phase in range(phases)
    ]
    triple_rows = [rows for _, rows in projected]
    joints = [exchange(joint) for joint, _ in projected]
    other_pieces = gathered(other_shards)
    chosen = jnp.stack([bases_low[0], bases_low[2], bases_low[3]])
    chosen = lax.dynamic_slice_in_dim(chosen, member * base_rows, base_rows, 1)
    expand_rows = 2 * FF // groups
    shrink_rows = FF // groups
    output_rows = list(
        other_pieces[:, :, expand_rows + shrink_rows :]
        .reshape(shards, groups, output_columns // lanes, phases, HEAD_DIM, lanes)
        .transpose(3, 0, 4, 1, 2, 5)
        .reshape(phases, shards * HEAD_DIM, width)
    )
    canonical = (shards, groups, piece) == (RUNS, GROUPS, LANES)
    if canonical:
        feed_pieces = other_pieces
    else:
        feed_pieces = [
            other_pieces[:, :, start:end]
            .transpose(1, 2, 0, 3)
            .reshape(GROUPS, -1, RUNS, LANES)
            .transpose(2, 0, 1, 3)
            for start, end in ((0, expand_rows), (expand_rows, expand_rows + shrink_rows))
        ]
        feed_pieces = jnp.concatenate(feed_pieces, axis=2)
    all_cosine, all_sine, joints[0] = tied(all_cosine, all_sine, joints[0])
    swap = functools.partial(lax.ppermute, axis_name="core", perm=[(0, 1), (1, 0)])
    both_lengths = jnp.concatenate([lengths, swap(lengths)])
    others, forwards, attends = [], [], []
    for phase in range(phases):
        others.append(swap(joints[phase]))
        outcome = attend_forward(both_lengths, joints[phase], others[phase])
        if phase:
            attends[-1], outcome = tied(attends[-1], outcome)
        if phase < phases - 1:
            joints[phase + 1], outcome = tied(joints[phase + 1], outcome)
        forwards.append(outcome)
        attend = jnp.stack([outcome[0][0], swap(outcome[0][1])], axis=1)
        attends.append(exchange(attend.reshape(shards, HEAD_DIM, count)))
    chosen, forwards[-1] = tied(chosen, forwards[-1])
    bases_full = gathered(chosen)
    attends = [attend.reshape(shards * HEAD_DIM, count) for attend in attends]
    expand_height = -(-expand_rows // (16 * shards)) * 16
    shrink_height = -(-shrink_rows // (16 * shards)) * 16

    def to_rows(block):
        block = exchange(block)
        return block.transpose(1, 0, 2).reshape(block.shape[1], -1)

    def padded(block, height):
        block = jnp.pad(block, ((0, height * shards - block.shape[0]), (0, 0)))
        return block.reshape(shards, height, piece)

    def by_phase(block):
        return (
            block.reshape(-1, phases, HEAD_DIM, piece)
            .transpose(1, 0, 2, 3)
            .reshape(phases, shards, -1, piece)
        )

    def from_phases(blocks):
        block = jnp.stack(blocks).astype(jnp.float32).reshape(phases, -1, HEAD_DIM, piece)
        return block.transpose(1, 0, 2, 3).reshape(-1, piece)

    moments = []
    for expand, shrink, triple in (
        (expand_first, shrink_first, triple_first),
        (expand_second, shrink_second, triple_second),
    ):
        moments += [padded(expand.T, expand_height), padded(shrink, shrink_height)]
        moments += list(by_phase(triple.T))
    moments, attends[-1], feed_pieces = tied(moments, attends[-1], feed_pieces)
    heights = [moment.shape[1] for moment in moments]
    moments = to_rows(jnp.concatenate(moments, axis=1))
    edges = [sum(heights[:index]) for index in range(len(heights) + 1)]
    moments = [moments[start:end] for start, end in zip(edges, edges[1:])]
    moments = list(zip(moments[: phases + 2], moments[phases + 2 :]))
    inside = jnp.clip(lengths - offset, 0, local_len)
    middle, second_normal, second_low, upstream_low, second_spread = enter_feed(
        attends,
        output_rows,
        inside,
        tokens.reshape(count, width),
        cotangent.reshape(count, width),
        norm_gains,
    )
    shrunk, second_change, parts = feed_forward(second_low, upstream_low, feed_pieces)
    moments, bases_full, shrunk, second_change, parts = tied(
        moments, bases_full, shrunk, second_change, parts
    )
    mixed, middle_back, branch_low, second_gain, *backs = leave_feed(
        output_rows,
        inside,
        shrunk,
        second_change,
        middle,
        second_normal,
        second_spread,
        upstream_low,
        norm_gains,
    )
    mixed = mixed.reshape(tokens.shape)
    second_gain = second_gain[0]
    backs = [back.reshape(shards, HEAD_DIM, count) for back in backs]
    attend_backs = [exchange(back) for back in backs]

    def halved(blocks, axis, dim):
        size = lax.axis_size(axis)
        place = lax.axis_index(axis)
        while size > 1:
            size //= 2
            shape = blocks.shape
            blocks = blocks.reshape(shape[:dim] + (2, size) + shape[dim + 1 :])
            side = (place // size) % 2
            mine = lax.dynamic_index_in_dim(blocks, side, dim, keepdims=False)
            other = lax.dynamic_index_in_dim(blocks, 1 - side, dim, keepdims=False)
            pairs = [(member, member ^ size) for member in range(lax.axis_size(axis))]
            other = lax.ppermute(other, axis, pairs)
            blocks = (mine.astype(jnp.float32) + other.astype(jnp.float32)).astype(jnp.bfloat16)
        return jnp.squeeze(blocks, dim)

    def doubled(block, axis):
        block = block[None]
        place = lax.axis_index(axis)
        step = 1
        while step < lax.axis_size(axis):
            pairs = [(member, member ^ step) for member in range(lax.axis_size(axis))]
            other = lax.ppermute(block, axis, pairs)
            upper = (place // step) % 2 == 1
            block = jnp.concatenate(
                [jnp.where(upper, other, block), jnp.where(upper, block, other)], axis=0
            )
            step *= 2
        return block

    def near_sum(blocks):
        return halved(halved(blocks, "core", 1), "outer", 0)

    def merged(*blocks):
        sizes = [math.prod(block.shape[1:]) for block in blocks]
        flat = [block.reshape(shards, -1, piece) for block in blocks]
        flat = exchange(jnp.concatenate(flat, axis=1))
        results, start = [], 0
        for block, size in zip(blocks, sizes):
            rows = size // piece
            results.append(flat[:, start : start + rows].reshape(block.shape))
            start += rows
        return results

    def widened(block):
        rows = piece * output_columns // count
        block = block.reshape(-1, piece // rows, rows, output_columns)
        return block.swapaxes(1, 2).reshape(shards, -1, count)

    def narrowed(block):
        rows = piece * output_columns // count
        block = block.reshape(-1, rows, piece // rows, output_columns)
        return block.swapaxes(1, 2).reshape(shards, -1, piece, output_columns)

    def far_sum(terms):
        return jnp.sum(terms.astype(jnp.float32), axis=0).astype(jnp.bfloat16)

    def cut_rows(rows):
        return rows.reshape(rows.shape[0], shards, piece).transpose(1, 0, 2)

    outer = lax.axis_size("outer")
    output_part = jnp.stack(
        [
            jnp.dot(attend, branch_low, preferred_element_type=jnp.float32)
            .astype(jnp.bfloat16)
            .reshape(shards, HEAD_DIM, width)
            for attend in attends
        ],
        axis=1,
    )
    output_terms = halved(
        output_part.reshape(shards, piece, outer, -1, output_columns).transpose(0, 2, 3, 1, 4),
        "core",
        2,
    )
    def cut(product, height):
        block = product.reshape(groups, -1, width)
        block = jnp.pad(block, ((0, 0), (0, height * shards - block.shape[1]), (0, 0)))
        return block.reshape(groups, shards, height, width)

    if not canonical:
        parts = parts.transpose(1, 0, 2, 3)
        parts = [
            cut(block.reshape(GROUPS, -1, width)[:, : size // GROUPS], height)
            for block, size, height in (
                (parts[:, :, :EXPAND_RUN], 2 * FF, expand_height),
                (parts[:, :, EXPAND_RUN:], FF, shrink_height),
            )
        ]
        parts = jnp.concatenate(parts, axis=2).transpose(1, 0, 2, 3)
    parts = parts.reshape(shards * groups, -1, width)
    owned = lax.psum_scatter(parts, everyone, scatter_dimension=0, tiled=False)
    feed_height = expand_height + shrink_height

    def soap_rows(rows, base, moment):
        rotated = plain_product(rows, base)
        direction = adam_step(rotated, *moment)[2]
        step = back_product(direction.astype(jnp.bfloat16), base)
        return rotated.astype(jnp.bfloat16), step.astype(jnp.bfloat16)

    output_terms = widened(output_terms)
    output_terms, attend_backs[0] = tied(output_terms, attend_backs[0])
    other_backs, grads = [], []
    for phase in range(phases):
        other_backs.append(swap(attend_backs[phase]))
        own_grad, other_grad = attend_backward(
            both_lengths,
            joints[phase],
            others[phase],
            attend_backs[phase],
            other_backs[phase],
            *forwards[phase],
            all_cosine,
            all_sine,
        )
        if phase < phases - 1:
            attend_backs[phase + 1], own_grad, other_grad = tied(
                attend_backs[phase + 1], own_grad, other_grad
            )
        else:
            grads, owned, bases_full, own_grad, other_grad = tied(
                grads, owned, bases_full, own_grad, other_grad
            )
        grad = own_grad.astype(jnp.float32) + swap(other_grad).astype(jnp.float32)
        grad = grad.astype(jnp.bfloat16)
        if phase == 0:
            grad = jnp.concatenate([grad, output_terms], axis=1)
        grads.append(exchange(grad))
    output_low = halved(far_sum(narrowed(grads[0][:, 3 * HEAD_DIM :])), "outer", 0)
    grads[0] = grads[0][:, : 3 * HEAD_DIM]
    output_left = outer_sum(bases_low[1], output_low).astype(jnp.bfloat16)
    output_left = output_left.reshape(shards, piece, output_columns)

    def triple_sum(grad):
        joint_back = grad.reshape(shards * 3 * HEAD_DIM, count)
        part = jnp.dot(joint_back, first_low, preferred_element_type=jnp.float32)
        part = part.astype(jnp.bfloat16).reshape(shards, 3, HEAD_DIM, width).swapaxes(0, 1)
        return near_sum(part.reshape(outer, groups // outer, shards, -1, width)), joint_back

    def triple_rest(terms, phase):
        rows = far_sum(terms)
        return jnp.concatenate([rows, *soap_rows(rows, bases_full[0], moments[2 + phase])])

    bases_full = bases_full.transpose(2, 0, 1, 3, 4).reshape(3, width, width)
    last = phases - 1
    summed = [triple_sum(grads[phase]) for phase in range(last)]
    feed_rows = jnp.concatenate(
        [
            owned,
            *soap_rows(owned[:expand_height], bases_full[1], moments[0]),
            *soap_rows(owned[expand_height:], bases_full[2], moments[1]),
        ]
    )
    settled = jnp.concatenate(
        [cut_rows(feed_rows), output_left.reshape(shards, -1, piece)], axis=1
    )
    grads[last], summed, settled = tied(grads[last], summed, settled)
    settled = exchange(settled)
    output_left = settled[:, feed_rows.shape[0] :].reshape(shards, piece, output_columns)
    output_left = far_sum(output_left)
    summed.append(triple_sum(grads[last]))
    joint_backs = [joint_back for _, joint_back in summed]
    terms = exchange(jnp.concatenate([term for term, _ in summed], axis=1))
    terms = jnp.split(terms, phases, axis=1)
    triple_done = [triple_rest(term, phase) for phase, term in enumerate(terms)]
    output_turned = plain_product(output_left, right_low).astype(jnp.bfloat16)
    output_turned = near_sum(
        output_turned.reshape(piece, outer, -1, output_columns).transpose(1, 2, 0, 3)
    ).astype(jnp.float32)
    output_average, output_variance, output_direction = adam_step(
        output_turned, output_first, output_second
    )
    output_wide = doubled(doubled(output_direction.astype(jnp.bfloat16), "core"), "outer")
    output_wide = output_wide.reshape(groups, piece, output_columns).swapaxes(0, 1)
    output_middle = back_product(output_wide.reshape(piece, width), right_low)
    *triple_done, output_middle = merged(
        *[cut_rows(rows) for rows in triple_done],
        jnp.broadcast_to(output_middle.astype(jnp.bfloat16), (shards, piece, output_columns)),
    )
    output_back = plain_product(bases_low[1], output_middle.reshape(width, output_columns))
    triple_lows, triple_turns, triple_steps = zip(
        *[jnp.split(done, 3, axis=1) for done in triple_done]
    )

    def settled_piece(start, height, size):
        return settled[:, start : start + height].reshape(-1, piece)[:size].astype(jnp.float32)

    expand_gradient, expand_turned_grad, expand_back = (
        settled_piece(start, expand_height, expand_rows).T
        for start in (0, feed_height, feed_height + expand_height)
    )
    shrink_gradient, shrink_turned_grad, shrink_back = (
        settled_piece(start, shrink_height, shrink_rows)
        for start in (
            expand_height,
            feed_height + 2 * expand_height,
            feed_height + 2 * expand_height + shrink_height,
        )
    )
    expand_average, expand_variance, _ = adam_step(expand_turned_grad, expand_first, expand_second)
    shrink_average, shrink_variance, _ = adam_step(shrink_turned_grad, shrink_first, shrink_second)
    triple_turned = from_phases(triple_turns).T
    triple_back = from_phases(triple_steps).T
    triple_gradient = from_phases(triple_lows).T
    triple_average, triple_variance, _ = adam_step(triple_turned, triple_first, triple_second)
    first_input, first_gain = first_back(
        sum(
            outer_sum(joint_back, rows.reshape(-1, width))
            for joint_back, rows in zip(joint_backs, triple_rows)
        )
    )
    token_gradient = (middle_back + first_input).astype(jnp.bfloat16).reshape(tokens.shape)
    gains_gradient = jnp.stack([first_gain, second_gain])
    for axis in ("core", "outer", "seq"):
        members = range(lax.axis_size(axis))
        for step in range(len(members).bit_length() - 1):
            pairs = [(member, member ^ (1 << step)) for member in members]
            gains_gradient = gains_gradient + lax.ppermute(gains_gradient, axis, pairs)
    gains_average, gains_variance, gains_direction = adam_step(
        gains_gradient, gains_first, gains_second
    )
    output_gradient = output_low.astype(jnp.float32)
    triple_updated = (triple_weight - WEIGHT_RATES[0] * triple_back) * (
        1.0 - WEIGHT_RATES[0] * DECAY_RATE
    )
    output_updated = (output_weight - WEIGHT_RATES[1] * output_back) * (
        1.0 - WEIGHT_RATES[1] * DECAY_RATE
    )
    expand_updated = (expand_weight - WEIGHT_RATES[2] * expand_back) * (
        1.0 - WEIGHT_RATES[2] * DECAY_RATE
    )
    shrink_updated = (shrink_weight - WEIGHT_RATES[3] * shrink_back) * (
        1.0 - WEIGHT_RATES[3] * DECAY_RATE
    )
    gains_updated = norm_gains - GAINS_RATE * gains_direction
    return (
        mixed,
        token_gradient,
        triple_gradient,
        output_gradient,
        expand_gradient,
        shrink_gradient,
        gains_gradient,
        triple_average,
        triple_variance,
        triple_updated,
        triple_updated.astype(jnp.bfloat16),
        output_average,
        output_variance,
        output_updated,
        output_updated.astype(jnp.bfloat16),
        expand_average,
        expand_variance,
        expand_updated,
        expand_updated.astype(jnp.bfloat16),
        shrink_average,
        shrink_variance,
        shrink_updated,
        shrink_updated.astype(jnp.bfloat16),
        gains_average,
        gains_variance,
        gains_updated,
    )


def solution(mesh):
    in_specs = (
        P(("outer", "core"), "seq", None),
        P(("outer", "core"), "seq", None),
        P(("outer", "core")),
        P("seq", ("outer", "core")),
        P("seq", ("outer", "core")),
        P("seq", ("outer", "core")),
        P(("outer", "core"), "seq"),
        P(),
        P(None, "seq", None),
        P(("outer", "core"), None),
        P("seq", ("outer", "core")),
        P("seq", ("outer", "core")),
        P("seq", ("outer", "core")),
        P("seq", ("outer", "core")),
        P("seq", ("outer", "core")),
        P("seq", ("outer", "core")),
        P(("outer", "core"), "seq"),
        P(("outer", "core"), "seq"),
        P(),
        P(),
    )
    out_specs = (
        P(("outer", "core"), "seq", None),
        P(("outer", "core"), "seq", None),
        P("seq", ("outer", "core")),
        P("seq", ("outer", "core")),
        P("seq", ("outer", "core")),
        P(("outer", "core"), "seq"),
        P(),
        P("seq", ("outer", "core")),
        P("seq", ("outer", "core")),
        P("seq", ("outer", "core")),
        P("seq", ("outer", "core")),
        P("seq", ("outer", "core")),
        P("seq", ("outer", "core")),
        P("seq", ("outer", "core")),
        P("seq", ("outer", "core")),
        P("seq", ("outer", "core")),
        P("seq", ("outer", "core")),
        P("seq", ("outer", "core")),
        P("seq", ("outer", "core")),
        P(("outer", "core"), "seq"),
        P(("outer", "core"), "seq"),
        P(("outer", "core"), "seq"),
        P(("outer", "core"), "seq"),
        P(),
        P(),
        P(),
    )
    groups = mesh.shape["fsdp"]
    devices = mesh.devices.reshape(mesh.shape["seq"], groups // 2, 2)
    split = Mesh(devices, ("seq", "outer", "core"))
    return jax.shard_map(body, mesh=split, in_specs=in_specs, out_specs=out_specs, check_vma=False)
```

```python
import functools
import math

import jax
import jax.numpy as jnp
from jax import lax
from jax.experimental import pallas as pl
from jax.experimental.pallas import tpu as pltpu
from jax.sharding import Mesh
from jax.sharding import PartitionSpec as P

HEADS = 16
HEAD_DIM = 64
FF = 2624
STEP = 10


ROPE_BASE = 160000.0
NORM_EPS = 1e-05
NEG_LARGE = -1e30
BETA_ONE = 0.95
BETA_TWO = 0.95
ADAM_EPS = 1e-08
DECAY_RATE = 0.01
WEIGHT_RATES = (0.03, 1.0, 0.03, 0.03)
GAINS_RATE = 0.8


def layer_norm(values, gain):
    centre = values - jnp.mean(values, axis=-1, keepdims=True)
    spread = jnp.mean(centre * centre, axis=-1, keepdims=True)
    return centre * lax.rsqrt(spread + NORM_EPS) * gain


def rotary_tables(position):
    halves = HEAD_DIM // 2
    frequency = ROPE_BASE ** (-2.0 * jnp.arange(halves, dtype=jnp.float32) / HEAD_DIM)
    angle = frequency[:, None] * position.astype(jnp.float32)[None, :]
    return jnp.cos(angle), jnp.sin(angle)


def outer_sum(left, right):
    return lax.dot_general(
        left, right, (((0,), (0,)), ((), ())), preferred_element_type=jnp.float32
    )


def back_product(left, right):
    return lax.dot_general(
        left, right, (((1,), (1,)), ((), ())), preferred_element_type=jnp.float32
    )


def plain_product(left, right):
    return jnp.dot(left, right, preferred_element_type=jnp.float32)


NT = (((1,), (1,)), ((), ()))
SAFE_BOUND = 60.0
MASK = -1e30
VMEM_LIMIT = 60 * 1024 * 1024


def extra_rows(rows, length, size=HEAD_DIM):
    place = lax.broadcasted_iota(jnp.int32, (size, length), 0)
    block = jnp.zeros((size, length), jnp.float32)
    for index, row in enumerate(rows):
        block = jnp.where(place == index, row, block)
    return block.astype(jnp.bfloat16)


def three_parts(row):
    high = row.astype(jnp.bfloat16).astype(jnp.float32)
    middle = (row - high).astype(jnp.bfloat16).astype(jnp.float32)
    return [high, middle, row - high - middle]


def mask_row(start, length, limit):
    place = start + lax.broadcasted_iota(jnp.int32, (1, length), 1)
    return jnp.where(place < limit, 0.0, MASK)


def project_kernel(pieces_ref, first_ref, cosine_ref, sine_ref, out_ref, rows_ref, *, group):
    shards, groups, size, _ = pieces_ref.shape
    cosine, sine = cosine_ref[...], sine_ref[...]
    half = HEAD_DIM // 2

    def chunk(part, head):
        start = (part * shards + head) * HEAD_DIM
        place = slice(start % size, start % size + HEAD_DIM)
        return jnp.concatenate(
            [pieces_ref[shard, start // size, place, :] for shard in range(shards)], axis=1
        )

    for begin in range(0, shards, group):
        heads = range(begin, begin + group)
        weight = jnp.concatenate([chunk(part, head) for head in heads for part in range(3)], axis=0)
        product = lax.dot_general(weight, first_ref[...], NT, preferred_element_type=jnp.float32)
        for index, head in enumerate(heads):
            for part in range(3):
                base = (3 * index + part) * HEAD_DIM
                rows_ref[head, part] = weight[base : base + HEAD_DIM]
            for part, scale in ((0, HEAD_DIM**-0.5), (1, 1.0)):
                base = (3 * index + part) * HEAD_DIM
                upper, lower = product[base : base + half], product[base + half : base + HEAD_DIM]
                turned_upper = (upper * cosine - lower * sine).astype(jnp.bfloat16)
                turned_lower = (lower * cosine + upper * sine).astype(jnp.bfloat16)
                place = part * HEAD_DIM
                scale = jnp.bfloat16(scale)
                out_ref[head, place : place + half, :] = turned_upper * scale
                out_ref[head, place + half : place + HEAD_DIM, :] = turned_lower * scale
            base = (3 * index + 2) * HEAD_DIM
            out_ref[head, 2 * HEAD_DIM :, :] = product[base : base + HEAD_DIM].astype(jnp.bfloat16)


def project_heads(pieces, first, cosine, sine, phase):
    shards, groups, _, size, lanes = pieces.shape
    count, width = first.shape
    half = HEAD_DIM // 2
    whole = lambda *shape: pl.BlockSpec(shape, lambda i: (0,) * len(shape))
    return pl.pallas_call(
        functools.partial(project_kernel, group=min(4, shards)),
        grid=(1,),
        in_specs=[
            pl.BlockSpec((shards, groups, None, size, lanes), lambda i: (0, 0, phase, 0, 0)),
            whole(count, width),
            whole(half, count),
            whole(half, count),
        ],
        out_specs=[whole(shards, 3 * HEAD_DIM, count), whole(shards, 3, HEAD_DIM, width)],
        out_shape=[
            jax.ShapeDtypeStruct((shards, 3 * HEAD_DIM, count), jnp.bfloat16),
            jax.ShapeDtypeStruct((shards, 3, HEAD_DIM, width), jnp.bfloat16),
        ],
        compiler_params=pltpu.CompilerParams(vmem_limit_bytes=VMEM_LIMIT),
        cost_estimate=pl.CostEstimate(
            flops=6 * width * shards * HEAD_DIM * count,
            bytes_accessed=20 * width * shards * HEAD_DIM,
            transcendentals=0,
        ),
    )(pieces, first, cosine, sine)


def forward_kernel(
    length_ref,
    own_ref,
    other_ref,
    out_ref,
    log_ref,
    query_ref,
    key_ref,
    value_ref,
    peak_ref,
    bound_ref,
):
    row, index = pl.program_id(0), pl.program_id(1)
    shards, _, local = own_ref.shape
    limit = length_ref[row]
    ratio = max(1, 2048 // local)
    blocks = (limit + local - 1) // local

    def prepare(joint_ref, first):
        query_most = jnp.zeros((1, 1), jnp.float32)
        key_most = jnp.zeros((1, 1), jnp.float32)
        for shard in range(shards):
            place = slice(shard * local, (shard + 1) * local)
            key = joint_ref[shard, HEAD_DIM : 2 * HEAD_DIM, :]
            wide_key = key.astype(jnp.float32)
            key_size = jnp.sum(wide_key * wide_key, axis=0, keepdims=True)
            key_most = jnp.maximum(key_most, jnp.max(key_size, axis=1, keepdims=True))
            extra = extra_rows([mask_row(shard * local, local, limit), 1.0], local)
            key_ref[place, :] = jnp.concatenate([key, extra], axis=0).T
            value_ref[:HEAD_DIM, place] = joint_ref[shard, 2 * HEAD_DIM :, :]
            value_ref[HEAD_DIM:, place] = extra_rows([1.0], local, 16)
        for block in range(shards // 2):
            query = joint_ref[2 * block + first, :HEAD_DIM, :]
            wide_query = query.astype(jnp.float32)
            query_size = jnp.sum(wide_query * wide_query, axis=0, keepdims=True)
            query_most = jnp.maximum(query_most, jnp.max(query_size, axis=1, keepdims=True))
            query_ref[block] = query
        bound_ref[0] = (jnp.sqrt(query_most) * jnp.sqrt(key_most))[0, 0]

    for which, joint_ref in enumerate((own_ref, other_ref)):
        pl.when((index == 0) & (row == which))(
            functools.partial(prepare, joint_ref, which)
        )

    mine = 2 * index + row < blocks

    @pl.when(jnp.logical_not(mine))
    def padding():
        out_ref[...] = jnp.zeros_like(out_ref)
        log_ref[...] = jnp.zeros_like(log_ref)

    @pl.when(mine)
    def compute():
        query = query_ref[index]
        peak_ref[...] = jnp.zeros_like(peak_ref)

        @pl.when(bound_ref[0] > SAFE_BOUND)
        def find_peak():
            plain = jnp.concatenate([query, extra_rows([1.0], local)], axis=0)

            def step(block, peak):
                place = pl.ds(pl.multiple_of(block * local, local), local)
                scores = jnp.dot(key_ref[place, :], plain, preferred_element_type=jnp.float32)
                return jnp.maximum(peak, jnp.max(scores, axis=0, keepdims=True))

            peak = lax.fori_loop(0, blocks, step, jnp.full((1, local), MASK, jnp.float32))
            peak_ref[...] = peak.astype(jnp.bfloat16).astype(jnp.float32)

        peak = peak_ref[...]
        augmented = jnp.concatenate([query, extra_rows([1.0, -peak], local)], axis=0)

        def attend(start, size, total):
            place = pl.ds(pl.multiple_of(start, local), size)
            scores = jnp.dot(key_ref[place, :], augmented, preferred_element_type=jnp.float32)
            weights = jnp.exp(scores).astype(jnp.bfloat16)
            return total + jnp.dot(
                value_ref[:, place], weights, preferred_element_type=jnp.float32
            )

        large = blocks // ratio
        total = lax.fori_loop(
            0,
            large,
            lambda block, total: attend(block * (ratio * local), ratio * local, total),
            jnp.zeros((HEAD_DIM + 16, local), jnp.float32),
        )
        total = lax.fori_loop(
            large * ratio, blocks, lambda block, total: attend(block * local, local, total), total
        )
        mass = total[HEAD_DIM : HEAD_DIM + 1, :]
        out_ref[0, 0] = (total[:HEAD_DIM, :] / mass).astype(jnp.bfloat16)
        log_ref[0, 0] = peak + jnp.log(mass)


def attend_forward(lengths, own, other):
    shards, _, local = own.shape
    total = shards * local
    half = shards // 2
    joint = pl.BlockSpec((shards, 3 * HEAD_DIM, local), lambda r, i: (0, 0, 0))
    return pl.pallas_call(
        forward_kernel,
        grid=(2, half),
        in_specs=[pl.BlockSpec(memory_space=pltpu.SMEM), joint, joint],
        out_specs=[
            pl.BlockSpec((1, 1, HEAD_DIM, local), lambda r, i: (r, i, 0, 0)),
            pl.BlockSpec((1, 1, 1, local), lambda r, i: (r, i, 0, 0)),
        ],
        out_shape=[
            jax.ShapeDtypeStruct((2, half, HEAD_DIM, local), jnp.bfloat16),
            jax.ShapeDtypeStruct((2, half, 1, local), jnp.float32),
        ],
        scratch_shapes=[
            pltpu.VMEM((half, HEAD_DIM, local), jnp.bfloat16),
            pltpu.VMEM((total, 2 * HEAD_DIM), jnp.bfloat16),
            pltpu.VMEM((HEAD_DIM + 16, total), jnp.bfloat16),
            pltpu.VMEM((1, local), jnp.float32),
            pltpu.SMEM((1,), jnp.float32),
        ],
        compiler_params=pltpu.CompilerParams(vmem_limit_bytes=VMEM_LIMIT),
        cost_estimate=pl.CostEstimate(
            flops=total * total,
            bytes_accessed=HEAD_DIM * total,
            transcendentals=0,
        ),
    )(lengths, own, other)


def backward_kernel(
    length_ref,
    own_ref,
    other_ref,
    own_back_ref,
    other_back_ref,
    out_ref,
    log_ref,
    cosine_ref,
    sine_ref,
    own_grad_ref,
    other_grad_ref,
    query_ref,
    wide_ref,
    query_flat,
    back_flat,
    query_sum,
):
    row, index = pl.program_id(0), pl.program_id(1)
    shards, _, local = own_ref.shape
    limit = length_ref[row]
    ratio = max(1, 2048 // local)
    blocks = (limit + local - 1) // local
    mine = (blocks + 1 - row) // 2
    half = HEAD_DIM // 2

    def turned_back(wide, shard):
        cosine, sine = cosine_ref[shard], sine_ref[shard]
        upper, lower = wide[:half], wide[half:]
        return jnp.concatenate(
            [upper * cosine + lower * sine, lower * cosine - upper * sine], axis=0
        ).astype(jnp.bfloat16)

    def prepare(joint_ref, back_ref, first):
        for block in range(shards // 2):
            place = slice(block * local, (block + 1) * local)
            query = joint_ref[2 * block + first, :HEAD_DIM, :]
            back = back_ref[2 * block + first]
            extra = extra_rows([1.0] + three_parts(-log_ref[first, block]), local)
            query_ref[place, :] = jnp.concatenate([query, extra], axis=0).T
            balance = jnp.sum(
                back.astype(jnp.float32) * out_ref[first, block].astype(jnp.float32),
                axis=0,
                keepdims=True,
            )
            extra = extra_rows(three_parts(-balance), local)
            wide_ref[place, :] = jnp.concatenate([back, extra], axis=0).T
            query_flat[:, place] = query
            back_flat[:, place] = back
        query_sum[...] = jnp.zeros_like(query_sum)

    def work(joint_ref, grad_ref):
        key = joint_ref[index, HEAD_DIM : 2 * HEAD_DIM, :]
        value = joint_ref[index, 2 * HEAD_DIM :, :]
        mask = mask_row(index * local, local, limit)
        wide_key = jnp.concatenate([key, extra_rows([mask, 1.0, 1.0, 1.0], local)], axis=0)
        wide_value = jnp.concatenate([value, extra_rows([1.0, 1.0, 1.0], local)], axis=0)

        def gather(start, size, carry):
            key_sum, value_sum = carry
            place = pl.ds(pl.multiple_of(start, local), size)
            scores = jnp.dot(query_ref[place, :], wide_key, preferred_element_type=jnp.float32)
            chance = jnp.exp(scores)
            change = jnp.dot(wide_ref[place, :], wide_value, preferred_element_type=jnp.float32)
            chance_low = chance.astype(jnp.bfloat16)
            score_back = (chance * change).astype(jnp.bfloat16)
            value_sum = value_sum + jnp.dot(
                back_flat[:, place], chance_low, preferred_element_type=jnp.float32
            )
            key_sum = key_sum + jnp.dot(
                query_flat[:, place], score_back, preferred_element_type=jnp.float32
            )
            query_sum[:, place] += lax.dot_general(
                key, score_back, NT, preferred_element_type=jnp.float32
            )
            return (key_sum, value_sum)

        large = mine // ratio
        zero = jnp.zeros((HEAD_DIM, local), jnp.float32)
        carry = lax.fori_loop(
            0,
            large,
            lambda block, carry: gather(block * (ratio * local), ratio * local, carry),
            (zero, zero),
        )
        key_sum, value_sum = lax.fori_loop(
            large * ratio, mine, lambda block, carry: gather(block * local, local, carry), carry
        )
        grad_ref[index, HEAD_DIM : 2 * HEAD_DIM, :] = turned_back(key_sum, index)
        grad_ref[index, 2 * HEAD_DIM :, :] = value_sum.astype(jnp.bfloat16)

    def padding(grad_ref):
        grad_ref[index, HEAD_DIM:, :] = jnp.zeros((2 * HEAD_DIM, local), jnp.bfloat16)

    def finish(grad_ref, first):
        for block in range(shards // 2):
            place = slice(block * local, (block + 1) * local)
            shard = 2 * block + first
            grad_ref[shard, :HEAD_DIM, :] = turned_back(
                query_sum[:, place] * HEAD_DIM**-0.5, shard
            )
            grad_ref[shard + 1 - 2 * first, :HEAD_DIM, :] = jnp.zeros(
                (HEAD_DIM, local), jnp.bfloat16
            )

    sides = ((own_ref, own_back_ref, own_grad_ref), (other_ref, other_back_ref, other_grad_ref))
    for which, (joint_ref, back_ref, grad_ref) in enumerate(sides):
        here = row == which
        pl.when(here & (index == 0))(functools.partial(prepare, joint_ref, back_ref, which))
        pl.when(here & (index < blocks))(functools.partial(work, joint_ref, grad_ref))
        pl.when(here & (index >= blocks))(functools.partial(padding, grad_ref))
        pl.when(here & (index == shards - 1))(functools.partial(finish, grad_ref, which))


def attend_backward(lengths, own, other, own_back, other_back, out, log_mass, cosine, sine):
    shards, _, local = own.shape
    total = shards * local
    half = shards // 2
    whole = lambda *shape: pl.BlockSpec(shape, lambda r, i: (0,) * len(shape))
    grad = jax.ShapeDtypeStruct((shards, 3 * HEAD_DIM, local), jnp.bfloat16)
    return pl.pallas_call(
        backward_kernel,
        grid=(2, shards),
        in_specs=[pl.BlockSpec(memory_space=pltpu.SMEM)]
        + [whole(shards, 3 * HEAD_DIM, local)] * 2
        + [whole(shards, HEAD_DIM, local)] * 2
        + [whole(2, half, HEAD_DIM, local), whole(2, half, 1, local)]
        + [whole(shards, HEAD_DIM // 2, local)] * 2,
        out_specs=[whole(shards, 3 * HEAD_DIM, local)] * 2,
        out_shape=[grad, grad],
        scratch_shapes=[
            pltpu.VMEM((total // 2, 2 * HEAD_DIM), jnp.bfloat16),
            pltpu.VMEM((total // 2, 2 * HEAD_DIM), jnp.bfloat16),
            pltpu.VMEM((HEAD_DIM, total // 2), jnp.bfloat16),
            pltpu.VMEM((HEAD_DIM, total // 2), jnp.bfloat16),
            pltpu.VMEM((HEAD_DIM, total // 2), jnp.float32),
        ],
        compiler_params=pltpu.CompilerParams(vmem_limit_bytes=VMEM_LIMIT),
        cost_estimate=pl.CostEstimate(
            flops=total * total,
            bytes_accessed=HEAD_DIM * total,
            transcendentals=0,
        ),
    )(lengths, own, other, own_back, other_back, out, log_mass, cosine, sine)


def backward_row_kernel(
    pick_ref,
    own_ref,
    other_ref,
    own_back_ref,
    other_back_ref,
    out_ref,
    log_ref,
    cosine_ref,
    sine_ref,
    grad_ref,
    joint_ref,
    back_ref,
    arrived_ref,
    query_ref,
    wide_ref,
    query_flat,
    back_flat,
    query_sum,
):
    index = pl.program_id(0)
    shards, _, local = joint_ref.shape
    first, limit = pick_ref[0], pick_ref[1]
    ratio = max(1, 2048 // local)
    blocks = (limit + local - 1) // local
    mine = (blocks + 1 - first) // 2
    half = HEAD_DIM // 2

    def turned_back(wide, shard):
        cosine, sine = cosine_ref[shard], sine_ref[shard]
        upper, lower = wide[:half], wide[half:]
        return jnp.concatenate(
            [upper * cosine + lower * sine, lower * cosine - upper * sine], axis=0
        ).astype(jnp.bfloat16)

    for which, sources in enumerate(((own_ref, own_back_ref), (other_ref, other_back_ref))):

        @pl.when((index == 0) & (first == which))
        def fetch(sources=sources):
            copies = [
                pltpu.make_async_copy(source, target, arrived_ref.at[number])
                for number, (source, target) in enumerate(zip(sources, (joint_ref, back_ref)))
            ]
            for copy in copies:
                copy.start()
            for copy in copies:
                copy.wait()

    @pl.when(index == 0)
    def prepare():
        for block in range(shards // 2):
            place = slice(block * local, (block + 1) * local)
            query = joint_ref[2 * block + first, :HEAD_DIM, :]
            back = back_ref[2 * block + first]
            extra = extra_rows([1.0] + three_parts(-log_ref[first, block]), local)
            query_ref[place, :] = jnp.concatenate([query, extra], axis=0).T
            balance = jnp.sum(
                back.astype(jnp.float32) * out_ref[first, block].astype(jnp.float32),
                axis=0,
                keepdims=True,
            )
            extra = extra_rows(three_parts(-balance), local)
            wide_ref[place, :] = jnp.concatenate([back, extra], axis=0).T
            query_flat[:, place] = query
            back_flat[:, place] = back
        query_sum[...] = jnp.zeros_like(query_sum)

    @pl.when(index < blocks)
    def work():
        key = joint_ref[index, HEAD_DIM : 2 * HEAD_DIM, :]
        value = joint_ref[index, 2 * HEAD_DIM :, :]
        mask = mask_row(index * local, local, limit)
        wide_key = jnp.concatenate([key, extra_rows([mask, 1.0, 1.0, 1.0], local)], axis=0)
        wide_value = jnp.concatenate([value, extra_rows([1.0, 1.0, 1.0], local)], axis=0)

        def gather(start, size, carry):
            key_sum, value_sum = carry
            place = pl.ds(pl.multiple_of(start, local), size)
            scores = jnp.dot(query_ref[place, :], wide_key, preferred_element_type=jnp.float32)
            chance = jnp.exp(scores)
            change = jnp.dot(wide_ref[place, :], wide_value, preferred_element_type=jnp.float32)
            chance_low = chance.astype(jnp.bfloat16)
            score_back = (chance * change).astype(jnp.bfloat16)
            value_sum = value_sum + jnp.dot(
                back_flat[:, place], chance_low, preferred_element_type=jnp.float32
            )
            key_sum = key_sum + jnp.dot(
                query_flat[:, place], score_back, preferred_element_type=jnp.float32
            )
            query_sum[:, place] += lax.dot_general(
                key, score_back, NT, preferred_element_type=jnp.float32
            )
            return (key_sum, value_sum)

        large = mine // ratio
        zero = jnp.zeros((HEAD_DIM, local), jnp.float32)
        carry = lax.fori_loop(
            0,
            large,
            lambda block, carry: gather(block * (ratio * local), ratio * local, carry),
            (zero, zero),
        )
        key_sum, value_sum = lax.fori_loop(
            large * ratio, mine, lambda block, carry: gather(block * local, local, carry), carry
        )
        grad_ref[index, HEAD_DIM : 2 * HEAD_DIM, :] = turned_back(key_sum, index)
        grad_ref[index, 2 * HEAD_DIM :, :] = value_sum.astype(jnp.bfloat16)

    @pl.when(index >= blocks)
    def padding():
        grad_ref[index, HEAD_DIM:, :] = jnp.zeros((2 * HEAD_DIM, local), jnp.bfloat16)

    @pl.when(index == shards - 1)
    def finish():
        for block in range(shards // 2):
            place = slice(block * local, (block + 1) * local)
            shard = 2 * block + first
            grad_ref[shard, :HEAD_DIM, :] = turned_back(
                query_sum[:, place] * HEAD_DIM**-0.5, shard
            )
            grad_ref[shard + 1 - 2 * first, :HEAD_DIM, :] = jnp.zeros(
                (HEAD_DIM, local), jnp.bfloat16
            )


def attend_backward_row(pick, own, other, own_back, other_back, out, log_mass, cosine, sine):
    shards, _, local = own.shape
    total = shards * local
    half = shards // 2
    whole = lambda *shape: pl.BlockSpec(shape, lambda i: (0,) * len(shape))
    return pl.pallas_call(
        backward_row_kernel,
        grid=(shards,),
        in_specs=[pl.BlockSpec(memory_space=pltpu.SMEM)]
        + [pl.BlockSpec(memory_space=pl.ANY)] * 4
        + [whole(2, half, HEAD_DIM, local), whole(2, half, 1, local)]
        + [whole(shards, HEAD_DIM // 2, local)] * 2,
        out_specs=whole(shards, 3 * HEAD_DIM, local),
        out_shape=jax.ShapeDtypeStruct((shards, 3 * HEAD_DIM, local), jnp.bfloat16),
        scratch_shapes=[
            pltpu.VMEM((shards, 3 * HEAD_DIM, local), jnp.bfloat16),
            pltpu.VMEM((shards, HEAD_DIM, local), jnp.bfloat16),
            pltpu.SemaphoreType.DMA((2,)),
            pltpu.VMEM((total // 2, 2 * HEAD_DIM), jnp.bfloat16),
            pltpu.VMEM((total // 2, 2 * HEAD_DIM), jnp.bfloat16),
            pltpu.VMEM((HEAD_DIM, total // 2), jnp.bfloat16),
            pltpu.VMEM((HEAD_DIM, total // 2), jnp.bfloat16),
            pltpu.VMEM((HEAD_DIM, total // 2), jnp.float32),
        ],
        compiler_params=pltpu.CompilerParams(vmem_limit_bytes=VMEM_LIMIT),
        cost_estimate=pl.CostEstimate(
            flops=total * total, bytes_accessed=HEAD_DIM * total, transcendentals=0
        ),
    )(pick, own, other, own_back, other_back, out, log_mass, cosine, sine)


TN = (((0,), (0,)), ((), ()))
PLAIN = (((1,), (0,)), ((), ()))
LANES = 128
GROUPS = 4
RUNS = 8
UNITS = FF // GROUPS
EXPAND_RUN = -(-2 * UNITS // (16 * RUNS)) * 16
SHRINK_RUN = -(-UNITS // (16 * RUNS)) * 16


def run_segments(start, stop, run):
    segments = []
    while start < stop:
        index = start // run
        end = min(stop, (index + 1) * run)
        segments.append((index, start - index * run, start, end - start))
        start = end
    return segments


def feed_kernel(
    second_ref,
    upstream_ref,
    active_ref,
    gate_ref,
    shrink_ref,
    shrunk_ref,
    second_back_ref,
    parts_ref,
    grads_ref,
    zero_ref,
    send_ref,
    zero_send_ref,
):
    index = pl.program_id(0)

    def joined(ref):
        return jnp.concatenate([ref[piece, 0] for piece in range(ref.shape[0])], axis=1)

    def product(left, right, dims):
        return lax.dot_general(left, right, dims, preferred_element_type=jnp.float32)

    def grad_copies(half, pair):
        moves = []
        for kind, member in ((0, pair), (1, pair + 2)):
            for run, place, offset, size in run_segments(
                half * UNITS, (half + 1) * UNITS, EXPAND_RUN
            ):
                moves.append((kind, offset - half * UNITS, run, member, place, size))
        for run, place, offset, size in run_segments(0, UNITS, SHRINK_RUN):
            moves.append((2, offset, run, 2 * pair + half, EXPAND_RUN + place, size))
        return [
            pltpu.make_async_copy(
                grads_ref.at[half, kind, pl.ds(offset, size), :],
                parts_ref.at[run, member, pl.ds(place, size), :],
                send_ref.at[half, number],
            )
            for number, (kind, offset, run, member, place, size) in enumerate(moves)
        ]

    def zero_copies():
        moves = []
        for member in range(GROUPS):
            for base, run_size, total in ((0, EXPAND_RUN, 2 * UNITS), (EXPAND_RUN, SHRINK_RUN, UNITS)):
                for run, place, _, size in run_segments(total, RUNS * run_size, run_size):
                    moves.append((run, member, base + place, size))
        return [
            pltpu.make_async_copy(
                zero_ref.at[pl.ds(0, size), :],
                parts_ref.at[run, member, pl.ds(place, size), :],
                zero_send_ref.at[number],
            )
            for number, (run, member, place, size) in enumerate(moves)
        ]

    @pl.when(index == 0)
    def fill():
        zero_ref[...] = jnp.zeros_like(zero_ref)
        for copy in zero_copies():
            copy.start()

    active, gate, shrink = joined(active_ref), joined(gate_ref), joined(shrink_ref)
    second, upstream = second_ref[...], upstream_ref[...]
    input_active = product(second, active, NT)
    input_gate = product(second, gate, NT)
    hidden_back = product(upstream, shrink, NT)
    below = 0.5 + 0.5 * lax.erf(input_active * 0.5**0.5)
    bell = jnp.exp(-0.5 * input_active * input_active) * (0.5 / math.pi) ** 0.5
    curve = input_active * below
    hidden = (curve * input_gate).astype(jnp.bfloat16)
    active_back = (hidden_back * input_gate * (below + input_active * bell)).astype(jnp.bfloat16)
    gate_back = (hidden_back * curve).astype(jnp.bfloat16)
    shrunk = product(hidden, shrink, PLAIN)
    second_back = product(active_back, active, PLAIN) + product(gate_back, gate, PLAIN)

    @pl.when(index == 0)
    def begin():
        shrunk_ref[...] = shrunk
        second_back_ref[...] = second_back

    @pl.when(index > 0)
    def add():
        shrunk_ref[...] += shrunk
        second_back_ref[...] += second_back

    for half in range(2):

        @pl.when(index % 2 == half)
        def send(half=half):
            pair = index // 2

            @pl.when(index >= 2)
            def free():
                for copy in grad_copies(half, pair - 1):
                    copy.wait()

            grads_ref[half, 0] = product(active_back, second, TN).astype(jnp.bfloat16)
            grads_ref[half, 1] = product(gate_back, second, TN).astype(jnp.bfloat16)
            grads_ref[half, 2] = product(hidden, upstream, TN).astype(jnp.bfloat16)
            for copy in grad_copies(half, pair):
                copy.start()

    @pl.when(index == GROUPS - 1)
    def drain():
        for half in range(2):
            for copy in grad_copies(half, 1):
                copy.wait()
        for copy in zero_copies():
            copy.wait()


def feed_forward(second, upstream, pieces):
    count, width = second.shape
    block = (RUNS, 1, UNITS, LANES)
    held = pl.BlockSpec((count, width), lambda i: (0, 0), pipeline_mode=pl.Buffered(1))
    wide = jax.ShapeDtypeStruct((count, width), jnp.float32)
    run = EXPAND_RUN + SHRINK_RUN
    copies = max(
        2 * len(run_segments(half * UNITS, (half + 1) * UNITS, EXPAND_RUN)) for half in range(2)
    ) + len(run_segments(0, UNITS, SHRINK_RUN))
    return pl.pallas_call(
        feed_kernel,
        grid=(GROUPS,),
        in_specs=[
            held,
            held,
            pl.BlockSpec(block, lambda i: (0, i // 2, i % 2, 0)),
            pl.BlockSpec(block, lambda i: (0, i // 2 + 2, i % 2, 0)),
            pl.BlockSpec(block, lambda i: (0, i, 2, 0)),
        ],
        out_specs=[held, held, pl.BlockSpec(memory_space=pl.ANY)],
        out_shape=[wide, wide, jax.ShapeDtypeStruct((RUNS, GROUPS, run, width), jnp.bfloat16)],
        scratch_shapes=[
            pltpu.VMEM((2, 3, UNITS, width), jnp.bfloat16),
            pltpu.VMEM((max(EXPAND_RUN, SHRINK_RUN), width), jnp.bfloat16),
            pltpu.SemaphoreType.DMA((2, copies)),
            pltpu.SemaphoreType.DMA((GROUPS * 8,)),
        ],
        compiler_params=pltpu.CompilerParams(vmem_limit_bytes=VMEM_LIMIT),
        cost_estimate=pl.CostEstimate(
            flops=count * width,
            bytes_accessed=count * width,
            transcendentals=0,
        ),
    )(second, upstream, pieces, pieces, pieces)


def enter_kernel(*refs):
    phases = (len(refs) - 9) // 2
    attend_refs, weight_refs = refs[:phases], refs[phases : 2 * phases]
    limit_ref, token_ref, cotangent_ref, gain_ref = refs[2 * phases : 2 * phases + 4]
    middle_ref, normal_ref, second_ref, upstream_ref, spread_ref = refs[2 * phases + 4 :]
    middle = token_ref[...].astype(jnp.float32)
    for attend_ref, weight_ref in zip(attend_refs, weight_refs):
        middle += lax.dot_general(
            attend_ref[...], weight_ref[...], TN, preferred_element_type=jnp.float32
        )
    block = middle.shape[0]
    centre = middle - jnp.mean(middle, axis=1, keepdims=True)
    scale = lax.rsqrt(jnp.mean(centre * centre, axis=1, keepdims=True) + NORM_EPS)
    normal = centre * scale
    place = pl.program_id(0) * block + lax.broadcasted_iota(jnp.int32, (block, 1), 0)
    middle_ref[...] = middle
    normal_ref[...] = normal
    spread_ref[...] = scale
    second_ref[...] = (normal * gain_ref[1:2, :]).astype(jnp.bfloat16)
    upstream_ref[...] = jnp.where(place < limit_ref[0], cotangent_ref[...], jnp.bfloat16(0.0))


def enter_feed(attends, weights, limit, tokens, cotangent, gains):
    count, width = tokens.shape
    block = min(256, count)
    rows = pl.BlockSpec((block, width), lambda i: (i, 0))
    wide = jax.ShapeDtypeStruct((count, width), jnp.float32)
    low = jax.ShapeDtypeStruct((count, width), jnp.bfloat16)
    return pl.pallas_call(
        enter_kernel,
        grid=(count // block,),
        in_specs=[pl.BlockSpec((attend.shape[0], block), lambda i: (0, i)) for attend in attends]
        + [pl.BlockSpec(weight.shape, lambda i: (0, 0)) for weight in weights]
        + [pl.BlockSpec(memory_space=pltpu.SMEM), rows, rows]
        + [pl.BlockSpec(gains.shape, lambda i: (0, 0))],
        out_specs=[rows, rows, rows, rows, pl.BlockSpec((block, 1), lambda i: (i, 0))],
        out_shape=[wide, wide, low, low, jax.ShapeDtypeStruct((count, 1), jnp.float32)],
        compiler_params=pltpu.CompilerParams(vmem_limit_bytes=VMEM_LIMIT),
        cost_estimate=pl.CostEstimate(
            flops=2 * count * width * width, bytes_accessed=20 * count * width, transcendentals=0
        ),
    )(*attends, *weights, limit, tokens, cotangent, gains)


def leave_kernel(*refs):
    phases = (len(refs) - 12) // 2
    weight_refs, back_refs = refs[:phases], refs[-phases:]
    limit_ref, shrunk_ref, change_ref, middle_ref, normal_ref, spread_ref = refs[phases : phases + 6]
    upstream_ref, gain_ref = refs[phases + 6 : phases + 8]
    mixed_ref, middle_back_ref, branch_ref, gain_grad_ref = refs[phases + 8 : phases + 12]
    index = pl.program_id(0)
    block = mixed_ref.shape[0]
    place = index * block + lax.broadcasted_iota(jnp.int32, (block, 1), 0)
    mixed = middle_ref[...] + shrunk_ref[...]
    mixed_ref[...] = jnp.where(place < limit_ref[0], mixed, 0.0).astype(jnp.bfloat16)
    change, normal = change_ref[...], normal_ref[...]
    gain_grad = jnp.sum(change * normal, axis=0, keepdims=True)

    @pl.when(index == 0)
    def begin():
        gain_grad_ref[...] = gain_grad

    @pl.when(index > 0)
    def add():
        gain_grad_ref[...] += gain_grad

    inner = change * gain_ref[1:2, :]
    inner = (
        inner
        - jnp.mean(inner, axis=1, keepdims=True)
        - normal * jnp.mean(inner * normal, axis=1, keepdims=True)
    )
    middle_back = upstream_ref[...].astype(jnp.float32) + spread_ref[...] * inner
    branch = middle_back.astype(jnp.bfloat16)
    middle_back_ref[...] = middle_back
    branch_ref[...] = branch
    for weight_ref, back_ref in zip(weight_refs, back_refs):
        back_ref[...] = lax.dot_general(
            weight_ref[...], branch, NT, preferred_element_type=jnp.float32
        ).astype(jnp.bfloat16)


def leave_feed(weights, limit, shrunk, change, middle, normal, spread, upstream, gains):
    count, width = shrunk.shape
    block = min(256, count)
    rows = pl.BlockSpec((block, width), lambda i: (i, 0))
    wide = jax.ShapeDtypeStruct((count, width), jnp.float32)
    low = jax.ShapeDtypeStruct((count, width), jnp.bfloat16)
    return pl.pallas_call(
        leave_kernel,
        grid=(count // block,),
        in_specs=[pl.BlockSpec(weight.shape, lambda i: (0, 0)) for weight in weights]
        + [pl.BlockSpec(memory_space=pltpu.SMEM), rows, rows, rows, rows]
        + [pl.BlockSpec((block, 1), lambda i: (i, 0)), rows]
        + [pl.BlockSpec(gains.shape, lambda i: (0, 0))],
        out_specs=[rows, rows, rows, pl.BlockSpec((1, width), lambda i: (0, 0))]
        + [pl.BlockSpec((weight.shape[0], block), lambda i: (0, i)) for weight in weights],
        out_shape=[low, wide, low, jax.ShapeDtypeStruct((1, width), jnp.float32)]
        + [jax.ShapeDtypeStruct((weight.shape[0], count), jnp.bfloat16) for weight in weights],
        compiler_params=pltpu.CompilerParams(vmem_limit_bytes=VMEM_LIMIT),
        cost_estimate=pl.CostEstimate(
            flops=2 * count * width * width, bytes_accessed=28 * count * width, transcendentals=0
        ),
    )(*weights, limit, shrunk, change, middle, normal, spread, upstream, gains)


def adam_step(rotated, first, second):
    average = BETA_ONE * first + (1.0 - BETA_ONE) * rotated
    variance = BETA_TWO * second + (1.0 - BETA_TWO) * rotated * rotated
    direction = (
        average / (1.0 - BETA_ONE**STEP) / (jnp.sqrt(variance / (1.0 - BETA_TWO**STEP)) + ADAM_EPS)
    )
    return (average, variance, direction)


def body(
    tokens,
    cotangent,
    lengths,
    triple_weight,
    output_weight,
    expand_weight,
    shrink_weight,
    norm_gains,
    side_bases,
    output_right,
    triple_first,
    triple_second,
    output_first,
    output_second,
    expand_first,
    expand_second,
    shrink_first,
    shrink_second,
    gains_first,
    gains_second,
):
    rows_here, local_len, width = tokens.shape
    count = rows_here * local_len
    shards = lax.axis_size("seq")
    groups = lax.axis_size("outer") * lax.axis_size("core")
    phases = HEADS // shards
    piece = width // shards
    fsdp = ("outer", "core")
    everyone = ("seq",) + fsdp
    offset = lax.axis_index("seq") * local_len
    position = offset + jnp.arange(local_len, dtype=jnp.int32)
    cosine, sine = rotary_tables(position)
    every = jnp.arange(shards * local_len, dtype=jnp.int32)
    all_cosine, all_sine = (
        table.reshape(HEAD_DIM // 2, shards, local_len).transpose(1, 0, 2)
        for table in rotary_tables(every)
    )
    valid = (position[None, :] < lengths[:, None]).astype(jnp.float32).reshape(count, 1)
    exchange = functools.partial(lax.all_to_all, axis_name="seq", split_axis=0, concat_axis=0)

    def tied(*values):
        return lax.optimization_barrier(values)

    def gathered(shard):
        flat = lax.all_gather(shard, everyone, axis=0, tiled=False)
        return flat.reshape((shards, groups) + shard.shape)

    triple_shards = (
        triple_weight.T.astype(jnp.bfloat16)
        .reshape(-1, phases, HEAD_DIM, piece)
        .transpose(1, 0, 2, 3)
        .reshape(phases, -1, piece)
    )
    triple_pieces = gathered(triple_shards)
    output_columns = width // groups
    lanes = min(piece, output_columns)

    def fold(block):
        rows = block.shape[0]
        return block.reshape(rows, -1, lanes).transpose(1, 0, 2).reshape(-1, lanes)

    bases_low = side_bases.astype(jnp.bfloat16)
    right_low = output_right.astype(jnp.bfloat16)
    member = lax.axis_index("outer") * lax.axis_size("core") + lax.axis_index("core")
    base_rows = piece // groups
    flat = tokens.reshape(count, width).astype(jnp.float32)
    first_normed, first_back = jax.vjp(layer_norm, flat, norm_gains[0])
    first_low = first_normed.astype(jnp.bfloat16)
    other_shards = jnp.concatenate(
        [
            expand_weight.T.astype(jnp.bfloat16),
            shrink_weight.astype(jnp.bfloat16),
            fold(output_weight.astype(jnp.bfloat16)),
        ],
        axis=0,
    )
    projected = [
        project_heads(triple_pieces, first_low, cosine, sine, phase) for phase in range(phases)
    ]
    triple_rows = [rows for _, rows in projected]
    joints = [exchange(joint) for joint, _ in projected]
    all_cosine, all_sine, joints[0] = tied(all_cosine, all_sine, joints[0])
    swap = functools.partial(lax.ppermute, axis_name="core", perm=[(0, 1), (1, 0)])
    both_lengths = jnp.concatenate([lengths, swap(lengths)])
    others, forwards, attends = [], [], []
    for phase in range(phases):
        others.append(swap(joints[phase]))
        outcome = attend_forward(both_lengths, joints[phase], others[phase])
        if phase:
            attends[-1], outcome = tied(attends[-1], outcome)
        if phase < phases - 1:
            joints[phase + 1], outcome = tied(joints[phase + 1], outcome)
        forwards.append(outcome)
        attend = jnp.stack([outcome[0][0], swap(outcome[0][1])], axis=1)
        attends.append(exchange(attend.reshape(shards, HEAD_DIM, count)))
    other_shards, forwards[0] = tied(other_shards, forwards[0])
    other_pieces = gathered(other_shards)
    chosen = jnp.stack([bases_low[0], bases_low[2], bases_low[3]])
    chosen = lax.dynamic_slice_in_dim(chosen, member * base_rows, base_rows, 1)
    expand_rows = 2 * FF // groups
    shrink_rows = FF // groups
    output_rows = list(
        other_pieces[:, :, expand_rows + shrink_rows :]
        .reshape(shards, groups, output_columns // lanes, phases, HEAD_DIM, lanes)
        .transpose(3, 0, 4, 1, 2, 5)
        .reshape(phases, shards * HEAD_DIM, width)
    )
    canonical = (shards, groups, piece) == (RUNS, GROUPS, LANES)
    if canonical:
        feed_pieces = other_pieces
    else:
        feed_pieces = [
            other_pieces[:, :, start:end]
            .transpose(1, 2, 0, 3)
            .reshape(GROUPS, -1, RUNS, LANES)
            .transpose(2, 0, 1, 3)
            for start, end in ((0, expand_rows), (expand_rows, expand_rows + shrink_rows))
        ]
        feed_pieces = jnp.concatenate(feed_pieces, axis=2)
    chosen, forwards[-1] = tied(chosen, forwards[-1])
    bases_full = gathered(chosen)
    attends = [attend.reshape(shards * HEAD_DIM, count) for attend in attends]
    expand_height = -(-expand_rows // (16 * shards)) * 16
    shrink_height = -(-shrink_rows // (16 * shards)) * 16

    def to_rows(block):
        block = exchange(block)
        return block.transpose(1, 0, 2).reshape(block.shape[1], -1)

    def padded(block, height):
        block = jnp.pad(block, ((0, height * shards - block.shape[0]), (0, 0)))
        return block.reshape(shards, height, piece)

    def by_phase(block):
        return (
            block.reshape(-1, phases, HEAD_DIM, piece)
            .transpose(1, 0, 2, 3)
            .reshape(phases, shards, -1, piece)
        )

    def from_phases(blocks):
        block = jnp.stack(blocks).astype(jnp.float32).reshape(phases, -1, HEAD_DIM, piece)
        return block.transpose(1, 0, 2, 3).reshape(-1, piece)

    moments = []
    for expand, shrink, triple in (
        (expand_first, shrink_first, triple_first),
        (expand_second, shrink_second, triple_second),
    ):
        moments += [padded(expand.T, expand_height), padded(shrink, shrink_height)]
        moments += list(by_phase(triple.T))
    moments, attends[-1], feed_pieces = tied(moments, attends[-1], feed_pieces)
    heights = [moment.shape[1] for moment in moments]
    moments = to_rows(jnp.concatenate(moments, axis=1))
    edges = [sum(heights[:index]) for index in range(len(heights) + 1)]
    moments = [moments[start:end] for start, end in zip(edges, edges[1:])]
    moments = list(zip(moments[: phases + 2], moments[phases + 2 :]))
    inside = jnp.clip(lengths - offset, 0, local_len)
    middle, second_normal, second_low, upstream_low, second_spread = enter_feed(
        attends,
        output_rows,
        inside,
        tokens.reshape(count, width),
        cotangent.reshape(count, width),
        norm_gains,
    )
    shrunk, second_change, parts = feed_forward(second_low, upstream_low, feed_pieces)
    moments, bases_full, shrunk, second_change, parts = tied(
        moments, bases_full, shrunk, second_change, parts
    )
    mixed, middle_back, branch_low, second_gain, *backs = leave_feed(
        output_rows,
        inside,
        shrunk,
        second_change,
        middle,
        second_normal,
        second_spread,
        upstream_low,
        norm_gains,
    )
    mixed = mixed.reshape(tokens.shape)
    second_gain = second_gain[0]
    backs = [back.reshape(shards, HEAD_DIM, count) for back in backs]
    attend_backs = [exchange(back) for back in backs]

    def halved(blocks, axis, dim):
        size = lax.axis_size(axis)
        place = lax.axis_index(axis)
        while size > 1:
            size //= 2
            shape = blocks.shape
            blocks = blocks.reshape(shape[:dim] + (2, size) + shape[dim + 1 :])
            side = (place // size) % 2
            mine = lax.dynamic_index_in_dim(blocks, side, dim, keepdims=False)
            other = lax.dynamic_index_in_dim(blocks, 1 - side, dim, keepdims=False)
            pairs = [(member, member ^ size) for member in range(lax.axis_size(axis))]
            other = lax.ppermute(other, axis, pairs)
            blocks = (mine.astype(jnp.float32) + other.astype(jnp.float32)).astype(jnp.bfloat16)
        return jnp.squeeze(blocks, dim)

    def doubled(block, axis):
        block = block[None]
        place = lax.axis_index(axis)
        step = 1
        while step < lax.axis_size(axis):
            pairs = [(member, member ^ step) for member in range(lax.axis_size(axis))]
            other = lax.ppermute(block, axis, pairs)
            upper = (place // step) % 2 == 1
            block = jnp.concatenate(
                [jnp.where(upper, other, block), jnp.where(upper, block, other)], axis=0
            )
            step *= 2
        return block

    def near_sum(blocks):
        return halved(halved(blocks, "core", 1), "outer", 0)

    def merged(*blocks):
        sizes = [math.prod(block.shape[1:]) for block in blocks]
        flat = [block.reshape(shards, -1, piece) for block in blocks]
        flat = exchange(jnp.concatenate(flat, axis=1))
        results, start = [], 0
        for block, size in zip(blocks, sizes):
            rows = size // piece
            results.append(flat[:, start : start + rows].reshape(block.shape))
            start += rows
        return results

    def widened(block):
        rows = piece * output_columns // count
        block = block.reshape(-1, piece // rows, rows, output_columns)
        return block.swapaxes(1, 2).reshape(shards, -1, count)

    def narrowed(block):
        rows = piece * output_columns // count
        block = block.reshape(-1, rows, piece // rows, output_columns)
        return block.swapaxes(1, 2).reshape(shards, -1, piece, output_columns)

    def far_sum(terms):
        return jnp.sum(terms.astype(jnp.float32), axis=0).astype(jnp.bfloat16)

    def cut_rows(rows):
        return rows.reshape(rows.shape[0], shards, piece).transpose(1, 0, 2)

    outer = lax.axis_size("outer")
    output_part = jnp.stack(
        [
            jnp.dot(attend, branch_low, preferred_element_type=jnp.float32)
            .astype(jnp.bfloat16)
            .reshape(shards, HEAD_DIM, width)
            for attend in attends
        ],
        axis=1,
    )
    output_terms = halved(
        output_part.reshape(shards, piece, outer, -1, output_columns).transpose(0, 2, 3, 1, 4),
        "core",
        2,
    )
    def cut(product, height):
        block = product.reshape(groups, -1, width)
        block = jnp.pad(block, ((0, 0), (0, height * shards - block.shape[1]), (0, 0)))
        return block.reshape(groups, shards, height, width)

    if not canonical:
        parts = parts.transpose(1, 0, 2, 3)
        parts = [
            cut(block.reshape(GROUPS, -1, width)[:, : size // GROUPS], height)
            for block, size, height in (
                (parts[:, :, :EXPAND_RUN], 2 * FF, expand_height),
                (parts[:, :, EXPAND_RUN:], FF, shrink_height),
            )
        ]
        parts = jnp.concatenate(parts, axis=2).transpose(1, 0, 2, 3)
    parts = parts.reshape(shards * groups, -1, width)
    owned = lax.psum_scatter(parts, everyone, scatter_dimension=0, tiled=False)
    feed_height = expand_height + shrink_height

    def soap_rows(rows, base, moment):
        rotated = plain_product(rows, base)
        direction = adam_step(rotated, *moment)[2]
        step = back_product(direction.astype(jnp.bfloat16), base)
        return rotated.astype(jnp.bfloat16), step.astype(jnp.bfloat16)

    output_terms = widened(output_terms)
    output_terms, attend_backs[0] = tied(output_terms, attend_backs[0])
    other_backs, grads = [], []
    for phase in range(phases - 1):
        other_backs.append(swap(attend_backs[phase]))
        own_grad, other_grad = attend_backward(
            both_lengths,
            joints[phase],
            others[phase],
            attend_backs[phase],
            other_backs[phase],
            *forwards[phase],
            all_cosine,
            all_sine,
        )
        attend_backs[phase + 1], own_grad, other_grad = tied(
            attend_backs[phase + 1], own_grad, other_grad
        )
        grad = own_grad.astype(jnp.float32) + swap(other_grad).astype(jnp.float32)
        grad = grad.astype(jnp.bfloat16)
        if phase == 0:
            grad = jnp.concatenate([grad, output_terms], axis=1)
        grads.append(exchange(grad))
    other_backs.append(swap(attend_backs[-1]))

    def last_row(pick):
        return attend_backward_row(
            pick,
            joints[-1],
            others[-1],
            attend_backs[-1],
            other_backs[-1],
            *forwards[-1],
            all_cosine,
            all_sine,
        )

    core = lax.axis_index("core")
    row_grad = last_row(jnp.stack([core, jnp.where(core == 0, both_lengths[0], both_lengths[1])]))
    if phases == 1:
        grads.append(exchange(output_terms))
    grads, owned, bases_full, row_grad = tied(grads, owned, bases_full, row_grad)
    output_low = grads[0][:, -output_terms.shape[1] :]
    output_low = halved(far_sum(narrowed(output_low)), "outer", 0)
    grads = [grad[:, : 3 * HEAD_DIM] for grad in grads[: phases - 1]]
    output_left = outer_sum(bases_low[1], output_low).astype(jnp.bfloat16)
    output_left = output_left.reshape(shards, piece, output_columns)
    bases_full = bases_full.transpose(2, 0, 1, 3, 4).reshape(3, width, width)

    def triple_sum(grad):
        joint_back = grad.reshape(shards * 3 * HEAD_DIM, count)
        part = jnp.dot(joint_back, first_low, preferred_element_type=jnp.float32)
        part = part.astype(jnp.bfloat16).reshape(shards, 3, HEAD_DIM, width).swapaxes(0, 1)
        return near_sum(part.reshape(outer, groups // outer, shards, -1, width)), joint_back

    def triple_rest(terms, phase):
        rows = far_sum(terms)
        return jnp.concatenate([rows, *soap_rows(rows, bases_full[0], moments[2 + phase])])

    feed_rows = jnp.concatenate(
        [
            owned,
            *soap_rows(owned[:expand_height], bases_full[1], moments[0]),
            *soap_rows(owned[expand_height:], bases_full[2], moments[1]),
        ]
    )
    settled = jnp.concatenate(
        [cut_rows(feed_rows), output_left.reshape(shards, -1, piece)], axis=1
    )
    pick = jnp.stack([1 - core, jnp.where(core == 0, both_lengths[1], both_lengths[0])])
    settled, pick = tied(settled, pick)
    settled = exchange(settled)
    next_grad = last_row(pick)
    settled, next_grad = tied(settled, next_grad)
    sent = lax.ppermute(row_grad, "core", [(1, 0)])
    next_sent = lax.ppermute(next_grad, "core", [(0, 1)])
    grad = jnp.where(
        core == 0,
        row_grad.astype(jnp.float32) + sent.astype(jnp.float32),
        next_grad.astype(jnp.float32) + next_sent.astype(jnp.float32),
    )
    grads.append(exchange(grad.astype(jnp.bfloat16)))
    summed = [triple_sum(grad) for grad in grads[:-1]]
    grads[-1], summed = tied(grads[-1], summed)
    output_left = settled[:, feed_rows.shape[0] :].reshape(shards, piece, output_columns)
    output_left = far_sum(output_left)
    summed.append(triple_sum(grads[-1]))
    joint_backs = [joint_back for _, joint_back in summed]
    terms = exchange(jnp.concatenate([term for term, _ in summed], axis=1))
    terms = jnp.split(terms, phases, axis=1)
    triple_done = [triple_rest(term, phase) for phase, term in enumerate(terms)]
    output_turned = plain_product(output_left, right_low).astype(jnp.bfloat16)
    output_turned = near_sum(
        output_turned.reshape(piece, outer, -1, output_columns).transpose(1, 2, 0, 3)
    ).astype(jnp.float32)
    output_average, output_variance, output_direction = adam_step(
        output_turned, output_first, output_second
    )
    output_wide = doubled(doubled(output_direction.astype(jnp.bfloat16), "core"), "outer")
    output_wide = output_wide.reshape(groups, piece, output_columns).swapaxes(0, 1)
    output_middle = back_product(output_wide.reshape(piece, width), right_low)
    *triple_done, output_middle = merged(
        *[cut_rows(rows) for rows in triple_done],
        jnp.broadcast_to(output_middle.astype(jnp.bfloat16), (shards, piece, output_columns)),
    )
    output_back = plain_product(bases_low[1], output_middle.reshape(width, output_columns))
    triple_lows, triple_turns, triple_steps = zip(
        *[jnp.split(done, 3, axis=1) for done in triple_done]
    )

    def settled_piece(start, height, size):
        return settled[:, start : start + height].reshape(-1, piece)[:size].astype(jnp.float32)

    expand_gradient, expand_turned_grad, expand_back = (
        settled_piece(start, expand_height, expand_rows).T
        for start in (0, feed_height, feed_height + expand_height)
    )
    shrink_gradient, shrink_turned_grad, shrink_back = (
        settled_piece(start, shrink_height, shrink_rows)
        for start in (
            expand_height,
            feed_height + 2 * expand_height,
            feed_height + 2 * expand_height + shrink_height,
        )
    )
    expand_average, expand_variance, _ = adam_step(expand_turned_grad, expand_first, expand_second)
    shrink_average, shrink_variance, _ = adam_step(shrink_turned_grad, shrink_first, shrink_second)
    triple_turned = from_phases(triple_turns).T
    triple_back = from_phases(triple_steps).T
    triple_gradient = from_phases(triple_lows).T
    triple_average, triple_variance, _ = adam_step(triple_turned, triple_first, triple_second)
    first_input, first_gain = first_back(
        sum(
            outer_sum(joint_back, rows.reshape(-1, width))
            for joint_back, rows in zip(joint_backs, triple_rows)
        )
    )
    token_gradient = (middle_back + first_input).astype(jnp.bfloat16).reshape(tokens.shape)
    gains_gradient = jnp.stack([first_gain, second_gain])
    for axis in ("core", "outer", "seq"):
        members = range(lax.axis_size(axis))
        for step in range(len(members).bit_length() - 1):
            pairs = [(member, member ^ (1 << step)) for member in members]
            gains_gradient = gains_gradient + lax.ppermute(gains_gradient, axis, pairs)
    gains_average, gains_variance, gains_direction = adam_step(
        gains_gradient, gains_first, gains_second
    )
    output_gradient = output_low.astype(jnp.float32)
    triple_updated = (triple_weight - WEIGHT_RATES[0] * triple_back) * (
        1.0 - WEIGHT_RATES[0] * DECAY_RATE
    )
    output_updated = (output_weight - WEIGHT_RATES[1] * output_back) * (
        1.0 - WEIGHT_RATES[1] * DECAY_RATE
    )
    expand_updated = (expand_weight - WEIGHT_RATES[2] * expand_back) * (
        1.0 - WEIGHT_RATES[2] * DECAY_RATE
    )
    shrink_updated = (shrink_weight - WEIGHT_RATES[3] * shrink_back) * (
        1.0 - WEIGHT_RATES[3] * DECAY_RATE
    )
    gains_updated = norm_gains - GAINS_RATE * gains_direction
    return (
        mixed,
        token_gradient,
        triple_gradient,
        output_gradient,
        expand_gradient,
        shrink_gradient,
        gains_gradient,
        triple_average,
        triple_variance,
        triple_updated,
        triple_updated.astype(jnp.bfloat16),
        output_average,
        output_variance,
        output_updated,
        output_updated.astype(jnp.bfloat16),
        expand_average,
        expand_variance,
        expand_updated,
        expand_updated.astype(jnp.bfloat16),
        shrink_average,
        shrink_variance,
        shrink_updated,
        shrink_updated.astype(jnp.bfloat16),
        gains_average,
        gains_variance,
        gains_updated,
    )


def solution(mesh):
    in_specs = (
        P(("outer", "core"), "seq", None),
        P(("outer", "core"), "seq", None),
        P(("outer", "core")),
        P("seq", ("outer", "core")),
        P("seq", ("outer", "core")),
        P("seq", ("outer", "core")),
        P(("outer", "core"), "seq"),
        P(),
        P(None, "seq", None),
        P(("outer", "core"), None),
        P("seq", ("outer", "core")),
        P("seq", ("outer", "core")),
        P("seq", ("outer", "core")),
        P("seq", ("outer", "core")),
        P("seq", ("outer", "core")),
        P("seq", ("outer", "core")),
        P(("outer", "core"), "seq"),
        P(("outer", "core"), "seq"),
        P(),
        P(),
    )
    out_specs = (
        P(("outer", "core"), "seq", None),
        P(("outer", "core"), "seq", None),
        P("seq", ("outer", "core")),
        P("seq", ("outer", "core")),
        P("seq", ("outer", "core")),
        P(("outer", "core"), "seq"),
        P(),
        P("seq", ("outer", "core")),
        P("seq", ("outer", "core")),
        P("seq", ("outer", "core")),
        P("seq", ("outer", "core")),
        P("seq", ("outer", "core")),
        P("seq", ("outer", "core")),
        P("seq", ("outer", "core")),
        P("seq", ("outer", "core")),
        P("seq", ("outer", "core")),
        P("seq", ("outer", "core")),
        P("seq", ("outer", "core")),
        P("seq", ("outer", "core")),
        P(("outer", "core"), "seq"),
        P(("outer", "core"), "seq"),
        P(("outer", "core"), "seq"),
        P(("outer", "core"), "seq"),
        P(),
        P(),
        P(),
    )
    groups = mesh.shape["fsdp"]
    devices = mesh.devices.reshape(mesh.shape["seq"], groups // 2, 2)
    split = Mesh(devices, ("seq", "outer", "core"))
    return jax.shard_map(body, mesh=split, in_specs=in_specs, out_specs=out_specs, check_vma=False)
```

```python
import functools
import math

import jax
import jax.numpy as jnp
from jax import lax
from jax.experimental import pallas as pl
from jax.experimental.pallas import tpu as pltpu
from jax.sharding import Mesh
from jax.sharding import PartitionSpec as P

HEADS = 16
HEAD_DIM = 64
FF = 2624
STEP = 10


ROPE_BASE = 160000.0
NORM_EPS = 1e-05
NEG_LARGE = -1e30
BETA_ONE = 0.95
BETA_TWO = 0.95
ADAM_EPS = 1e-08
DECAY_RATE = 0.01
WEIGHT_RATES = (0.03, 1.0, 0.03, 0.03)
GAINS_RATE = 0.8


def layer_norm(values, gain):
    centre = values - jnp.mean(values, axis=-1, keepdims=True)
    spread = jnp.mean(centre * centre, axis=-1, keepdims=True)
    return centre * lax.rsqrt(spread + NORM_EPS) * gain


def rotary_tables(position):
    halves = HEAD_DIM // 2
    frequency = ROPE_BASE ** (-2.0 * jnp.arange(halves, dtype=jnp.float32) / HEAD_DIM)
    angle = frequency[:, None] * position.astype(jnp.float32)[None, :]
    return jnp.cos(angle), jnp.sin(angle)


def outer_sum(left, right):
    return lax.dot_general(
        left, right, (((0,), (0,)), ((), ())), preferred_element_type=jnp.float32
    )


def back_product(left, right):
    return lax.dot_general(
        left, right, (((1,), (1,)), ((), ())), preferred_element_type=jnp.float32
    )


def plain_product(left, right):
    return jnp.dot(left, right, preferred_element_type=jnp.float32)


NT = (((1,), (1,)), ((), ()))
SAFE_BOUND = 60.0
MASK = -1e30
VMEM_LIMIT = 60 * 1024 * 1024


def extra_rows(rows, length, size=HEAD_DIM):
    place = lax.broadcasted_iota(jnp.int32, (size, length), 0)
    block = jnp.zeros((size, length), jnp.float32)
    for index, row in enumerate(rows):
        block = jnp.where(place == index, row, block)
    return block.astype(jnp.bfloat16)


def three_parts(row):
    high = row.astype(jnp.bfloat16).astype(jnp.float32)
    middle = (row - high).astype(jnp.bfloat16).astype(jnp.float32)
    return [high, middle, row - high - middle]


def mask_row(start, length, limit):
    place = start + lax.broadcasted_iota(jnp.int32, (1, length), 1)
    return jnp.where(place < limit, 0.0, MASK)


def project_kernel(pieces_ref, first_ref, cosine_ref, sine_ref, out_ref, rows_ref, *, group):
    shards, groups, size, _ = pieces_ref.shape
    cosine, sine = cosine_ref[...], sine_ref[...]
    half = HEAD_DIM // 2

    def chunk(part, head):
        start = (part * shards + head) * HEAD_DIM
        place = slice(start % size, start % size + HEAD_DIM)
        return jnp.concatenate(
            [pieces_ref[shard, start // size, place, :] for shard in range(shards)], axis=1
        )

    for begin in range(0, shards, group):
        heads = range(begin, begin + group)
        weight = jnp.concatenate([chunk(part, head) for head in heads for part in range(3)], axis=0)
        product = lax.dot_general(weight, first_ref[...], NT, preferred_element_type=jnp.float32)
        for index, head in enumerate(heads):
            for part in range(3):
                base = (3 * index + part) * HEAD_DIM
                rows_ref[head, part] = weight[base : base + HEAD_DIM]
            for part, scale in ((0, HEAD_DIM**-0.5), (1, 1.0)):
                base = (3 * index + part) * HEAD_DIM
                upper, lower = product[base : base + half], product[base + half : base + HEAD_DIM]
                turned_upper = (upper * cosine - lower * sine).astype(jnp.bfloat16)
                turned_lower = (lower * cosine + upper * sine).astype(jnp.bfloat16)
                place = part * HEAD_DIM
                scale = jnp.bfloat16(scale)
                out_ref[head, place : place + half, :] = turned_upper * scale
                out_ref[head, place + half : place + HEAD_DIM, :] = turned_lower * scale
            base = (3 * index + 2) * HEAD_DIM
            out_ref[head, 2 * HEAD_DIM :, :] = product[base : base + HEAD_DIM].astype(jnp.bfloat16)


def project_heads(pieces, first, cosine, sine):
    shards, groups, size, lanes = pieces.shape
    count, width = first.shape
    half = HEAD_DIM // 2
    whole = lambda *shape: pl.BlockSpec(shape, lambda i: (0,) * len(shape))
    return pl.pallas_call(
        functools.partial(project_kernel, group=min(4, shards)),
        grid=(1,),
        in_specs=[
            whole(shards, groups, size, lanes),
            whole(count, width),
            whole(half, count),
            whole(half, count),
        ],
        out_specs=[whole(shards, 3 * HEAD_DIM, count), whole(shards, 3, HEAD_DIM, width)],
        out_shape=[
            jax.ShapeDtypeStruct((shards, 3 * HEAD_DIM, count), jnp.bfloat16),
            jax.ShapeDtypeStruct((shards, 3, HEAD_DIM, width), jnp.bfloat16),
        ],
        compiler_params=pltpu.CompilerParams(vmem_limit_bytes=VMEM_LIMIT),
        cost_estimate=pl.CostEstimate(
            flops=6 * width * shards * HEAD_DIM * count,
            bytes_accessed=20 * width * shards * HEAD_DIM,
            transcendentals=0,
        ),
    )(pieces, first, cosine, sine)


def forward_kernel(length_ref, joint_ref, out_ref, log_ref, key_ref, value_ref, peak_ref, bound_ref):
    index = pl.program_id(0)
    shards, _, local = joint_ref.shape
    limit = length_ref[0]
    ratio = max(1, 2048 // local)
    blocks = (limit + local - 1) // local

    @pl.when(index == 0)
    def prepare():
        query_most = jnp.zeros((1, 1), jnp.float32)
        key_most = jnp.zeros((1, 1), jnp.float32)
        for shard in range(shards):
            place = slice(shard * local, (shard + 1) * local)
            query = joint_ref[shard, :HEAD_DIM, :].astype(jnp.float32)
            key = joint_ref[shard, HEAD_DIM : 2 * HEAD_DIM, :]
            wide_key = key.astype(jnp.float32)
            query_size = jnp.sum(query * query, axis=0, keepdims=True)
            key_size = jnp.sum(wide_key * wide_key, axis=0, keepdims=True)
            query_most = jnp.maximum(query_most, jnp.max(query_size, axis=1, keepdims=True))
            key_most = jnp.maximum(key_most, jnp.max(key_size, axis=1, keepdims=True))
            extra = extra_rows([mask_row(shard * local, local, limit), 1.0], local)
            key_ref[place, :] = jnp.concatenate([key, extra], axis=0).T
            value_ref[:HEAD_DIM, place] = joint_ref[shard, 2 * HEAD_DIM :, :]
            value_ref[HEAD_DIM:, place] = extra_rows([1.0], local, 16)
        bound_ref[0] = (jnp.sqrt(query_most) * jnp.sqrt(key_most))[0, 0]

    @pl.when(index >= blocks)
    def padding():
        out_ref[...] = jnp.zeros_like(out_ref)
        log_ref[...] = jnp.zeros_like(log_ref)

    @pl.when(index < blocks)
    def compute():
        query = joint_ref[index, :HEAD_DIM, :]
        peak_ref[...] = jnp.zeros_like(peak_ref)

        @pl.when(bound_ref[0] > SAFE_BOUND)
        def find_peak():
            plain = jnp.concatenate([query, extra_rows([1.0], local)], axis=0)

            def step(block, peak):
                place = pl.ds(pl.multiple_of(block * local, local), local)
                scores = jnp.dot(key_ref[place, :], plain, preferred_element_type=jnp.float32)
                return jnp.maximum(peak, jnp.max(scores, axis=0, keepdims=True))

            peak = lax.fori_loop(0, blocks, step, jnp.full((1, local), MASK, jnp.float32))
            peak_ref[...] = peak.astype(jnp.bfloat16).astype(jnp.float32)

        peak = peak_ref[...]
        augmented = jnp.concatenate([query, extra_rows([1.0, -peak], local)], axis=0)

        def attend(start, size, total):
            place = pl.ds(pl.multiple_of(start, local), size)
            scores = jnp.dot(key_ref[place, :], augmented, preferred_element_type=jnp.float32)
            weights = jnp.exp(scores).astype(jnp.bfloat16)
            return total + jnp.dot(
                value_ref[:, place], weights, preferred_element_type=jnp.float32
            )

        large = blocks // ratio
        total = lax.fori_loop(
            0,
            large,
            lambda block, total: attend(block * (ratio * local), ratio * local, total),
            jnp.zeros((HEAD_DIM + 16, local), jnp.float32),
        )
        total = lax.fori_loop(
            large * ratio, blocks, lambda block, total: attend(block * local, local, total), total
        )
        mass = total[HEAD_DIM : HEAD_DIM + 1, :]
        out_ref[0] = (total[:HEAD_DIM, :] / mass).astype(jnp.bfloat16)
        log_ref[0] = peak + jnp.log(mass)


def attend_forward(length, joint):
    shards, _, local = joint.shape
    total = shards * local
    return pl.pallas_call(
        forward_kernel,
        grid=(shards,),
        in_specs=[
            pl.BlockSpec(memory_space=pltpu.SMEM),
            pl.BlockSpec((shards, 3 * HEAD_DIM, local), lambda i: (0, 0, 0)),
        ],
        out_specs=[
            pl.BlockSpec((1, HEAD_DIM, local), lambda i: (i, 0, 0)),
            pl.BlockSpec((1, 1, local), lambda i: (i, 0, 0)),
        ],
        out_shape=[
            jax.ShapeDtypeStruct((shards, HEAD_DIM, local), jnp.bfloat16),
            jax.ShapeDtypeStruct((shards, 1, local), jnp.float32),
        ],
        scratch_shapes=[
            pltpu.VMEM((total, 2 * HEAD_DIM), jnp.bfloat16),
            pltpu.VMEM((HEAD_DIM + 16, total), jnp.bfloat16),
            pltpu.VMEM((1, local), jnp.float32),
            pltpu.SMEM((1,), jnp.float32),
        ],
        compiler_params=pltpu.CompilerParams(vmem_limit_bytes=VMEM_LIMIT),
        cost_estimate=pl.CostEstimate(
            flops=total * total,
            bytes_accessed=HEAD_DIM * total,
            transcendentals=0,
        ),
    )(length, joint)


def backward_kernel(
    length_ref,
    joint_ref,
    back_ref,
    out_ref,
    log_ref,
    cosine_ref,
    sine_ref,
    grad_ref,
    query_ref,
    wide_ref,
    query_flat,
    back_flat,
    query_sum,
):
    index = pl.program_id(0)
    shards, _, local = joint_ref.shape
    limit = length_ref[0]
    ratio = max(1, 2048 // local)
    blocks = (limit + local - 1) // local
    half = HEAD_DIM // 2

    def turned_back(wide, shard):
        cosine, sine = cosine_ref[shard], sine_ref[shard]
        upper, lower = wide[:half], wide[half:]
        return jnp.concatenate(
            [upper * cosine + lower * sine, lower * cosine - upper * sine], axis=0
        ).astype(jnp.bfloat16)

    @pl.when(index == 0)
    def prepare():
        for shard in range(shards):
            place = slice(shard * local, (shard + 1) * local)
            query = joint_ref[shard, :HEAD_DIM, :]
            back = back_ref[shard]
            extra = extra_rows([1.0] + three_parts(-log_ref[shard]), local)
            query_ref[place, :] = jnp.concatenate([query, extra], axis=0).T
            balance = jnp.sum(
                back.astype(jnp.float32) * out_ref[shard].astype(jnp.float32),
                axis=0,
                keepdims=True,
            )
            extra = extra_rows(three_parts(-balance), local)
            wide_ref[place, :] = jnp.concatenate([back, extra], axis=0).T
            query_flat[:, place] = query
            back_flat[:, place] = back
        query_sum[...] = jnp.zeros_like(query_sum)

    @pl.when(index >= blocks)
    def padding():
        grad_ref[index, HEAD_DIM:, :] = jnp.zeros((2 * HEAD_DIM, local), jnp.bfloat16)

    @pl.when(index < blocks)
    def compute():
        key = joint_ref[index, HEAD_DIM : 2 * HEAD_DIM, :]
        value = joint_ref[index, 2 * HEAD_DIM :, :]
        mask = mask_row(index * local, local, limit)
        wide_key = jnp.concatenate([key, extra_rows([mask, 1.0, 1.0, 1.0], local)], axis=0)
        wide_value = jnp.concatenate([value, extra_rows([1.0, 1.0, 1.0], local)], axis=0)

        def gather(start, size, carry):
            key_sum, value_sum = carry
            place = pl.ds(pl.multiple_of(start, local), size)
            scores = jnp.dot(query_ref[place, :], wide_key, preferred_element_type=jnp.float32)
            chance = jnp.exp(scores)
            change = jnp.dot(wide_ref[place, :], wide_value, preferred_element_type=jnp.float32)
            chance_low = chance.astype(jnp.bfloat16)
            score_back = (chance * change).astype(jnp.bfloat16)
            value_sum = value_sum + jnp.dot(
                back_flat[:, place], chance_low, preferred_element_type=jnp.float32
            )
            key_sum = key_sum + jnp.dot(
                query_flat[:, place], score_back, preferred_element_type=jnp.float32
            )
            query_sum[:, place] += lax.dot_general(
                key, score_back, NT, preferred_element_type=jnp.float32
            )
            return (key_sum, value_sum)

        large = blocks // ratio
        zero = jnp.zeros((HEAD_DIM, local), jnp.float32)
        carry = lax.fori_loop(
            0,
            large,
            lambda block, carry: gather(block * (ratio * local), ratio * local, carry),
            (zero, zero),
        )
        key_sum, value_sum = lax.fori_loop(
            large * ratio, blocks, lambda block, carry: gather(block * local, local, carry), carry
        )
        grad_ref[index, HEAD_DIM : 2 * HEAD_DIM, :] = turned_back(key_sum, index)
        grad_ref[index, 2 * HEAD_DIM :, :] = value_sum.astype(jnp.bfloat16)

    @pl.when(index == shards - 1)
    def finish():
        for shard in range(shards):
            place = slice(shard * local, (shard + 1) * local)
            grad_ref[shard, :HEAD_DIM, :] = turned_back(
                query_sum[:, place] * HEAD_DIM**-0.5, shard
            )


def attend_backward(length, joint, back, attend, log_mass, cosine, sine):
    shards, _, local = joint.shape
    total = shards * local
    whole = lambda rows: pl.BlockSpec((shards, rows, local), lambda i: (0, 0, 0))
    return pl.pallas_call(
        backward_kernel,
        grid=(shards,),
        in_specs=[
            pl.BlockSpec(memory_space=pltpu.SMEM),
            whole(3 * HEAD_DIM),
            whole(HEAD_DIM),
            whole(HEAD_DIM),
            whole(1),
            whole(HEAD_DIM // 2),
            whole(HEAD_DIM // 2),
        ],
        out_specs=whole(3 * HEAD_DIM),
        out_shape=jax.ShapeDtypeStruct((shards, 3 * HEAD_DIM, local), jnp.bfloat16),
        scratch_shapes=[
            pltpu.VMEM((total, 2 * HEAD_DIM), jnp.bfloat16),
            pltpu.VMEM((total, 2 * HEAD_DIM), jnp.bfloat16),
            pltpu.VMEM((HEAD_DIM, total), jnp.bfloat16),
            pltpu.VMEM((HEAD_DIM, total), jnp.bfloat16),
            pltpu.VMEM((HEAD_DIM, total), jnp.float32),
        ],
        compiler_params=pltpu.CompilerParams(vmem_limit_bytes=VMEM_LIMIT),
        cost_estimate=pl.CostEstimate(
            flops=total * total,
            bytes_accessed=HEAD_DIM * total,
            transcendentals=0,
        ),
    )(length, joint, back, attend, log_mass, cosine, sine)


TN = (((0,), (0,)), ((), ()))
PLAIN = (((1,), (0,)), ((), ()))
LANES = 128
GROUPS = 4
RUNS = 8
UNITS = FF // GROUPS
EXPAND_RUN = -(-2 * UNITS // (16 * RUNS)) * 16
SHRINK_RUN = -(-UNITS // (16 * RUNS)) * 16


def run_segments(start, stop, run):
    segments = []
    while start < stop:
        index = start // run
        end = min(stop, (index + 1) * run)
        segments.append((index, start - index * run, start, end - start))
        start = end
    return segments


def feed_kernel(
    second_ref,
    upstream_ref,
    active_ref,
    gate_ref,
    shrink_ref,
    shrunk_ref,
    second_back_ref,
    parts_ref,
    grads_ref,
    zero_ref,
    send_ref,
    zero_send_ref,
):
    index = pl.program_id(0)

    def joined(ref):
        return jnp.concatenate([ref[piece, 0] for piece in range(ref.shape[0])], axis=1)

    def product(left, right, dims):
        return lax.dot_general(left, right, dims, preferred_element_type=jnp.float32)

    def grad_copies(half, pair):
        moves = []
        for kind, member in ((0, pair), (1, pair + 2)):
            for run, place, offset, size in run_segments(
                half * UNITS, (half + 1) * UNITS, EXPAND_RUN
            ):
                moves.append((kind, offset - half * UNITS, run, member, place, size))
        for run, place, offset, size in run_segments(0, UNITS, SHRINK_RUN):
            moves.append((2, offset, run, 2 * pair + half, EXPAND_RUN + place, size))
        return [
            pltpu.make_async_copy(
                grads_ref.at[half, kind, pl.ds(offset, size), :],
                parts_ref.at[run, member, pl.ds(place, size), :],
                send_ref.at[half, number],
            )
            for number, (kind, offset, run, member, place, size) in enumerate(moves)
        ]

    def zero_copies():
        moves = []
        for member in range(GROUPS):
            for base, run_size, total in ((0, EXPAND_RUN, 2 * UNITS), (EXPAND_RUN, SHRINK_RUN, UNITS)):
                for run, place, _, size in run_segments(total, RUNS * run_size, run_size):
                    moves.append((run, member, base + place, size))
        return [
            pltpu.make_async_copy(
                zero_ref.at[pl.ds(0, size), :],
                parts_ref.at[run, member, pl.ds(place, size), :],
                zero_send_ref.at[number],
            )
            for number, (run, member, place, size) in enumerate(moves)
        ]

    @pl.when(index == 0)
    def fill():
        zero_ref[...] = jnp.zeros_like(zero_ref)
        for copy in zero_copies():
            copy.start()

    active, gate, shrink = joined(active_ref), joined(gate_ref), joined(shrink_ref)
    second, upstream = second_ref[...], upstream_ref[...]
    input_active = product(second, active, NT)
    input_gate = product(second, gate, NT)
    hidden_back = product(upstream, shrink, NT)
    below = 0.5 + 0.5 * lax.erf(input_active * 0.5**0.5)
    bell = jnp.exp(-0.5 * input_active * input_active) * (0.5 / math.pi) ** 0.5
    curve = input_active * below
    hidden = (curve * input_gate).astype(jnp.bfloat16)
    active_back = (hidden_back * input_gate * (below + input_active * bell)).astype(jnp.bfloat16)
    gate_back = (hidden_back * curve).astype(jnp.bfloat16)
    shrunk = product(hidden, shrink, PLAIN)
    second_back = product(active_back, active, PLAIN) + product(gate_back, gate, PLAIN)

    @pl.when(index == 0)
    def begin():
        shrunk_ref[...] = shrunk
        second_back_ref[...] = second_back

    @pl.when(index > 0)
    def add():
        shrunk_ref[...] += shrunk
        second_back_ref[...] += second_back

    for half in range(2):

        @pl.when(index % 2 == half)
        def send(half=half):
            pair = index // 2

            @pl.when(index >= 2)
            def free():
                for copy in grad_copies(half, pair - 1):
                    copy.wait()

            grads_ref[half, 0] = product(active_back, second, TN).astype(jnp.bfloat16)
            grads_ref[half, 1] = product(gate_back, second, TN).astype(jnp.bfloat16)
            grads_ref[half, 2] = product(hidden, upstream, TN).astype(jnp.bfloat16)
            for copy in grad_copies(half, pair):
                copy.start()

    @pl.when(index == GROUPS - 1)
    def drain():
        for half in range(2):
            for copy in grad_copies(half, 1):
                copy.wait()
        for copy in zero_copies():
            copy.wait()


def feed_forward(second, upstream, pieces):
    count, width = second.shape
    block = (RUNS, 1, UNITS, LANES)
    held = pl.BlockSpec((count, width), lambda i: (0, 0), pipeline_mode=pl.Buffered(1))
    wide = jax.ShapeDtypeStruct((count, width), jnp.float32)
    run = EXPAND_RUN + SHRINK_RUN
    copies = max(
        2 * len(run_segments(half * UNITS, (half + 1) * UNITS, EXPAND_RUN)) for half in range(2)
    ) + len(run_segments(0, UNITS, SHRINK_RUN))
    return pl.pallas_call(
        feed_kernel,
        grid=(GROUPS,),
        in_specs=[
            held,
            held,
            pl.BlockSpec(block, lambda i: (0, i // 2, i % 2, 0)),
            pl.BlockSpec(block, lambda i: (0, i // 2 + 2, i % 2, 0)),
            pl.BlockSpec(block, lambda i: (0, i, 2, 0)),
        ],
        out_specs=[held, held, pl.BlockSpec(memory_space=pl.ANY)],
        out_shape=[wide, wide, jax.ShapeDtypeStruct((RUNS, GROUPS, run, width), jnp.bfloat16)],
        scratch_shapes=[
            pltpu.VMEM((2, 3, UNITS, width), jnp.bfloat16),
            pltpu.VMEM((max(EXPAND_RUN, SHRINK_RUN), width), jnp.bfloat16),
            pltpu.SemaphoreType.DMA((2, copies)),
            pltpu.SemaphoreType.DMA((GROUPS * 8,)),
        ],
        compiler_params=pltpu.CompilerParams(vmem_limit_bytes=VMEM_LIMIT),
        cost_estimate=pl.CostEstimate(
            flops=count * width,
            bytes_accessed=count * width,
            transcendentals=0,
        ),
    )(second, upstream, pieces, pieces, pieces)


def enter_kernel(*refs):
    phases = (len(refs) - 9) // 2
    attend_refs, weight_refs = refs[:phases], refs[phases : 2 * phases]
    limit_ref, token_ref, cotangent_ref, gain_ref = refs[2 * phases : 2 * phases + 4]
    middle_ref, normal_ref, second_ref, upstream_ref, spread_ref = refs[2 * phases + 4 :]
    middle = token_ref[...].astype(jnp.float32)
    for attend_ref, weight_ref in zip(attend_refs, weight_refs):
        middle += lax.dot_general(
            attend_ref[...], weight_ref[...], TN, preferred_element_type=jnp.float32
        )
    block = middle.shape[0]
    centre = middle - jnp.mean(middle, axis=1, keepdims=True)
    scale = lax.rsqrt(jnp.mean(centre * centre, axis=1, keepdims=True) + NORM_EPS)
    normal = centre * scale
    place = pl.program_id(0) * block + lax.broadcasted_iota(jnp.int32, (block, 1), 0)
    middle_ref[...] = middle
    normal_ref[...] = normal
    spread_ref[...] = scale
    second_ref[...] = (normal * gain_ref[1:2, :]).astype(jnp.bfloat16)
    upstream_ref[...] = jnp.where(place < limit_ref[0], cotangent_ref[...], jnp.bfloat16(0.0))


def enter_feed(attends, weights, limit, tokens, cotangent, gains):
    count, width = tokens.shape
    block = min(256, count)
    rows = pl.BlockSpec((block, width), lambda i: (i, 0))
    wide = jax.ShapeDtypeStruct((count, width), jnp.float32)
    low = jax.ShapeDtypeStruct((count, width), jnp.bfloat16)
    return pl.pallas_call(
        enter_kernel,
        grid=(count // block,),
        in_specs=[pl.BlockSpec((attend.shape[0], block), lambda i: (0, i)) for attend in attends]
        + [pl.BlockSpec(weight.shape, lambda i: (0, 0)) for weight in weights]
        + [pl.BlockSpec(memory_space=pltpu.SMEM), rows, rows]
        + [pl.BlockSpec(gains.shape, lambda i: (0, 0))],
        out_specs=[rows, rows, rows, rows, pl.BlockSpec((block, 1), lambda i: (i, 0))],
        out_shape=[wide, wide, low, low, jax.ShapeDtypeStruct((count, 1), jnp.float32)],
        compiler_params=pltpu.CompilerParams(vmem_limit_bytes=VMEM_LIMIT),
        cost_estimate=pl.CostEstimate(
            flops=2 * count * width * width, bytes_accessed=20 * count * width, transcendentals=0
        ),
    )(*attends, *weights, limit, tokens, cotangent, gains)


def leave_kernel(*refs):
    phases = (len(refs) - 12) // 2
    weight_refs, back_refs = refs[:phases], refs[-phases:]
    limit_ref, shrunk_ref, change_ref, middle_ref, normal_ref, spread_ref = refs[phases : phases + 6]
    upstream_ref, gain_ref = refs[phases + 6 : phases + 8]
    mixed_ref, middle_back_ref, branch_ref, gain_grad_ref = refs[phases + 8 : phases + 12]
    index = pl.program_id(0)
    block = mixed_ref.shape[0]
    place = index * block + lax.broadcasted_iota(jnp.int32, (block, 1), 0)
    mixed = middle_ref[...] + shrunk_ref[...]
    mixed_ref[...] = jnp.where(place < limit_ref[0], mixed, 0.0).astype(jnp.bfloat16)
    change, normal = change_ref[...], normal_ref[...]
    gain_grad = jnp.sum(change * normal, axis=0, keepdims=True)

    @pl.when(index == 0)
    def begin():
        gain_grad_ref[...] = gain_grad

    @pl.when(index > 0)
    def add():
        gain_grad_ref[...] += gain_grad

    inner = change * gain_ref[1:2, :]
    inner = (
        inner
        - jnp.mean(inner, axis=1, keepdims=True)
        - normal * jnp.mean(inner * normal, axis=1, keepdims=True)
    )
    middle_back = upstream_ref[...].astype(jnp.float32) + spread_ref[...] * inner
    branch = middle_back.astype(jnp.bfloat16)
    middle_back_ref[...] = middle_back
    branch_ref[...] = branch
    for weight_ref, back_ref in zip(weight_refs, back_refs):
        back_ref[...] = lax.dot_general(
            weight_ref[...], branch, NT, preferred_element_type=jnp.float32
        ).astype(jnp.bfloat16)


def leave_feed(weights, limit, shrunk, change, middle, normal, spread, upstream, gains):
    count, width = shrunk.shape
    block = min(256, count)
    rows = pl.BlockSpec((block, width), lambda i: (i, 0))
    wide = jax.ShapeDtypeStruct((count, width), jnp.float32)
    low = jax.ShapeDtypeStruct((count, width), jnp.bfloat16)
    return pl.pallas_call(
        leave_kernel,
        grid=(count // block,),
        in_specs=[pl.BlockSpec(weight.shape, lambda i: (0, 0)) for weight in weights]
        + [pl.BlockSpec(memory_space=pltpu.SMEM), rows, rows, rows, rows]
        + [pl.BlockSpec((block, 1), lambda i: (i, 0)), rows]
        + [pl.BlockSpec(gains.shape, lambda i: (0, 0))],
        out_specs=[rows, rows, rows, pl.BlockSpec((1, width), lambda i: (0, 0))]
        + [pl.BlockSpec((weight.shape[0], block), lambda i: (0, i)) for weight in weights],
        out_shape=[low, wide, low, jax.ShapeDtypeStruct((1, width), jnp.float32)]
        + [jax.ShapeDtypeStruct((weight.shape[0], count), jnp.bfloat16) for weight in weights],
        compiler_params=pltpu.CompilerParams(vmem_limit_bytes=VMEM_LIMIT),
        cost_estimate=pl.CostEstimate(
            flops=2 * count * width * width, bytes_accessed=28 * count * width, transcendentals=0
        ),
    )(*weights, limit, shrunk, change, middle, normal, spread, upstream, gains)


def adam_step(rotated, first, second):
    average = BETA_ONE * first + (1.0 - BETA_ONE) * rotated
    variance = BETA_TWO * second + (1.0 - BETA_TWO) * rotated * rotated
    direction = (
        average / (1.0 - BETA_ONE**STEP) / (jnp.sqrt(variance / (1.0 - BETA_TWO**STEP)) + ADAM_EPS)
    )
    return (average, variance, direction)


def body(
    tokens,
    cotangent,
    lengths,
    triple_weight,
    output_weight,
    expand_weight,
    shrink_weight,
    norm_gains,
    side_bases,
    output_right,
    triple_first,
    triple_second,
    output_first,
    output_second,
    expand_first,
    expand_second,
    shrink_first,
    shrink_second,
    gains_first,
    gains_second,
):
    rows_here, local_len, width = tokens.shape
    count = rows_here * local_len
    shards = lax.axis_size("seq")
    groups = lax.axis_size("outer") * lax.axis_size("core")
    split = HEADS // shards
    core = lax.axis_index("core")
    swap = functools.partial(lax.ppermute, axis_name="core", perm=[(0, 1), (1, 0)])
    other_lengths = swap(lengths)
    ahead = (lengths > other_lengths) | ((lengths == other_lengths) & (core == 0))

    def by_length(own, other):
        return [jnp.where(ahead[0], own, other), jnp.where(ahead[0], other, own)]

    def by_core(mine, other):
        return [jnp.where(core == 0, mine, other), jnp.where(core == 0, other, mine)]

    def both_rows(own):
        return by_length(own, swap(own)) if split == 2 else [own]

    piece = width // shards
    fsdp = ("outer", "core")
    everyone = ("seq",) + fsdp
    offset = lax.axis_index("seq") * local_len
    position = offset + jnp.arange(local_len, dtype=jnp.int32)
    cosine, sine = rotary_tables(position)
    every = jnp.arange(shards * local_len, dtype=jnp.int32)
    all_cosine, all_sine = (
        table.reshape(HEAD_DIM // 2, shards, local_len).transpose(1, 0, 2)
        for table in rotary_tables(every)
    )
    valid = (position[None, :] < lengths[:, None]).astype(jnp.float32).reshape(count, 1)
    exchange = functools.partial(lax.all_to_all, axis_name="seq", split_axis=0, concat_axis=0)

    def tied(*values):
        return lax.optimization_barrier(values)

    def gathered(shard):
        flat = lax.all_gather(shard, everyone, axis=0, tiled=False)
        return flat.reshape((shards, groups) + shard.shape)

    triple_shards = (
        triple_weight.T.astype(jnp.bfloat16)
        .reshape(-1, split, HEAD_DIM, piece)
        .transpose(1, 0, 2, 3)
        .reshape(split, -1, piece)
    )
    if split == 2:
        mine = lax.dynamic_index_in_dim(triple_shards, core, 0, keepdims=False)
        other = lax.dynamic_index_in_dim(triple_shards, 1 - core, 0, keepdims=False)
        triple_shards = jnp.stack(by_core(mine, swap(other)))
        triple_pieces = lax.all_gather(triple_shards, ("seq", "outer"), axis=0, tiled=False)
    else:
        triple_pieces = gathered(triple_shards[0])
    triple_pieces = triple_pieces.reshape(shards, groups, -1, piece)
    output_columns = width // groups
    lanes = min(piece, output_columns)

    def fold(block):
        rows = block.shape[0]
        return block.reshape(rows, -1, lanes).transpose(1, 0, 2).reshape(-1, lanes)

    bases_low = side_bases.astype(jnp.bfloat16)
    right_low = output_right.astype(jnp.bfloat16)
    member = lax.axis_index("outer") * lax.axis_size("core") + lax.axis_index("core")
    base_rows = piece // groups
    flat = tokens.reshape(count, width).astype(jnp.float32)
    first_normed, first_back = jax.vjp(layer_norm, flat, norm_gains[0])
    first_low = first_normed.astype(jnp.bfloat16)
    other_shards = jnp.concatenate(
        [
            expand_weight.T.astype(jnp.bfloat16),
            shrink_weight.astype(jnp.bfloat16),
            fold(output_weight.astype(jnp.bfloat16)),
        ],
        axis=0,
    )
    firsts = both_rows(first_low)
    projected = [project_heads(triple_pieces, first, cosine, sine) for first in firsts]
    triple_rows = projected[0][1].reshape(-1, width)
    joints = [exchange(joint) for joint, _ in projected]
    all_cosine, all_sine, joints[0] = tied(all_cosine, all_sine, joints[0])
    row_lengths = both_rows(lengths)
    forwards, attends = [], []
    for row, joint in enumerate(joints):
        outcome = attend_forward(row_lengths[row], joint)
        if row:
            attends[-1], outcome = tied(attends[-1], outcome)
        if row < split - 1:
            joints[row + 1], outcome = tied(joints[row + 1], outcome)
        forwards.append(outcome)
        attends.append(exchange(outcome[0]))
    other_shards, forwards[0] = tied(other_shards, forwards[0])
    other_pieces = gathered(other_shards)
    chosen = jnp.stack([bases_low[0], bases_low[2], bases_low[3]])
    chosen = lax.dynamic_slice_in_dim(chosen, member * base_rows, base_rows, 1)
    expand_rows = 2 * FF // groups
    shrink_rows = FF // groups
    output_rows = list(
        other_pieces[:, :, expand_rows + shrink_rows :]
        .reshape(shards, groups, output_columns // lanes, split, HEAD_DIM, lanes)
        .transpose(3, 0, 4, 1, 2, 5)
        .reshape(split, shards * HEAD_DIM, width)
    )
    canonical = (shards, groups, piece) == (RUNS, GROUPS, LANES)
    if canonical:
        feed_pieces = other_pieces
    else:
        feed_pieces = [
            other_pieces[:, :, start:end]
            .transpose(1, 2, 0, 3)
            .reshape(GROUPS, -1, RUNS, LANES)
            .transpose(2, 0, 1, 3)
            for start, end in ((0, expand_rows), (expand_rows, expand_rows + shrink_rows))
        ]
        feed_pieces = jnp.concatenate(feed_pieces, axis=2)
    chosen, forwards[-1] = tied(chosen, forwards[-1])
    bases_full = gathered(chosen)
    attends = [attend.reshape(shards * HEAD_DIM, count) for attend in attends]
    if split == 2:
        own, other = by_length(*attends)
        attends = by_core(own, swap(other))
    expand_height = -(-expand_rows // (16 * shards)) * 16
    shrink_height = -(-shrink_rows // (16 * shards)) * 16

    def to_rows(block):
        block = exchange(block)
        return block.transpose(1, 0, 2).reshape(block.shape[1], -1)

    def padded(block, height):
        block = jnp.pad(block, ((0, height * shards - block.shape[0]), (0, 0)))
        return block.reshape(shards, height, piece)

    def by_heads(block):
        return (
            block.reshape(-1, split, HEAD_DIM, piece)
            .transpose(1, 0, 2, 3)
            .reshape(split, shards, -1, piece)
        )

    def from_heads(blocks):
        block = jnp.stack(blocks).astype(jnp.float32).reshape(split, -1, HEAD_DIM, piece)
        return block.transpose(1, 0, 2, 3).reshape(-1, piece)

    moments = []
    for expand, shrink, triple in (
        (expand_first, shrink_first, triple_first),
        (expand_second, shrink_second, triple_second),
    ):
        moments += [padded(expand.T, expand_height), padded(shrink, shrink_height)]
        moments += list(by_heads(triple.T))
    moments, attends[-1], feed_pieces = tied(moments, attends[-1], feed_pieces)
    heights = [moment.shape[1] for moment in moments]
    moments = to_rows(jnp.concatenate(moments, axis=1))
    edges = [sum(heights[:index]) for index in range(len(heights) + 1)]
    moments = [moments[start:end] for start, end in zip(edges, edges[1:])]
    moments = list(zip(moments[: split + 2], moments[split + 2 :]))
    inside = jnp.clip(lengths - offset, 0, local_len)
    middle, second_normal, second_low, upstream_low, second_spread = enter_feed(
        attends,
        output_rows,
        inside,
        tokens.reshape(count, width),
        cotangent.reshape(count, width),
        norm_gains,
    )
    shrunk, second_change, parts = feed_forward(second_low, upstream_low, feed_pieces)
    moments, bases_full, shrunk, second_change, parts = tied(
        moments, bases_full, shrunk, second_change, parts
    )
    mixed, middle_back, branch_low, second_gain, *backs = leave_feed(
        output_rows,
        inside,
        shrunk,
        second_change,
        middle,
        second_normal,
        second_spread,
        upstream_low,
        norm_gains,
    )
    mixed = mixed.reshape(tokens.shape)
    second_gain = second_gain[0]
    backs = [back.reshape(shards, HEAD_DIM, count) for back in backs]
    if split == 2:
        mine, other = by_core(*backs)
        backs = by_length(mine, swap(other))
    attend_backs = [exchange(back) for back in backs]

    def halved(blocks, axis, dim):
        size = lax.axis_size(axis)
        place = lax.axis_index(axis)
        while size > 1:
            size //= 2
            shape = blocks.shape
            blocks = blocks.reshape(shape[:dim] + (2, size) + shape[dim + 1 :])
            side = (place // size) % 2
            mine = lax.dynamic_index_in_dim(blocks, side, dim, keepdims=False)
            other = lax.dynamic_index_in_dim(blocks, 1 - side, dim, keepdims=False)
            pairs = [(member, member ^ size) for member in range(lax.axis_size(axis))]
            other = lax.ppermute(other, axis, pairs)
            blocks = (mine.astype(jnp.float32) + other.astype(jnp.float32)).astype(jnp.bfloat16)
        return jnp.squeeze(blocks, dim)

    def doubled(block, axis):
        block = block[None]
        place = lax.axis_index(axis)
        step = 1
        while step < lax.axis_size(axis):
            pairs = [(member, member ^ step) for member in range(lax.axis_size(axis))]
            other = lax.ppermute(block, axis, pairs)
            upper = (place // step) % 2 == 1
            block = jnp.concatenate(
                [jnp.where(upper, other, block), jnp.where(upper, block, other)], axis=0
            )
            step *= 2
        return block

    def near_sum(blocks):
        return halved(halved(blocks, "core", 1), "outer", 0)

    def merged(*blocks):
        sizes = [math.prod(block.shape[1:]) for block in blocks]
        flat = [block.reshape(shards, -1, piece) for block in blocks]
        flat = exchange(jnp.concatenate(flat, axis=1))
        results, start = [], 0
        for block, size in zip(blocks, sizes):
            rows = size // piece
            results.append(flat[:, start : start + rows].reshape(block.shape))
            start += rows
        return results

    def widened(block):
        rows = piece * output_columns // count
        block = block.reshape(-1, piece // rows, rows, output_columns)
        return block.swapaxes(1, 2).reshape(shards, -1, count)

    def narrowed(block):
        rows = piece * output_columns // count
        block = block.reshape(-1, rows, piece // rows, output_columns)
        return block.swapaxes(1, 2).reshape(shards, -1, piece, output_columns)

    def far_sum(terms):
        return jnp.sum(terms.astype(jnp.float32), axis=0).astype(jnp.bfloat16)

    def cut_rows(rows):
        return rows.reshape(rows.shape[0], shards, piece).transpose(1, 0, 2)

    outer = lax.axis_size("outer")
    output_part = jnp.stack(
        [
            jnp.dot(attend, branch_low, preferred_element_type=jnp.float32)
            .astype(jnp.bfloat16)
            .reshape(shards, HEAD_DIM, width)
            for attend in attends
        ],
        axis=1,
    )
    output_terms = halved(
        output_part.reshape(shards, piece, outer, -1, output_columns).transpose(0, 2, 3, 1, 4),
        "core",
        2,
    )
    def cut(product, height):
        block = product.reshape(groups, -1, width)
        block = jnp.pad(block, ((0, 0), (0, height * shards - block.shape[1]), (0, 0)))
        return block.reshape(groups, shards, height, width)

    if not canonical:
        parts = parts.transpose(1, 0, 2, 3)
        parts = [
            cut(block.reshape(GROUPS, -1, width)[:, : size // GROUPS], height)
            for block, size, height in (
                (parts[:, :, :EXPAND_RUN], 2 * FF, expand_height),
                (parts[:, :, EXPAND_RUN:], FF, shrink_height),
            )
        ]
        parts = jnp.concatenate(parts, axis=2).transpose(1, 0, 2, 3)
    parts = parts.reshape(shards * groups, -1, width)
    owned = lax.psum_scatter(parts, everyone, scatter_dimension=0, tiled=False)
    feed_height = expand_height + shrink_height

    def soap_rows(rows, base, moment):
        rotated = plain_product(rows, base)
        direction = adam_step(rotated, *moment)[2]
        step = back_product(direction.astype(jnp.bfloat16), base)
        return rotated.astype(jnp.bfloat16), step.astype(jnp.bfloat16)

    output_terms = widened(output_terms)
    order = list(range(split))[::-1]
    output_terms, attend_backs[order[0]] = tied(output_terms, attend_backs[order[0]])
    grads = [None] * split
    for step, row in enumerate(order):
        grad = attend_backward(
            row_lengths[row],
            joints[row],
            attend_backs[row],
            *forwards[row],
            all_cosine,
            all_sine,
        )
        if step < split - 1:
            following = order[step + 1]
            attend_backs[following], grad = tied(attend_backs[following], grad)
        else:
            grads, owned, bases_full, grad = tied(grads, owned, bases_full, grad)
        if step == 0:
            grad = jnp.concatenate([grad, output_terms], axis=1)
        grads[row] = exchange(grad)
    output_low = halved(far_sum(narrowed(grads[order[0]][:, 3 * HEAD_DIM :])), "outer", 0)
    joint_backs = [grad[:, : 3 * HEAD_DIM].reshape(-1, count) for grad in grads]
    output_left = outer_sum(bases_low[1], output_low).astype(jnp.bfloat16)
    output_left = output_left.reshape(shards, piece, output_columns)

    def triple_part(row):
        return jnp.dot(joint_backs[row], firsts[row], preferred_element_type=jnp.float32)

    def triple_rest(rows, head):
        return jnp.concatenate([rows, *soap_rows(rows, bases_full[0], moments[2 + head])])

    bases_full = bases_full.transpose(2, 0, 1, 3, 4).reshape(3, width, width)
    feed_rows = jnp.concatenate(
        [
            owned,
            *soap_rows(owned[:expand_height], bases_full[1], moments[0]),
            *soap_rows(owned[expand_height:], bases_full[2], moments[1]),
        ]
    )
    settled = jnp.concatenate(
        [cut_rows(feed_rows), output_left.reshape(shards, -1, piece)], axis=1
    )
    early = [triple_part(row) for row in order[:-1]]
    joint_backs[order[-1]], early, settled = tied(joint_backs[order[-1]], early, settled)
    settled = exchange(settled)
    output_left = settled[:, feed_rows.shape[0] :].reshape(shards, piece, output_columns)
    output_left = far_sum(output_left)
    part = sum(early, triple_part(order[-1])).astype(jnp.bfloat16)
    part = part.reshape(shards, 3, HEAD_DIM, width).swapaxes(0, 1)
    part = part.reshape(outer, groups // outer, shards, -1, width)
    if split == 2:
        part = halved(part, "outer", 0).swapaxes(0, 1)
        rows = far_sum(exchange(part))
        mine = lax.dynamic_index_in_dim(rows, core, 0, keepdims=False)
        other = lax.dynamic_index_in_dim(rows, 1 - core, 0, keepdims=False)
        head_rows = by_core(mine, swap(other))
    else:
        head_rows = [far_sum(exchange(near_sum(part)))]
    triple_done = [triple_rest(rows, head) for head, rows in enumerate(head_rows)]
    output_turned = plain_product(output_left, right_low).astype(jnp.bfloat16)
    output_turned = near_sum(
        output_turned.reshape(piece, outer, -1, output_columns).transpose(1, 2, 0, 3)
    ).astype(jnp.float32)
    output_average, output_variance, output_direction = adam_step(
        output_turned, output_first, output_second
    )
    output_wide = doubled(doubled(output_direction.astype(jnp.bfloat16), "core"), "outer")
    output_wide = output_wide.reshape(groups, piece, output_columns).swapaxes(0, 1)
    output_middle = back_product(output_wide.reshape(piece, width), right_low)
    *triple_done, output_middle = merged(
        *[cut_rows(rows) for rows in triple_done],
        jnp.broadcast_to(output_middle.astype(jnp.bfloat16), (shards, piece, output_columns)),
    )
    output_back = plain_product(bases_low[1], output_middle.reshape(width, output_columns))
    triple_lows, triple_turns, triple_steps = zip(
        *[jnp.split(done, 3, axis=1) for done in triple_done]
    )

    def settled_piece(start, height, size):
        return settled[:, start : start + height].reshape(-1, piece)[:size].astype(jnp.float32)

    expand_gradient, expand_turned_grad, expand_back = (
        settled_piece(start, expand_height, expand_rows).T
        for start in (0, feed_height, feed_height + expand_height)
    )
    shrink_gradient, shrink_turned_grad, shrink_back = (
        settled_piece(start, shrink_height, shrink_rows)
        for start in (
            expand_height,
            feed_height + 2 * expand_height,
            feed_height + 2 * expand_height + shrink_height,
        )
    )
    expand_average, expand_variance, _ = adam_step(expand_turned_grad, expand_first, expand_second)
    shrink_average, shrink_variance, _ = adam_step(shrink_turned_grad, shrink_first, shrink_second)
    triple_turned = from_heads(triple_turns).T
    triple_back = from_heads(triple_steps).T
    triple_gradient = from_heads(triple_lows).T
    triple_average, triple_variance, _ = adam_step(triple_turned, triple_first, triple_second)
    changes = [outer_sum(joint_back, triple_rows) for joint_back in joint_backs]
    if split == 2:
        own, other = by_length(*changes)
        first_change = own + swap(other.astype(jnp.bfloat16)).astype(jnp.float32)
    else:
        first_change = changes[0]
    first_input, first_gain = first_back(first_change)
    token_gradient = (middle_back + first_input).astype(jnp.bfloat16).reshape(tokens.shape)
    gains_gradient = jnp.stack([first_gain, second_gain])
    for axis in ("core", "outer", "seq"):
        members = range(lax.axis_size(axis))
        for step in range(len(members).bit_length() - 1):
            pairs = [(member, member ^ (1 << step)) for member in members]
            gains_gradient = gains_gradient + lax.ppermute(gains_gradient, axis, pairs)
    gains_average, gains_variance, gains_direction = adam_step(
        gains_gradient, gains_first, gains_second
    )
    output_gradient = output_low.astype(jnp.float32)
    triple_updated = (triple_weight - WEIGHT_RATES[0] * triple_back) * (
        1.0 - WEIGHT_RATES[0] * DECAY_RATE
    )
    output_updated = (output_weight - WEIGHT_RATES[1] * output_back) * (
        1.0 - WEIGHT_RATES[1] * DECAY_RATE
    )
    expand_updated = (expand_weight - WEIGHT_RATES[2] * expand_back) * (
        1.0 - WEIGHT_RATES[2] * DECAY_RATE
    )
    shrink_updated = (shrink_weight - WEIGHT_RATES[3] * shrink_back) * (
        1.0 - WEIGHT_RATES[3] * DECAY_RATE
    )
    gains_updated = norm_gains - GAINS_RATE * gains_direction
    return (
        mixed,
        token_gradient,
        triple_gradient,
        output_gradient,
        expand_gradient,
        shrink_gradient,
        gains_gradient,
        triple_average,
        triple_variance,
        triple_updated,
        triple_updated.astype(jnp.bfloat16),
        output_average,
        output_variance,
        output_updated,
        output_updated.astype(jnp.bfloat16),
        expand_average,
        expand_variance,
        expand_updated,
        expand_updated.astype(jnp.bfloat16),
        shrink_average,
        shrink_variance,
        shrink_updated,
        shrink_updated.astype(jnp.bfloat16),
        gains_average,
        gains_variance,
        gains_updated,
    )


def solution(mesh):
    in_specs = (
        P(("outer", "core"), "seq", None),
        P(("outer", "core"), "seq", None),
        P(("outer", "core")),
        P("seq", ("outer", "core")),
        P("seq", ("outer", "core")),
        P("seq", ("outer", "core")),
        P(("outer", "core"), "seq"),
        P(),
        P(None, "seq", None),
        P(("outer", "core"), None),
        P("seq", ("outer", "core")),
        P("seq", ("outer", "core")),
        P("seq", ("outer", "core")),
        P("seq", ("outer", "core")),
        P("seq", ("outer", "core")),
        P("seq", ("outer", "core")),
        P(("outer", "core"), "seq"),
        P(("outer", "core"), "seq"),
        P(),
        P(),
    )
    out_specs = (
        P(("outer", "core"), "seq", None),
        P(("outer", "core"), "seq", None),
        P("seq", ("outer", "core")),
        P("seq", ("outer", "core")),
        P("seq", ("outer", "core")),
        P(("outer", "core"), "seq"),
        P(),
        P("seq", ("outer", "core")),
        P("seq", ("outer", "core")),
        P("seq", ("outer", "core")),
        P("seq", ("outer", "core")),
        P("seq", ("outer", "core")),
        P("seq", ("outer", "core")),
        P("seq", ("outer", "core")),
        P("seq", ("outer", "core")),
        P("seq", ("outer", "core")),
        P("seq", ("outer", "core")),
        P("seq", ("outer", "core")),
        P("seq", ("outer", "core")),
        P(("outer", "core"), "seq"),
        P(("outer", "core"), "seq"),
        P(("outer", "core"), "seq"),
        P(("outer", "core"), "seq"),
        P(),
        P(),
        P(),
    )
    groups = mesh.shape["fsdp"]
    devices = mesh.devices.reshape(mesh.shape["seq"], groups // 2, 2)
    split = Mesh(devices, ("seq", "outer", "core"))
    return jax.shard_map(body, mesh=split, in_specs=in_specs, out_specs=out_specs, check_vma=False)
```

```python
import functools
import math

import jax
import jax.numpy as jnp
from jax import lax
from jax.experimental import pallas as pl
from jax.experimental.pallas import tpu as pltpu
from jax.sharding import Mesh
from jax.sharding import PartitionSpec as P

HEADS = 16
HEAD_DIM = 64
FF = 2624
STEP = 10


ROPE_BASE = 160000.0
NORM_EPS = 1e-05
NEG_LARGE = -1e30
BETA_ONE = 0.95
BETA_TWO = 0.95
ADAM_EPS = 1e-08
DECAY_RATE = 0.01
WEIGHT_RATES = (0.03, 1.0, 0.03, 0.03)
GAINS_RATE = 0.8


def layer_norm(values, gain):
    centre = values - jnp.mean(values, axis=-1, keepdims=True)
    spread = jnp.mean(centre * centre, axis=-1, keepdims=True)
    return centre * lax.rsqrt(spread + NORM_EPS) * gain


def rotary_tables(position):
    halves = HEAD_DIM // 2
    frequency = ROPE_BASE ** (-2.0 * jnp.arange(halves, dtype=jnp.float32) / HEAD_DIM)
    angle = frequency[:, None] * position.astype(jnp.float32)[None, :]
    return jnp.cos(angle), jnp.sin(angle)


def outer_sum(left, right):
    return lax.dot_general(
        left, right, (((0,), (0,)), ((), ())), preferred_element_type=jnp.float32
    )


def back_product(left, right):
    return lax.dot_general(
        left, right, (((1,), (1,)), ((), ())), preferred_element_type=jnp.float32
    )


def plain_product(left, right):
    return jnp.dot(left, right, preferred_element_type=jnp.float32)


NT = (((1,), (1,)), ((), ()))
SAFE_BOUND = 60.0
MASK = -1e30
VMEM_LIMIT = 60 * 1024 * 1024


def extra_rows(rows, length, size=HEAD_DIM):
    place = lax.broadcasted_iota(jnp.int32, (size, length), 0)
    block = jnp.zeros((size, length), jnp.float32)
    for index, row in enumerate(rows):
        block = jnp.where(place == index, row, block)
    return block.astype(jnp.bfloat16)


def three_parts(row):
    high = row.astype(jnp.bfloat16).astype(jnp.float32)
    middle = (row - high).astype(jnp.bfloat16).astype(jnp.float32)
    return [high, middle, row - high - middle]


def mask_row(start, length, limit):
    place = start + lax.broadcasted_iota(jnp.int32, (1, length), 1)
    return jnp.where(place < limit, 0.0, MASK)


def project_kernel(pieces_ref, first_ref, cosine_ref, sine_ref, out_ref, rows_ref, *, group):
    shards, groups, size, _ = pieces_ref.shape
    cosine, sine = cosine_ref[...], sine_ref[...]
    half = HEAD_DIM // 2

    def chunk(part, head):
        start = (part * shards + head) * HEAD_DIM
        place = slice(start % size, start % size + HEAD_DIM)
        return jnp.concatenate(
            [pieces_ref[shard, start // size, place, :] for shard in range(shards)], axis=1
        )

    for begin in range(0, shards, group):
        heads = range(begin, begin + group)
        weight = jnp.concatenate([chunk(part, head) for head in heads for part in range(3)], axis=0)
        product = lax.dot_general(weight, first_ref[...], NT, preferred_element_type=jnp.float32)
        for index, head in enumerate(heads):
            for part in range(3):
                base = (3 * index + part) * HEAD_DIM
                rows_ref[head, part] = weight[base : base + HEAD_DIM]
            for part, scale in ((0, HEAD_DIM**-0.5), (1, 1.0)):
                base = (3 * index + part) * HEAD_DIM
                upper, lower = product[base : base + half], product[base + half : base + HEAD_DIM]
                turned_upper = (upper * cosine - lower * sine).astype(jnp.bfloat16)
                turned_lower = (lower * cosine + upper * sine).astype(jnp.bfloat16)
                place = part * HEAD_DIM
                scale = jnp.bfloat16(scale)
                out_ref[head, place : place + half, :] = turned_upper * scale
                out_ref[head, place + half : place + HEAD_DIM, :] = turned_lower * scale
            base = (3 * index + 2) * HEAD_DIM
            out_ref[head, 2 * HEAD_DIM :, :] = product[base : base + HEAD_DIM].astype(jnp.bfloat16)


def project_heads(pieces, first, cosine, sine):
    shards, groups, size, lanes = pieces.shape
    count, width = first.shape
    half = HEAD_DIM // 2
    whole = lambda *shape: pl.BlockSpec(shape, lambda i: (0,) * len(shape))
    return pl.pallas_call(
        functools.partial(project_kernel, group=min(4, shards)),
        grid=(1,),
        in_specs=[
            whole(shards, groups, size, lanes),
            whole(count, width),
            whole(half, count),
            whole(half, count),
        ],
        out_specs=[whole(shards, 3 * HEAD_DIM, count), whole(shards, 3, HEAD_DIM, width)],
        out_shape=[
            jax.ShapeDtypeStruct((shards, 3 * HEAD_DIM, count), jnp.bfloat16),
            jax.ShapeDtypeStruct((shards, 3, HEAD_DIM, width), jnp.bfloat16),
        ],
        compiler_params=pltpu.CompilerParams(vmem_limit_bytes=VMEM_LIMIT),
        cost_estimate=pl.CostEstimate(
            flops=6 * width * shards * HEAD_DIM * count,
            bytes_accessed=20 * width * shards * HEAD_DIM,
            transcendentals=0,
        ),
    )(pieces, first, cosine, sine)


def forward_kernel(length_ref, joint_ref, out_ref, log_ref, key_ref, value_ref, peak_ref, bound_ref):
    index = pl.program_id(0)
    shards, _, local = joint_ref.shape
    limit = length_ref[0]
    ratio = max(1, 2048 // local)
    blocks = (limit + local - 1) // local

    @pl.when(index == 0)
    def prepare():
        query_most = jnp.zeros((1, 1), jnp.float32)
        key_most = jnp.zeros((1, 1), jnp.float32)
        for shard in range(shards):
            place = slice(shard * local, (shard + 1) * local)
            query = joint_ref[shard, :HEAD_DIM, :].astype(jnp.float32)
            key = joint_ref[shard, HEAD_DIM : 2 * HEAD_DIM, :]
            wide_key = key.astype(jnp.float32)
            query_size = jnp.sum(query * query, axis=0, keepdims=True)
            key_size = jnp.sum(wide_key * wide_key, axis=0, keepdims=True)
            query_most = jnp.maximum(query_most, jnp.max(query_size, axis=1, keepdims=True))
            key_most = jnp.maximum(key_most, jnp.max(key_size, axis=1, keepdims=True))
            extra = extra_rows([mask_row(shard * local, local, limit), 1.0], local)
            key_ref[place, :] = jnp.concatenate([key, extra], axis=0).T
            value_ref[:HEAD_DIM, place] = joint_ref[shard, 2 * HEAD_DIM :, :]
            value_ref[HEAD_DIM:, place] = extra_rows([1.0], local, 16)
        bound_ref[0] = (jnp.sqrt(query_most) * jnp.sqrt(key_most))[0, 0]

    @pl.when(index >= blocks)
    def padding():
        out_ref[...] = jnp.zeros_like(out_ref)
        log_ref[...] = jnp.zeros_like(log_ref)

    @pl.when(index < blocks)
    def compute():
        query = joint_ref[index, :HEAD_DIM, :]
        peak_ref[...] = jnp.zeros_like(peak_ref)

        @pl.when(bound_ref[0] > SAFE_BOUND)
        def find_peak():
            plain = jnp.concatenate([query, extra_rows([1.0], local)], axis=0)

            def step(block, peak):
                place = pl.ds(pl.multiple_of(block * local, local), local)
                scores = jnp.dot(key_ref[place, :], plain, preferred_element_type=jnp.float32)
                return jnp.maximum(peak, jnp.max(scores, axis=0, keepdims=True))

            peak = lax.fori_loop(0, blocks, step, jnp.full((1, local), MASK, jnp.float32))
            peak_ref[...] = peak.astype(jnp.bfloat16).astype(jnp.float32)

        peak = peak_ref[...]
        augmented = jnp.concatenate([query, extra_rows([1.0, -peak], local)], axis=0)

        def attend(start, size, total):
            place = pl.ds(pl.multiple_of(start, local), size)
            scores = jnp.dot(key_ref[place, :], augmented, preferred_element_type=jnp.float32)
            weights = jnp.exp(scores).astype(jnp.bfloat16)
            return total + jnp.dot(
                value_ref[:, place], weights, preferred_element_type=jnp.float32
            )

        large = blocks // ratio
        total = lax.fori_loop(
            0,
            large,
            lambda block, total: attend(block * (ratio * local), ratio * local, total),
            jnp.zeros((HEAD_DIM + 16, local), jnp.float32),
        )
        total = lax.fori_loop(
            large * ratio, blocks, lambda block, total: attend(block * local, local, total), total
        )
        mass = total[HEAD_DIM : HEAD_DIM + 1, :]
        out_ref[0] = (total[:HEAD_DIM, :] / mass).astype(jnp.bfloat16)
        log_ref[0] = peak + jnp.log(mass)


def attend_forward(length, joint):
    shards, _, local = joint.shape
    total = shards * local
    return pl.pallas_call(
        forward_kernel,
        grid=(shards,),
        in_specs=[
            pl.BlockSpec(memory_space=pltpu.SMEM),
            pl.BlockSpec((shards, 3 * HEAD_DIM, local), lambda i: (0, 0, 0)),
        ],
        out_specs=[
            pl.BlockSpec((1, HEAD_DIM, local), lambda i: (i, 0, 0)),
            pl.BlockSpec((1, 1, local), lambda i: (i, 0, 0)),
        ],
        out_shape=[
            jax.ShapeDtypeStruct((shards, HEAD_DIM, local), jnp.bfloat16),
            jax.ShapeDtypeStruct((shards, 1, local), jnp.float32),
        ],
        scratch_shapes=[
            pltpu.VMEM((total, 2 * HEAD_DIM), jnp.bfloat16),
            pltpu.VMEM((HEAD_DIM + 16, total), jnp.bfloat16),
            pltpu.VMEM((1, local), jnp.float32),
            pltpu.SMEM((1,), jnp.float32),
        ],
        compiler_params=pltpu.CompilerParams(vmem_limit_bytes=VMEM_LIMIT),
        cost_estimate=pl.CostEstimate(
            flops=total * total,
            bytes_accessed=HEAD_DIM * total,
            transcendentals=0,
        ),
    )(length, joint)


def backward_kernel(
    length_ref,
    joint_ref,
    back_ref,
    out_ref,
    log_ref,
    cosine_ref,
    sine_ref,
    grad_ref,
    query_ref,
    wide_ref,
    query_flat,
    back_flat,
    query_sum,
):
    index = pl.program_id(0)
    shards, _, local = joint_ref.shape
    limit = length_ref[0]
    ratio = max(1, 2048 // local)
    blocks = (limit + local - 1) // local
    half = HEAD_DIM // 2

    def turned_back(wide, shard):
        cosine, sine = cosine_ref[shard], sine_ref[shard]
        upper, lower = wide[:half], wide[half:]
        return jnp.concatenate(
            [upper * cosine + lower * sine, lower * cosine - upper * sine], axis=0
        ).astype(jnp.bfloat16)

    @pl.when(index == 0)
    def prepare():
        for shard in range(shards):
            place = slice(shard * local, (shard + 1) * local)
            query = joint_ref[shard, :HEAD_DIM, :]
            back = back_ref[shard]
            extra = extra_rows([1.0] + three_parts(-log_ref[shard]), local)
            query_ref[place, :] = jnp.concatenate([query, extra], axis=0).T
            balance = jnp.sum(
                back.astype(jnp.float32) * out_ref[shard].astype(jnp.float32),
                axis=0,
                keepdims=True,
            )
            extra = extra_rows(three_parts(-balance), local)
            wide_ref[place, :] = jnp.concatenate([back, extra], axis=0).T
            query_flat[:, place] = query
            back_flat[:, place] = back
        query_sum[...] = jnp.zeros_like(query_sum)

    @pl.when(index >= blocks)
    def padding():
        grad_ref[index, HEAD_DIM:, :] = jnp.zeros((2 * HEAD_DIM, local), jnp.bfloat16)

    @pl.when(index < blocks)
    def compute():
        key = joint_ref[index, HEAD_DIM : 2 * HEAD_DIM, :]
        value = joint_ref[index, 2 * HEAD_DIM :, :]
        mask = mask_row(index * local, local, limit)
        wide_key = jnp.concatenate([key, extra_rows([mask, 1.0, 1.0, 1.0], local)], axis=0)
        wide_value = jnp.concatenate([value, extra_rows([1.0, 1.0, 1.0], local)], axis=0)

        def gather(start, size, carry):
            key_sum, value_sum = carry
            place = pl.ds(pl.multiple_of(start, local), size)
            scores = jnp.dot(query_ref[place, :], wide_key, preferred_element_type=jnp.float32)
            chance = jnp.exp(scores)
            change = jnp.dot(wide_ref[place, :], wide_value, preferred_element_type=jnp.float32)
            chance_low = chance.astype(jnp.bfloat16)
            score_back = (chance * change).astype(jnp.bfloat16)
            value_sum = value_sum + jnp.dot(
                back_flat[:, place], chance_low, preferred_element_type=jnp.float32
            )
            key_sum = key_sum + jnp.dot(
                query_flat[:, place], score_back, preferred_element_type=jnp.float32
            )
            query_sum[:, place] += lax.dot_general(
                key, score_back, NT, preferred_element_type=jnp.float32
            )
            return (key_sum, value_sum)

        large = blocks // ratio
        zero = jnp.zeros((HEAD_DIM, local), jnp.float32)
        carry = lax.fori_loop(
            0,
            large,
            lambda block, carry: gather(block * (ratio * local), ratio * local, carry),
            (zero, zero),
        )
        key_sum, value_sum = lax.fori_loop(
            large * ratio, blocks, lambda block, carry: gather(block * local, local, carry), carry
        )
        grad_ref[index, HEAD_DIM : 2 * HEAD_DIM, :] = turned_back(key_sum, index)
        grad_ref[index, 2 * HEAD_DIM :, :] = value_sum.astype(jnp.bfloat16)

    @pl.when(index == shards - 1)
    def finish():
        for shard in range(shards):
            place = slice(shard * local, (shard + 1) * local)
            grad_ref[shard, :HEAD_DIM, :] = turned_back(
                query_sum[:, place] * HEAD_DIM**-0.5, shard
            )


def attend_backward(length, joint, back, attend, log_mass, cosine, sine):
    shards, _, local = joint.shape
    total = shards * local
    whole = lambda rows: pl.BlockSpec((shards, rows, local), lambda i: (0, 0, 0))
    return pl.pallas_call(
        backward_kernel,
        grid=(shards,),
        in_specs=[
            pl.BlockSpec(memory_space=pltpu.SMEM),
            whole(3 * HEAD_DIM),
            whole(HEAD_DIM),
            whole(HEAD_DIM),
            whole(1),
            whole(HEAD_DIM // 2),
            whole(HEAD_DIM // 2),
        ],
        out_specs=whole(3 * HEAD_DIM),
        out_shape=jax.ShapeDtypeStruct((shards, 3 * HEAD_DIM, local), jnp.bfloat16),
        scratch_shapes=[
            pltpu.VMEM((total, 2 * HEAD_DIM), jnp.bfloat16),
            pltpu.VMEM((total, 2 * HEAD_DIM), jnp.bfloat16),
            pltpu.VMEM((HEAD_DIM, total), jnp.bfloat16),
            pltpu.VMEM((HEAD_DIM, total), jnp.bfloat16),
            pltpu.VMEM((HEAD_DIM, total), jnp.float32),
        ],
        compiler_params=pltpu.CompilerParams(vmem_limit_bytes=VMEM_LIMIT),
        cost_estimate=pl.CostEstimate(
            flops=total * total,
            bytes_accessed=HEAD_DIM * total,
            transcendentals=0,
        ),
    )(length, joint, back, attend, log_mass, cosine, sine)


TN = (((0,), (0,)), ((), ()))
PLAIN = (((1,), (0,)), ((), ()))
LANES = 128
GROUPS = 4
RUNS = 8
UNITS = FF // GROUPS
EXPAND_RUN = -(-2 * UNITS // (16 * RUNS)) * 16
SHRINK_RUN = -(-UNITS // (16 * RUNS)) * 16


def run_segments(start, stop, run):
    segments = []
    while start < stop:
        index = start // run
        end = min(stop, (index + 1) * run)
        segments.append((index, start - index * run, start, end - start))
        start = end
    return segments


def feed_kernel(
    second_ref,
    upstream_ref,
    active_ref,
    gate_ref,
    shrink_ref,
    shrunk_ref,
    second_back_ref,
    parts_ref,
    grads_ref,
    zero_ref,
    send_ref,
    zero_send_ref,
):
    index = pl.program_id(0)

    def joined(ref):
        return jnp.concatenate([ref[piece, 0] for piece in range(ref.shape[0])], axis=1)

    def product(left, right, dims):
        return lax.dot_general(left, right, dims, preferred_element_type=jnp.float32)

    def grad_copies(half, pair):
        moves = []
        for kind, member in ((0, pair), (1, pair + 2)):
            for run, place, offset, size in run_segments(
                half * UNITS, (half + 1) * UNITS, EXPAND_RUN
            ):
                moves.append((kind, offset - half * UNITS, run, member, place, size))
        for run, place, offset, size in run_segments(0, UNITS, SHRINK_RUN):
            moves.append((2, offset, run, 2 * pair + half, EXPAND_RUN + place, size))
        return [
            pltpu.make_async_copy(
                grads_ref.at[half, kind, pl.ds(offset, size), :],
                parts_ref.at[run, member, pl.ds(place, size), :],
                send_ref.at[half, number],
            )
            for number, (kind, offset, run, member, place, size) in enumerate(moves)
        ]

    def zero_copies():
        moves = []
        for member in range(GROUPS):
            for base, run_size, total in ((0, EXPAND_RUN, 2 * UNITS), (EXPAND_RUN, SHRINK_RUN, UNITS)):
                for run, place, _, size in run_segments(total, RUNS * run_size, run_size):
                    moves.append((run, member, base + place, size))
        return [
            pltpu.make_async_copy(
                zero_ref.at[pl.ds(0, size), :],
                parts_ref.at[run, member, pl.ds(place, size), :],
                zero_send_ref.at[number],
            )
            for number, (run, member, place, size) in enumerate(moves)
        ]

    @pl.when(index == 0)
    def fill():
        zero_ref[...] = jnp.zeros_like(zero_ref)
        for copy in zero_copies():
            copy.start()

    active, gate, shrink = joined(active_ref), joined(gate_ref), joined(shrink_ref)
    second, upstream = second_ref[...], upstream_ref[...]
    input_active = product(second, active, NT)
    input_gate = product(second, gate, NT)
    hidden_back = product(upstream, shrink, NT)
    below = 0.5 + 0.5 * lax.erf(input_active * 0.5**0.5)
    bell = jnp.exp(-0.5 * input_active * input_active) * (0.5 / math.pi) ** 0.5
    curve = input_active * below
    hidden = (curve * input_gate).astype(jnp.bfloat16)
    active_back = (hidden_back * input_gate * (below + input_active * bell)).astype(jnp.bfloat16)
    gate_back = (hidden_back * curve).astype(jnp.bfloat16)
    shrunk = product(hidden, shrink, PLAIN)
    second_back = product(active_back, active, PLAIN) + product(gate_back, gate, PLAIN)

    @pl.when(index == 0)
    def begin():
        shrunk_ref[...] = shrunk
        second_back_ref[...] = second_back

    @pl.when(index > 0)
    def add():
        shrunk_ref[...] += shrunk
        second_back_ref[...] += second_back

    for half in range(2):

        @pl.when(index % 2 == half)
        def send(half=half):
            pair = index // 2

            @pl.when(index >= 2)
            def free():
                for copy in grad_copies(half, pair - 1):
                    copy.wait()

            grads_ref[half, 0] = product(active_back, second, TN).astype(jnp.bfloat16)
            grads_ref[half, 1] = product(gate_back, second, TN).astype(jnp.bfloat16)
            grads_ref[half, 2] = product(hidden, upstream, TN).astype(jnp.bfloat16)
            for copy in grad_copies(half, pair):
                copy.start()

    @pl.when(index == GROUPS - 1)
    def drain():
        for half in range(2):
            for copy in grad_copies(half, 1):
                copy.wait()
        for copy in zero_copies():
            copy.wait()


def feed_forward(second, upstream, pieces):
    count, width = second.shape
    block = (RUNS, 1, UNITS, LANES)
    held = pl.BlockSpec((count, width), lambda i: (0, 0), pipeline_mode=pl.Buffered(1))
    wide = jax.ShapeDtypeStruct((count, width), jnp.float32)
    run = EXPAND_RUN + SHRINK_RUN
    copies = max(
        2 * len(run_segments(half * UNITS, (half + 1) * UNITS, EXPAND_RUN)) for half in range(2)
    ) + len(run_segments(0, UNITS, SHRINK_RUN))
    return pl.pallas_call(
        feed_kernel,
        grid=(GROUPS,),
        in_specs=[
            held,
            held,
            pl.BlockSpec(block, lambda i: (0, i // 2, i % 2, 0)),
            pl.BlockSpec(block, lambda i: (0, i // 2 + 2, i % 2, 0)),
            pl.BlockSpec(block, lambda i: (0, i, 2, 0)),
        ],
        out_specs=[held, held, pl.BlockSpec(memory_space=pl.ANY)],
        out_shape=[wide, wide, jax.ShapeDtypeStruct((RUNS, GROUPS, run, width), jnp.bfloat16)],
        scratch_shapes=[
            pltpu.VMEM((2, 3, UNITS, width), jnp.bfloat16),
            pltpu.VMEM((max(EXPAND_RUN, SHRINK_RUN), width), jnp.bfloat16),
            pltpu.SemaphoreType.DMA((2, copies)),
            pltpu.SemaphoreType.DMA((GROUPS * 8,)),
        ],
        compiler_params=pltpu.CompilerParams(vmem_limit_bytes=VMEM_LIMIT),
        cost_estimate=pl.CostEstimate(
            flops=count * width,
            bytes_accessed=count * width,
            transcendentals=0,
        ),
    )(second, upstream, pieces, pieces, pieces)


def enter_kernel(*refs):
    phases = (len(refs) - 9) // 2
    attend_refs, weight_refs = refs[:phases], refs[phases : 2 * phases]
    limit_ref, token_ref, cotangent_ref, gain_ref = refs[2 * phases : 2 * phases + 4]
    middle_ref, normal_ref, second_ref, upstream_ref, spread_ref = refs[2 * phases + 4 :]
    middle = token_ref[...].astype(jnp.float32)
    for attend_ref, weight_ref in zip(attend_refs, weight_refs):
        middle += lax.dot_general(
            attend_ref[...], weight_ref[...], TN, preferred_element_type=jnp.float32
        )
    block = middle.shape[0]
    centre = middle - jnp.mean(middle, axis=1, keepdims=True)
    scale = lax.rsqrt(jnp.mean(centre * centre, axis=1, keepdims=True) + NORM_EPS)
    normal = centre * scale
    place = pl.program_id(0) * block + lax.broadcasted_iota(jnp.int32, (block, 1), 0)
    middle_ref[...] = middle
    normal_ref[...] = normal
    spread_ref[...] = scale
    second_ref[...] = (normal * gain_ref[1:2, :]).astype(jnp.bfloat16)
    upstream_ref[...] = jnp.where(place < limit_ref[0], cotangent_ref[...], jnp.bfloat16(0.0))


def enter_feed(attends, weights, limit, tokens, cotangent, gains):
    count, width = tokens.shape
    block = min(256, count)
    rows = pl.BlockSpec((block, width), lambda i: (i, 0))
    wide = jax.ShapeDtypeStruct((count, width), jnp.float32)
    low = jax.ShapeDtypeStruct((count, width), jnp.bfloat16)
    return pl.pallas_call(
        enter_kernel,
        grid=(count // block,),
        in_specs=[pl.BlockSpec((attend.shape[0], block), lambda i: (0, i)) for attend in attends]
        + [pl.BlockSpec(weight.shape, lambda i: (0, 0)) for weight in weights]
        + [pl.BlockSpec(memory_space=pltpu.SMEM), rows, rows]
        + [pl.BlockSpec(gains.shape, lambda i: (0, 0))],
        out_specs=[rows, rows, rows, rows, pl.BlockSpec((block, 1), lambda i: (i, 0))],
        out_shape=[wide, wide, low, low, jax.ShapeDtypeStruct((count, 1), jnp.float32)],
        compiler_params=pltpu.CompilerParams(vmem_limit_bytes=VMEM_LIMIT),
        cost_estimate=pl.CostEstimate(
            flops=2 * count * width * width, bytes_accessed=20 * count * width, transcendentals=0
        ),
    )(*attends, *weights, limit, tokens, cotangent, gains)


def leave_kernel(*refs):
    phases = (len(refs) - 12) // 2
    weight_refs, back_refs = refs[:phases], refs[-phases:]
    limit_ref, shrunk_ref, change_ref, middle_ref, normal_ref, spread_ref = refs[phases : phases + 6]
    upstream_ref, gain_ref = refs[phases + 6 : phases + 8]
    mixed_ref, middle_back_ref, branch_ref, gain_grad_ref = refs[phases + 8 : phases + 12]
    index = pl.program_id(0)
    block = mixed_ref.shape[0]
    place = index * block + lax.broadcasted_iota(jnp.int32, (block, 1), 0)
    mixed = middle_ref[...] + shrunk_ref[...]
    mixed_ref[...] = jnp.where(place < limit_ref[0], mixed, 0.0).astype(jnp.bfloat16)
    change, normal = change_ref[...], normal_ref[...]
    gain_grad = jnp.sum(change * normal, axis=0, keepdims=True)

    @pl.when(index == 0)
    def begin():
        gain_grad_ref[...] = gain_grad

    @pl.when(index > 0)
    def add():
        gain_grad_ref[...] += gain_grad

    inner = change * gain_ref[1:2, :]
    inner = (
        inner
        - jnp.mean(inner, axis=1, keepdims=True)
        - normal * jnp.mean(inner * normal, axis=1, keepdims=True)
    )
    middle_back = upstream_ref[...].astype(jnp.float32) + spread_ref[...] * inner
    branch = middle_back.astype(jnp.bfloat16)
    middle_back_ref[...] = middle_back
    branch_ref[...] = branch
    for weight_ref, back_ref in zip(weight_refs, back_refs):
        back_ref[...] = lax.dot_general(
            weight_ref[...], branch, NT, preferred_element_type=jnp.float32
        ).astype(jnp.bfloat16)


def leave_feed(weights, limit, shrunk, change, middle, normal, spread, upstream, gains):
    count, width = shrunk.shape
    block = min(256, count)
    rows = pl.BlockSpec((block, width), lambda i: (i, 0))
    wide = jax.ShapeDtypeStruct((count, width), jnp.float32)
    low = jax.ShapeDtypeStruct((count, width), jnp.bfloat16)
    return pl.pallas_call(
        leave_kernel,
        grid=(count // block,),
        in_specs=[pl.BlockSpec(weight.shape, lambda i: (0, 0)) for weight in weights]
        + [pl.BlockSpec(memory_space=pltpu.SMEM), rows, rows, rows, rows]
        + [pl.BlockSpec((block, 1), lambda i: (i, 0)), rows]
        + [pl.BlockSpec(gains.shape, lambda i: (0, 0))],
        out_specs=[rows, rows, rows, pl.BlockSpec((1, width), lambda i: (0, 0))]
        + [pl.BlockSpec((weight.shape[0], block), lambda i: (0, i)) for weight in weights],
        out_shape=[low, wide, low, jax.ShapeDtypeStruct((1, width), jnp.float32)]
        + [jax.ShapeDtypeStruct((weight.shape[0], count), jnp.bfloat16) for weight in weights],
        compiler_params=pltpu.CompilerParams(vmem_limit_bytes=VMEM_LIMIT),
        cost_estimate=pl.CostEstimate(
            flops=2 * count * width * width, bytes_accessed=28 * count * width, transcendentals=0
        ),
    )(*weights, limit, shrunk, change, middle, normal, spread, upstream, gains)


def adam_step(rotated, first, second):
    average = BETA_ONE * first + (1.0 - BETA_ONE) * rotated
    variance = BETA_TWO * second + (1.0 - BETA_TWO) * rotated * rotated
    direction = (
        average / (1.0 - BETA_ONE**STEP) / (jnp.sqrt(variance / (1.0 - BETA_TWO**STEP)) + ADAM_EPS)
    )
    return (average, variance, direction)


def body(
    tokens,
    cotangent,
    lengths,
    triple_weight,
    output_weight,
    expand_weight,
    shrink_weight,
    norm_gains,
    side_bases,
    output_right,
    triple_first,
    triple_second,
    output_first,
    output_second,
    expand_first,
    expand_second,
    shrink_first,
    shrink_second,
    gains_first,
    gains_second,
):
    rows_here, local_len, width = tokens.shape
    count = rows_here * local_len
    shards = lax.axis_size("seq")
    groups = lax.axis_size("outer") * lax.axis_size("core")
    split = HEADS // shards
    core = lax.axis_index("core")
    swap = functools.partial(lax.ppermute, axis_name="core", perm=[(0, 1), (1, 0)])
    other_lengths = swap(lengths)
    ahead = (lengths > other_lengths) | ((lengths == other_lengths) & (core == 0))

    def by_length(own, other):
        return [jnp.where(ahead[0], own, other), jnp.where(ahead[0], other, own)]

    def by_core(mine, other):
        return [jnp.where(core == 0, mine, other), jnp.where(core == 0, other, mine)]

    def both_rows(own):
        return by_length(own, swap(own)) if split == 2 else [own]

    piece = width // shards
    fsdp = ("outer", "core")
    everyone = ("seq",) + fsdp
    offset = lax.axis_index("seq") * local_len
    position = offset + jnp.arange(local_len, dtype=jnp.int32)
    cosine, sine = rotary_tables(position)
    every = jnp.arange(shards * local_len, dtype=jnp.int32)
    all_cosine, all_sine = (
        table.reshape(HEAD_DIM // 2, shards, local_len).transpose(1, 0, 2)
        for table in rotary_tables(every)
    )
    valid = (position[None, :] < lengths[:, None]).astype(jnp.float32).reshape(count, 1)
    exchange = functools.partial(lax.all_to_all, axis_name="seq", split_axis=0, concat_axis=0)

    def tied(*values):
        return lax.optimization_barrier(values)

    def gathered(shard):
        flat = lax.all_gather(shard, everyone, axis=0, tiled=False)
        return flat.reshape((shards, groups) + shard.shape)

    triple_shards = (
        triple_weight.T.astype(jnp.bfloat16)
        .reshape(-1, split, HEAD_DIM, piece)
        .transpose(1, 0, 2, 3)
        .reshape(split, -1, piece)
    )
    if split == 2:
        mine = lax.dynamic_index_in_dim(triple_shards, core, 0, keepdims=False)
        other = lax.dynamic_index_in_dim(triple_shards, 1 - core, 0, keepdims=False)
        triple_shards = jnp.stack(by_core(mine, swap(other)))
        triple_pieces = lax.all_gather(triple_shards, ("seq", "outer"), axis=0, tiled=False)
    else:
        triple_pieces = gathered(triple_shards[0])
    triple_pieces = triple_pieces.reshape(shards, groups, -1, piece)
    all_cosine, all_sine, triple_pieces = tied(all_cosine, all_sine, triple_pieces)
    output_columns = width // groups
    lanes = min(piece, output_columns)

    def fold(block):
        rows = block.shape[0]
        return block.reshape(rows, -1, lanes).transpose(1, 0, 2).reshape(-1, lanes)

    bases_low = side_bases.astype(jnp.bfloat16)
    right_low = output_right.astype(jnp.bfloat16)
    member = lax.axis_index("outer") * lax.axis_size("core") + lax.axis_index("core")
    base_rows = piece // groups
    flat = tokens.reshape(count, width).astype(jnp.float32)
    first_normed, first_back = jax.vjp(layer_norm, flat, norm_gains[0])
    first_low = first_normed.astype(jnp.bfloat16)
    other_shards = jnp.concatenate(
        [
            expand_weight.T.astype(jnp.bfloat16),
            shrink_weight.astype(jnp.bfloat16),
            fold(output_weight.astype(jnp.bfloat16)),
        ],
        axis=0,
    )
    firsts = both_rows(first_low)
    projected = [project_heads(triple_pieces, first, cosine, sine) for first in firsts]
    triple_rows = projected[0][1].reshape(-1, width)
    joints = [exchange(joint) for joint, _ in projected]
    other_shards, joints[0] = tied(other_shards, joints[0])
    other_pieces = gathered(other_shards)
    chosen = jnp.stack([bases_low[0], bases_low[2], bases_low[3]])
    chosen = lax.dynamic_slice_in_dim(chosen, member * base_rows, base_rows, 1)
    expand_rows = 2 * FF // groups
    shrink_rows = FF // groups
    output_pieces = other_pieces[:, :, expand_rows + shrink_rows :].reshape(
        shards, groups, output_columns // lanes, split, HEAD_DIM, lanes
    )
    output_rows = [
        output_pieces[:, :, :, head].transpose(0, 3, 1, 2, 4).reshape(shards * HEAD_DIM, width)
        for head in range(split)
    ]
    canonical = (shards, groups, piece) == (RUNS, GROUPS, LANES)
    if canonical:
        feed_pieces = other_pieces
    else:
        feed_pieces = [
            other_pieces[:, :, start:end]
            .transpose(1, 2, 0, 3)
            .reshape(GROUPS, -1, RUNS, LANES)
            .transpose(2, 0, 1, 3)
            for start, end in ((0, expand_rows), (expand_rows, expand_rows + shrink_rows))
        ]
        feed_pieces = jnp.concatenate(feed_pieces, axis=2)
    row_lengths = both_rows(lengths)
    forwards, attends = [], []
    for row, joint in enumerate(joints):
        outcome = attend_forward(row_lengths[row], joint)
        if row:
            attends[-1], outcome = tied(attends[-1], outcome)
        if row < split - 1:
            joints[row + 1], outcome = tied(joints[row + 1], outcome)
        forwards.append(outcome)
        attends.append(exchange(outcome[0]))
    chosen, forwards[-1] = tied(chosen, forwards[-1])
    bases_full = gathered(chosen)
    attends = [attend.reshape(shards * HEAD_DIM, count) for attend in attends]
    if split == 2:
        own, other = by_length(*attends)
        attends = by_core(own, swap(other))
    expand_height = -(-expand_rows // (16 * shards)) * 16
    shrink_height = -(-shrink_rows // (16 * shards)) * 16

    def to_rows(block):
        block = exchange(block)
        return block.transpose(1, 0, 2).reshape(block.shape[1], -1)

    def padded(block, height):
        block = jnp.pad(block, ((0, height * shards - block.shape[0]), (0, 0)))
        return block.reshape(shards, height, piece)

    def by_heads(block):
        return (
            block.reshape(-1, split, HEAD_DIM, piece)
            .transpose(1, 0, 2, 3)
            .reshape(split, shards, -1, piece)
        )

    def from_heads(blocks):
        block = jnp.stack(blocks).astype(jnp.float32).reshape(split, -1, HEAD_DIM, piece)
        return block.transpose(1, 0, 2, 3).reshape(-1, piece)

    moments = []
    for expand, shrink, triple in (
        (expand_first, shrink_first, triple_first),
        (expand_second, shrink_second, triple_second),
    ):
        moments += [padded(expand.T, expand_height), padded(shrink, shrink_height)]
        moments += list(by_heads(triple.T))
    moments, attends[-1], feed_pieces = tied(moments, attends[-1], feed_pieces)
    heights = [moment.shape[1] for moment in moments]
    moments = to_rows(jnp.concatenate(moments, axis=1))
    edges = [sum(heights[:index]) for index in range(len(heights) + 1)]
    moments = [moments[start:end] for start, end in zip(edges, edges[1:])]
    moments = list(zip(moments[: split + 2], moments[split + 2 :]))
    inside = jnp.clip(lengths - offset, 0, local_len)
    middle, second_normal, second_low, upstream_low, second_spread = enter_feed(
        attends,
        output_rows,
        inside,
        tokens.reshape(count, width),
        cotangent.reshape(count, width),
        norm_gains,
    )
    shrunk, second_change, parts = feed_forward(second_low, upstream_low, feed_pieces)
    moments, bases_full, shrunk, second_change, parts = tied(
        moments, bases_full, shrunk, second_change, parts
    )
    mixed, middle_back, branch_low, second_gain, *backs = leave_feed(
        output_rows,
        inside,
        shrunk,
        second_change,
        middle,
        second_normal,
        second_spread,
        upstream_low,
        norm_gains,
    )
    mixed = mixed.reshape(tokens.shape)
    second_gain = second_gain[0]
    backs = [back.reshape(shards, HEAD_DIM, count) for back in backs]
    if split == 2:
        mine, other = by_core(*backs)
        backs = by_length(mine, swap(other))
    attend_backs = jnp.split(exchange(jnp.concatenate(backs, axis=1)), split, axis=1)

    def halved(blocks, axis, dim):
        size = lax.axis_size(axis)
        place = lax.axis_index(axis)
        while size > 1:
            size //= 2
            shape = blocks.shape
            blocks = blocks.reshape(shape[:dim] + (2, size) + shape[dim + 1 :])
            side = (place // size) % 2
            mine = lax.dynamic_index_in_dim(blocks, side, dim, keepdims=False)
            other = lax.dynamic_index_in_dim(blocks, 1 - side, dim, keepdims=False)
            pairs = [(member, member ^ size) for member in range(lax.axis_size(axis))]
            other = lax.ppermute(other, axis, pairs)
            blocks = (mine.astype(jnp.float32) + other.astype(jnp.float32)).astype(jnp.bfloat16)
        return jnp.squeeze(blocks, dim)

    def doubled(block, axis):
        block = block[None]
        place = lax.axis_index(axis)
        step = 1
        while step < lax.axis_size(axis):
            pairs = [(member, member ^ step) for member in range(lax.axis_size(axis))]
            other = lax.ppermute(block, axis, pairs)
            upper = (place // step) % 2 == 1
            block = jnp.concatenate(
                [jnp.where(upper, other, block), jnp.where(upper, block, other)], axis=0
            )
            step *= 2
        return block

    def near_sum(blocks):
        return halved(halved(blocks, "core", 1), "outer", 0)

    def merged(*blocks):
        sizes = [math.prod(block.shape[1:]) for block in blocks]
        flat = [block.reshape(shards, -1, piece) for block in blocks]
        flat = exchange(jnp.concatenate(flat, axis=1))
        results, start = [], 0
        for block, size in zip(blocks, sizes):
            rows = size // piece
            results.append(flat[:, start : start + rows].reshape(block.shape))
            start += rows
        return results

    def widened(block):
        rows = piece * output_columns // count
        block = block.reshape(-1, piece // rows, rows, output_columns)
        return block.swapaxes(1, 2).reshape(shards, -1, count)

    def narrowed(block):
        rows = piece * output_columns // count
        block = block.reshape(-1, rows, piece // rows, output_columns)
        return block.swapaxes(1, 2).reshape(shards, -1, piece, output_columns)

    def far_sum(terms):
        return jnp.sum(terms.astype(jnp.float32), axis=0).astype(jnp.bfloat16)

    def cut_rows(rows):
        return rows.reshape(rows.shape[0], shards, piece).transpose(1, 0, 2)

    outer = lax.axis_size("outer")
    output_part = jnp.stack(
        [
            jnp.dot(attend, branch_low, preferred_element_type=jnp.float32)
            .astype(jnp.bfloat16)
            .reshape(shards, HEAD_DIM, width)
            for attend in attends
        ],
        axis=1,
    )
    output_terms = halved(
        output_part.reshape(shards, piece, outer, -1, output_columns).transpose(0, 2, 3, 1, 4),
        "core",
        2,
    )
    def cut(product, height):
        block = product.reshape(groups, -1, width)
        block = jnp.pad(block, ((0, 0), (0, height * shards - block.shape[1]), (0, 0)))
        return block.reshape(groups, shards, height, width)

    if not canonical:
        parts = parts.transpose(1, 0, 2, 3)
        parts = [
            cut(block.reshape(GROUPS, -1, width)[:, : size // GROUPS], height)
            for block, size, height in (
                (parts[:, :, :EXPAND_RUN], 2 * FF, expand_height),
                (parts[:, :, EXPAND_RUN:], FF, shrink_height),
            )
        ]
        parts = jnp.concatenate(parts, axis=2).transpose(1, 0, 2, 3)
    parts = parts.reshape(shards * groups, -1, width)
    owned = lax.psum_scatter(parts, everyone, scatter_dimension=0, tiled=False)
    feed_height = expand_height + shrink_height

    def soap_rows(rows, base, moment):
        rotated = plain_product(rows, base)
        direction = adam_step(rotated, *moment)[2]
        step = back_product(direction.astype(jnp.bfloat16), base)
        return rotated.astype(jnp.bfloat16), step.astype(jnp.bfloat16)

    output_terms = widened(output_terms)
    order = list(range(split))[::-1]
    output_terms, attend_backs = tied(output_terms, attend_backs)
    grads = [None] * split
    for step, row in enumerate(order):
        grad = attend_backward(
            row_lengths[row],
            joints[row],
            attend_backs[row],
            *forwards[row],
            all_cosine,
            all_sine,
        )
        if step == split - 1:
            grads, owned, bases_full, grad = tied(grads, owned, bases_full, grad)
        if step == 0:
            grad = jnp.concatenate([grad, output_terms], axis=1)
        grads[row] = exchange(grad)
    output_low = halved(far_sum(narrowed(grads[order[0]][:, 3 * HEAD_DIM :])), "outer", 0)
    joint_backs = [grad[:, : 3 * HEAD_DIM].reshape(-1, count) for grad in grads]
    output_left = outer_sum(bases_low[1], output_low).astype(jnp.bfloat16)
    output_left = output_left.reshape(shards, piece, output_columns)

    def triple_part(row):
        return jnp.dot(joint_backs[row], firsts[row], preferred_element_type=jnp.float32)

    def triple_rest(rows, head):
        return jnp.concatenate([rows, *soap_rows(rows, bases_full[0], moments[2 + head])])

    bases_full = bases_full.transpose(2, 0, 1, 3, 4).reshape(3, width, width)
    feed_rows = jnp.concatenate(
        [
            owned,
            *soap_rows(owned[:expand_height], bases_full[1], moments[0]),
            *soap_rows(owned[expand_height:], bases_full[2], moments[1]),
        ]
    )
    settled = jnp.concatenate(
        [cut_rows(feed_rows), output_left.reshape(shards, -1, piece)], axis=1
    )
    early = [triple_part(row) for row in order[:-1]]
    joint_backs[order[-1]], early, settled = tied(joint_backs[order[-1]], early, settled)
    settled = exchange(settled)
    output_left = settled[:, feed_rows.shape[0] :].reshape(shards, piece, output_columns)
    output_left = far_sum(output_left)
    part = sum(early, triple_part(order[-1])).astype(jnp.bfloat16)
    part = part.reshape(shards, 3, HEAD_DIM, width).swapaxes(0, 1)
    part = part.reshape(outer, groups // outer, shards, -1, width)
    if split == 2:
        part = halved(part, "outer", 0).swapaxes(0, 1)
        rows = far_sum(exchange(part))
        mine = lax.dynamic_index_in_dim(rows, core, 0, keepdims=False)
        other = lax.dynamic_index_in_dim(rows, 1 - core, 0, keepdims=False)
        head_rows = by_core(mine, swap(other))
    else:
        head_rows = [far_sum(exchange(near_sum(part)))]
    triple_done = [triple_rest(rows, head) for head, rows in enumerate(head_rows)]
    output_turned = plain_product(output_left, right_low).astype(jnp.bfloat16)
    output_turned = near_sum(
        output_turned.reshape(piece, outer, -1, output_columns).transpose(1, 2, 0, 3)
    ).astype(jnp.float32)
    output_average, output_variance, output_direction = adam_step(
        output_turned, output_first, output_second
    )
    output_wide = doubled(doubled(output_direction.astype(jnp.bfloat16), "core"), "outer")
    output_wide = output_wide.reshape(groups, piece, output_columns).swapaxes(0, 1)
    output_middle = back_product(output_wide.reshape(piece, width), right_low)
    output_middle = doubled(output_middle.astype(jnp.bfloat16), "seq")
    output_back = plain_product(bases_low[1], output_middle.reshape(width, output_columns))
    triple_done = merged(*[cut_rows(rows) for rows in triple_done])
    triple_lows, triple_turns, triple_steps = zip(
        *[jnp.split(done, 3, axis=1) for done in triple_done]
    )

    def settled_piece(start, height, size):
        return settled[:, start : start + height].reshape(-1, piece)[:size].astype(jnp.float32)

    expand_gradient, expand_turned_grad, expand_back = (
        settled_piece(start, expand_height, expand_rows).T
        for start in (0, feed_height, feed_height + expand_height)
    )
    shrink_gradient, shrink_turned_grad, shrink_back = (
        settled_piece(start, shrink_height, shrink_rows)
        for start in (
            expand_height,
            feed_height + 2 * expand_height,
            feed_height + 2 * expand_height + shrink_height,
        )
    )
    expand_average, expand_variance, _ = adam_step(expand_turned_grad, expand_first, expand_second)
    shrink_average, shrink_variance, _ = adam_step(shrink_turned_grad, shrink_first, shrink_second)
    triple_turned = from_heads(triple_turns).T
    triple_back = from_heads(triple_steps).T
    triple_gradient = from_heads(triple_lows).T
    triple_average, triple_variance, _ = adam_step(triple_turned, triple_first, triple_second)
    changes = [outer_sum(joint_back, triple_rows) for joint_back in joint_backs]
    if split == 2:
        own, other = by_length(*changes)
        first_change = own + swap(other.astype(jnp.bfloat16)).astype(jnp.float32)
    else:
        first_change = changes[0]
    first_input, first_gain = first_back(first_change)
    token_gradient = (middle_back + first_input).astype(jnp.bfloat16).reshape(tokens.shape)
    gains_gradient = jnp.stack([first_gain, second_gain])
    for axis in ("core", "outer", "seq"):
        members = range(lax.axis_size(axis))
        for step in range(len(members).bit_length() - 1):
            pairs = [(member, member ^ (1 << step)) for member in members]
            gains_gradient = gains_gradient + lax.ppermute(gains_gradient, axis, pairs)
    gains_average, gains_variance, gains_direction = adam_step(
        gains_gradient, gains_first, gains_second
    )
    output_gradient = output_low.astype(jnp.float32)
    triple_updated = (triple_weight - WEIGHT_RATES[0] * triple_back) * (
        1.0 - WEIGHT_RATES[0] * DECAY_RATE
    )
    output_updated = (output_weight - WEIGHT_RATES[1] * output_back) * (
        1.0 - WEIGHT_RATES[1] * DECAY_RATE
    )
    expand_updated = (expand_weight - WEIGHT_RATES[2] * expand_back) * (
        1.0 - WEIGHT_RATES[2] * DECAY_RATE
    )
    shrink_updated = (shrink_weight - WEIGHT_RATES[3] * shrink_back) * (
        1.0 - WEIGHT_RATES[3] * DECAY_RATE
    )
    gains_updated = norm_gains - GAINS_RATE * gains_direction
    return (
        mixed,
        token_gradient,
        triple_gradient,
        output_gradient,
        expand_gradient,
        shrink_gradient,
        gains_gradient,
        triple_average,
        triple_variance,
        triple_updated,
        triple_updated.astype(jnp.bfloat16),
        output_average,
        output_variance,
        output_updated,
        output_updated.astype(jnp.bfloat16),
        expand_average,
        expand_variance,
        expand_updated,
        expand_updated.astype(jnp.bfloat16),
        shrink_average,
        shrink_variance,
        shrink_updated,
        shrink_updated.astype(jnp.bfloat16),
        gains_average,
        gains_variance,
        gains_updated,
    )


def solution(mesh):
    in_specs = (
        P(("outer", "core"), "seq", None),
        P(("outer", "core"), "seq", None),
        P(("outer", "core")),
        P("seq", ("outer", "core")),
        P("seq", ("outer", "core")),
        P("seq", ("outer", "core")),
        P(("outer", "core"), "seq"),
        P(),
        P(None, "seq", None),
        P(("outer", "core"), None),
        P("seq", ("outer", "core")),
        P("seq", ("outer", "core")),
        P("seq", ("outer", "core")),
        P("seq", ("outer", "core")),
        P("seq", ("outer", "core")),
        P("seq", ("outer", "core")),
        P(("outer", "core"), "seq"),
        P(("outer", "core"), "seq"),
        P(),
        P(),
    )
    out_specs = (
        P(("outer", "core"), "seq", None),
        P(("outer", "core"), "seq", None),
        P("seq", ("outer", "core")),
        P("seq", ("outer", "core")),
        P("seq", ("outer", "core")),
        P(("outer", "core"), "seq"),
        P(),
        P("seq", ("outer", "core")),
        P("seq", ("outer", "core")),
        P("seq", ("outer", "core")),
        P("seq", ("outer", "core")),
        P("seq", ("outer", "core")),
        P("seq", ("outer", "core")),
        P("seq", ("outer", "core")),
        P("seq", ("outer", "core")),
        P("seq", ("outer", "core")),
        P("seq", ("outer", "core")),
        P("seq", ("outer", "core")),
        P("seq", ("outer", "core")),
        P(("outer", "core"), "seq"),
        P(("outer", "core"), "seq"),
        P(("outer", "core"), "seq"),
        P(("outer", "core"), "seq"),
        P(),
        P(),
        P(),
    )
    groups = mesh.shape["fsdp"]
    devices = mesh.devices.reshape(mesh.shape["seq"], groups // 2, 2)
    split = Mesh(devices, ("seq", "outer", "core"))
    return jax.shard_map(body, mesh=split, in_specs=in_specs, out_specs=out_specs, check_vma=False)
```

```python
import functools
import math

import jax
import jax.numpy as jnp
from jax import lax
from jax.experimental import pallas as pl
from jax.experimental.pallas import tpu as pltpu
from jax.sharding import Mesh
from jax.sharding import PartitionSpec as P

HEADS = 16
HEAD_DIM = 64
FF = 2624
STEP = 10


ROPE_BASE = 160000.0
NORM_EPS = 1e-05
NEG_LARGE = -1e30
BETA_ONE = 0.95
BETA_TWO = 0.95
ADAM_EPS = 1e-08
DECAY_RATE = 0.01
WEIGHT_RATES = (0.03, 1.0, 0.03, 0.03)
GAINS_RATE = 0.8


def layer_norm(values, gain):
    centre = values - jnp.mean(values, axis=-1, keepdims=True)
    spread = jnp.mean(centre * centre, axis=-1, keepdims=True)
    return centre * lax.rsqrt(spread + NORM_EPS) * gain


def rotary_tables(position):
    halves = HEAD_DIM // 2
    frequency = ROPE_BASE ** (-2.0 * jnp.arange(halves, dtype=jnp.float32) / HEAD_DIM)
    angle = frequency[:, None] * position.astype(jnp.float32)[None, :]
    return jnp.cos(angle), jnp.sin(angle)


def outer_sum(left, right):
    return lax.dot_general(
        left, right, (((0,), (0,)), ((), ())), preferred_element_type=jnp.float32
    )


def back_product(left, right):
    return lax.dot_general(
        left, right, (((1,), (1,)), ((), ())), preferred_element_type=jnp.float32
    )


def plain_product(left, right):
    return jnp.dot(left, right, preferred_element_type=jnp.float32)


NT = (((1,), (1,)), ((), ()))
SAFE_BOUND = 60.0
MASK = -1e30
VMEM_LIMIT = 60 * 1024 * 1024


def extra_rows(rows, length, size=HEAD_DIM):
    place = lax.broadcasted_iota(jnp.int32, (size, length), 0)
    block = jnp.zeros((size, length), jnp.float32)
    for index, row in enumerate(rows):
        block = jnp.where(place == index, row, block)
    return block.astype(jnp.bfloat16)


def three_parts(row):
    high = row.astype(jnp.bfloat16).astype(jnp.float32)
    middle = (row - high).astype(jnp.bfloat16).astype(jnp.float32)
    return [high, middle, row - high - middle]


def mask_row(start, length, limit):
    place = start + lax.broadcasted_iota(jnp.int32, (1, length), 1)
    return jnp.where(place < limit, 0.0, MASK)


def project_kernel(pieces_ref, first_ref, cosine_ref, sine_ref, out_ref, rows_ref, *, group):
    shards, groups, size, _ = pieces_ref.shape
    cosine, sine = cosine_ref[...], sine_ref[...]
    half = HEAD_DIM // 2

    def chunk(part, head):
        start = (part * shards + head) * HEAD_DIM
        place = slice(start % size, start % size + HEAD_DIM)
        return jnp.concatenate(
            [pieces_ref[shard, start // size, place, :] for shard in range(shards)], axis=1
        )

    for begin in range(0, shards, group):
        heads = range(begin, begin + group)
        weight = jnp.concatenate([chunk(part, head) for head in heads for part in range(3)], axis=0)
        product = lax.dot_general(weight, first_ref[...], NT, preferred_element_type=jnp.float32)
        for index, head in enumerate(heads):
            for part in range(3):
                base = (3 * index + part) * HEAD_DIM
                rows_ref[head, part] = weight[base : base + HEAD_DIM]
            for part, scale in ((0, HEAD_DIM**-0.5), (1, 1.0)):
                base = (3 * index + part) * HEAD_DIM
                upper, lower = product[base : base + half], product[base + half : base + HEAD_DIM]
                turned_upper = (upper * cosine - lower * sine).astype(jnp.bfloat16)
                turned_lower = (lower * cosine + upper * sine).astype(jnp.bfloat16)
                place = part * HEAD_DIM
                scale = jnp.bfloat16(scale)
                out_ref[head, place : place + half, :] = turned_upper * scale
                out_ref[head, place + half : place + HEAD_DIM, :] = turned_lower * scale
            base = (3 * index + 2) * HEAD_DIM
            out_ref[head, 2 * HEAD_DIM :, :] = product[base : base + HEAD_DIM].astype(jnp.bfloat16)


def project_heads(pieces, first, cosine, sine):
    shards, groups, size, lanes = pieces.shape
    count, width = first.shape
    half = HEAD_DIM // 2
    whole = lambda *shape: pl.BlockSpec(shape, lambda i: (0,) * len(shape))
    return pl.pallas_call(
        functools.partial(project_kernel, group=min(4, shards)),
        grid=(1,),
        in_specs=[
            whole(shards, groups, size, lanes),
            whole(count, width),
            whole(half, count),
            whole(half, count),
        ],
        out_specs=[whole(shards, 3 * HEAD_DIM, count), whole(shards, 3, HEAD_DIM, width)],
        out_shape=[
            jax.ShapeDtypeStruct((shards, 3 * HEAD_DIM, count), jnp.bfloat16),
            jax.ShapeDtypeStruct((shards, 3, HEAD_DIM, width), jnp.bfloat16),
        ],
        compiler_params=pltpu.CompilerParams(vmem_limit_bytes=VMEM_LIMIT),
        cost_estimate=pl.CostEstimate(
            flops=6 * width * shards * HEAD_DIM * count,
            bytes_accessed=20 * width * shards * HEAD_DIM,
            transcendentals=0,
        ),
    )(pieces, first, cosine, sine)


def forward_kernel(length_ref, joint_ref, out_ref, log_ref, key_ref, value_ref, peak_ref, bound_ref):
    index = pl.program_id(0)
    shards, _, local = joint_ref.shape
    limit = length_ref[0]
    ratio = max(1, 2048 // local)
    blocks = (limit + local - 1) // local

    @pl.when(index == 0)
    def prepare():
        query_most = jnp.zeros((1, 1), jnp.float32)
        key_most = jnp.zeros((1, 1), jnp.float32)
        for shard in range(shards):
            place = slice(shard * local, (shard + 1) * local)
            query = joint_ref[shard, :HEAD_DIM, :].astype(jnp.float32)
            key = joint_ref[shard, HEAD_DIM : 2 * HEAD_DIM, :]
            wide_key = key.astype(jnp.float32)
            query_size = jnp.sum(query * query, axis=0, keepdims=True)
            key_size = jnp.sum(wide_key * wide_key, axis=0, keepdims=True)
            query_most = jnp.maximum(query_most, jnp.max(query_size, axis=1, keepdims=True))
            key_most = jnp.maximum(key_most, jnp.max(key_size, axis=1, keepdims=True))
            extra = extra_rows([mask_row(shard * local, local, limit), 1.0], local)
            key_ref[place, :] = jnp.concatenate([key, extra], axis=0).T
            value_ref[:HEAD_DIM, place] = joint_ref[shard, 2 * HEAD_DIM :, :]
            value_ref[HEAD_DIM:, place] = extra_rows([1.0], local, 16)
        bound_ref[0] = (jnp.sqrt(query_most) * jnp.sqrt(key_most))[0, 0]

    @pl.when(index >= blocks)
    def padding():
        out_ref[...] = jnp.zeros_like(out_ref)
        log_ref[...] = jnp.zeros_like(log_ref)

    @pl.when(index < blocks)
    def compute():
        query = joint_ref[index, :HEAD_DIM, :]
        peak_ref[...] = jnp.zeros_like(peak_ref)

        @pl.when(bound_ref[0] > SAFE_BOUND)
        def find_peak():
            plain = jnp.concatenate([query, extra_rows([1.0], local)], axis=0)

            def step(block, peak):
                place = pl.ds(pl.multiple_of(block * local, local), local)
                scores = jnp.dot(key_ref[place, :], plain, preferred_element_type=jnp.float32)
                return jnp.maximum(peak, jnp.max(scores, axis=0, keepdims=True))

            peak = lax.fori_loop(0, blocks, step, jnp.full((1, local), MASK, jnp.float32))
            peak_ref[...] = peak.astype(jnp.bfloat16).astype(jnp.float32)

        peak = peak_ref[...]
        augmented = jnp.concatenate([query, extra_rows([1.0, -peak], local)], axis=0)

        def attend(start, size, total):
            place = pl.ds(pl.multiple_of(start, local), size)
            scores = jnp.dot(key_ref[place, :], augmented, preferred_element_type=jnp.float32)
            weights = jnp.exp(scores).astype(jnp.bfloat16)
            return total + jnp.dot(
                value_ref[:, place], weights, preferred_element_type=jnp.float32
            )

        large = blocks // ratio
        total = lax.fori_loop(
            0,
            large,
            lambda block, total: attend(block * (ratio * local), ratio * local, total),
            jnp.zeros((HEAD_DIM + 16, local), jnp.float32),
        )
        total = lax.fori_loop(
            large * ratio, blocks, lambda block, total: attend(block * local, local, total), total
        )
        mass = total[HEAD_DIM : HEAD_DIM + 1, :]
        out_ref[0] = (total[:HEAD_DIM, :] / mass).astype(jnp.bfloat16)
        log_ref[0] = peak + jnp.log(mass)


def attend_forward(length, joint):
    shards, _, local = joint.shape
    total = shards * local
    return pl.pallas_call(
        forward_kernel,
        grid=(shards,),
        in_specs=[
            pl.BlockSpec(memory_space=pltpu.SMEM),
            pl.BlockSpec((shards, 3 * HEAD_DIM, local), lambda i: (0, 0, 0)),
        ],
        out_specs=[
            pl.BlockSpec((1, HEAD_DIM, local), lambda i: (i, 0, 0)),
            pl.BlockSpec((1, 1, local), lambda i: (i, 0, 0)),
        ],
        out_shape=[
            jax.ShapeDtypeStruct((shards, HEAD_DIM, local), jnp.bfloat16),
            jax.ShapeDtypeStruct((shards, 1, local), jnp.float32),
        ],
        scratch_shapes=[
            pltpu.VMEM((total, 2 * HEAD_DIM), jnp.bfloat16),
            pltpu.VMEM((HEAD_DIM + 16, total), jnp.bfloat16),
            pltpu.VMEM((1, local), jnp.float32),
            pltpu.SMEM((1,), jnp.float32),
        ],
        compiler_params=pltpu.CompilerParams(vmem_limit_bytes=VMEM_LIMIT),
        cost_estimate=pl.CostEstimate(
            flops=total * total,
            bytes_accessed=HEAD_DIM * total,
            transcendentals=0,
        ),
    )(length, joint)


def backward_kernel(
    length_ref,
    joint_ref,
    back_ref,
    out_ref,
    log_ref,
    cosine_ref,
    sine_ref,
    grad_ref,
    query_ref,
    wide_ref,
    query_flat,
    back_flat,
    query_sum,
):
    index = pl.program_id(0)
    shards, _, local = joint_ref.shape
    limit = length_ref[0]
    ratio = max(1, 2048 // local)
    blocks = (limit + local - 1) // local
    half = HEAD_DIM // 2

    def turned_back(wide, shard):
        cosine, sine = cosine_ref[shard], sine_ref[shard]
        upper, lower = wide[:half], wide[half:]
        return jnp.concatenate(
            [upper * cosine + lower * sine, lower * cosine - upper * sine], axis=0
        ).astype(jnp.bfloat16)

    @pl.when(index == 0)
    def prepare():
        for shard in range(shards):
            place = slice(shard * local, (shard + 1) * local)
            query = joint_ref[shard, :HEAD_DIM, :]
            back = back_ref[shard]
            extra = extra_rows([1.0] + three_parts(-log_ref[shard]), local)
            query_ref[place, :] = jnp.concatenate([query, extra], axis=0).T
            balance = jnp.sum(
                back.astype(jnp.float32) * out_ref[shard].astype(jnp.float32),
                axis=0,
                keepdims=True,
            )
            extra = extra_rows(three_parts(-balance), local)
            wide_ref[place, :] = jnp.concatenate([back, extra], axis=0).T
            query_flat[:, place] = query
            back_flat[:, place] = back
        query_sum[...] = jnp.zeros_like(query_sum)

    @pl.when(index >= blocks)
    def padding():
        grad_ref[index, HEAD_DIM:, :] = jnp.zeros((2 * HEAD_DIM, local), jnp.bfloat16)

    @pl.when(index < blocks)
    def compute():
        key = joint_ref[index, HEAD_DIM : 2 * HEAD_DIM, :]
        value = joint_ref[index, 2 * HEAD_DIM :, :]
        mask = mask_row(index * local, local, limit)
        wide_key = jnp.concatenate([key, extra_rows([mask, 1.0, 1.0, 1.0], local)], axis=0)
        wide_value = jnp.concatenate([value, extra_rows([1.0, 1.0, 1.0], local)], axis=0)

        def gather(start, size, carry):
            key_sum, value_sum = carry
            place = pl.ds(pl.multiple_of(start, local), size)
            scores = jnp.dot(query_ref[place, :], wide_key, preferred_element_type=jnp.float32)
            chance = jnp.exp(scores)
            change = jnp.dot(wide_ref[place, :], wide_value, preferred_element_type=jnp.float32)
            chance_low = chance.astype(jnp.bfloat16)
            score_back = (chance * change).astype(jnp.bfloat16)
            value_sum = value_sum + jnp.dot(
                back_flat[:, place], chance_low, preferred_element_type=jnp.float32
            )
            key_sum = key_sum + jnp.dot(
                query_flat[:, place], score_back, preferred_element_type=jnp.float32
            )
            query_sum[:, place] += lax.dot_general(
                key, score_back, NT, preferred_element_type=jnp.float32
            )
            return (key_sum, value_sum)

        large = blocks // ratio
        zero = jnp.zeros((HEAD_DIM, local), jnp.float32)
        carry = lax.fori_loop(
            0,
            large,
            lambda block, carry: gather(block * (ratio * local), ratio * local, carry),
            (zero, zero),
        )
        key_sum, value_sum = lax.fori_loop(
            large * ratio, blocks, lambda block, carry: gather(block * local, local, carry), carry
        )
        grad_ref[index, HEAD_DIM : 2 * HEAD_DIM, :] = turned_back(key_sum, index)
        grad_ref[index, 2 * HEAD_DIM :, :] = value_sum.astype(jnp.bfloat16)

    @pl.when(index == shards - 1)
    def finish():
        for shard in range(shards):
            place = slice(shard * local, (shard + 1) * local)
            grad_ref[shard, :HEAD_DIM, :] = turned_back(
                query_sum[:, place] * HEAD_DIM**-0.5, shard
            )


def attend_backward(length, joint, back, attend, log_mass, cosine, sine):
    shards, _, local = joint.shape
    total = shards * local
    whole = lambda rows: pl.BlockSpec((shards, rows, local), lambda i: (0, 0, 0))
    return pl.pallas_call(
        backward_kernel,
        grid=(shards,),
        in_specs=[
            pl.BlockSpec(memory_space=pltpu.SMEM),
            whole(3 * HEAD_DIM),
            whole(HEAD_DIM),
            whole(HEAD_DIM),
            whole(1),
            whole(HEAD_DIM // 2),
            whole(HEAD_DIM // 2),
        ],
        out_specs=whole(3 * HEAD_DIM),
        out_shape=jax.ShapeDtypeStruct((shards, 3 * HEAD_DIM, local), jnp.bfloat16),
        scratch_shapes=[
            pltpu.VMEM((total, 2 * HEAD_DIM), jnp.bfloat16),
            pltpu.VMEM((total, 2 * HEAD_DIM), jnp.bfloat16),
            pltpu.VMEM((HEAD_DIM, total), jnp.bfloat16),
            pltpu.VMEM((HEAD_DIM, total), jnp.bfloat16),
            pltpu.VMEM((HEAD_DIM, total), jnp.float32),
        ],
        compiler_params=pltpu.CompilerParams(vmem_limit_bytes=VMEM_LIMIT),
        cost_estimate=pl.CostEstimate(
            flops=total * total,
            bytes_accessed=HEAD_DIM * total,
            transcendentals=0,
        ),
    )(length, joint, back, attend, log_mass, cosine, sine)


TN = (((0,), (0,)), ((), ()))
PLAIN = (((1,), (0,)), ((), ()))
LANES = 128
GROUPS = 4
RUNS = 8
UNITS = FF // GROUPS
EXPAND_RUN = -(-2 * UNITS // (16 * RUNS)) * 16
SHRINK_RUN = -(-UNITS // (16 * RUNS)) * 16


def run_segments(start, stop, run):
    segments = []
    while start < stop:
        index = start // run
        end = min(stop, (index + 1) * run)
        segments.append((index, start - index * run, start, end - start))
        start = end
    return segments


def feed_kernel(
    second_ref,
    upstream_ref,
    active_ref,
    gate_ref,
    shrink_ref,
    shrunk_ref,
    second_back_ref,
    parts_ref,
    grads_ref,
    zero_ref,
    send_ref,
    zero_send_ref,
):
    index = pl.program_id(0)

    def joined(ref):
        return jnp.concatenate([ref[piece, 0] for piece in range(ref.shape[0])], axis=1)

    def product(left, right, dims):
        return lax.dot_general(left, right, dims, preferred_element_type=jnp.float32)

    def grad_copies(half, pair):
        moves = []
        for kind, member in ((0, pair), (1, pair + 2)):
            for run, place, offset, size in run_segments(
                half * UNITS, (half + 1) * UNITS, EXPAND_RUN
            ):
                moves.append((kind, offset - half * UNITS, run, member, place, size))
        for run, place, offset, size in run_segments(0, UNITS, SHRINK_RUN):
            moves.append((2, offset, run, 2 * pair + half, EXPAND_RUN + place, size))
        return [
            pltpu.make_async_copy(
                grads_ref.at[half, kind, pl.ds(offset, size), :],
                parts_ref.at[run, member, pl.ds(place, size), :],
                send_ref.at[half, number],
            )
            for number, (kind, offset, run, member, place, size) in enumerate(moves)
        ]

    def zero_copies():
        moves = []
        for member in range(GROUPS):
            for base, run_size, total in ((0, EXPAND_RUN, 2 * UNITS), (EXPAND_RUN, SHRINK_RUN, UNITS)):
                for run, place, _, size in run_segments(total, RUNS * run_size, run_size):
                    moves.append((run, member, base + place, size))
        return [
            pltpu.make_async_copy(
                zero_ref.at[pl.ds(0, size), :],
                parts_ref.at[run, member, pl.ds(place, size), :],
                zero_send_ref.at[number],
            )
            for number, (run, member, place, size) in enumerate(moves)
        ]

    @pl.when(index == 0)
    def fill():
        zero_ref[...] = jnp.zeros_like(zero_ref)
        for copy in zero_copies():
            copy.start()

    active, gate, shrink = joined(active_ref), joined(gate_ref), joined(shrink_ref)
    second, upstream = second_ref[...], upstream_ref[...]
    input_active = product(second, active, NT)
    input_gate = product(second, gate, NT)
    hidden_back = product(upstream, shrink, NT)
    below = 0.5 + 0.5 * lax.erf(input_active * 0.5**0.5)
    bell = jnp.exp(-0.5 * input_active * input_active) * (0.5 / math.pi) ** 0.5
    curve = input_active * below
    hidden = (curve * input_gate).astype(jnp.bfloat16)
    active_back = (hidden_back * input_gate * (below + input_active * bell)).astype(jnp.bfloat16)
    gate_back = (hidden_back * curve).astype(jnp.bfloat16)
    shrunk = product(hidden, shrink, PLAIN)
    second_back = product(active_back, active, PLAIN) + product(gate_back, gate, PLAIN)

    @pl.when(index == 0)
    def begin():
        shrunk_ref[...] = shrunk
        second_back_ref[...] = second_back

    @pl.when(index > 0)
    def add():
        shrunk_ref[...] += shrunk
        second_back_ref[...] += second_back

    for half in range(2):

        @pl.when(index % 2 == half)
        def send(half=half):
            pair = index // 2

            @pl.when(index >= 2)
            def free():
                for copy in grad_copies(half, pair - 1):
                    copy.wait()

            grads_ref[half, 0] = product(active_back, second, TN).astype(jnp.bfloat16)
            grads_ref[half, 1] = product(gate_back, second, TN).astype(jnp.bfloat16)
            grads_ref[half, 2] = product(hidden, upstream, TN).astype(jnp.bfloat16)
            for copy in grad_copies(half, pair):
                copy.start()

    @pl.when(index == GROUPS - 1)
    def drain():
        for half in range(2):
            for copy in grad_copies(half, 1):
                copy.wait()
        for copy in zero_copies():
            copy.wait()


def feed_forward(second, upstream, pieces):
    count, width = second.shape
    block = (RUNS, 1, UNITS, LANES)
    held = pl.BlockSpec((count, width), lambda i: (0, 0), pipeline_mode=pl.Buffered(1))
    wide = jax.ShapeDtypeStruct((count, width), jnp.float32)
    run = EXPAND_RUN + SHRINK_RUN
    copies = max(
        2 * len(run_segments(half * UNITS, (half + 1) * UNITS, EXPAND_RUN)) for half in range(2)
    ) + len(run_segments(0, UNITS, SHRINK_RUN))
    return pl.pallas_call(
        feed_kernel,
        grid=(GROUPS,),
        in_specs=[
            held,
            held,
            pl.BlockSpec(block, lambda i: (0, i // 2, i % 2, 0)),
            pl.BlockSpec(block, lambda i: (0, i // 2 + 2, i % 2, 0)),
            pl.BlockSpec(block, lambda i: (0, i, 2, 0)),
        ],
        out_specs=[held, held, pl.BlockSpec(memory_space=pl.ANY)],
        out_shape=[wide, wide, jax.ShapeDtypeStruct((RUNS, GROUPS, run, width), jnp.bfloat16)],
        scratch_shapes=[
            pltpu.VMEM((2, 3, UNITS, width), jnp.bfloat16),
            pltpu.VMEM((max(EXPAND_RUN, SHRINK_RUN), width), jnp.bfloat16),
            pltpu.SemaphoreType.DMA((2, copies)),
            pltpu.SemaphoreType.DMA((GROUPS * 8,)),
        ],
        compiler_params=pltpu.CompilerParams(vmem_limit_bytes=VMEM_LIMIT),
        cost_estimate=pl.CostEstimate(
            flops=count * width,
            bytes_accessed=count * width,
            transcendentals=0,
        ),
    )(second, upstream, pieces, pieces, pieces)


def enter_kernel(*refs):
    phases = (len(refs) - 9) // 2
    attend_refs, weight_refs = refs[:phases], refs[phases : 2 * phases]
    limit_ref, token_ref, cotangent_ref, gain_ref = refs[2 * phases : 2 * phases + 4]
    middle_ref, normal_ref, second_ref, upstream_ref, spread_ref = refs[2 * phases + 4 :]
    middle = token_ref[...].astype(jnp.float32)
    for attend_ref, weight_ref in zip(attend_refs, weight_refs):
        middle += lax.dot_general(
            attend_ref[...], weight_ref[...], TN, preferred_element_type=jnp.float32
        )
    block = middle.shape[0]
    centre = middle - jnp.mean(middle, axis=1, keepdims=True)
    scale = lax.rsqrt(jnp.mean(centre * centre, axis=1, keepdims=True) + NORM_EPS)
    normal = centre * scale
    place = pl.program_id(0) * block + lax.broadcasted_iota(jnp.int32, (block, 1), 0)
    middle_ref[...] = middle
    normal_ref[...] = normal
    spread_ref[...] = scale
    second_ref[...] = (normal * gain_ref[1:2, :]).astype(jnp.bfloat16)
    upstream_ref[...] = jnp.where(place < limit_ref[0], cotangent_ref[...], jnp.bfloat16(0.0))


def enter_feed(attends, weights, limit, tokens, cotangent, gains):
    count, width = tokens.shape
    block = min(256, count)
    rows = pl.BlockSpec((block, width), lambda i: (i, 0))
    wide = jax.ShapeDtypeStruct((count, width), jnp.float32)
    low = jax.ShapeDtypeStruct((count, width), jnp.bfloat16)
    return pl.pallas_call(
        enter_kernel,
        grid=(count // block,),
        in_specs=[pl.BlockSpec((attend.shape[0], block), lambda i: (0, i)) for attend in attends]
        + [pl.BlockSpec(weight.shape, lambda i: (0, 0)) for weight in weights]
        + [pl.BlockSpec(memory_space=pltpu.SMEM), rows, rows]
        + [pl.BlockSpec(gains.shape, lambda i: (0, 0))],
        out_specs=[rows, rows, rows, rows, pl.BlockSpec((block, 1), lambda i: (i, 0))],
        out_shape=[wide, wide, low, low, jax.ShapeDtypeStruct((count, 1), jnp.float32)],
        compiler_params=pltpu.CompilerParams(vmem_limit_bytes=VMEM_LIMIT),
        cost_estimate=pl.CostEstimate(
            flops=2 * count * width * width, bytes_accessed=20 * count * width, transcendentals=0
        ),
    )(*attends, *weights, limit, tokens, cotangent, gains)


def leave_kernel(*refs):
    phases = (len(refs) - 12) // 2
    weight_refs, back_refs = refs[:phases], refs[-phases:]
    limit_ref, shrunk_ref, change_ref, middle_ref, normal_ref, spread_ref = refs[phases : phases + 6]
    upstream_ref, gain_ref = refs[phases + 6 : phases + 8]
    mixed_ref, middle_back_ref, branch_ref, gain_grad_ref = refs[phases + 8 : phases + 12]
    index = pl.program_id(0)
    block = mixed_ref.shape[0]
    place = index * block + lax.broadcasted_iota(jnp.int32, (block, 1), 0)
    mixed = middle_ref[...] + shrunk_ref[...]
    mixed_ref[...] = jnp.where(place < limit_ref[0], mixed, 0.0).astype(jnp.bfloat16)
    change, normal = change_ref[...], normal_ref[...]
    gain_grad = jnp.sum(change * normal, axis=0, keepdims=True)

    @pl.when(index == 0)
    def begin():
        gain_grad_ref[...] = gain_grad

    @pl.when(index > 0)
    def add():
        gain_grad_ref[...] += gain_grad

    inner = change * gain_ref[1:2, :]
    inner = (
        inner
        - jnp.mean(inner, axis=1, keepdims=True)
        - normal * jnp.mean(inner * normal, axis=1, keepdims=True)
    )
    middle_back = upstream_ref[...].astype(jnp.float32) + spread_ref[...] * inner
    branch = middle_back.astype(jnp.bfloat16)
    middle_back_ref[...] = middle_back
    branch_ref[...] = branch
    for weight_ref, back_ref in zip(weight_refs, back_refs):
        back_ref[...] = lax.dot_general(
            weight_ref[...], branch, NT, preferred_element_type=jnp.float32
        ).astype(jnp.bfloat16)


def leave_feed(weights, limit, shrunk, change, middle, normal, spread, upstream, gains):
    count, width = shrunk.shape
    block = min(256, count)
    rows = pl.BlockSpec((block, width), lambda i: (i, 0))
    wide = jax.ShapeDtypeStruct((count, width), jnp.float32)
    low = jax.ShapeDtypeStruct((count, width), jnp.bfloat16)
    return pl.pallas_call(
        leave_kernel,
        grid=(count // block,),
        in_specs=[pl.BlockSpec(weight.shape, lambda i: (0, 0)) for weight in weights]
        + [pl.BlockSpec(memory_space=pltpu.SMEM), rows, rows, rows, rows]
        + [pl.BlockSpec((block, 1), lambda i: (i, 0)), rows]
        + [pl.BlockSpec(gains.shape, lambda i: (0, 0))],
        out_specs=[rows, rows, rows, pl.BlockSpec((1, width), lambda i: (0, 0))]
        + [pl.BlockSpec((weight.shape[0], block), lambda i: (0, i)) for weight in weights],
        out_shape=[low, wide, low, jax.ShapeDtypeStruct((1, width), jnp.float32)]
        + [jax.ShapeDtypeStruct((weight.shape[0], count), jnp.bfloat16) for weight in weights],
        compiler_params=pltpu.CompilerParams(vmem_limit_bytes=VMEM_LIMIT),
        cost_estimate=pl.CostEstimate(
            flops=2 * count * width * width, bytes_accessed=28 * count * width, transcendentals=0
        ),
    )(*weights, limit, shrunk, change, middle, normal, spread, upstream, gains)


def adam_step(rotated, first, second):
    average = BETA_ONE * first + (1.0 - BETA_ONE) * rotated
    variance = BETA_TWO * second + (1.0 - BETA_TWO) * rotated * rotated
    direction = (
        average / (1.0 - BETA_ONE**STEP) / (jnp.sqrt(variance / (1.0 - BETA_TWO**STEP)) + ADAM_EPS)
    )
    return (average, variance, direction)


def body(
    tokens,
    cotangent,
    lengths,
    triple_weight,
    output_weight,
    expand_weight,
    shrink_weight,
    norm_gains,
    side_bases,
    output_right,
    triple_first,
    triple_second,
    output_first,
    output_second,
    expand_first,
    expand_second,
    shrink_first,
    shrink_second,
    gains_first,
    gains_second,
):
    rows_here, local_len, width = tokens.shape
    count = rows_here * local_len
    shards = lax.axis_size("seq")
    groups = lax.axis_size("outer") * lax.axis_size("core")
    split = HEADS // shards
    core = lax.axis_index("core")
    swap = functools.partial(lax.ppermute, axis_name="core", perm=[(0, 1), (1, 0)])
    other_lengths = swap(lengths)
    ahead = (lengths > other_lengths) | ((lengths == other_lengths) & (core == 0))

    def by_length(own, other):
        return [jnp.where(ahead[0], own, other), jnp.where(ahead[0], other, own)]

    def by_core(mine, other):
        return [jnp.where(core == 0, mine, other), jnp.where(core == 0, other, mine)]

    def both_rows(own):
        return by_length(own, swap(own)) if split == 2 else [own]

    piece = width // shards
    fsdp = ("outer", "core")
    everyone = ("seq",) + fsdp
    offset = lax.axis_index("seq") * local_len
    position = offset + jnp.arange(local_len, dtype=jnp.int32)
    cosine, sine = rotary_tables(position)
    every = jnp.arange(shards * local_len, dtype=jnp.int32)
    all_cosine, all_sine = (
        table.reshape(HEAD_DIM // 2, shards, local_len).transpose(1, 0, 2)
        for table in rotary_tables(every)
    )
    valid = (position[None, :] < lengths[:, None]).astype(jnp.float32).reshape(count, 1)
    exchange = functools.partial(lax.all_to_all, axis_name="seq", split_axis=0, concat_axis=0)

    def tied(*values):
        return lax.optimization_barrier(values)

    def gathered(shard):
        flat = lax.all_gather(shard, everyone, axis=0, tiled=False)
        return flat.reshape((shards, groups) + shard.shape)

    triple_shards = (
        triple_weight.T.astype(jnp.bfloat16)
        .reshape(-1, split, HEAD_DIM, piece)
        .transpose(1, 0, 2, 3)
        .reshape(split, -1, piece)
    )
    if split == 2:
        mine = lax.dynamic_index_in_dim(triple_shards, core, 0, keepdims=False)
        other = lax.dynamic_index_in_dim(triple_shards, 1 - core, 0, keepdims=False)
        triple_shards = jnp.stack(by_core(mine, swap(other)))
        triple_pieces = lax.all_gather(triple_shards, ("seq", "outer"), axis=0, tiled=False)
    else:
        triple_pieces = gathered(triple_shards[0])
    triple_pieces = triple_pieces.reshape(shards, groups, -1, piece)
    all_cosine, all_sine, triple_pieces = tied(all_cosine, all_sine, triple_pieces)
    output_columns = width // groups
    lanes = min(piece, output_columns)

    def fold(block):
        rows = block.shape[0]
        return block.reshape(rows, -1, lanes).transpose(1, 0, 2).reshape(-1, lanes)

    bases_low = side_bases.astype(jnp.bfloat16)
    right_low = output_right.astype(jnp.bfloat16)
    member = lax.axis_index("outer") * lax.axis_size("core") + lax.axis_index("core")
    base_rows = piece // groups
    flat = tokens.reshape(count, width).astype(jnp.float32)
    first_normed, first_back = jax.vjp(layer_norm, flat, norm_gains[0])
    first_low = first_normed.astype(jnp.bfloat16)
    other_shards = jnp.concatenate(
        [
            expand_weight.T.astype(jnp.bfloat16),
            shrink_weight.astype(jnp.bfloat16),
            fold(output_weight.astype(jnp.bfloat16)),
        ],
        axis=0,
    )
    firsts = both_rows(first_low)
    projected = [project_heads(triple_pieces, first, cosine, sine) for first in firsts]
    triple_rows = projected[0][1].reshape(-1, width)
    joints = [exchange(joint) for joint, _ in projected]
    other_shards, joints[0] = tied(other_shards, joints[0])
    other_pieces = gathered(other_shards)
    chosen = jnp.stack([bases_low[0], bases_low[2], bases_low[3]])
    chosen = lax.dynamic_slice_in_dim(chosen, member * base_rows, base_rows, 1)
    expand_rows = 2 * FF // groups
    shrink_rows = FF // groups
    output_pieces = other_pieces[:, :, expand_rows + shrink_rows :].reshape(
        shards, groups, output_columns // lanes, split, HEAD_DIM, lanes
    )
    output_rows = [
        output_pieces[:, :, :, head].transpose(0, 3, 1, 2, 4).reshape(shards * HEAD_DIM, width)
        for head in range(split)
    ]
    canonical = (shards, groups, piece) == (RUNS, GROUPS, LANES)
    if canonical:
        feed_pieces = other_pieces
    else:
        feed_pieces = [
            other_pieces[:, :, start:end]
            .transpose(1, 2, 0, 3)
            .reshape(GROUPS, -1, RUNS, LANES)
            .transpose(2, 0, 1, 3)
            for start, end in ((0, expand_rows), (expand_rows, expand_rows + shrink_rows))
        ]
        feed_pieces = jnp.concatenate(feed_pieces, axis=2)
    row_lengths = both_rows(lengths)
    forwards, attends = [], []
    for row, joint in enumerate(joints):
        outcome = attend_forward(row_lengths[row], joint)
        if row:
            attends[-1], outcome = tied(attends[-1], outcome)
        if row < split - 1:
            joints[row + 1], outcome = tied(joints[row + 1], outcome)
        forwards.append(outcome)
        attends.append(exchange(outcome[0]))
    chosen, forwards[-1] = tied(chosen, forwards[-1])
    bases_full = gathered(chosen)
    attends = [attend.reshape(shards * HEAD_DIM, count) for attend in attends]
    if split == 2:
        own, other = by_length(*attends)
        attends = by_core(own, swap(other))
    expand_height = -(-expand_rows // (16 * shards)) * 16
    shrink_height = -(-shrink_rows // (16 * shards)) * 16

    def to_rows(block):
        block = exchange(block)
        return block.transpose(1, 0, 2).reshape(block.shape[1], -1)

    def padded(block, height):
        block = jnp.pad(block, ((0, height * shards - block.shape[0]), (0, 0)))
        return block.reshape(shards, height, piece)

    def by_heads(block):
        return (
            block.reshape(-1, split, HEAD_DIM, piece)
            .transpose(1, 0, 2, 3)
            .reshape(split, shards, -1, piece)
        )

    def from_heads(blocks):
        block = jnp.stack(blocks).astype(jnp.float32).reshape(split, -1, HEAD_DIM, piece)
        return block.transpose(1, 0, 2, 3).reshape(-1, piece)

    moments = []
    for expand, shrink, triple in (
        (expand_first, shrink_first, triple_first),
        (expand_second, shrink_second, triple_second),
    ):
        moments += [padded(expand.T, expand_height), padded(shrink, shrink_height)]
        moments += list(by_heads(triple.T))
    moments, attends[-1], feed_pieces = tied(moments, attends[-1], feed_pieces)
    heights = [moment.shape[1] for moment in moments]
    moments = to_rows(jnp.concatenate(moments, axis=1))
    edges = [sum(heights[:index]) for index in range(len(heights) + 1)]
    moments = [moments[start:end] for start, end in zip(edges, edges[1:])]
    moments = list(zip(moments[: split + 2], moments[split + 2 :]))
    inside = jnp.clip(lengths - offset, 0, local_len)
    middle, second_normal, second_low, upstream_low, second_spread = enter_feed(
        attends,
        output_rows,
        inside,
        tokens.reshape(count, width),
        cotangent.reshape(count, width),
        norm_gains,
    )
    shrunk, second_change, parts = feed_forward(second_low, upstream_low, feed_pieces)
    moments, bases_full, shrunk, second_change, parts = tied(
        moments, bases_full, shrunk, second_change, parts
    )
    mixed, middle_back, branch_low, second_gain, *backs = leave_feed(
        output_rows,
        inside,
        shrunk,
        second_change,
        middle,
        second_normal,
        second_spread,
        upstream_low,
        norm_gains,
    )
    mixed = mixed.reshape(tokens.shape)
    second_gain = second_gain[0]
    backs = [back.reshape(shards, HEAD_DIM, count) for back in backs]
    if split == 2:
        mine, other = by_core(*backs)
        backs = by_length(mine, swap(other))
    order = list(range(split))[::-1]
    attend_backs = [exchange(back) for back in backs]

    def halved(blocks, axis, dim):
        size = lax.axis_size(axis)
        place = lax.axis_index(axis)
        while size > 1:
            size //= 2
            shape = blocks.shape
            blocks = blocks.reshape(shape[:dim] + (2, size) + shape[dim + 1 :])
            side = (place // size) % 2
            mine = lax.dynamic_index_in_dim(blocks, side, dim, keepdims=False)
            other = lax.dynamic_index_in_dim(blocks, 1 - side, dim, keepdims=False)
            pairs = [(member, member ^ size) for member in range(lax.axis_size(axis))]
            other = lax.ppermute(other, axis, pairs)
            blocks = (mine.astype(jnp.float32) + other.astype(jnp.float32)).astype(jnp.bfloat16)
        return jnp.squeeze(blocks, dim)

    def doubled(block, axis):
        size = lax.axis_size(axis)
        place = lax.axis_index(axis)
        shape = block.shape
        step, done = size // 2, 0
        while step:
            pairs = [(member, member ^ step) for member in range(size)]
            other = lax.ppermute(block, axis, pairs)
            upper = (place // step) % 2 == 1
            block = jnp.stack(
                [jnp.where(upper, other, block), jnp.where(upper, block, other)], axis=done
            )
            step //= 2
            done += 1
        return block.reshape((size,) + shape)

    def near_sum(blocks):
        return halved(halved(blocks, "core", 1), "outer", 0)

    def merged(*blocks):
        sizes = [math.prod(block.shape[1:]) for block in blocks]
        flat = [block.reshape(shards, -1, piece) for block in blocks]
        flat = exchange(jnp.concatenate(flat, axis=1))
        results, start = [], 0
        for block, size in zip(blocks, sizes):
            rows = size // piece
            results.append(flat[:, start : start + rows].reshape(block.shape))
            start += rows
        return results

    def widened(block):
        rows = piece * output_columns // count
        block = block.reshape(-1, piece // rows, rows, output_columns)
        return block.swapaxes(1, 2).reshape(shards, -1, count)

    def narrowed(block):
        rows = piece * output_columns // count
        block = block.reshape(-1, rows, piece // rows, output_columns)
        return block.swapaxes(1, 2).reshape(shards, -1, piece, output_columns)

    def far_sum(terms):
        return jnp.sum(terms.astype(jnp.float32), axis=0).astype(jnp.bfloat16)

    def cut_rows(rows):
        return rows.reshape(rows.shape[0], shards, piece).transpose(1, 0, 2)

    outer = lax.axis_size("outer")
    output_part = jnp.stack(
        [
            jnp.dot(attend, branch_low, preferred_element_type=jnp.float32)
            .astype(jnp.bfloat16)
            .reshape(shards, HEAD_DIM, width)
            for attend in attends
        ],
        axis=1,
    )
    output_terms = halved(
        output_part.reshape(shards, piece, outer, -1, output_columns).transpose(0, 2, 3, 1, 4),
        "core",
        2,
    )
    output_terms = widened(output_terms)
    parts, output_terms, attend_backs[order[0]] = tied(
        parts, output_terms, attend_backs[order[0]]
    )

    def cut(product, height):
        block = product.reshape(groups, -1, width)
        block = jnp.pad(block, ((0, 0), (0, height * shards - block.shape[1]), (0, 0)))
        return block.reshape(groups, shards, height, width)

    if not canonical:
        parts = parts.transpose(1, 0, 2, 3)
        parts = [
            cut(block.reshape(GROUPS, -1, width)[:, : size // GROUPS], height)
            for block, size, height in (
                (parts[:, :, :EXPAND_RUN], 2 * FF, expand_height),
                (parts[:, :, EXPAND_RUN:], FF, shrink_height),
            )
        ]
        parts = jnp.concatenate(parts, axis=2).transpose(1, 0, 2, 3)
    parts = parts.reshape(shards * groups, -1, width)
    owned = lax.psum_scatter(parts, everyone, scatter_dimension=0, tiled=False)
    feed_height = expand_height + shrink_height

    def soap_rows(rows, base, moment):
        rotated = plain_product(rows, base)
        direction = adam_step(rotated, *moment)[2]
        step = back_product(direction.astype(jnp.bfloat16), base)
        return rotated.astype(jnp.bfloat16), step.astype(jnp.bfloat16)

    grads = [None] * split
    for step, row in enumerate(order):
        grad = attend_backward(
            row_lengths[row],
            joints[row],
            attend_backs[row],
            *forwards[row],
            all_cosine,
            all_sine,
        )
        if step < split - 1:
            following = order[step + 1]
            attend_backs[following], grad = tied(attend_backs[following], grad)
        else:
            grads, owned, bases_full, grad = tied(grads, owned, bases_full, grad)
        if step == 0:
            grad = jnp.concatenate([grad, output_terms], axis=1)
        grads[row] = exchange(grad)
    output_low = halved(far_sum(narrowed(grads[order[0]][:, 3 * HEAD_DIM :])), "outer", 0)
    joint_backs = [grad[:, : 3 * HEAD_DIM].reshape(-1, count) for grad in grads]
    output_left = outer_sum(bases_low[1], output_low).astype(jnp.bfloat16)
    output_left = output_left.reshape(shards, piece, output_columns)

    def triple_part(row):
        return jnp.dot(joint_backs[row], firsts[row], preferred_element_type=jnp.float32)

    def triple_rest(rows, head):
        return jnp.concatenate([rows, *soap_rows(rows, bases_full[0], moments[2 + head])])

    bases_full = bases_full.transpose(2, 0, 1, 3, 4).reshape(3, width, width)
    feed_rows = jnp.concatenate(
        [
            owned,
            *soap_rows(owned[:expand_height], bases_full[1], moments[0]),
            *soap_rows(owned[expand_height:], bases_full[2], moments[1]),
        ]
    )
    settled = jnp.concatenate(
        [cut_rows(feed_rows), output_left.reshape(shards, -1, piece)], axis=1
    )
    early = [triple_part(row) for row in order[:-1]]
    joint_backs[order[-1]], early, settled = tied(joint_backs[order[-1]], early, settled)
    settled = exchange(settled)
    output_left = settled[:, feed_rows.shape[0] :].reshape(shards, piece, output_columns)
    output_left = far_sum(output_left)
    part = sum(early, triple_part(order[-1])).astype(jnp.bfloat16)
    part = part.reshape(shards, 3, HEAD_DIM, width).swapaxes(0, 1)
    part = part.reshape(outer, groups // outer, shards, -1, width)
    if split == 2:
        part = halved(part, "outer", 0).swapaxes(0, 1)
        rows = far_sum(exchange(part))
        mine = lax.dynamic_index_in_dim(rows, core, 0, keepdims=False)
        other = lax.dynamic_index_in_dim(rows, 1 - core, 0, keepdims=False)
        head_rows = by_core(mine, swap(other))
    else:
        head_rows = [far_sum(exchange(near_sum(part)))]
    triple_done = [triple_rest(rows, head) for head, rows in enumerate(head_rows)]
    output_turned = plain_product(output_left, right_low).astype(jnp.bfloat16)
    output_turned = near_sum(
        output_turned.reshape(piece, outer, -1, output_columns).transpose(1, 2, 0, 3)
    ).astype(jnp.float32)
    output_average, output_variance, output_direction = adam_step(
        output_turned, output_first, output_second
    )
    output_wide = doubled(doubled(output_direction.astype(jnp.bfloat16), "core"), "outer")
    output_wide = output_wide.reshape(groups, piece, output_columns).swapaxes(0, 1)
    output_middle = back_product(output_wide.reshape(piece, width), right_low)
    output_middle = doubled(output_middle.astype(jnp.bfloat16), "seq")
    output_back = plain_product(bases_low[1], output_middle.reshape(width, output_columns))
    triple_done = merged(*[cut_rows(rows) for rows in triple_done])
    triple_lows, triple_turns, triple_steps = zip(
        *[jnp.split(done, 3, axis=1) for done in triple_done]
    )

    def settled_piece(start, height, size):
        return settled[:, start : start + height].reshape(-1, piece)[:size].astype(jnp.float32)

    expand_gradient, expand_turned_grad, expand_back = (
        settled_piece(start, expand_height, expand_rows).T
        for start in (0, feed_height, feed_height + expand_height)
    )
    shrink_gradient, shrink_turned_grad, shrink_back = (
        settled_piece(start, shrink_height, shrink_rows)
        for start in (
            expand_height,
            feed_height + 2 * expand_height,
            feed_height + 2 * expand_height + shrink_height,
        )
    )
    expand_average, expand_variance, _ = adam_step(expand_turned_grad, expand_first, expand_second)
    shrink_average, shrink_variance, _ = adam_step(shrink_turned_grad, shrink_first, shrink_second)
    triple_turned = from_heads(triple_turns).T
    triple_back = from_heads(triple_steps).T
    triple_gradient = from_heads(triple_lows).T
    triple_average, triple_variance, _ = adam_step(triple_turned, triple_first, triple_second)
    changes = [outer_sum(joint_back, triple_rows) for joint_back in joint_backs]
    if split == 2:
        own, other = by_length(*changes)
        first_change = own + swap(other.astype(jnp.bfloat16)).astype(jnp.float32)
    else:
        first_change = changes[0]
    first_input, first_gain = first_back(first_change)
    token_gradient = (middle_back + first_input).astype(jnp.bfloat16).reshape(tokens.shape)
    gains_gradient = jnp.stack([first_gain, second_gain])
    for axis in ("core", "outer", "seq"):
        members = range(lax.axis_size(axis))
        for step in range(len(members).bit_length() - 1):
            pairs = [(member, member ^ (1 << step)) for member in members]
            gains_gradient = gains_gradient + lax.ppermute(gains_gradient, axis, pairs)
    gains_average, gains_variance, gains_direction = adam_step(
        gains_gradient, gains_first, gains_second
    )
    output_gradient = output_low.astype(jnp.float32)
    triple_updated = (triple_weight - WEIGHT_RATES[0] * triple_back) * (
        1.0 - WEIGHT_RATES[0] * DECAY_RATE
    )
    output_updated = (output_weight - WEIGHT_RATES[1] * output_back) * (
        1.0 - WEIGHT_RATES[1] * DECAY_RATE
    )
    expand_updated = (expand_weight - WEIGHT_RATES[2] * expand_back) * (
        1.0 - WEIGHT_RATES[2] * DECAY_RATE
    )
    shrink_updated = (shrink_weight - WEIGHT_RATES[3] * shrink_back) * (
        1.0 - WEIGHT_RATES[3] * DECAY_RATE
    )
    gains_updated = norm_gains - GAINS_RATE * gains_direction
    return (
        mixed,
        token_gradient,
        triple_gradient,
        output_gradient,
        expand_gradient,
        shrink_gradient,
        gains_gradient,
        triple_average,
        triple_variance,
        triple_updated,
        triple_updated.astype(jnp.bfloat16),
        output_average,
        output_variance,
        output_updated,
        output_updated.astype(jnp.bfloat16),
        expand_average,
        expand_variance,
        expand_updated,
        expand_updated.astype(jnp.bfloat16),
        shrink_average,
        shrink_variance,
        shrink_updated,
        shrink_updated.astype(jnp.bfloat16),
        gains_average,
        gains_variance,
        gains_updated,
    )


def solution(mesh):
    in_specs = (
        P(("outer", "core"), "seq", None),
        P(("outer", "core"), "seq", None),
        P(("outer", "core")),
        P("seq", ("outer", "core")),
        P("seq", ("outer", "core")),
        P("seq", ("outer", "core")),
        P(("outer", "core"), "seq"),
        P(),
        P(None, "seq", None),
        P(("outer", "core"), None),
        P("seq", ("outer", "core")),
        P("seq", ("outer", "core")),
        P("seq", ("outer", "core")),
        P("seq", ("outer", "core")),
        P("seq", ("outer", "core")),
        P("seq", ("outer", "core")),
        P(("outer", "core"), "seq"),
        P(("outer", "core"), "seq"),
        P(),
        P(),
    )
    out_specs = (
        P(("outer", "core"), "seq", None),
        P(("outer", "core"), "seq", None),
        P("seq", ("outer", "core")),
        P("seq", ("outer", "core")),
        P("seq", ("outer", "core")),
        P(("outer", "core"), "seq"),
        P(),
        P("seq", ("outer", "core")),
        P("seq", ("outer", "core")),
        P("seq", ("outer", "core")),
        P("seq", ("outer", "core")),
        P("seq", ("outer", "core")),
        P("seq", ("outer", "core")),
        P("seq", ("outer", "core")),
        P("seq", ("outer", "core")),
        P("seq", ("outer", "core")),
        P("seq", ("outer", "core")),
        P("seq", ("outer", "core")),
        P("seq", ("outer", "core")),
        P(("outer", "core"), "seq"),
        P(("outer", "core"), "seq"),
        P(("outer", "core"), "seq"),
        P(("outer", "core"), "seq"),
        P(),
        P(),
        P(),
    )
    groups = mesh.shape["fsdp"]
    devices = mesh.devices.reshape(mesh.shape["seq"], groups // 2, 2)
    split = Mesh(devices, ("seq", "outer", "core"))
    return jax.shard_map(body, mesh=split, in_specs=in_specs, out_specs=out_specs, check_vma=False)
```

```python
import functools
import math

import jax
import jax.numpy as jnp
from jax import lax
from jax.experimental import pallas as pl
from jax.experimental.pallas import tpu as pltpu
from jax.sharding import Mesh
from jax.sharding import PartitionSpec as P

HEADS = 16
HEAD_DIM = 64
FF = 2624
STEP = 10


ROPE_BASE = 160000.0
NORM_EPS = 1e-05
NEG_LARGE = -1e30
BETA_ONE = 0.95
BETA_TWO = 0.95
ADAM_EPS = 1e-08
DECAY_RATE = 0.01
WEIGHT_RATES = (0.03, 1.0, 0.03, 0.03)
GAINS_RATE = 0.8


def layer_norm(values, gain):
    centre = values - jnp.mean(values, axis=-1, keepdims=True)
    spread = jnp.mean(centre * centre, axis=-1, keepdims=True)
    return centre * lax.rsqrt(spread + NORM_EPS) * gain


def rotary_tables(position):
    halves = HEAD_DIM // 2
    frequency = ROPE_BASE ** (-2.0 * jnp.arange(halves, dtype=jnp.float32) / HEAD_DIM)
    angle = frequency[:, None] * position.astype(jnp.float32)[None, :]
    return jnp.cos(angle), jnp.sin(angle)


def outer_sum(left, right):
    return lax.dot_general(
        left, right, (((0,), (0,)), ((), ())), preferred_element_type=jnp.float32
    )


def back_product(left, right):
    return lax.dot_general(
        left, right, (((1,), (1,)), ((), ())), preferred_element_type=jnp.float32
    )


def plain_product(left, right):
    return jnp.dot(left, right, preferred_element_type=jnp.float32)


NT = (((1,), (1,)), ((), ()))
SAFE_BOUND = 60.0
MASK = -1e30
VMEM_LIMIT = 60 * 1024 * 1024


def extra_rows(rows, length, size=HEAD_DIM):
    place = lax.broadcasted_iota(jnp.int32, (size, length), 0)
    block = jnp.zeros((size, length), jnp.float32)
    for index, row in enumerate(rows):
        block = jnp.where(place == index, row, block)
    return block.astype(jnp.bfloat16)


def three_parts(row):
    high = row.astype(jnp.bfloat16).astype(jnp.float32)
    middle = (row - high).astype(jnp.bfloat16).astype(jnp.float32)
    return [high, middle, row - high - middle]


def mask_row(start, length, limit):
    place = start + lax.broadcasted_iota(jnp.int32, (1, length), 1)
    return jnp.where(place < limit, 0.0, MASK)


def project_kernel(pick_ref, pieces_ref, first_ref, cosine_ref, sine_ref, out_ref, rows_ref, *, group):
    shards, groups, size, _ = pieces_ref.shape
    cosine, sine = cosine_ref[...], sine_ref[...]
    half = HEAD_DIM // 2

    def chunk(part, head):
        start = (part * shards + head) * HEAD_DIM
        place = slice(start % size, start % size + HEAD_DIM)
        return jnp.concatenate(
            [pieces_ref[shard, start // size, place, :] for shard in range(shards)], axis=1
        )

    for begin in range(0, shards, group):
        heads = range(begin, begin + group)
        weight = jnp.concatenate([chunk(part, head) for head in heads for part in range(3)], axis=0)
        product = lax.dot_general(weight, first_ref[...], NT, preferred_element_type=jnp.float32)
        for index, head in enumerate(heads):
            for part in range(3):
                base = (3 * index + part) * HEAD_DIM
                rows_ref[head, part] = weight[base : base + HEAD_DIM]
            for part, scale in ((0, HEAD_DIM**-0.5), (1, 1.0)):
                base = (3 * index + part) * HEAD_DIM
                upper, lower = product[base : base + half], product[base + half : base + HEAD_DIM]
                turned_upper = (upper * cosine - lower * sine).astype(jnp.bfloat16)
                turned_lower = (lower * cosine + upper * sine).astype(jnp.bfloat16)
                place = part * HEAD_DIM
                scale = jnp.bfloat16(scale)
                out_ref[head, place : place + half, :] = turned_upper * scale
                out_ref[head, place + half : place + HEAD_DIM, :] = turned_lower * scale
            base = (3 * index + 2) * HEAD_DIM
            out_ref[head, 2 * HEAD_DIM :, :] = product[base : base + HEAD_DIM].astype(jnp.bfloat16)


def project_heads(pick, pieces, first, cosine, sine):
    shards, groups, _, size, lanes = pieces.shape
    count, width = first.shape
    half = HEAD_DIM // 2
    whole = lambda *shape: pl.BlockSpec(shape, lambda i, pick: (0,) * len(shape))
    return pl.pallas_call(
        functools.partial(project_kernel, group=min(4, shards)),
        grid_spec=pltpu.PrefetchScalarGridSpec(
            num_scalar_prefetch=1,
            grid=(1,),
            in_specs=[
                pl.BlockSpec(
                    (shards, groups, None, size, lanes), lambda i, pick: (0, 0, pick[0], 0, 0)
                ),
                whole(count, width),
                whole(half, count),
                whole(half, count),
            ],
            out_specs=[whole(shards, 3 * HEAD_DIM, count), whole(shards, 3, HEAD_DIM, width)],
        ),
        out_shape=[
            jax.ShapeDtypeStruct((shards, 3 * HEAD_DIM, count), jnp.bfloat16),
            jax.ShapeDtypeStruct((shards, 3, HEAD_DIM, width), jnp.bfloat16),
        ],
        compiler_params=pltpu.CompilerParams(vmem_limit_bytes=VMEM_LIMIT),
        cost_estimate=pl.CostEstimate(
            flops=6 * width * shards * HEAD_DIM * count,
            bytes_accessed=20 * width * shards * HEAD_DIM,
            transcendentals=0,
        ),
    )(pick, pieces, first, cosine, sine)


def forward_kernel(length_ref, joint_ref, out_ref, log_ref, key_ref, value_ref, peak_ref, bound_ref):
    index = pl.program_id(0)
    shards, _, local = joint_ref.shape
    limit = length_ref[0]
    ratio = max(1, 2048 // local)
    blocks = (limit + local - 1) // local

    @pl.when(index == 0)
    def prepare():
        query_most = jnp.zeros((1, 1), jnp.float32)
        key_most = jnp.zeros((1, 1), jnp.float32)
        for shard in range(shards):
            place = slice(shard * local, (shard + 1) * local)
            query = joint_ref[shard, :HEAD_DIM, :].astype(jnp.float32)
            key = joint_ref[shard, HEAD_DIM : 2 * HEAD_DIM, :]
            wide_key = key.astype(jnp.float32)
            query_size = jnp.sum(query * query, axis=0, keepdims=True)
            key_size = jnp.sum(wide_key * wide_key, axis=0, keepdims=True)
            query_most = jnp.maximum(query_most, jnp.max(query_size, axis=1, keepdims=True))
            key_most = jnp.maximum(key_most, jnp.max(key_size, axis=1, keepdims=True))
            extra = extra_rows([mask_row(shard * local, local, limit), 1.0], local)
            key_ref[place, :] = jnp.concatenate([key, extra], axis=0).T
            value_ref[:HEAD_DIM, place] = joint_ref[shard, 2 * HEAD_DIM :, :]
            value_ref[HEAD_DIM:, place] = extra_rows([1.0], local, 16)
        bound_ref[0] = (jnp.sqrt(query_most) * jnp.sqrt(key_most))[0, 0]

    @pl.when(index >= blocks)
    def padding():
        out_ref[...] = jnp.zeros_like(out_ref)
        log_ref[...] = jnp.zeros_like(log_ref)

    @pl.when(index < blocks)
    def compute():
        query = joint_ref[index, :HEAD_DIM, :]
        peak_ref[...] = jnp.zeros_like(peak_ref)

        @pl.when(bound_ref[0] > SAFE_BOUND)
        def find_peak():
            plain = jnp.concatenate([query, extra_rows([1.0], local)], axis=0)

            def step(block, peak):
                place = pl.ds(pl.multiple_of(block * local, local), local)
                scores = jnp.dot(key_ref[place, :], plain, preferred_element_type=jnp.float32)
                return jnp.maximum(peak, jnp.max(scores, axis=0, keepdims=True))

            peak = lax.fori_loop(0, blocks, step, jnp.full((1, local), MASK, jnp.float32))
            peak_ref[...] = peak.astype(jnp.bfloat16).astype(jnp.float32)

        peak = peak_ref[...]
        augmented = jnp.concatenate([query, extra_rows([1.0, -peak], local)], axis=0)

        def attend(start, size, total):
            place = pl.ds(pl.multiple_of(start, local), size)
            scores = jnp.dot(key_ref[place, :], augmented, preferred_element_type=jnp.float32)
            weights = jnp.exp(scores).astype(jnp.bfloat16)
            return total + jnp.dot(
                value_ref[:, place], weights, preferred_element_type=jnp.float32
            )

        large = blocks // ratio
        total = lax.fori_loop(
            0,
            large,
            lambda block, total: attend(block * (ratio * local), ratio * local, total),
            jnp.zeros((HEAD_DIM + 16, local), jnp.float32),
        )
        total = lax.fori_loop(
            large * ratio, blocks, lambda block, total: attend(block * local, local, total), total
        )
        mass = total[HEAD_DIM : HEAD_DIM + 1, :]
        out_ref[0] = (total[:HEAD_DIM, :] / mass).astype(jnp.bfloat16)
        log_ref[0] = peak + jnp.log(mass)


def attend_forward(length, joint):
    shards, _, local = joint.shape
    total = shards * local
    return pl.pallas_call(
        forward_kernel,
        grid=(shards,),
        in_specs=[
            pl.BlockSpec(memory_space=pltpu.SMEM),
            pl.BlockSpec((shards, 3 * HEAD_DIM, local), lambda i: (0, 0, 0)),
        ],
        out_specs=[
            pl.BlockSpec((1, HEAD_DIM, local), lambda i: (i, 0, 0)),
            pl.BlockSpec((1, 1, local), lambda i: (i, 0, 0)),
        ],
        out_shape=[
            jax.ShapeDtypeStruct((shards, HEAD_DIM, local), jnp.bfloat16),
            jax.ShapeDtypeStruct((shards, 1, local), jnp.float32),
        ],
        scratch_shapes=[
            pltpu.VMEM((total, 2 * HEAD_DIM), jnp.bfloat16),
            pltpu.VMEM((HEAD_DIM + 16, total), jnp.bfloat16),
            pltpu.VMEM((1, local), jnp.float32),
            pltpu.SMEM((1,), jnp.float32),
        ],
        compiler_params=pltpu.CompilerParams(vmem_limit_bytes=VMEM_LIMIT),
        cost_estimate=pl.CostEstimate(
            flops=total * total,
            bytes_accessed=HEAD_DIM * total,
            transcendentals=0,
        ),
    )(length, joint)


def backward_kernel(
    length_ref,
    joint_ref,
    back_ref,
    out_ref,
    log_ref,
    cosine_ref,
    sine_ref,
    grad_ref,
    query_ref,
    wide_ref,
    query_flat,
    back_flat,
    query_sum,
):
    index = pl.program_id(0)
    shards, _, local = joint_ref.shape
    limit = length_ref[0]
    ratio = max(1, 2048 // local)
    blocks = (limit + local - 1) // local
    half = HEAD_DIM // 2

    def turned_back(wide, shard):
        cosine, sine = cosine_ref[shard], sine_ref[shard]
        upper, lower = wide[:half], wide[half:]
        return jnp.concatenate(
            [upper * cosine + lower * sine, lower * cosine - upper * sine], axis=0
        ).astype(jnp.bfloat16)

    @pl.when(index == 0)
    def prepare():
        for shard in range(shards):
            place = slice(shard * local, (shard + 1) * local)
            query = joint_ref[shard, :HEAD_DIM, :]
            back = back_ref[shard]
            extra = extra_rows([1.0] + three_parts(-log_ref[shard]), local)
            query_ref[place, :] = jnp.concatenate([query, extra], axis=0).T
            balance = jnp.sum(
                back.astype(jnp.float32) * out_ref[shard].astype(jnp.float32),
                axis=0,
                keepdims=True,
            )
            extra = extra_rows(three_parts(-balance), local)
            wide_ref[place, :] = jnp.concatenate([back, extra], axis=0).T
            query_flat[:, place] = query
            back_flat[:, place] = back
        query_sum[...] = jnp.zeros_like(query_sum)

    @pl.when(index >= blocks)
    def padding():
        grad_ref[index, HEAD_DIM:, :] = jnp.zeros((2 * HEAD_DIM, local), jnp.bfloat16)

    @pl.when(index < blocks)
    def compute():
        key = joint_ref[index, HEAD_DIM : 2 * HEAD_DIM, :]
        value = joint_ref[index, 2 * HEAD_DIM :, :]
        mask = mask_row(index * local, local, limit)
        wide_key = jnp.concatenate([key, extra_rows([mask, 1.0, 1.0, 1.0], local)], axis=0)
        wide_value = jnp.concatenate([value, extra_rows([1.0, 1.0, 1.0], local)], axis=0)

        def gather(start, size, carry):
            key_sum, value_sum = carry
            place = pl.ds(pl.multiple_of(start, local), size)
            scores = jnp.dot(query_ref[place, :], wide_key, preferred_element_type=jnp.float32)
            chance = jnp.exp(scores)
            change = jnp.dot(wide_ref[place, :], wide_value, preferred_element_type=jnp.float32)
            chance_low = chance.astype(jnp.bfloat16)
            score_back = (chance * change).astype(jnp.bfloat16)
            value_sum = value_sum + jnp.dot(
                back_flat[:, place], chance_low, preferred_element_type=jnp.float32
            )
            key_sum = key_sum + jnp.dot(
                query_flat[:, place], score_back, preferred_element_type=jnp.float32
            )
            query_sum[:, place] += lax.dot_general(
                key, score_back, NT, preferred_element_type=jnp.float32
            )
            return (key_sum, value_sum)

        large = blocks // ratio
        zero = jnp.zeros((HEAD_DIM, local), jnp.float32)
        carry = lax.fori_loop(
            0,
            large,
            lambda block, carry: gather(block * (ratio * local), ratio * local, carry),
            (zero, zero),
        )
        key_sum, value_sum = lax.fori_loop(
            large * ratio, blocks, lambda block, carry: gather(block * local, local, carry), carry
        )
        grad_ref[index, HEAD_DIM : 2 * HEAD_DIM, :] = turned_back(key_sum, index)
        grad_ref[index, 2 * HEAD_DIM :, :] = value_sum.astype(jnp.bfloat16)

    @pl.when(index == shards - 1)
    def finish():
        for shard in range(shards):
            place = slice(shard * local, (shard + 1) * local)
            grad_ref[shard, :HEAD_DIM, :] = turned_back(
                query_sum[:, place] * HEAD_DIM**-0.5, shard
            )


def attend_backward(length, joint, back, attend, log_mass, cosine, sine):
    shards, _, local = joint.shape
    total = shards * local
    whole = lambda rows: pl.BlockSpec((shards, rows, local), lambda i: (0, 0, 0))
    return pl.pallas_call(
        backward_kernel,
        grid=(shards,),
        in_specs=[
            pl.BlockSpec(memory_space=pltpu.SMEM),
            whole(3 * HEAD_DIM),
            whole(HEAD_DIM),
            whole(HEAD_DIM),
            whole(1),
            whole(HEAD_DIM // 2),
            whole(HEAD_DIM // 2),
        ],
        out_specs=whole(3 * HEAD_DIM),
        out_shape=jax.ShapeDtypeStruct((shards, 3 * HEAD_DIM, local), jnp.bfloat16),
        scratch_shapes=[
            pltpu.VMEM((total, 2 * HEAD_DIM), jnp.bfloat16),
            pltpu.VMEM((total, 2 * HEAD_DIM), jnp.bfloat16),
            pltpu.VMEM((HEAD_DIM, total), jnp.bfloat16),
            pltpu.VMEM((HEAD_DIM, total), jnp.bfloat16),
            pltpu.VMEM((HEAD_DIM, total), jnp.float32),
        ],
        compiler_params=pltpu.CompilerParams(vmem_limit_bytes=VMEM_LIMIT),
        cost_estimate=pl.CostEstimate(
            flops=total * total,
            bytes_accessed=HEAD_DIM * total,
            transcendentals=0,
        ),
    )(length, joint, back, attend, log_mass, cosine, sine)


TN = (((0,), (0,)), ((), ()))
PLAIN = (((1,), (0,)), ((), ()))
LANES = 128
GROUPS = 4
RUNS = 8
UNITS = FF // GROUPS
EXPAND_RUN = -(-2 * UNITS // (16 * RUNS)) * 16
SHRINK_RUN = -(-UNITS // (16 * RUNS)) * 16


def run_segments(start, stop, run):
    segments = []
    while start < stop:
        index = start // run
        end = min(stop, (index + 1) * run)
        segments.append((index, start - index * run, start, end - start))
        start = end
    return segments


def feed_kernel(
    second_ref,
    upstream_ref,
    active_ref,
    gate_ref,
    shrink_ref,
    shrunk_ref,
    second_back_ref,
    parts_ref,
    grads_ref,
    zero_ref,
    send_ref,
    zero_send_ref,
):
    index = pl.program_id(0)

    def joined(ref):
        return jnp.concatenate([ref[piece, 0] for piece in range(ref.shape[0])], axis=1)

    def product(left, right, dims):
        return lax.dot_general(left, right, dims, preferred_element_type=jnp.float32)

    def grad_copies(half, pair):
        moves = []
        for kind, member in ((0, pair), (1, pair + 2)):
            for run, place, offset, size in run_segments(
                half * UNITS, (half + 1) * UNITS, EXPAND_RUN
            ):
                moves.append((kind, offset - half * UNITS, run, member, place, size))
        for run, place, offset, size in run_segments(0, UNITS, SHRINK_RUN):
            moves.append((2, offset, run, 2 * pair + half, EXPAND_RUN + place, size))
        return [
            pltpu.make_async_copy(
                grads_ref.at[half, kind, pl.ds(offset, size), :],
                parts_ref.at[run, member, pl.ds(place, size), :],
                send_ref.at[half, number],
            )
            for number, (kind, offset, run, member, place, size) in enumerate(moves)
        ]

    def zero_copies():
        moves = []
        for member in range(GROUPS):
            for base, run_size, total in ((0, EXPAND_RUN, 2 * UNITS), (EXPAND_RUN, SHRINK_RUN, UNITS)):
                for run, place, _, size in run_segments(total, RUNS * run_size, run_size):
                    moves.append((run, member, base + place, size))
        return [
            pltpu.make_async_copy(
                zero_ref.at[pl.ds(0, size), :],
                parts_ref.at[run, member, pl.ds(place, size), :],
                zero_send_ref.at[number],
            )
            for number, (run, member, place, size) in enumerate(moves)
        ]

    @pl.when(index == 0)
    def fill():
        zero_ref[...] = jnp.zeros_like(zero_ref)
        for copy in zero_copies():
            copy.start()

    active, gate, shrink = joined(active_ref), joined(gate_ref), joined(shrink_ref)
    second, upstream = second_ref[...], upstream_ref[...]
    input_active = product(second, active, NT)
    input_gate = product(second, gate, NT)
    hidden_back = product(upstream, shrink, NT)
    below = 0.5 + 0.5 * lax.erf(input_active * 0.5**0.5)
    bell = jnp.exp(-0.5 * input_active * input_active) * (0.5 / math.pi) ** 0.5
    curve = input_active * below
    hidden = (curve * input_gate).astype(jnp.bfloat16)
    active_back = (hidden_back * input_gate * (below + input_active * bell)).astype(jnp.bfloat16)
    gate_back = (hidden_back * curve).astype(jnp.bfloat16)
    shrunk = product(hidden, shrink, PLAIN)
    second_back = product(active_back, active, PLAIN) + product(gate_back, gate, PLAIN)

    @pl.when(index == 0)
    def begin():
        shrunk_ref[...] = shrunk
        second_back_ref[...] = second_back

    @pl.when(index > 0)
    def add():
        shrunk_ref[...] += shrunk
        second_back_ref[...] += second_back

    for half in range(2):

        @pl.when(index % 2 == half)
        def send(half=half):
            pair = index // 2

            @pl.when(index >= 2)
            def free():
                for copy in grad_copies(half, pair - 1):
                    copy.wait()

            grads_ref[half, 0] = product(active_back, second, TN).astype(jnp.bfloat16)
            grads_ref[half, 1] = product(gate_back, second, TN).astype(jnp.bfloat16)
            grads_ref[half, 2] = product(hidden, upstream, TN).astype(jnp.bfloat16)
            for copy in grad_copies(half, pair):
                copy.start()

    @pl.when(index == GROUPS - 1)
    def drain():
        for half in range(2):
            for copy in grad_copies(half, 1):
                copy.wait()
        for copy in zero_copies():
            copy.wait()


def feed_forward(second, upstream, pieces):
    count, width = second.shape
    block = (RUNS, 1, UNITS, LANES)
    held = pl.BlockSpec((count, width), lambda i: (0, 0), pipeline_mode=pl.Buffered(1))
    wide = jax.ShapeDtypeStruct((count, width), jnp.float32)
    run = EXPAND_RUN + SHRINK_RUN
    copies = max(
        2 * len(run_segments(half * UNITS, (half + 1) * UNITS, EXPAND_RUN)) for half in range(2)
    ) + len(run_segments(0, UNITS, SHRINK_RUN))
    return pl.pallas_call(
        feed_kernel,
        grid=(GROUPS,),
        in_specs=[
            held,
            held,
            pl.BlockSpec(block, lambda i: (0, i // 2, i % 2, 0)),
            pl.BlockSpec(block, lambda i: (0, i // 2 + 2, i % 2, 0)),
            pl.BlockSpec(block, lambda i: (0, i, 2, 0)),
        ],
        out_specs=[held, held, pl.BlockSpec(memory_space=pl.ANY)],
        out_shape=[wide, wide, jax.ShapeDtypeStruct((RUNS, GROUPS, run, width), jnp.bfloat16)],
        scratch_shapes=[
            pltpu.VMEM((2, 3, UNITS, width), jnp.bfloat16),
            pltpu.VMEM((max(EXPAND_RUN, SHRINK_RUN), width), jnp.bfloat16),
            pltpu.SemaphoreType.DMA((2, copies)),
            pltpu.SemaphoreType.DMA((GROUPS * 8,)),
        ],
        compiler_params=pltpu.CompilerParams(vmem_limit_bytes=VMEM_LIMIT),
        cost_estimate=pl.CostEstimate(
            flops=count * width,
            bytes_accessed=count * width,
            transcendentals=0,
        ),
    )(second, upstream, pieces, pieces, pieces)


def enter_slots(
    attend_refs,
    weight_refs,
    limit_ref,
    token_ref,
    cotangent_ref,
    gain_ref,
    middle_ref,
    normal_ref,
    second_ref,
    upstream_ref,
    spread_ref,
):
    middle = token_ref[...].astype(jnp.float32)
    for attend_ref, weight_ref in zip(attend_refs, weight_refs):
        middle += lax.dot_general(
            attend_ref[...], weight_ref[...], TN, preferred_element_type=jnp.float32
        )
    block = middle.shape[0]
    centre = middle - jnp.mean(middle, axis=1, keepdims=True)
    scale = lax.rsqrt(jnp.mean(centre * centre, axis=1, keepdims=True) + NORM_EPS)
    normal = centre * scale
    place = pl.program_id(0) * block + lax.broadcasted_iota(jnp.int32, (block, 1), 0)
    middle_ref[...] = middle
    normal_ref[...] = normal
    spread_ref[...] = scale
    second_ref[...] = (normal * gain_ref[1:2, :]).astype(jnp.bfloat16)
    upstream_ref[...] = jnp.where(place < limit_ref[0], cotangent_ref[...], jnp.bfloat16(0.0))


def enter_kernel(*refs, split):
    enter_slots(refs[:split], refs[split : 2 * split], *refs[2 * split :])


def enter_pieces_kernel(*refs, split, start):
    attend_refs, pieces_ref = refs[:split], refs[split]
    weight_refs, (held_ref, arrived_ref) = refs[-2 - split : -2], refs[-2:]
    shards, groups, rows, lanes = held_ref.shape
    piece = split * HEAD_DIM

    @pl.when(pl.program_id(0) == 0)
    def lay_out():
        copy = pltpu.make_async_copy(
            pieces_ref.at[:, :, pl.ds(start, rows), :], held_ref, arrived_ref
        )
        copy.start()
        copy.wait()
        for head, weight_ref in enumerate(weight_refs):
            for shard in range(shards):
                parts = [
                    held_ref[shard, group, first : first + HEAD_DIM, :]
                    for group in range(groups)
                    for first in range(head * HEAD_DIM, rows, piece)
                ]
                place = slice(shard * HEAD_DIM, (shard + 1) * HEAD_DIM)
                weight_ref[place, :] = jnp.concatenate(parts, axis=1)

    enter_slots(attend_refs, weight_refs, *refs[split + 1 : -2 - split])


def enter_feed(attends, weights, pieces, start, limit, tokens, cotangent, gains):
    split = len(attends)
    count, width = tokens.shape
    block = min(256, count)
    rows = pl.BlockSpec((block, width), lambda i: (i, 0))
    wide = jax.ShapeDtypeStruct((count, width), jnp.float32)
    low = jax.ShapeDtypeStruct((count, width), jnp.bfloat16)
    whole = lambda *shape: pl.BlockSpec(shape, lambda i: (0,) * len(shape))
    attend_specs = [pl.BlockSpec((attend.shape[0], block), lambda i: (0, i)) for attend in attends]
    slot_specs = [pl.BlockSpec(memory_space=pltpu.SMEM), rows, rows, whole(*gains.shape)]
    out_specs = [rows, rows, rows, rows, pl.BlockSpec((block, 1), lambda i: (i, 0))]
    out_shape = [wide, wide, low, low, jax.ShapeDtypeStruct((count, 1), jnp.float32)]
    options = dict(
        grid=(count // block,),
        compiler_params=pltpu.CompilerParams(vmem_limit_bytes=VMEM_LIMIT),
        cost_estimate=pl.CostEstimate(
            flops=2 * count * width * width, bytes_accessed=20 * count * width, transcendentals=0
        ),
    )
    if weights is not None:
        results = pl.pallas_call(
            functools.partial(enter_kernel, split=split),
            in_specs=attend_specs + [whole(*weight.shape) for weight in weights] + slot_specs,
            out_specs=out_specs,
            out_shape=out_shape,
            **options,
        )(*attends, *weights, limit, tokens, cotangent, gains)
        return list(results) + list(weights)
    depth = attends[0].shape[0]
    return pl.pallas_call(
        functools.partial(enter_pieces_kernel, split=split, start=start),
        in_specs=attend_specs + [pl.BlockSpec(memory_space=pl.ANY)] + slot_specs,
        out_specs=out_specs + [whole(depth, width)] * split,
        out_shape=out_shape + [jax.ShapeDtypeStruct((depth, width), jnp.bfloat16)] * split,
        scratch_shapes=[
            pltpu.VMEM(pieces.shape[:2] + (pieces.shape[2] - start, pieces.shape[3]), jnp.bfloat16),
            pltpu.SemaphoreType.DMA(()),
        ],
        **options,
    )(*attends, pieces, limit, tokens, cotangent, gains)


def leave_kernel(*refs):
    phases = (len(refs) - 12) // 2
    weight_refs, back_refs = refs[:phases], refs[-phases:]
    limit_ref, shrunk_ref, change_ref, middle_ref, normal_ref, spread_ref = refs[phases : phases + 6]
    upstream_ref, gain_ref = refs[phases + 6 : phases + 8]
    mixed_ref, middle_back_ref, branch_ref, gain_grad_ref = refs[phases + 8 : phases + 12]
    index = pl.program_id(0)
    block = mixed_ref.shape[0]
    place = index * block + lax.broadcasted_iota(jnp.int32, (block, 1), 0)
    mixed = middle_ref[...] + shrunk_ref[...]
    mixed_ref[...] = jnp.where(place < limit_ref[0], mixed, 0.0).astype(jnp.bfloat16)
    change, normal = change_ref[...], normal_ref[...]
    gain_grad = jnp.sum(change * normal, axis=0, keepdims=True)

    @pl.when(index == 0)
    def begin():
        gain_grad_ref[...] = gain_grad

    @pl.when(index > 0)
    def add():
        gain_grad_ref[...] += gain_grad

    inner = change * gain_ref[1:2, :]
    inner = (
        inner
        - jnp.mean(inner, axis=1, keepdims=True)
        - normal * jnp.mean(inner * normal, axis=1, keepdims=True)
    )
    middle_back = upstream_ref[...].astype(jnp.float32) + spread_ref[...] * inner
    branch = middle_back.astype(jnp.bfloat16)
    middle_back_ref[...] = middle_back
    branch_ref[...] = branch
    for weight_ref, back_ref in zip(weight_refs, back_refs):
        back_ref[...] = lax.dot_general(
            weight_ref[...], branch, NT, preferred_element_type=jnp.float32
        ).astype(jnp.bfloat16)


def leave_feed(weights, limit, shrunk, change, middle, normal, spread, upstream, gains):
    count, width = shrunk.shape
    block = min(256, count)
    rows = pl.BlockSpec((block, width), lambda i: (i, 0))
    wide = jax.ShapeDtypeStruct((count, width), jnp.float32)
    low = jax.ShapeDtypeStruct((count, width), jnp.bfloat16)
    return pl.pallas_call(
        leave_kernel,
        grid=(count // block,),
        in_specs=[pl.BlockSpec(weight.shape, lambda i: (0, 0)) for weight in weights]
        + [pl.BlockSpec(memory_space=pltpu.SMEM), rows, rows, rows, rows]
        + [pl.BlockSpec((block, 1), lambda i: (i, 0)), rows]
        + [pl.BlockSpec(gains.shape, lambda i: (0, 0))],
        out_specs=[rows, rows, rows, pl.BlockSpec((1, width), lambda i: (0, 0))]
        + [pl.BlockSpec((weight.shape[0], block), lambda i: (0, i)) for weight in weights],
        out_shape=[low, wide, low, jax.ShapeDtypeStruct((1, width), jnp.float32)]
        + [jax.ShapeDtypeStruct((weight.shape[0], count), jnp.bfloat16) for weight in weights],
        compiler_params=pltpu.CompilerParams(vmem_limit_bytes=VMEM_LIMIT),
        cost_estimate=pl.CostEstimate(
            flops=2 * count * width * width, bytes_accessed=28 * count * width, transcendentals=0
        ),
    )(*weights, limit, shrunk, change, middle, normal, spread, upstream, gains)


def adam_step(rotated, first, second):
    average = BETA_ONE * first + (1.0 - BETA_ONE) * rotated
    variance = BETA_TWO * second + (1.0 - BETA_TWO) * rotated * rotated
    direction = (
        average / (1.0 - BETA_ONE**STEP) / (jnp.sqrt(variance / (1.0 - BETA_TWO**STEP)) + ADAM_EPS)
    )
    return (average, variance, direction)


def body(
    tokens,
    cotangent,
    lengths,
    triple_weight,
    output_weight,
    expand_weight,
    shrink_weight,
    norm_gains,
    side_bases,
    output_right,
    triple_first,
    triple_second,
    output_first,
    output_second,
    expand_first,
    expand_second,
    shrink_first,
    shrink_second,
    gains_first,
    gains_second,
):
    rows_here, local_len, width = tokens.shape
    count = rows_here * local_len
    shards = lax.axis_size("seq")
    groups = lax.axis_size("outer") * lax.axis_size("core")
    split = HEADS // shards
    core = lax.axis_index("core")
    swap = functools.partial(lax.ppermute, axis_name="core", perm=[(0, 1), (1, 0)])
    other_lengths = swap(lengths)
    ahead = (lengths > other_lengths) | ((lengths == other_lengths) & (core == 0))

    def by_length(own, other):
        return [jnp.where(ahead[0], own, other), jnp.where(ahead[0], other, own)]

    def by_core(mine, other):
        return [jnp.where(core == 0, mine, other), jnp.where(core == 0, other, mine)]

    def both_rows(own):
        return by_length(own, swap(own)) if split == 2 else [own]

    piece = width // shards
    fsdp = ("outer", "core")
    everyone = ("seq",) + fsdp
    offset = lax.axis_index("seq") * local_len
    position = offset + jnp.arange(local_len, dtype=jnp.int32)
    cosine, sine = rotary_tables(position)
    every = jnp.arange(shards * local_len, dtype=jnp.int32)
    all_cosine, all_sine = (
        table.reshape(HEAD_DIM // 2, shards, local_len).transpose(1, 0, 2)
        for table in rotary_tables(every)
    )
    valid = (position[None, :] < lengths[:, None]).astype(jnp.float32).reshape(count, 1)
    exchange = functools.partial(lax.all_to_all, axis_name="seq", split_axis=0, concat_axis=0)

    def tied(*values):
        return lax.optimization_barrier(values)

    def gathered(shard):
        flat = lax.all_gather(shard, everyone, axis=0, tiled=False)
        return flat.reshape((shards, groups) + shard.shape)

    triple_shards = (
        triple_weight.T.astype(jnp.bfloat16)
        .reshape(-1, split, HEAD_DIM, piece)
        .transpose(1, 0, 2, 3)
        .reshape(split, -1, piece)
    )
    triple_pieces = gathered(triple_shards)
    all_cosine, all_sine, triple_pieces = tied(all_cosine, all_sine, triple_pieces)
    output_columns = width // groups
    lanes = min(piece, output_columns)

    def fold(block):
        rows = block.shape[0]
        return block.reshape(rows, -1, lanes).transpose(1, 0, 2).reshape(-1, lanes)

    bases_low = side_bases.astype(jnp.bfloat16)
    right_low = output_right.astype(jnp.bfloat16)
    member = lax.axis_index("outer") * lax.axis_size("core") + lax.axis_index("core")
    base_rows = piece // groups
    flat = tokens.reshape(count, width).astype(jnp.float32)
    first_normed, first_back = jax.vjp(layer_norm, flat, norm_gains[0])
    first_low = first_normed.astype(jnp.bfloat16)
    other_shards = jnp.concatenate(
        [
            expand_weight.T.astype(jnp.bfloat16),
            shrink_weight.astype(jnp.bfloat16),
            fold(output_weight.astype(jnp.bfloat16)),
        ],
        axis=0,
    )
    firsts = both_rows(first_low)
    pick = jnp.where(split == 2, core, 0).reshape(1)
    projected = [project_heads(pick, triple_pieces, first, cosine, sine) for first in firsts]
    triple_rows = projected[0][1].reshape(-1, width)
    joints = [exchange(joint) for joint, _ in projected]
    other_shards, joints[0] = tied(other_shards, joints[0])
    other_pieces = gathered(other_shards)
    chosen = jnp.stack([bases_low[0], bases_low[2], bases_low[3]])
    chosen = lax.dynamic_slice_in_dim(chosen, member * base_rows, base_rows, 1)
    expand_rows = 2 * FF // groups
    shrink_rows = FF // groups
    canonical = (shards, groups, piece) == (RUNS, GROUPS, LANES)
    if canonical:
        feed_pieces, output_rows = other_pieces, None
    else:
        output_pieces = other_pieces[:, :, expand_rows + shrink_rows :].reshape(
            shards, groups, output_columns // lanes, split, HEAD_DIM, lanes
        )
        output_rows = [
            output_pieces[:, :, :, head].transpose(0, 3, 1, 2, 4).reshape(shards * HEAD_DIM, width)
            for head in range(split)
        ]
        feed_pieces = [
            other_pieces[:, :, start:end]
            .transpose(1, 2, 0, 3)
            .reshape(GROUPS, -1, RUNS, LANES)
            .transpose(2, 0, 1, 3)
            for start, end in ((0, expand_rows), (expand_rows, expand_rows + shrink_rows))
        ]
        feed_pieces = jnp.concatenate(feed_pieces, axis=2)
    row_lengths = both_rows(lengths)
    forwards, attends = [], []
    for row, joint in enumerate(joints):
        outcome = attend_forward(row_lengths[row], joint)
        if row:
            attends[-1], outcome = tied(attends[-1], outcome)
        if row < split - 1:
            joints[row + 1], outcome = tied(joints[row + 1], outcome)
        forwards.append(outcome)
        attends.append(exchange(outcome[0]))
    chosen, forwards[-1] = tied(chosen, forwards[-1])
    bases_full = gathered(chosen)
    attends = [attend.reshape(shards * HEAD_DIM, count) for attend in attends]
    if split == 2:
        own, other = by_length(*attends)
        attends = by_core(own, swap(other))
    expand_height = -(-expand_rows // (16 * shards)) * 16
    shrink_height = -(-shrink_rows // (16 * shards)) * 16

    def to_rows(block):
        block = exchange(block)
        return block.transpose(1, 0, 2).reshape(block.shape[1], -1)

    def padded(block, height):
        block = jnp.pad(block, ((0, height * shards - block.shape[0]), (0, 0)))
        return block.reshape(shards, height, piece)

    def by_heads(block):
        return (
            block.reshape(-1, split, HEAD_DIM, piece)
            .transpose(1, 0, 2, 3)
            .reshape(split, shards, -1, piece)
        )

    def from_heads(blocks):
        block = jnp.stack(blocks).astype(jnp.float32).reshape(split, -1, HEAD_DIM, piece)
        return block.transpose(1, 0, 2, 3).reshape(-1, piece)

    moments = []
    for expand, shrink, triple in (
        (expand_first, shrink_first, triple_first),
        (expand_second, shrink_second, triple_second),
    ):
        moments += [padded(expand.T, expand_height), padded(shrink, shrink_height)]
        moments += list(by_heads(triple.T))
    moments, attends[-1], feed_pieces = tied(moments, attends[-1], feed_pieces)
    heights = [moment.shape[1] for moment in moments]
    moments = to_rows(jnp.concatenate(moments, axis=1))
    edges = [sum(heights[:index]) for index in range(len(heights) + 1)]
    moments = [moments[start:end] for start, end in zip(edges, edges[1:])]
    moments = list(zip(moments[: split + 2], moments[split + 2 :]))
    inside = jnp.clip(lengths - offset, 0, local_len)
    middle, second_normal, second_low, upstream_low, second_spread, *output_rows = enter_feed(
        attends,
        output_rows,
        feed_pieces,
        expand_rows + shrink_rows,
        inside,
        tokens.reshape(count, width),
        cotangent.reshape(count, width),
        norm_gains,
    )
    shrunk, second_change, parts = feed_forward(second_low, upstream_low, feed_pieces)
    moments, bases_full, shrunk, second_change, parts = tied(
        moments, bases_full, shrunk, second_change, parts
    )
    mixed, middle_back, branch_low, second_gain, *backs = leave_feed(
        output_rows,
        inside,
        shrunk,
        second_change,
        middle,
        second_normal,
        second_spread,
        upstream_low,
        norm_gains,
    )
    mixed = mixed.reshape(tokens.shape)
    second_gain = second_gain[0]
    backs = [back.reshape(shards, HEAD_DIM, count) for back in backs]
    if split == 2:
        mine, other = by_core(*backs)
        backs = by_length(mine, swap(other))
    order = list(range(split))[::-1]
    attend_backs = [exchange(back) for back in backs]

    def halved(blocks, axis, dim):
        size = lax.axis_size(axis)
        place = lax.axis_index(axis)
        while size > 1:
            size //= 2
            shape = blocks.shape
            blocks = blocks.reshape(shape[:dim] + (2, size) + shape[dim + 1 :])
            side = (place // size) % 2
            mine = lax.dynamic_index_in_dim(blocks, side, dim, keepdims=False)
            other = lax.dynamic_index_in_dim(blocks, 1 - side, dim, keepdims=False)
            pairs = [(member, member ^ size) for member in range(lax.axis_size(axis))]
            other = lax.ppermute(other, axis, pairs)
            blocks = (mine.astype(jnp.float32) + other.astype(jnp.float32)).astype(jnp.bfloat16)
        return jnp.squeeze(blocks, dim)

    def doubled(block, axis):
        size = lax.axis_size(axis)
        place = lax.axis_index(axis)
        shape = block.shape
        step, done = size // 2, 0
        while step:
            pairs = [(member, member ^ step) for member in range(size)]
            other = lax.ppermute(block, axis, pairs)
            upper = (place // step) % 2 == 1
            block = jnp.stack(
                [jnp.where(upper, other, block), jnp.where(upper, block, other)], axis=done
            )
            step //= 2
            done += 1
        return block.reshape((size,) + shape)

    def near_sum(blocks):
        return halved(halved(blocks, "core", 1), "outer", 0)

    def merged(*blocks):
        sizes = [math.prod(block.shape[1:]) for block in blocks]
        flat = [block.reshape(shards, -1, piece) for block in blocks]
        flat = exchange(jnp.concatenate(flat, axis=1))
        results, start = [], 0
        for block, size in zip(blocks, sizes):
            rows = size // piece
            results.append(flat[:, start : start + rows].reshape(block.shape))
            start += rows
        return results

    def widened(block):
        rows = piece * output_columns // count
        block = block.reshape(-1, piece // rows, rows, output_columns)
        return block.swapaxes(1, 2).reshape(shards, -1, count)

    def narrowed(block):
        rows = piece * output_columns // count
        block = block.reshape(-1, rows, piece // rows, output_columns)
        return block.swapaxes(1, 2).reshape(shards, -1, piece, output_columns)

    def far_sum(terms):
        return jnp.sum(terms.astype(jnp.float32), axis=0).astype(jnp.bfloat16)

    def cut_rows(rows):
        return rows.reshape(rows.shape[0], shards, piece).transpose(1, 0, 2)

    outer = lax.axis_size("outer")
    output_part = jnp.stack(
        [
            jnp.dot(attend, branch_low, preferred_element_type=jnp.float32)
            .astype(jnp.bfloat16)
            .reshape(shards, HEAD_DIM, width)
            for attend in attends
        ],
        axis=1,
    )
    output_terms = halved(
        output_part.reshape(shards, piece, outer, -1, output_columns).transpose(0, 2, 3, 1, 4),
        "core",
        2,
    )
    output_terms = widened(output_terms)
    parts, output_terms, attend_backs[order[0]] = tied(
        parts, output_terms, attend_backs[order[0]]
    )

    def cut(product, height):
        block = product.reshape(groups, -1, width)
        block = jnp.pad(block, ((0, 0), (0, height * shards - block.shape[1]), (0, 0)))
        return block.reshape(groups, shards, height, width)

    if not canonical:
        parts = parts.transpose(1, 0, 2, 3)
        parts = [
            cut(block.reshape(GROUPS, -1, width)[:, : size // GROUPS], height)
            for block, size, height in (
                (parts[:, :, :EXPAND_RUN], 2 * FF, expand_height),
                (parts[:, :, EXPAND_RUN:], FF, shrink_height),
            )
        ]
        parts = jnp.concatenate(parts, axis=2).transpose(1, 0, 2, 3)
    parts = parts.reshape(shards * groups, -1, width)
    owned = lax.psum_scatter(parts, everyone, scatter_dimension=0, tiled=False)
    feed_height = expand_height + shrink_height

    def soap_rows(rows, base, moment):
        rotated = plain_product(rows, base)
        direction = adam_step(rotated, *moment)[2]
        step = back_product(direction.astype(jnp.bfloat16), base)
        return rotated.astype(jnp.bfloat16), step.astype(jnp.bfloat16)

    grads = [None] * split
    for step, row in enumerate(order):
        grad = attend_backward(
            row_lengths[row],
            joints[row],
            attend_backs[row],
            *forwards[row],
            all_cosine,
            all_sine,
        )
        if step < split - 1:
            following = order[step + 1]
            attend_backs[following], grad = tied(attend_backs[following], grad)
        else:
            grads, owned, bases_full, grad = tied(grads, owned, bases_full, grad)
        if step == 0:
            grad = jnp.concatenate([grad, output_terms], axis=1)
        grads[row] = exchange(grad)
    output_low = halved(far_sum(narrowed(grads[order[0]][:, 3 * HEAD_DIM :])), "outer", 0)
    joint_backs = [grad[:, : 3 * HEAD_DIM].reshape(-1, count) for grad in grads]
    output_left = outer_sum(bases_low[1], output_low).astype(jnp.bfloat16)
    output_left = output_left.reshape(shards, piece, output_columns)

    def triple_part(row):
        return jnp.dot(joint_backs[row], firsts[row], preferred_element_type=jnp.float32)

    def triple_rest(rows, head):
        return jnp.concatenate([rows, *soap_rows(rows, bases_full[0], moments[2 + head])])

    bases_full = bases_full.transpose(2, 0, 1, 3, 4).reshape(3, width, width)
    feed_rows = jnp.concatenate(
        [
            owned,
            *soap_rows(owned[:expand_height], bases_full[1], moments[0]),
            *soap_rows(owned[expand_height:], bases_full[2], moments[1]),
        ]
    )
    settled = jnp.concatenate(
        [cut_rows(feed_rows), output_left.reshape(shards, -1, piece)], axis=1
    )
    early = [triple_part(row) for row in order[:-1]]
    joint_backs[order[-1]], early, settled = tied(joint_backs[order[-1]], early, settled)
    settled = exchange(settled)
    output_left = settled[:, feed_rows.shape[0] :].reshape(shards, piece, output_columns)
    output_left = far_sum(output_left)
    part = sum(early, triple_part(order[-1])).astype(jnp.bfloat16)
    part = part.reshape(shards, 3, HEAD_DIM, width).swapaxes(0, 1)
    part = part.reshape(outer, groups // outer, shards, -1, width)
    if split == 2:
        part = halved(part, "outer", 0).swapaxes(0, 1)
        rows = far_sum(exchange(part))
        mine = lax.dynamic_index_in_dim(rows, core, 0, keepdims=False)
        other = lax.dynamic_index_in_dim(rows, 1 - core, 0, keepdims=False)
        head_rows = by_core(mine, swap(other))
    else:
        head_rows = [far_sum(exchange(near_sum(part)))]
    triple_done = [triple_rest(rows, head) for head, rows in enumerate(head_rows)]
    output_turned = plain_product(output_left, right_low).astype(jnp.bfloat16)
    output_turned = near_sum(
        output_turned.reshape(piece, outer, -1, output_columns).transpose(1, 2, 0, 3)
    ).astype(jnp.float32)
    output_average, output_variance, output_direction = adam_step(
        output_turned, output_first, output_second
    )
    output_wide = doubled(doubled(output_direction.astype(jnp.bfloat16), "core"), "outer")
    output_wide = output_wide.reshape(groups, piece, output_columns).swapaxes(0, 1)
    output_middle = back_product(output_wide.reshape(piece, width), right_low)
    output_middle = doubled(output_middle.astype(jnp.bfloat16), "seq")
    output_back = plain_product(bases_low[1], output_middle.reshape(width, output_columns))
    triple_done = merged(*[cut_rows(rows) for rows in triple_done])
    triple_lows, triple_turns, triple_steps = zip(
        *[jnp.split(done, 3, axis=1) for done in triple_done]
    )

    def settled_piece(start, height, size):
        return settled[:, start : start + height].reshape(-1, piece)[:size].astype(jnp.float32)

    expand_gradient, expand_turned_grad, expand_back = (
        settled_piece(start, expand_height, expand_rows).T
        for start in (0, feed_height, feed_height + expand_height)
    )
    shrink_gradient, shrink_turned_grad, shrink_back = (
        settled_piece(start, shrink_height, shrink_rows)
        for start in (
            expand_height,
            feed_height + 2 * expand_height,
            feed_height + 2 * expand_height + shrink_height,
        )
    )
    expand_average, expand_variance, _ = adam_step(expand_turned_grad, expand_first, expand_second)
    shrink_average, shrink_variance, _ = adam_step(shrink_turned_grad, shrink_first, shrink_second)
    triple_turned = from_heads(triple_turns).T
    triple_back = from_heads(triple_steps).T
    triple_gradient = from_heads(triple_lows).T
    triple_average, triple_variance, _ = adam_step(triple_turned, triple_first, triple_second)
    changes = [outer_sum(joint_back, triple_rows) for joint_back in joint_backs]
    if split == 2:
        own, other = by_length(*changes)
        first_change = own + swap(other.astype(jnp.bfloat16)).astype(jnp.float32)
    else:
        first_change = changes[0]
    first_input, first_gain = first_back(first_change)
    token_gradient = (middle_back + first_input).astype(jnp.bfloat16).reshape(tokens.shape)
    gains_gradient = jnp.stack([first_gain, second_gain])
    for axis in ("core", "outer", "seq"):
        members = range(lax.axis_size(axis))
        for step in range(len(members).bit_length() - 1):
            pairs = [(member, member ^ (1 << step)) for member in members]
            gains_gradient = gains_gradient + lax.ppermute(gains_gradient, axis, pairs)
    gains_average, gains_variance, gains_direction = adam_step(
        gains_gradient, gains_first, gains_second
    )
    output_gradient = output_low.astype(jnp.float32)
    triple_updated = (triple_weight - WEIGHT_RATES[0] * triple_back) * (
        1.0 - WEIGHT_RATES[0] * DECAY_RATE
    )
    output_updated = (output_weight - WEIGHT_RATES[1] * output_back) * (
        1.0 - WEIGHT_RATES[1] * DECAY_RATE
    )
    expand_updated = (expand_weight - WEIGHT_RATES[2] * expand_back) * (
        1.0 - WEIGHT_RATES[2] * DECAY_RATE
    )
    shrink_updated = (shrink_weight - WEIGHT_RATES[3] * shrink_back) * (
        1.0 - WEIGHT_RATES[3] * DECAY_RATE
    )
    gains_updated = norm_gains - GAINS_RATE * gains_direction
    return (
        mixed,
        token_gradient,
        triple_gradient,
        output_gradient,
        expand_gradient,
        shrink_gradient,
        gains_gradient,
        triple_average,
        triple_variance,
        triple_updated,
        triple_updated.astype(jnp.bfloat16),
        output_average,
        output_variance,
        output_updated,
        output_updated.astype(jnp.bfloat16),
        expand_average,
        expand_variance,
        expand_updated,
        expand_updated.astype(jnp.bfloat16),
        shrink_average,
        shrink_variance,
        shrink_updated,
        shrink_updated.astype(jnp.bfloat16),
        gains_average,
        gains_variance,
        gains_updated,
    )


def solution(mesh):
    in_specs = (
        P(("outer", "core"), "seq", None),
        P(("outer", "core"), "seq", None),
        P(("outer", "core")),
        P("seq", ("outer", "core")),
        P("seq", ("outer", "core")),
        P("seq", ("outer", "core")),
        P(("outer", "core"), "seq"),
        P(),
        P(None, "seq", None),
        P(("outer", "core"), None),
        P("seq", ("outer", "core")),
        P("seq", ("outer", "core")),
        P("seq", ("outer", "core")),
        P("seq", ("outer", "core")),
        P("seq", ("outer", "core")),
        P("seq", ("outer", "core")),
        P(("outer", "core"), "seq"),
        P(("outer", "core"), "seq"),
        P(),
        P(),
    )
    out_specs = (
        P(("outer", "core"), "seq", None),
        P(("outer", "core"), "seq", None),
        P("seq", ("outer", "core")),
        P("seq", ("outer", "core")),
        P("seq", ("outer", "core")),
        P(("outer", "core"), "seq"),
        P(),
        P("seq", ("outer", "core")),
        P("seq", ("outer", "core")),
        P("seq", ("outer", "core")),
        P("seq", ("outer", "core")),
        P("seq", ("outer", "core")),
        P("seq", ("outer", "core")),
        P("seq", ("outer", "core")),
        P("seq", ("outer", "core")),
        P("seq", ("outer", "core")),
        P("seq", ("outer", "core")),
        P("seq", ("outer", "core")),
        P("seq", ("outer", "core")),
        P(("outer", "core"), "seq"),
        P(("outer", "core"), "seq"),
        P(("outer", "core"), "seq"),
        P(("outer", "core"), "seq"),
        P(),
        P(),
        P(),
    )
    groups = mesh.shape["fsdp"]
    devices = mesh.devices.reshape(mesh.shape["seq"], groups // 2, 2)
    split = Mesh(devices, ("seq", "outer", "core"))
    return jax.shard_map(body, mesh=split, in_specs=in_specs, out_specs=out_specs, check_vma=False)
```
